128 devices in a mesh: row: 32 (over z, y_hi, x), ch: 4 (over y_lo, core).
Axes of the slice: x: 4, y: 4 (y_hi: 2, y_lo: 2; y = y_hi * 2 + y_lo), z: 4, core: 2. Of those that a mesh axis runs over, the one named last changes fastest.
Arguments:
- features: bfloat16 [4, 64, 384, 128], P(None, 'row', 'ch'), may hold values from -4 to 4
- gain_in: bfloat16 [384], P('ch'), may hold values from 0.25 to 1.75
- w_conv: bfloat16 [27, 384, 384], P(None, 'ch'), may hold values from -0.0625 to 0.0625
- gain_attn: bfloat16 [384], P('ch'), may hold values from 0.25 to 1.75
- w_qkv: bfloat16 [384, 1152], replicated, may hold values from -8 to 8
- w_out: bfloat16 [384, 384], replicated, may hold values from -0.4375 to 0.4375
- cotangent: bfloat16 [4, 64, 384, 128], P(None, 'row', 'ch'), may hold values from -4 to 4
Outputs:
- grad_features: bfloat16 [4, 64, 384, 128], P(None, 'row', 'ch')
- grad_weights: float32 [27, 384, 384], P(None, 'ch')
The draws below stay inside these ranges and needn't reach their ends.
All inputs are finite; a program needn't handle non-finite values.
Results may differ from the reference program's by a relative error of at most 0.015.
Values may be sent and summed in bfloat16 or wider, within the bound.
A program may use at most 192 MiB of HBM per device.

```python
import math
import jax
import jax.numpy as jnp
from jax import lax

C = 384
WIDTH = 128
FRAMES = 4
HEIGHT = 64


def draw_w_qkv(key, part):
    key = jax.random.fold_in(key, 11)
    key_base = jax.random.fold_in(key, 0)
    key_other = jax.random.fold_in(key, 3)
    key_sign_q = jax.random.fold_in(key, 4)
    key_sign_k = jax.random.fold_in(key, 5)
    base = jax.random.truncated_normal(key_base, -4.0, 4.0, (C, 3 * C), jnp.float32) / math.sqrt(C)
    positions = jnp.arange(C)
    identity = (positions[:, None] == positions[None, :]).astype(jnp.float32)
    sign_query = jax.random.rademacher(key_sign_q, (1, C)).astype(jnp.float32)
    sign_key = jax.random.rademacher(key_sign_k, (1, C)).astype(jnp.float32)
    other = jax.random.truncated_normal(key_other, -4.0, 4.0, (C, C), jnp.float32) / math.sqrt(C)
    query_part = 1.35 * (identity * sign_query + 0.6 * base[:, :C])
    key_part = 1.35 * (identity * sign_key + 0.6 * other)
    whole = jnp.concatenate([query_part, key_part, base[:, 2 * C:]], axis=1)
    return jnp.clip(whole, -8.0, 8.0).astype(jnp.bfloat16)


def level_of(key, extent, cuts, smallest, top_value):
    def one(axis_at, blocks):
        heights = jax.random.uniform(jax.random.fold_in(jax.random.fold_in(key, 6), axis_at), (blocks,), jnp.float32, smallest / len(cuts), top_value / len(cuts))
        return jnp.repeat(jnp.exp(heights), extent[axis_at] // blocks).reshape((-1,) + (1,) * (len(extent) - axis_at - 1))

    loudness = one(*cuts[0])
    for cut in cuts[1:]:
        loudness = loudness * one(*cut)
    return loudness


def scatter_about(own_key, shape, width, bound, cuts=(), dtype=jnp.bfloat16):
    values = jax.random.normal(own_key, shape, jnp.float32) * width
    if len(cuts) > 0:
        values = level_of(own_key, shape, cuts, -0.22, 0.18) * values
    return jnp.clip(values, min=-bound, max=bound).astype(dtype)


def setup_inputs(seed: int = 0) -> dict:
    key_list = jax.random.split(jax.random.key(seed), 8)
    return {
        "features": scatter_about(key_list[0], (FRAMES, HEIGHT, C, WIDTH), 1.0, 4.0, ((1, 32), (2, 4))),
        "gain_in": jnp.clip(1.0 + 0.15 * jax.random.normal(key_list[1], (C,), jnp.float32), 0.25, 1.75).astype(jnp.bfloat16),
        "w_conv": scatter_about(key_list[2], (27, C, C), (27 * C) ** -0.5, 0.0625, ((1, 4),)),
        "gain_attn": jnp.clip(1.0 + 0.15 * jax.random.normal(key_list[3], (C,), jnp.float32), 0.25, 1.75).astype(jnp.bfloat16),
        "w_qkv": draw_w_qkv(jax.random.fold_in(key_list[7], 71), 0),
        "w_out": scatter_about(key_list[5], (C, C), (C // 2) ** -0.5, 0.4375),
        "cotangent": scatter_about(key_list[6], (FRAMES, HEIGHT, C, WIDTH), 1.0, 4.0, ((1, 32), (2, 4))),
    }


EPSILON = 1e-06

def silu_slope(before):
    sig_value = jax.nn.sigmoid(before)
    return sig_value * (1.0 + before * (1.0 - sig_value))

def tap_slab(padded, t_off, h_off, frames, row_count, col_count):
    return jnp.concatenate([padded[t_off:t_off + frames, h_off:h_off + row_count, :, w_off:w_off + col_count] for w_off in range(3)], axis=2)

def conv_forward(padded, weights, frames, row_count, col_count):
    running = jnp.zeros((frames, row_count, weights.shape[1], col_count), jnp.float32)
    for t_off in range(3):
        for h_off in range(3):
            slab = tap_slab(padded, t_off, h_off, frames, row_count, col_count).astype(jnp.float32)
            kernel = jnp.concatenate([weights[9 * t_off + 3 * h_off + w_off] for w_off in range(3)], axis=1).astype(jnp.float32)
            running = running + jnp.einsum('ok,fhkw->fhow', kernel, slab)
    return running

def conv_input_grad(padded, weights, frames, row_count, col_count):
    running = jnp.zeros((frames, row_count, weights.shape[2], col_count), jnp.float32)
    for t_off in range(3):
        for h_off in range(3):
            slab = tap_slab(padded, t_off, h_off, frames, row_count, col_count).astype(jnp.float32)
            kernel = jnp.concatenate([weights[9 * (2 - t_off) + 3 * (2 - h_off) + (2 - w_off)].T for w_off in range(3)], axis=1).astype(jnp.float32)
            running = running + jnp.einsum('ik,fhkw->fhiw', kernel, slab)
    return running

def conv_weight_grad(padded, grad_out, frames, row_count, col_count):
    grad_f32 = grad_out.astype(jnp.float32)
    pieces = []
    for t_off in range(3):
        for h_off in range(3):
            slab = tap_slab(padded, t_off, h_off, frames, row_count, col_count).astype(jnp.float32)
            block = jnp.einsum('fhow,fhkw->ok', grad_f32, slab)
            pieces.append(block.reshape(block.shape[0], 3, -1).transpose(1, 0, 2))
    return jnp.concatenate(pieces, axis=0)

def frame_grads(inputs):
    queries, keys_all, values_all, grad_o = inputs
    score_scale = 1.0 / math.sqrt(C)
    scores = jnp.dot(queries, keys_all.T, preferred_element_type=jnp.float32) * score_scale
    row_max = lax.optimization_barrier(jnp.max(scores, -1, keepdims=True))
    exp_scores = jnp.exp(scores - row_max)
    totals = lax.optimization_barrier(jnp.sum(exp_scores, -1, keepdims=True))
    prob_f32 = exp_scores / totals
    prob_bf16 = prob_f32.astype(jnp.bfloat16)
    attended = jnp.dot(prob_bf16, values_all, preferred_element_type=jnp.float32).astype(jnp.bfloat16)
    row_delta = lax.optimization_barrier(jnp.sum(grad_o.astype(jnp.float32) * lax.optimization_barrier(attended).astype(jnp.float32), -1, keepdims=True))
    grad_p = jnp.dot(grad_o, values_all.T, preferred_element_type=jnp.float32)
    grad_s = (prob_f32 * (grad_p - row_delta) * score_scale).astype(jnp.bfloat16)
    grad_q = jnp.dot(grad_s, keys_all, preferred_element_type=jnp.float32).astype(jnp.bfloat16)
    grad_k = jnp.dot(grad_s.T, queries, preferred_element_type=jnp.float32).astype(jnp.bfloat16)
    grad_v = jnp.dot(prob_bf16.T, grad_o, preferred_element_type=jnp.float32).astype(jnp.bfloat16)
    return (grad_q, grad_k, grad_v)

def reference(features, gain_in, w_conv, gain_attn, w_qkv, w_out, cotangent):
    frames, row_count, channels, col_count = features.shape
    feat_f32 = features.astype(jnp.float32)
    gain_in_col = gain_in.astype(jnp.float32)[:, None]
    gain_attn_col = gain_attn.astype(jnp.float32)[:, None]
    inv_in = lax.rsqrt(lax.optimization_barrier(jnp.mean(feat_f32 * feat_f32, 2, keepdims=True)) + EPSILON)
    before = feat_f32 * inv_in * gain_in_col
    activated = jax.nn.silu(before).astype(jnp.bfloat16)
    padded_act = jnp.pad(activated, ((2, 0), (1, 1), (0, 0), (1, 1)))
    conv_out = conv_forward(padded_act, w_conv, frames, row_count, col_count)
    residual = (feat_f32 + conv_out).astype(jnp.bfloat16)
    res_f32 = lax.optimization_barrier(residual).astype(jnp.float32)
    inv_attn = lax.rsqrt(lax.optimization_barrier(jnp.mean(res_f32 * res_f32, 2, keepdims=True)) + EPSILON)
    normed = (res_f32 * inv_attn * gain_attn_col).astype(jnp.bfloat16)
    normed_tok = normed.transpose(0, 1, 3, 2)
    cot_tok = cotangent.transpose(0, 1, 3, 2)
    projected = jnp.dot(normed_tok, w_qkv, preferred_element_type=jnp.float32).astype(jnp.bfloat16)
    grad_o = jnp.dot(cot_tok, w_out.T, preferred_element_type=jnp.float32).astype(jnp.bfloat16)
    token_count = row_count * col_count
    queries = projected[..., :channels].reshape(frames, token_count, channels)
    keys_all = projected[..., channels:2 * channels].reshape(frames, token_count, channels)
    values_all = projected[..., 2 * channels:].reshape(frames, token_count, channels)
    grad_q, grad_k, grad_v = lax.map(frame_grads, (queries, keys_all, values_all, grad_o.reshape(frames, token_count, channels)))
    grad_qkv = jnp.concatenate([grad_q, grad_k, grad_v], -1).reshape(frames, row_count, col_count, 3 * channels)
    grad_normed = jnp.dot(grad_qkv, w_qkv.T, preferred_element_type=jnp.float32).astype(jnp.bfloat16).transpose(0, 1, 3, 2)
    scaled = lax.optimization_barrier(grad_normed).astype(jnp.float32) * gain_attn_col
    inner = lax.optimization_barrier(jnp.mean(res_f32 * scaled, 2, keepdims=True))
    grad_res = cotangent.astype(jnp.float32) + inv_attn * scaled - res_f32 * inv_attn * inv_attn * inv_attn * inner
    grad_conv_out = grad_res.astype(jnp.bfloat16)
    padded_grad = jnp.pad(grad_conv_out, ((0, 2), (1, 1), (0, 0), (1, 1)))
    grad_act = conv_input_grad(padded_grad, w_conv, frames, row_count, col_count)
    scaled_in = grad_act * silu_slope(before) * gain_in_col
    inner_in = lax.optimization_barrier(jnp.mean(feat_f32 * scaled_in, 2, keepdims=True))
    grad_features = grad_res + inv_in * scaled_in - feat_f32 * inv_in * inv_in * inv_in * inner_in
    cell_scale = 1.0 / math.sqrt(frames * row_count * col_count)
    grad_weights = conv_weight_grad(padded_act, grad_conv_out, frames, row_count, col_count) * cell_scale
    return (grad_features.astype(jnp.bfloat16), grad_weights)
```

```python
import functools
import math

import jax
import jax.numpy as jnp
from jax import lax
from jax.experimental import pallas as pl
from jax.experimental.pallas import tpu as pltpu
from jax.sharding import PartitionSpec as P

EPSILON = 1e-06
MESH = pl.DeviceIdType.MESH
F32 = jnp.float32
BF16 = jnp.bfloat16
ROWS = 32
CH = 4
VMEM_BYTES = 56 * 1024 * 1024


def coords():
    return lax.axis_index("row"), lax.axis_index("ch")


def exchange(cid, ins, outs, plan, count):
    def body(*refs):
        srcs, dsts = refs[: len(ins)], refs[len(ins) : len(ins) + len(outs)]
        send, recv, own = refs[len(ins) + len(outs) :]
        remote, local, peers = plan(srcs, dsts)
        barrier = pltpu.get_barrier_semaphore()
        for peer in peers:
            pl.semaphore_signal(barrier, inc=1, device_id=peer, device_id_type=MESH)
        here = [pltpu.make_async_copy(s, d, own.at[k]) for k, (s, d) in enumerate(local)]
        for copy in here:
            copy.start()
        pl.semaphore_wait(barrier, len(peers))
        there = [
            pltpu.make_async_remote_copy(
                src_ref=s,
                dst_ref=d,
                send_sem=send.at[k],
                recv_sem=recv.at[k],
                device_id=peer,
                device_id_type=MESH,
            )
            for k, (s, d, peer) in enumerate(remote)
        ]
        for copy in there:
            copy.start()
        for copy in here:
            copy.wait()
        for copy in there:
            copy.wait()

    return pl.pallas_call(
        body,
        out_shape=[jax.ShapeDtypeStruct(s, t) for s, t in outs],
        in_specs=[pl.BlockSpec(memory_space=pl.ANY)] * len(ins),
        out_specs=[pl.BlockSpec(memory_space=pl.ANY)] * len(outs),
        scratch_shapes=[
            pltpu.SemaphoreType.DMA((count[0],)),
            pltpu.SemaphoreType.DMA((count[0],)),
            pltpu.SemaphoreType.DMA((max(count[1], 1),)),
        ],
        compiler_params=pltpu.CompilerParams(collective_id=cid, has_side_effects=True),
        name="exchange_%d" % cid,
    )(*ins)


def compute(body, outs, *ins, scratch=(), name):
    return pl.pallas_call(
        body,
        out_shape=[jax.ShapeDtypeStruct(s, t) for s, t in outs],
        in_specs=[pl.BlockSpec(memory_space=pltpu.VMEM)] * len(ins),
        out_specs=[pl.BlockSpec(memory_space=pltpu.VMEM)] * len(outs),
        scratch_shapes=list(scratch),
        compiler_params=pltpu.CompilerParams(vmem_limit_bytes=VMEM_BYTES),
        name=name,
    )(*ins)


def dot(a, b):
    return lax.dot_general(a, b, (((1,), (0,)), ((), ())), preferred_element_type=F32)


def dot_t(a, b):
    return lax.dot_general(a, b, (((1,), (1,)), ((), ())), preferred_element_type=F32)


def move(block, by):
    lanes = block.shape[1]
    at = lax.broadcasted_iota(jnp.int32, block.shape, 1)
    if by > 0:
        return jnp.where(at == 0, 0.0, pltpu.roll(block, 1, axis=1))
    return jnp.where(at == lanes - 1, 0.0, pltpu.roll(block, lanes - 1, axis=1))


def ch_peers(r, c):
    return [(r, lax.rem(c + d, CH)) for d in range(1, CH)]


def near_rows(r):
    return lax.rem(r + ROWS - 1, ROWS), lax.rem(r + 1, ROWS)


def start_plan(srcs, dsts):
    feat, cot, gain = srcs
    all_feat, prev_feat, next_feat, cot_frame, all_gain = dsts
    r, c = coords()
    low, high = near_rows(r)
    remote, peers = [], []
    for row, c_to in ch_peers(r, c):
        remote.append((feat, all_feat.at[c], (row, c_to)))
        remote.append((cot.at[c_to], cot_frame.at[c], (row, c_to)))
        remote.append((gain, all_gain.at[c], (row, c_to)))
        peers.append((row, c_to))
    for d in range(CH):
        c_to = lax.rem(c + d, CH)
        remote.append((feat.at[:, 1], prev_feat.at[c], (high, c_to)))
        remote.append((feat.at[:, 0], next_feat.at[c], (low, c_to)))
        peers += [(high, c_to), (low, c_to)]
    local = [(feat, all_feat.at[c]), (cot.at[c], cot_frame.at[c]), (gain, all_gain.at[c])]
    return remote, local, peers


def frame_plan(srcs, dsts):
    (res,), (res_frame,) = srcs, dsts
    r, c = coords()
    peers = ch_peers(r, c)
    remote = [(res.at[to[1]], res_frame.at[c], to) for to in peers]
    return remote, [(res.at[c], res_frame.at[c])], peers


def key_peers(r, c):
    z, yx = r // 8, lax.rem(r, 8)
    return [(lax.rem(z + d, 4) * 8 + yx, c) for d in range(1, 4)]


def query_peers(r, c):
    z, y, x = r // 8, lax.rem(r // 4, 2), lax.rem(r, 4)
    found = []
    for dy in range(2):
        for dx in range(4):
            if dy or dx:
                found.append((z * 8 + lax.rem(y + dy, 2) * 4 + lax.rem(x + dx, 4), c))
    return found


def gather_plan(srcs, dsts):
    q, g, k, v = srcs
    all_q, all_g, all_k, all_v = dsts
    r, c = coords()
    z, yx = r // 8, lax.rem(r, 8)
    remote, peers = [], []
    for to in query_peers(r, c):
        remote += [(q, all_q.at[yx], to), (g, all_g.at[yx], to)]
        peers.append(to)
    for to in key_peers(r, c):
        remote += [(k, all_k.at[z], to), (v, all_v.at[z], to)]
        peers.append(to)
    local = [(q, all_q.at[yx]), (g, all_g.at[yx]), (k, all_k.at[z]), (v, all_v.at[z])]
    return remote, local, peers


def stats_plan(srcs, dsts):
    (own,), (every,) = srcs, dsts
    r, c = coords()
    yx = lax.rem(r, 8)
    peers = query_peers(r, c)
    return [(own, every.at[yx], to) for to in peers], [(own, every.at[yx])], peers


def back_plan(srcs, dsts):
    dq, dk, dv = srcs
    all_q, all_k, all_v = dsts
    r, c = coords()
    z, yx = r // 8, lax.rem(r, 8)
    remote, peers = [], []
    for to in query_peers(r, c):
        remote.append((dq.at[lax.rem(to[0], 8)], all_q.at[yx], to))
        peers.append(to)
    for to in key_peers(r, c):
        at = to[0] // 8
        remote += [(dk.at[at], all_k.at[z], to), (dv.at[at], all_v.at[z], to)]
        peers.append(to)
    local = [(dq.at[yx], all_q.at[yx]), (dk.at[z], all_k.at[z]), (dv.at[z], all_v.at[z])]
    return remote, local, peers


def grad_plan(srcs, dsts):
    (g,), (own, prev_g, next_g) = srcs, dsts
    r, c = coords()
    low, high = near_rows(r)
    remote, peers = [], []
    for to in ch_peers(r, c):
        remote.append((g.at[to[1]], own.at[c], to))
        peers.append(to)
    for d in range(CH):
        c_to = lax.rem(c + d, CH)
        remote.append((g.at[c_to, 1], prev_g.at[c], (high, c_to)))
        remote.append((g.at[c_to, 0], next_g.at[c], (low, c_to)))
        peers += [(high, c_to), (low, c_to)]
    return remote, [(g.at[c], own.at[c])], peers


def row_peers(r, c):
    return [(lax.rem(r + d, ROWS), c) for d in range(1, ROWS)]


def scatter_plan(srcs, dsts):
    weight, part, inner = srcs
    all_weight, all_part, all_inner = dsts
    r, c = coords()
    remote, peers = [], []
    for to in ch_peers(r, c):
        remote += [(part.at[to[1]], all_part.at[c], to), (inner, all_inner.at[c], to)]
        peers.append(to)
    for to in row_peers(r, c):
        remote.append((weight.at[to[0]], all_weight.at[r], to))
        peers.append(to)
    local = [
        (part.at[c], all_part.at[c]),
        (inner, all_inner.at[c]),
        (weight.at[r], all_weight.at[r]),
    ]
    return remote, local, peers


def spread_plan(srcs, dsts):
    (own,), (every,) = srcs, dsts
    r, c = coords()
    peers = row_peers(r, c)
    return [(own, every.at[r], to) for to in peers], [(own, every.at[r])], peers


def sigmoid(v):
    return 1.0 / (1.0 + jnp.exp(-v))


def conv_kernel(feat, all_feat, prev_feat, next_feat, gains, w, cot, w_out, res, act, inv_in, grad_o, full):
    r = lax.axis_index("row")
    gain = jnp.concatenate([gains[b, 0] for b in range(CH)], 0).astype(F32)
    for f in range(4):
        for h in range(4):
            blocks = [
                prev_feat[b, f] if h == 0 else next_feat[b, f] if h == 3 else all_feat[b, f, h - 1]
                for b in range(CH)
            ]
            x = jnp.concatenate(blocks, 0).astype(F32)
            inv = lax.rsqrt(jnp.mean(x * x, 0, keepdims=True) + EPSILON)
            before = x * inv * gain
            a = before * sigmoid(before)
            if h == 0:
                a = jnp.where(r == 0, 0.0, a)
            elif h == 3:
                a = jnp.where(r == ROWS - 1, 0.0, a)
            else:
                inv_in[2 * f + h - 1, :] = inv[0]
            act[:, pl.ds((4 * f + h) * 128, 128)] = a.astype(BF16)
    for f in range(4):
        acc = jnp.zeros((288, 256), F32)
        for t in range(3):
            source = f + t - 2
            if source < 0:
                continue
            for h in range(3):
                acc += dot(w[3 * t + h], act[:, pl.ds((4 * source + h) * 128, 256)])
        for h in range(2):
            y = acc[:, 128 * h : 128 * h + 128]
            out = move(y[:96], 1) + y[96:192] + move(y[192:], -1)
            res[f, h] = (feat[f, h].astype(F32) + out).astype(BF16)
    for b in range(CH):
        for h in range(2):
            full[pl.ds(96 * b, 96), pl.ds(128 * h, 128)] = cot[b, h]
    grad_o[...] = dot(w_out[...], full[...]).astype(BF16)


def attn_norm(res_frame, full):
    for b in range(CH):
        for h in range(2):
            full[pl.ds(96 * b, 96), pl.ds(128 * h, 128)] = res_frame[b, h]
    x = full[...].astype(F32)
    return x, lax.rsqrt(jnp.mean(x * x, 0, keepdims=True) + EPSILON)


def project_kernel(res_frame, gains, w_qkv, q, k, v, full):
    gain = jnp.concatenate([gains[b, 1] for b in range(CH)], 0).astype(F32)
    gain = jnp.concatenate([gain, gain], 1)
    x, inv = attn_norm(res_frame, full)
    normed = (x * inv * gain).astype(BF16).astype(F32)
    out = dot(normed.T.astype(BF16), w_qkv[...])
    q[...] = out[:, :384].T.astype(BF16)
    k[...] = out[:, 384:768].astype(BF16)
    v[...] = out[:, 768:].astype(BF16)


def stats_kernel(scale, q, g, k, v, stats):
    keys, values = k[...].reshape(1024, 384), v[...].reshape(1024, 384)

    def step(b, carry):
        s = dot(keys, q[b]) * scale
        m = jnp.max(s, 0, keepdims=True)
        e = jnp.exp(s - m)
        stats[b, 0:1, :] = m
        stats[b, 1:2, :] = jnp.sum(e, 0, keepdims=True)
        stats[b, 2:3, :] = jnp.sum(e * dot(values, g[b]), 0, keepdims=True)
        stats[b, 3:8, :] = jnp.zeros((5, 256), F32)
        return carry

    lax.fori_loop(0, 8, step, 0)


def attn_kernel(scale, q, g, k, v, stats, dq, dk, dv, acc_k, acc_v):
    keys, values = k[...].reshape(1024, 384), v[...].reshape(1024, 384)
    keys_t = keys.T
    acc_k[...] = jnp.zeros_like(acc_k)
    acc_v[...] = jnp.zeros_like(acc_v)

    def step(b, carry):
        part = [stats[i, b] for i in range(8)]
        top = functools.reduce(jnp.maximum, [p[0:1] for p in part])
        shift = [jnp.exp(p[0:1] - top) for p in part]
        total = sum(p[1:2] * w for p, w in zip(part, shift))
        delta = sum(p[2:3] * w for p, w in zip(part, shift)) / total
        offset = top + jnp.log(total)
        prob = jnp.exp(dot(keys, q[b]) * scale - offset)
        grad_s = (prob * (dot(values, g[b]) - delta)).astype(BF16)
        acc_v[...] += dot_t(prob.astype(BF16), g[b])
        acc_k[...] += dot_t(grad_s, q[b])
        dq[b] = (dot(keys_t, grad_s) * scale).astype(BF16)
        return carry

    lax.fori_loop(0, 8, step, 0)
    dk[...] = (acc_k[...] * scale).astype(BF16).reshape(4, 256, 384)
    dv[...] = acc_v[...].astype(BF16).reshape(4, 256, 384)


def total_of(ref, count):
    total = ref[0].astype(F32)
    for i in range(1, count):
        total += ref[i].astype(F32)
    return total


def residual_kernel(dq, dk, dv, res_frame, cot, gains, w_qkv, grad, full, cot_full):
    gain = jnp.concatenate([gains[b, 1] for b in range(CH)], 0).astype(F32)
    gain = jnp.concatenate([gain, gain], 1)
    x, inv = attn_norm(res_frame, full)
    for b in range(CH):
        for h in range(2):
            cot_full[pl.ds(96 * b, 96), pl.ds(128 * h, 128)] = cot[b, h]
    w = w_qkv[...]
    normed = (
        dot(w[:, :384], total_of(dq, 8).astype(BF16))
        + dot_t(w[:, 384:768], total_of(dk, 4).astype(BF16))
        + dot_t(w[:, 768:], total_of(dv, 4).astype(BF16))
    )
    scaled = normed.astype(BF16).astype(F32) * gain
    inner = jnp.mean(x * scaled, 0, keepdims=True)
    out = cot_full[...].astype(F32) + inv * scaled - x * (inv * inv * inv * inner)
    for b in range(CH):
        for h in range(2):
            grad[b, h] = out[96 * b : 96 * b + 96, 128 * h : 128 * h + 128].astype(BF16)


def grad_kernel(own, prev_g, next_g, act, w_t, all_feat, inv_in, gains, weight, part, inner, rows, lines):
    r = lax.axis_index("row")
    for f in range(4):
        rows[f, 0] = jnp.where(r == 0, 0.0, prev_g[f].astype(F32)).astype(BF16)
        rows[f, 1] = own[f, 0]
        rows[f, 2] = own[f, 1]
        rows[f, 3] = jnp.where(r == ROWS - 1, 0.0, next_g[f].astype(F32)).astype(BF16)
    moved = []
    for f in range(4):
        both = []
        for h in range(2):
            y = own[f, h].astype(F32)
            both.append(jnp.concatenate([move(y, -1), y, move(y, 1)], 0).astype(BF16))
        moved.append(jnp.concatenate(both, 1))
    for t in range(3):
        for h in range(3):
            acc = jnp.zeros((288, 384), F32)
            for f in range(4):
                source = f + t - 2
                if source < 0:
                    continue
                acc += dot_t(moved[f], act[:, pl.ds((4 * source + h) * 128, 256)])
            for lane in range(3):
                at = (3 * (3 * t + h) + lane) * 288
                weight[pl.ds(at, 288), :] = acc[:, 128 * lane : 128 * lane + 128].astype(BF16)
    weight[pl.ds(27 * 288, 416), :] = jnp.zeros((416, 128), BF16)
    for f in range(4):
        for h in range(3):
            for k in range(2):
                lines[f, pl.ds(96 * h, 96), pl.ds(128 * k, 128)] = rows[f, 2 - h + k]
    gain = jnp.concatenate([gains[b, 0] for b in range(CH)], 0).astype(F32)
    for f in range(4):
        acc = jnp.zeros((1152, 256), F32)
        for t in range(3):
            source = f + 2 - t
            if source > 3:
                continue
            acc += dot(w_t[t], lines[source])
        for h in range(2):
            y = acc[:, 128 * h : 128 * h + 128]
            out = move(y[:384], -1) + y[384:768] + move(y[768:], 1)
            x = jnp.concatenate([all_feat[b, f, h] for b in range(CH)], 0).astype(F32)
            before = x * inv_in[2 * f + h : 2 * f + h + 1, :] * gain
            sig = sigmoid(before)
            slope = sig * (1.0 + before * (1.0 - sig))
            inner[2 * f + h : 2 * f + h + 1, :] = jnp.sum(x * slope * gain * out, 0, keepdims=True)
            for b in range(CH):
                part[b, f, h] = out[96 * b : 96 * b + 96].astype(BF16)


def finish_kernel(feat, own, part, inner, inv_in, gain_own, weights, out, weight):
    total = total_of(weights, ROWS)
    weight[...] = total.astype(BF16)
    mean = (inner[0] + inner[1] + inner[2] + inner[3]) / 384.0
    gain = gain_own[0].astype(F32)
    for f in range(4):
        for h in range(2):
            x = feat[f, h].astype(F32)
            inv = inv_in[2 * f + h : 2 * f + h + 1, :]
            act = part[0, f, h].astype(F32)
            for b in range(1, CH):
                act += part[b, f, h].astype(F32)
            before = x * inv * gain
            sig = sigmoid(before)
            scaled = act * (sig * (1.0 + before * (1.0 - sig))) * gain
            cube = inv * inv * inv * mean[2 * f + h : 2 * f + h + 1, :]
            out[f, h] = (own[f, h].astype(F32) + inv * scaled - x * cube).astype(BF16)


def widen_kernel(scale, flat, out):
    for k in range(9):
        for lane in range(3):
            piece = flat[pl.ds((3 * k + lane) * 288, 288), :].astype(F32) * scale
            out[pl.ds(288 * k, 288), pl.ds(128 * lane, 128)] = piece


def on_device(features, gain_in, w_conv, gain_attn, w_qkv, w_out, cotangent):
    scale = 1.0 / math.sqrt(384)
    gain_own = jnp.broadcast_to(jnp.stack([gain_in, gain_attn])[:, :, None], (2, 96, 128))
    w_rows = w_conv.reshape(9, 288, 384)
    w_t = w_conv.reshape(3, 3, 3, 96, 384).transpose(0, 2, 4, 1, 3).reshape(3, 1152, 288)
    all_feat, prev_feat, next_feat, cot_frame, gains = exchange(
        0,
        (features, cotangent, gain_own),
        [
            ((4, 4, 2, 96, 128), BF16),
            ((4, 4, 96, 128), BF16),
            ((4, 4, 96, 128), BF16),
            ((4, 2, 96, 128), BF16),
            ((4, 2, 96, 128), BF16),
        ],
        start_plan,
        (17, 3),
    )
    res, act, inv_in, grad_o = compute(
        conv_kernel,
        [((4, 2, 96, 128), BF16), ((384, 2048), BF16), ((8, 128), F32), ((384, 256), BF16)],
        features,
        all_feat,
        prev_feat,
        next_feat,
        gains,
        w_rows,
        cot_frame,
        w_out,
        scratch=[pltpu.VMEM((384, 256), BF16)],
        name="conv",
    )
    (res_frame,) = exchange(1, (res,), [((4, 2, 96, 128), BF16)], frame_plan, (3, 1))
    q, k, v = compute(
        project_kernel,
        [((384, 256), BF16), ((256, 384), BF16), ((256, 384), BF16)],
        res_frame,
        gains,
        w_qkv,
        scratch=[pltpu.VMEM((384, 256), BF16)],
        name="project",
    )
    all_q, all_g, all_k, all_v = exchange(
        2,
        (q, grad_o, k, v),
        [((8, 384, 256), BF16)] * 2 + [((4, 256, 384), BF16)] * 2,
        gather_plan,
        (20, 4),
    )
    (stats,) = compute(
        functools.partial(stats_kernel, scale),
        [((8, 8, 256), F32)],
        all_q,
        all_g,
        all_k,
        all_v,
        name="stats",
    )
    (all_stats,) = exchange(3, (stats,), [((8, 8, 8, 256), F32)], stats_plan, (7, 1))
    dq, dk, dv = compute(
        functools.partial(attn_kernel, scale),
        [((8, 384, 256), BF16)] + [((4, 256, 384), BF16)] * 2,
        all_q,
        all_g,
        all_k,
        all_v,
        all_stats,
        scratch=[pltpu.VMEM((1024, 384), F32)] * 2,
        name="attn",
    )
    all_dq, all_dk, all_dv = exchange(
        4,
        (dq, dk, dv),
        [((8, 384, 256), BF16)] + [((4, 256, 384), BF16)] * 2,
        back_plan,
        (13, 3),
    )
    (grad,) = compute(
        residual_kernel,
        [((4, 2, 96, 128), BF16)],
        all_dq,
        all_dk,
        all_dv,
        res_frame,
        cot_frame,
        gains,
        w_qkv,
        scratch=[pltpu.VMEM((384, 256), BF16)] * 2,
        name="residual",
    )
    own, prev_g, next_g = exchange(
        5,
        (grad,),
        [((4, 2, 96, 128), BF16), ((4, 96, 128), BF16), ((4, 96, 128), BF16)],
        grad_plan,
        (11, 1),
    )
    weight, part, inner = compute(
        grad_kernel,
        [((8192, 128), BF16), ((4, 4, 2, 96, 128), BF16), ((8, 128), F32)],
        own,
        prev_g,
        next_g,
        act,
        w_t,
        all_feat,
        inv_in,
        gains,
        scratch=[pltpu.VMEM((4, 4, 96, 128), BF16), pltpu.VMEM((4, 288, 256), BF16)],
        name="grad",
    )
    weights, parts, inners = exchange(
        6,
        (weight.reshape(ROWS, 256, 128), part, inner),
        [((ROWS, 256, 128), BF16), ((4, 4, 2, 96, 128), BF16), ((4, 8, 128), F32)],
        scatter_plan,
        (37, 3),
    )
    out, weight_sum = compute(
        finish_kernel,
        [((4, 2, 96, 128), BF16), ((256, 128), BF16)],
        features,
        own,
        parts,
        inners,
        inv_in,
        gain_own,
        weights,
        name="finish",
    )
    (flat,) = exchange(7, (weight_sum,), [((ROWS, 256, 128), BF16)], spread_plan, (31, 1))
    cell_scale = 1.0 / math.sqrt(32768)
    (grad_weights,) = compute(
        functools.partial(widen_kernel, cell_scale),
        [((2592, 384), F32)],
        flat.reshape(8192, 128),
        name="widen",
    )
    return out, grad_weights.reshape(27, 96, 384)


def solution(mesh):
    return jax.shard_map(
        on_device,
        mesh=mesh,
        in_specs=(
            P(None, "row", "ch", None),
            P("ch"),
            P(None, "ch", None),
            P("ch"),
            P(),
            P(),
            P(None, "row", "ch", None),
        ),
        out_specs=(P(None, "row", "ch", None), P(None, "ch", None)),
        check_vma=False,
    )
```

```python
import functools
import math

import jax
import jax.numpy as jnp
from jax import lax
from jax.experimental import pallas as pl
from jax.experimental.pallas import tpu as pltpu
from jax.sharding import PartitionSpec as P

EPSILON = 1e-06
MESH = pl.DeviceIdType.MESH
F32 = jnp.float32
BF16 = jnp.bfloat16
ROWS = 32
CH = 4
VMEM_BYTES = 56 * 1024 * 1024


def coords():
    return lax.axis_index("row"), lax.axis_index("ch")


def place(r, c):
    return lax.rem(r, 4), lax.rem(r // 4, 2), r // 8, c // 2, lax.rem(c, 2)


def device(x, y_hi, z, y_lo, core):
    return z * 8 + y_hi * 4 + x, y_lo * 2 + core


def owner(f, row):
    x, y_hi, z, _, _ = place(row, 0)
    return device(x, f // 2, z, f % 2, y_hi)


class Links:
    def __init__(self, send, recv):
        self.send, self.recv, self.sent, self.at = send, recv, [], 0

    def greet(self, peers, count):
        barrier = pltpu.get_barrier_semaphore()
        for peer in peers:
            pl.semaphore_signal(barrier, inc=1, device_id=peer, device_id_type=MESH)
        pl.semaphore_wait(barrier, count)

    def copy(self, src, dst, to, own=None, recv=None):
        k = self.at
        self.at += 1
        mark = self.recv.at[k if recv is None else recv]
        far = pltpu.make_async_remote_copy(
            src_ref=src,
            dst_ref=dst,
            send_sem=self.send.at[k],
            recv_sem=mark,
            device_id=to,
            device_id_type=MESH,
        )
        if own is None:
            far.start()
        else:
            pl.when(jnp.logical_not(own))(far.start)
            pl.when(own)(pltpu.make_async_copy(src, dst, mark).start)
        self.sent.append((far, own))
        return far

    def arrive(self, dst, k):
        pltpu.make_async_copy(dst, dst, self.recv.at[k]).wait()

    def finish(self):
        for far, own in self.sent:
            if own is None:
                far.wait_send()
            else:
                pl.when(jnp.logical_not(own))(far.wait_send)


def exchange(cid, body, ins, outs, count, local=0, held=(), made=()):
    def kernel(*refs):
        n_in, n_out = len(ins) + len(held), len(outs) + len(made)
        send, recv, own = refs[n_in + n_out :]
        body(Links(send, recv), own, refs[:n_in], refs[n_in : n_in + n_out])

    far = pl.BlockSpec(memory_space=pl.ANY)
    near = pl.BlockSpec(memory_space=pltpu.VMEM)
    return pl.pallas_call(
        kernel,
        out_shape=[jax.ShapeDtypeStruct(s, t) for s, t in list(outs) + list(made)],
        in_specs=[far] * len(ins) + [near] * len(held),
        out_specs=[far] * len(outs) + [near] * len(made),
        scratch_shapes=[
            pltpu.SemaphoreType.DMA((count,)),
            pltpu.SemaphoreType.DMA((count,)),
            pltpu.SemaphoreType.DMA((max(local, 1),)),
        ],
        compiler_params=pltpu.CompilerParams(
            collective_id=cid, has_side_effects=True, vmem_limit_bytes=VMEM_BYTES
        ),
        name="exchange_%d" % cid,
    )(*ins, *held)


def simple(plan):
    def body(links, own, srcs, dsts):
        remote, local, peers = plan(srcs, dsts)
        here = [pltpu.make_async_copy(s, d, own.at[k]) for k, (s, d) in enumerate(local)]
        for copy in here:
            copy.start()
        links.greet(peers, len(peers))
        there = [links.copy(s, d, to) for s, d, to in remote]
        for copy in here:
            copy.wait()
        for copy in there:
            copy.wait_recv()
        links.finish()

    return body


def compute(body, outs, *ins, scratch=(), name):
    return pl.pallas_call(
        body,
        out_shape=[jax.ShapeDtypeStruct(s, t) for s, t in outs],
        in_specs=[pl.BlockSpec(memory_space=pltpu.VMEM)] * len(ins),
        out_specs=[pl.BlockSpec(memory_space=pltpu.VMEM)] * len(outs),
        scratch_shapes=list(scratch),
        compiler_params=pltpu.CompilerParams(vmem_limit_bytes=VMEM_BYTES),
        name=name,
    )(*ins)


def dot(a, b):
    return lax.dot_general(a, b, (((1,), (0,)), ((), ())), preferred_element_type=F32)


def dot_t(a, b):
    return lax.dot_general(a, b, (((1,), (1,)), ((), ())), preferred_element_type=F32)


def move(block, by):
    lanes = block.shape[1]
    at = lax.broadcasted_iota(jnp.int32, block.shape, 1)
    if by > 0:
        return jnp.where(at == 0, 0.0, pltpu.roll(block, 1, axis=1))
    return jnp.where(at == lanes - 1, 0.0, pltpu.roll(block, lanes - 1, axis=1))


def ch_peers(r, c):
    return [(r, lax.rem(c + d, CH)) for d in range(1, CH)]


def near_rows(r):
    return lax.rem(r + ROWS - 1, ROWS), lax.rem(r + 1, ROWS)


def same(a, b):
    return jnp.logical_and(a[0] == b[0], a[1] == b[1])


def greet_frames(links, me, sources, targets):
    barrier = pltpu.get_barrier_semaphore()
    for peer in sources:
        def tell(peer=peer):
            pl.semaphore_signal(barrier, inc=1, device_id=peer, device_id_type=MESH)

        pl.when(jnp.logical_not(same(peer, me)))(tell)
    _, y_hi, _, _, core = place(*me)
    pl.semaphore_wait(barrier, len(targets) - 1 + (core - y_hi) * (core - y_hi))


def start_body(links, own, srcs, dsts):
    feat, cot, gain, w = srcs
    all_feat, prev_feat, next_feat, cot_frame, all_gain, w_t = dsts
    r, c = coords()
    low, high = near_rows(r)
    x, y_hi, z, y_lo, core = place(r, c)
    here = [
        pltpu.make_async_copy(feat, all_feat.at[c], own.at[0]),
        pltpu.make_async_copy(gain, all_gain.at[c], own.at[1]),
    ]
    for copy in here:
        copy.start()
    targets = [owner(f, r) for f in range(4)]
    sources = [(z * 8 + core * 4 + x, b) for b in range(4)]
    others = ch_peers(r, c) + [(row, b) for row in (low, high) for b in range(CH)]
    greet_frames(links, (r, c), sources + others, targets + others)
    for f in range(4):
        links.copy(cot.at[f], cot_frame.at[c], targets[f], own=same(targets[f], (r, c)), recv=c)
    there = []
    for to in ch_peers(r, c):
        there.append(links.copy(feat, all_feat.at[c], to))
        there.append(links.copy(gain, all_gain.at[c], to))
    for d in range(CH):
        c_to = lax.rem(c + d, CH)
        there.append(links.copy(feat.at[:, 1], prev_feat.at[c], (high, c_to)))
        there.append(links.copy(feat.at[:, 0], next_feat.at[c], (low, c_to)))
    for t in range(3):
        for k in range(3):
            piece = jnp.concatenate([w[9 * t + 3 * h + k] for h in range(3)], 0)
            w_t[t, pl.ds(384 * k, 384), :] = piece.T
    for copy in here:
        copy.wait()
    for b in range(CH):
        links.arrive(cot_frame.at[b], b)
    for copy in there:
        copy.wait_recv()
    links.finish()


def frame_body(links, own, srcs, dsts):
    (res,), (res_frame,) = srcs, dsts
    r, c = coords()
    x, y_hi, z, y_lo, core = place(r, c)
    targets = [owner(f, r) for f in range(4)]
    sources = [(z * 8 + core * 4 + x, b) for b in range(4)]
    greet_frames(links, (r, c), sources, targets)
    for f in range(4):
        links.copy(res.at[f], res_frame.at[c], targets[f], own=same(targets[f], (r, c)), recv=c)
    for b in range(CH):
        links.arrive(res_frame.at[b], b)
    links.finish()


def key_peers(r, c):
    return [(lax.rem(r + 8 * d, ROWS), c) for d in range(1, 4)]


def query_peers(r, c):
    x, y_hi, z, y_lo, core = place(r, c)
    found = []
    for dk in range(2):
        for dx in range(4):
            if dk or dx:
                found.append(device(lax.rem(x + dx, 4), y_hi, z, y_lo, lax.rem(core + dk, 2)))
    return found


def gather_body(links, own, srcs, dsts):
    q, g, k, v = srcs
    all_q, all_g, all_k, all_v = dsts
    r, c = coords()
    x, y_hi, z, y_lo, core = place(r, c)
    slot = core * 4 + x
    local = [(q, all_q.at[slot]), (g, all_g.at[slot]), (k, all_k.at[z]), (v, all_v.at[z])]
    here = [pltpu.make_async_copy(s, d, own.at[i]) for i, (s, d) in enumerate(local)]
    for copy in here:
        copy.start()
    sibling = (r, y_lo * 2 + 1 - core)
    x_next, x_back = lax.rem(x + 1, 4), lax.rem(x + 3, 4)
    z_next, z_back = lax.rem(z + 1, 4), lax.rem(z + 3, 4)
    xs = [device(i, y_hi, z, y_lo, core) for i in (x_next, x_back)]
    zs = [device(x, y_hi, i, y_lo, core) for i in (z_next, z_back)]
    links.greet(xs + zs + [sibling], 5)
    pairs = ((q, all_q, core * 4, x, xs), (g, all_g, core * 4, x, xs), (k, all_k, 0, z, zs), (v, all_v, 0, z, zs))
    first = []
    for src, dst, base, i, to in pairs:
        first.append([links.copy(src, dst.at[base + i], peer) for peer in to])
    relayed = []
    for src, dst in ((q, all_q), (g, all_g)):
        relayed.append(links.copy(src, dst.at[slot], sibling))
    for n in (0, 2, 1, 3):
        src, dst, base, i, to = pairs[n]
        half = src.shape[0] // 2
        for side in range(2):
            first[n][side].wait_recv()
            came = base + lax.rem(i + 3 - 2 * side, 4)
            part = dst.at[came, pl.ds(half * side, half)]
            relayed.append(links.copy(part, part, to[side]))
            if n < 2:
                relayed.append(links.copy(dst.at[came], dst.at[came], sibling))
    far = relayed[2:]
    for n, dst in ((0, all_q), (6, all_g)):
        at = core * 4 + lax.rem(x + 2, 4)
        far[n].wait_recv()
        far[n + 2].wait_recv()
        relayed.append(links.copy(dst.at[at], dst.at[at], sibling))
    for n, copy in enumerate(relayed):
        if n - 2 not in (0, 2, 6, 8):
            copy.wait_recv()
    for copy in here:
        copy.wait()
    links.finish()


def stats_plan(srcs, dsts):
    (own,), (every,) = srcs, dsts
    r, c = coords()
    x, y_hi, z, y_lo, core = place(r, c)
    slot = core * 4 + x
    peers = query_peers(r, c)
    return [(own, every.at[slot], to) for to in peers], [(own, every.at[slot])], peers


def back_plan(srcs, dsts):
    dq, dk, dv = srcs
    all_q, all_k, all_v = dsts
    r, c = coords()
    x, y_hi, z, y_lo, core = place(r, c)
    slot = core * 4 + x
    remote, peers = [], []
    for to in query_peers(r, c):
        there = lax.rem(to[1], 2) * 4 + lax.rem(to[0], 4)
        remote.append((dq.at[there], all_q.at[slot], to))
        peers.append(to)
    for to in key_peers(r, c):
        at = to[0] // 8
        remote += [(dk.at[at], all_k.at[z], to), (dv.at[at], all_v.at[z], to)]
        peers.append(to)
    local = [(dq.at[slot], all_q.at[slot]), (dk.at[z], all_k.at[z]), (dv.at[z], all_v.at[z])]
    return remote, local, peers


def grad_body(links, own, srcs, dsts):
    (g,), (mine, prev_g, next_g) = srcs, dsts
    r, c = coords()
    x, y_hi, z, y_lo, core = place(r, c)
    frame = y_hi * 2 + y_lo
    row = z * 8 + core * 4 + x
    row_low, row_high = near_rows(row)
    low, high = near_rows(r)
    targets = [(row, b) for b in range(CH)]
    around = [(i, b) for i in (row_low, row_high) for b in range(CH)]
    sources = [owner(f, i) for i in (r, low, high) for f in range(4)]
    greet_frames(links, (r, c), sources, targets + around)
    for b in range(CH):
        links.copy(g.at[b], mine.at[frame], (row, b), own=same((row, b), (r, c)), recv=frame)
    for b in range(CH):
        links.copy(g.at[b, 1], prev_g.at[frame], (row_high, b), recv=4 + frame)
        links.copy(g.at[b, 0], next_g.at[frame], (row_low, b), recv=8 + frame)
    for f in range(4):
        links.arrive(mine.at[f], f)
        links.arrive(prev_g.at[f], 4 + f)
        links.arrive(next_g.at[f], 8 + f)
    links.finish()


def row_peers(r, c):
    return [(lax.rem(r + d, ROWS), c) for d in range(1, ROWS)]


def scatter_plan(srcs, dsts):
    weight, part, inner = srcs
    all_weight, all_part, all_inner = dsts
    r, c = coords()
    remote, peers = [], []
    for to in ch_peers(r, c):
        remote += [(part.at[to[1]], all_part.at[c], to), (inner, all_inner.at[c], to)]
        peers.append(to)
    for to in row_peers(r, c):
        remote.append((weight.at[to[0]], all_weight.at[r], to))
        peers.append(to)
    local = [
        (part.at[c], all_part.at[c]),
        (inner, all_inner.at[c]),
        (weight.at[r], all_weight.at[r]),
    ]
    return remote, local, peers


def spread_plan(srcs, dsts):
    (own,), (every,) = srcs, dsts
    r, c = coords()
    peers = row_peers(r, c)
    return [(own, every.at[r], to) for to in peers], [(own, every.at[r])], peers


def sigmoid(v):
    return 1.0 / (1.0 + jnp.exp(-v))


def conv_kernel(feat, all_feat, prev_feat, next_feat, gains, w, cot, w_out, res, act, inv_in, grad_o, full):
    r = lax.axis_index("row")
    gain = jnp.concatenate([gains[b, 0] for b in range(CH)], 0).astype(F32)
    for f in range(4):
        for h in range(4):
            blocks = [
                prev_feat[b, f] if h == 0 else next_feat[b, f] if h == 3 else all_feat[b, f, h - 1]
                for b in range(CH)
            ]
            x = jnp.concatenate(blocks, 0).astype(F32)
            inv = lax.rsqrt(jnp.mean(x * x, 0, keepdims=True) + EPSILON)
            before = x * inv * gain
            a = before * sigmoid(before)
            if h == 0:
                a = jnp.where(r == 0, 0.0, a)
            elif h == 3:
                a = jnp.where(r == ROWS - 1, 0.0, a)
            else:
                inv_in[2 * f + h - 1, :] = inv[0]
            act[:, pl.ds((4 * f + h) * 128, 128)] = a.astype(BF16)
    for f in range(4):
        acc = jnp.zeros((288, 256), F32)
        for t in range(3):
            source = f + t - 2
            if source < 0:
                continue
            for h in range(3):
                acc += dot(w[3 * t + h], act[:, pl.ds((4 * source + h) * 128, 256)])
        for h in range(2):
            y = acc[:, 128 * h : 128 * h + 128]
            out = move(y[:96], 1) + y[96:192] + move(y[192:], -1)
            res[f, h] = (feat[f, h].astype(F32) + out).astype(BF16)
    for b in range(CH):
        for h in range(2):
            full[pl.ds(96 * b, 96), pl.ds(128 * h, 128)] = cot[b, h]
    grad_o[...] = dot(w_out[...], full[...]).astype(BF16)


def attn_norm(res_frame, full):
    for b in range(CH):
        for h in range(2):
            full[pl.ds(96 * b, 96), pl.ds(128 * h, 128)] = res_frame[b, h]
    x = full[...].astype(F32)
    return x, lax.rsqrt(jnp.mean(x * x, 0, keepdims=True) + EPSILON)


def project_kernel(res_frame, gains, w_qkv, q, k, v, full):
    gain = jnp.concatenate([gains[b, 1] for b in range(CH)], 0).astype(F32)
    gain = jnp.concatenate([gain, gain], 1)
    x, inv = attn_norm(res_frame, full)
    normed = (x * inv * gain).astype(BF16).astype(F32)
    out = dot(normed.T.astype(BF16), w_qkv[...])
    q[...] = out[:, :384].T.astype(BF16)
    k[...] = out[:, 384:768].astype(BF16)
    v[...] = out[:, 768:].astype(BF16)


def stats_kernel(scale, q, g, k, v, stats):
    keys, values = k[...].reshape(1024, 384), v[...].reshape(1024, 384)

    def step(b, carry):
        s = dot(keys, q[b]) * scale
        m = jnp.max(s, 0, keepdims=True)
        e = jnp.exp(s - m)
        stats[0, pl.ds(b, 1), :] = m
        stats[1, pl.ds(b, 1), :] = jnp.sum(e, 0, keepdims=True)
        stats[2, pl.ds(b, 1), :] = jnp.sum(e * dot(values, g[b]), 0, keepdims=True)
        return carry

    lax.fori_loop(0, 8, step, 0)


def attn_kernel(scale, q, g, k, v, stats, dq, dk, dv, acc_k, acc_v):
    keys, values = k[...].reshape(1024, 384), v[...].reshape(1024, 384)
    keys_t = keys.T
    acc_k[...] = jnp.zeros_like(acc_k)
    acc_v[...] = jnp.zeros_like(acc_v)

    def step(b, carry):
        part = [[stats[i, n, pl.ds(b, 1), :] for n in range(3)] for i in range(8)]
        top = functools.reduce(jnp.maximum, [p[0] for p in part])
        shift = [jnp.exp(p[0] - top) for p in part]
        total = sum(p[1] * w for p, w in zip(part, shift))
        delta = sum(p[2] * w for p, w in zip(part, shift)) / total
        offset = top + jnp.log(total)
        prob = jnp.exp(dot(keys, q[b]) * scale - offset)
        grad_s = (prob * (dot(values, g[b]) - delta)).astype(BF16)
        acc_v[...] += dot_t(prob.astype(BF16), g[b])
        acc_k[...] += dot_t(grad_s, q[b])
        dq[b] = (dot(keys_t, grad_s) * scale).astype(BF16)
        return carry

    lax.fori_loop(0, 8, step, 0)
    dk[...] = (acc_k[...] * scale).astype(BF16).reshape(4, 256, 384)
    dv[...] = acc_v[...].astype(BF16).reshape(4, 256, 384)


def total_of(ref, count):
    total = ref[0].astype(F32)
    for i in range(1, count):
        total += ref[i].astype(F32)
    return total


def residual_kernel(dq, dk, dv, res_frame, cot, gains, w_qkv, grad, full, cot_full):
    gain = jnp.concatenate([gains[b, 1] for b in range(CH)], 0).astype(F32)
    gain = jnp.concatenate([gain, gain], 1)
    x, inv = attn_norm(res_frame, full)
    for b in range(CH):
        for h in range(2):
            cot_full[pl.ds(96 * b, 96), pl.ds(128 * h, 128)] = cot[b, h]
    w = w_qkv[...]
    normed = (
        dot(w[:, :384], total_of(dq, 8).astype(BF16))
        + dot_t(w[:, 384:768], total_of(dk, 4).astype(BF16))
        + dot_t(w[:, 768:], total_of(dv, 4).astype(BF16))
    )
    scaled = normed.astype(BF16).astype(F32) * gain
    inner = jnp.mean(x * scaled, 0, keepdims=True)
    out = cot_full[...].astype(F32) + inv * scaled - x * (inv * inv * inv * inner)
    for b in range(CH):
        for h in range(2):
            grad[b, h] = out[96 * b : 96 * b + 96, 128 * h : 128 * h + 128].astype(BF16)


def grad_kernel(own, prev_g, next_g, act, w_t, all_feat, inv_in, gains, weight, part, inner, rows, lines):
    r = lax.axis_index("row")
    for f in range(4):
        rows[f, 0] = jnp.where(r == 0, 0.0, prev_g[f].astype(F32)).astype(BF16)
        rows[f, 1] = own[f, 0]
        rows[f, 2] = own[f, 1]
        rows[f, 3] = jnp.where(r == ROWS - 1, 0.0, next_g[f].astype(F32)).astype(BF16)
    moved = []
    for f in range(4):
        both = []
        for h in range(2):
            y = own[f, h].astype(F32)
            both.append(jnp.concatenate([move(y, -1), y, move(y, 1)], 0).astype(BF16))
        moved.append(jnp.concatenate(both, 1))
    for t in range(3):
        for h in range(3):
            acc = jnp.zeros((288, 384), F32)
            for f in range(4):
                source = f + t - 2
                if source < 0:
                    continue
                acc += dot_t(moved[f], act[:, pl.ds((4 * source + h) * 128, 256)])
            for lane in range(3):
                at = (3 * (3 * t + h) + lane) * 288
                weight[pl.ds(at, 288), :] = acc[:, 128 * lane : 128 * lane + 128].astype(BF16)
    weight[pl.ds(27 * 288, 416), :] = jnp.zeros((416, 128), BF16)
    for f in range(4):
        for h in range(3):
            for k in range(2):
                lines[f, pl.ds(96 * h, 96), pl.ds(128 * k, 128)] = rows[f, 2 - h + k]
    gain = jnp.concatenate([gains[b, 0] for b in range(CH)], 0).astype(F32)
    for f in range(4):
        acc = jnp.zeros((1152, 256), F32)
        for t in range(3):
            source = f + 2 - t
            if source > 3:
                continue
            acc += dot(w_t[t], lines[source])
        for h in range(2):
            y = acc[:, 128 * h : 128 * h + 128]
            out = move(y[:384], -1) + y[384:768] + move(y[768:], 1)
            x = jnp.concatenate([all_feat[b, f, h] for b in range(CH)], 0).astype(F32)
            before = x * inv_in[2 * f + h : 2 * f + h + 1, :] * gain
            sig = sigmoid(before)
            slope = sig * (1.0 + before * (1.0 - sig))
            inner[2 * f + h : 2 * f + h + 1, :] = jnp.sum(x * slope * gain * out, 0, keepdims=True)
            for b in range(CH):
                part[b, f, h] = out[96 * b : 96 * b + 96].astype(BF16)


def finish_kernel(feat, own, part, inner, inv_in, gain_own, weights, out, weight):
    total = total_of(weights, ROWS)
    weight[...] = total.astype(BF16)
    mean = (inner[0] + inner[1] + inner[2] + inner[3]) / 384.0
    gain = gain_own[0].astype(F32)
    for f in range(4):
        for h in range(2):
            x = feat[f, h].astype(F32)
            inv = inv_in[2 * f + h : 2 * f + h + 1, :]
            act = part[0, f, h].astype(F32)
            for b in range(1, CH):
                act += part[b, f, h].astype(F32)
            before = x * inv * gain
            sig = sigmoid(before)
            scaled = act * (sig * (1.0 + before * (1.0 - sig))) * gain
            cube = inv * inv * inv * mean[2 * f + h : 2 * f + h + 1, :]
            out[f, h] = (own[f, h].astype(F32) + inv * scaled - x * cube).astype(BF16)


def widen_kernel(scale, flat, out):
    for k in range(9):
        for lane in range(3):
            piece = flat[pl.ds((3 * k + lane) * 288, 288), :].astype(F32) * scale
            out[pl.ds(288 * k, 288), pl.ds(128 * lane, 128)] = piece


def on_device(features, gain_in, w_conv, gain_attn, w_qkv, w_out, cotangent):
    scale = 1.0 / math.sqrt(384)
    gain_own = jnp.broadcast_to(jnp.stack([gain_in, gain_attn])[:, :, None], (2, 96, 128))
    w_rows = w_conv.reshape(9, 288, 384)
    all_feat, prev_feat, next_feat, cot_frame, gains, w_t = exchange(
        0,
        start_body,
        (features, cotangent, gain_own),
        [
            ((4, 4, 2, 96, 128), BF16),
            ((4, 4, 96, 128), BF16),
            ((4, 4, 96, 128), BF16),
            ((4, 2, 96, 128), BF16),
            ((4, 2, 96, 128), BF16),
        ],
        18,
        local=2,
        held=(w_conv,),
        made=[((3, 1152, 288), BF16)],
    )
    res, act, inv_in, grad_o = compute(
        conv_kernel,
        [((4, 2, 96, 128), BF16), ((384, 2048), BF16), ((8, 128), F32), ((384, 256), BF16)],
        features,
        all_feat,
        prev_feat,
        next_feat,
        gains,
        w_rows,
        cot_frame,
        w_out,
        scratch=[pltpu.VMEM((384, 256), BF16)],
        name="conv",
    )
    (res_frame,) = exchange(1, frame_body, (res,), [((4, 2, 96, 128), BF16)], 4)
    q, k, v = compute(
        project_kernel,
        [((384, 256), BF16), ((256, 384), BF16), ((256, 384), BF16)],
        res_frame,
        gains,
        w_qkv,
        scratch=[pltpu.VMEM((384, 256), BF16)],
        name="project",
    )
    all_q, all_g, all_k, all_v = exchange(
        2,
        gather_body,
        (q, grad_o, k, v),
        [((8, 384, 256), BF16)] * 2 + [((4, 256, 384), BF16)] * 2,
        24,
        local=4,
    )
    (stats,) = compute(
        functools.partial(stats_kernel, scale),
        [((3, 8, 256), F32)],
        all_q,
        all_g,
        all_k,
        all_v,
        name="stats",
    )
    (all_stats,) = exchange(3, simple(stats_plan), (stats,), [((8, 3, 8, 256), F32)], 7, local=1)
    dq, dk, dv = compute(
        functools.partial(attn_kernel, scale),
        [((8, 384, 256), BF16)] + [((4, 256, 384), BF16)] * 2,
        all_q,
        all_g,
        all_k,
        all_v,
        all_stats,
        scratch=[pltpu.VMEM((1024, 384), F32)] * 2,
        name="attn",
    )
    all_dq, all_dk, all_dv = exchange(
        4,
        simple(back_plan),
        (dq, dk, dv),
        [((8, 384, 256), BF16)] + [((4, 256, 384), BF16)] * 2,
        13,
        local=3,
    )
    (grad,) = compute(
        residual_kernel,
        [((4, 2, 96, 128), BF16)],
        all_dq,
        all_dk,
        all_dv,
        res_frame,
        cot_frame,
        gains,
        w_qkv,
        scratch=[pltpu.VMEM((384, 256), BF16)] * 2,
        name="residual",
    )
    own, prev_g, next_g = exchange(
        5,
        grad_body,
        (grad,),
        [((4, 2, 96, 128), BF16), ((4, 96, 128), BF16), ((4, 96, 128), BF16)],
        12,
    )
    weight, part, inner = compute(
        grad_kernel,
        [((8192, 128), BF16), ((4, 4, 2, 96, 128), BF16), ((8, 128), F32)],
        own,
        prev_g,
        next_g,
        act,
        w_t,
        all_feat,
        inv_in,
        gains,
        scratch=[pltpu.VMEM((4, 4, 96, 128), BF16), pltpu.VMEM((4, 288, 256), BF16)],
        name="grad",
    )
    weights, parts, inners = exchange(
        6,
        simple(scatter_plan),
        (weight.reshape(ROWS, 256, 128), part, inner),
        [((ROWS, 256, 128), BF16), ((4, 4, 2, 96, 128), BF16), ((4, 8, 128), F32)],
        37,
        local=3,
    )
    out, weight_sum = compute(
        finish_kernel,
        [((4, 2, 96, 128), BF16), ((256, 128), BF16)],
        features,
        own,
        parts,
        inners,
        inv_in,
        gain_own,
        weights,
        name="finish",
    )
    (flat,) = exchange(7, simple(spread_plan), (weight_sum,), [((ROWS, 256, 128), BF16)], 31, local=1)
    cell_scale = 1.0 / math.sqrt(32768)
    (grad_weights,) = compute(
        functools.partial(widen_kernel, cell_scale),
        [((2592, 384), F32)],
        flat.reshape(8192, 128),
        name="widen",
    )
    return out, grad_weights.reshape(27, 96, 384)


def solution(mesh):
    return jax.shard_map(
        on_device,
        mesh=mesh,
        in_specs=(
            P(None, "row", "ch", None),
            P("ch"),
            P(None, "ch", None),
            P("ch"),
            P(),
            P(),
            P(None, "row", "ch", None),
        ),
        out_specs=(P(None, "row", "ch", None), P(None, "ch", None)),
        check_vma=False,
    )
```

```python
import functools
import math

import jax
import jax.numpy as jnp
from jax import lax
from jax.experimental import pallas as pl
from jax.experimental.pallas import tpu as pltpu
from jax.sharding import PartitionSpec as P

EPSILON = 1e-06
MESH = pl.DeviceIdType.MESH
F32 = jnp.float32
BF16 = jnp.bfloat16
ROWS = 32
CH = 4
VMEM_BYTES = 56 * 1024 * 1024


def coords():
    return lax.axis_index("row"), lax.axis_index("ch")


def place(r, c):
    return lax.rem(r, 4), lax.rem(r // 4, 2), r // 8, c // 2, lax.rem(c, 2)


def device(x, y_hi, z, y_lo, core):
    return z * 8 + y_hi * 4 + x, y_lo * 2 + core


def owner(f, row):
    x, y_hi, z, _, _ = place(row, 0)
    return device(x, f // 2, z, f % 2, y_hi)


class Links:
    def __init__(self, send, recv):
        self.send, self.recv, self.sent, self.at = send, recv, [], 0

    def greet(self, peers, count):
        barrier = pltpu.get_barrier_semaphore()
        for peer in peers:
            pl.semaphore_signal(barrier, inc=1, device_id=peer, device_id_type=MESH)
        pl.semaphore_wait(barrier, count)

    def copy(self, src, dst, to, own=None, recv=None):
        k = self.at
        self.at += 1
        mark = self.recv.at[k if recv is None else recv]
        far = pltpu.make_async_remote_copy(
            src_ref=src,
            dst_ref=dst,
            send_sem=self.send.at[k],
            recv_sem=mark,
            device_id=to,
            device_id_type=MESH,
        )
        if own is None:
            far.start()
        else:
            pl.when(jnp.logical_not(own))(far.start)
            pl.when(own)(pltpu.make_async_copy(src, dst, mark).start)
        self.sent.append((far, own))
        return far

    def arrive(self, dst, k):
        pltpu.make_async_copy(dst, dst, self.recv.at[k]).wait()

    def finish(self):
        for far, own in self.sent:
            if own is None:
                far.wait_send()
            else:
                pl.when(jnp.logical_not(own))(far.wait_send)


def exchange(cid, body, ins, outs, count, local=0, held=(), made=()):
    def kernel(*refs):
        n_in, n_out = len(ins) + len(held), len(outs) + len(made)
        send, recv, own = refs[n_in + n_out :]
        body(Links(send, recv), own, refs[:n_in], refs[n_in : n_in + n_out])

    far = pl.BlockSpec(memory_space=pl.ANY)
    near = pl.BlockSpec(memory_space=pltpu.VMEM)
    return pl.pallas_call(
        kernel,
        out_shape=[jax.ShapeDtypeStruct(s, t) for s, t in list(outs) + list(made)],
        in_specs=[far] * len(ins) + [near] * len(held),
        out_specs=[far] * len(outs) + [near] * len(made),
        scratch_shapes=[
            pltpu.SemaphoreType.DMA((count,)),
            pltpu.SemaphoreType.DMA((count,)),
            pltpu.SemaphoreType.DMA((max(local, 1),)),
        ],
        compiler_params=pltpu.CompilerParams(
            collective_id=cid, has_side_effects=True, vmem_limit_bytes=VMEM_BYTES
        ),
        name="exchange_%d" % cid,
    )(*ins, *held)


def fused(cid, body, held, made, scratch, count):
    def kernel(*refs):
        n_in, n_out = len(held), len(held) + len(made)
        send, recv = refs[-2:]
        body(Links(send, recv), refs[:n_in], refs[n_in:n_out], refs[n_out:-2])

    return pl.pallas_call(
        kernel,
        out_shape=[jax.ShapeDtypeStruct(s, t) for s, t, _ in made],
        in_specs=[pl.BlockSpec(memory_space=pltpu.VMEM)] * len(held),
        out_specs=[pl.BlockSpec(memory_space=m) for _, _, m in made],
        scratch_shapes=list(scratch) + [pltpu.SemaphoreType.DMA((count,))] * 2,
        compiler_params=pltpu.CompilerParams(
            collective_id=cid, has_side_effects=True, vmem_limit_bytes=VMEM_BYTES
        ),
        name="fused_%d" % cid,
    )(*held)


def simple(plan):
    def body(links, own, srcs, dsts):
        remote, local, peers = plan(srcs, dsts)
        here = [pltpu.make_async_copy(s, d, own.at[k]) for k, (s, d) in enumerate(local)]
        for copy in here:
            copy.start()
        links.greet(peers, len(peers))
        there = [links.copy(s, d, to) for s, d, to in remote]
        for copy in here:
            copy.wait()
        for copy in there:
            copy.wait_recv()
        links.finish()

    return body


def compute(body, outs, *ins, scratch=(), name):
    return pl.pallas_call(
        body,
        out_shape=[jax.ShapeDtypeStruct(s, t) for s, t in outs],
        in_specs=[pl.BlockSpec(memory_space=pltpu.VMEM)] * len(ins),
        out_specs=[pl.BlockSpec(memory_space=pltpu.VMEM)] * len(outs),
        scratch_shapes=list(scratch),
        compiler_params=pltpu.CompilerParams(vmem_limit_bytes=VMEM_BYTES),
        name=name,
    )(*ins)


def dot(a, b):
    return lax.dot_general(a, b, (((1,), (0,)), ((), ())), preferred_element_type=F32)


def dot_t(a, b):
    return lax.dot_general(a, b, (((1,), (1,)), ((), ())), preferred_element_type=F32)


def move(block, by):
    lanes = block.shape[1]
    at = lax.broadcasted_iota(jnp.int32, block.shape, 1)
    if by > 0:
        return jnp.where(at == 0, 0.0, pltpu.roll(block, 1, axis=1))
    return jnp.where(at == lanes - 1, 0.0, pltpu.roll(block, lanes - 1, axis=1))


def ch_peers(r, c):
    return [(r, lax.rem(c + d, CH)) for d in range(1, CH)]


def near_rows(r):
    return lax.rem(r + ROWS - 1, ROWS), lax.rem(r + 1, ROWS)


def same(a, b):
    return jnp.logical_and(a[0] == b[0], a[1] == b[1])


def greet_frames(links, me, sources, targets):
    barrier = pltpu.get_barrier_semaphore()
    for peer in sources:
        def tell(peer=peer):
            pl.semaphore_signal(barrier, inc=1, device_id=peer, device_id_type=MESH)

        pl.when(jnp.logical_not(same(peer, me)))(tell)
    _, y_hi, _, _, core = place(*me)
    pl.semaphore_wait(barrier, len(targets) - 1 + (core - y_hi) * (core - y_hi))


def start_body(links, own, srcs, dsts):
    feat, cot, gain, w = srcs
    all_feat, prev_feat, next_feat, cot_frame, all_gain, w_t = dsts
    r, c = coords()
    low, high = near_rows(r)
    x, y_hi, z, y_lo, core = place(r, c)
    here = [
        pltpu.make_async_copy(feat, all_feat.at[c], own.at[0]),
        pltpu.make_async_copy(gain, all_gain.at[c], own.at[1]),
    ]
    for copy in here:
        copy.start()
    targets = [owner(f, r) for f in range(4)]
    sources = [(z * 8 + core * 4 + x, b) for b in range(4)]
    others = ch_peers(r, c) + [(row, b) for row in (low, high) for b in range(CH)]
    greet_frames(links, (r, c), sources + others, targets + others)
    for f in range(4):
        links.copy(cot.at[f], cot_frame.at[c], targets[f], own=same(targets[f], (r, c)), recv=c)
    there = []
    for to in ch_peers(r, c):
        there.append(links.copy(feat, all_feat.at[c], to))
        there.append(links.copy(gain, all_gain.at[c], to))
    for d in range(CH):
        c_to = lax.rem(c + d, CH)
        there.append(links.copy(feat.at[:, 1], prev_feat.at[c], (high, c_to)))
        there.append(links.copy(feat.at[:, 0], next_feat.at[c], (low, c_to)))
    for t in range(3):
        for k in range(3):
            piece = jnp.concatenate([w[9 * t + 3 * h + k] for h in range(3)], 0)
            w_t[t, pl.ds(384 * k, 384), :] = piece.T
    for copy in here:
        copy.wait()
    for b in range(CH):
        links.arrive(cot_frame.at[b], b)
    for copy in there:
        copy.wait_recv()
    links.finish()


def frame_body(links, own, srcs, dsts):
    (res,), (res_frame,) = srcs, dsts
    r, c = coords()
    x, y_hi, z, y_lo, core = place(r, c)
    targets = [owner(f, r) for f in range(4)]
    sources = [(z * 8 + core * 4 + x, b) for b in range(4)]
    greet_frames(links, (r, c), sources, targets)
    for f in range(4):
        links.copy(res.at[f], res_frame.at[c], targets[f], own=same(targets[f], (r, c)), recv=c)
    for b in range(CH):
        links.arrive(res_frame.at[b], b)
    links.finish()


def key_peers(r, c):
    return [(lax.rem(r + 8 * d, ROWS), c) for d in range(1, 4)]


def query_peers(r, c):
    x, y_hi, z, y_lo, core = place(r, c)
    found = []
    for dk in range(2):
        for dx in range(4):
            if dk or dx:
                found.append(device(lax.rem(x + dx, 4), y_hi, z, y_lo, lax.rem(core + dk, 2)))
    return found


def gather_body(links, own, srcs, dsts):
    q, g, k, v = srcs
    all_q, all_g, all_k, all_v = dsts
    r, c = coords()
    x, y_hi, z, y_lo, core = place(r, c)
    slot = core * 4 + x
    local = [(q, all_q.at[slot]), (g, all_g.at[slot]), (k, all_k.at[z]), (v, all_v.at[z])]
    here = [pltpu.make_async_copy(s, d, own.at[i]) for i, (s, d) in enumerate(local)]
    for copy in here:
        copy.start()
    sibling = (r, y_lo * 2 + 1 - core)
    x_next, x_back = lax.rem(x + 1, 4), lax.rem(x + 3, 4)
    z_next, z_back = lax.rem(z + 1, 4), lax.rem(z + 3, 4)
    xs = [device(i, y_hi, z, y_lo, core) for i in (x_next, x_back)]
    zs = [device(x, y_hi, i, y_lo, core) for i in (z_next, z_back)]
    links.greet(xs + zs + [sibling], 5)
    pairs = ((q, all_q, core * 4, x, xs), (g, all_g, core * 4, x, xs), (k, all_k, 0, z, zs), (v, all_v, 0, z, zs))
    first = []
    for src, dst, base, i, to in pairs:
        first.append([links.copy(src, dst.at[base + i], peer) for peer in to])
    relayed = []
    for src, dst in ((q, all_q), (g, all_g)):
        relayed.append(links.copy(src, dst.at[slot], sibling))
    for n in (0, 2, 1, 3):
        src, dst, base, i, to = pairs[n]
        half = src.shape[0] // 2
        for side in range(2):
            first[n][side].wait_recv()
            came = base + lax.rem(i + 3 - 2 * side, 4)
            part = dst.at[came, pl.ds(half * side, half)]
            relayed.append(links.copy(part, part, to[side]))
            if n < 2:
                relayed.append(links.copy(dst.at[came], dst.at[came], sibling))
    far = relayed[2:]
    for n, dst in ((0, all_q), (6, all_g)):
        at = core * 4 + lax.rem(x + 2, 4)
        far[n].wait_recv()
        far[n + 2].wait_recv()
        relayed.append(links.copy(dst.at[at], dst.at[at], sibling))
    for n, copy in enumerate(relayed):
        if n - 2 not in (0, 2, 6, 8):
            copy.wait_recv()
    for copy in here:
        copy.wait()
    links.finish()


def stats_plan(srcs, dsts):
    (own,), (every,) = srcs, dsts
    r, c = coords()
    x, y_hi, z, y_lo, core = place(r, c)
    slot = core * 4 + x
    peers = query_peers(r, c)
    return [(own, every.at[slot], to) for to in peers], [(own, every.at[slot])], peers


def back_plan(srcs, dsts):
    dq, dk, dv = srcs
    all_q, all_k, all_v = dsts
    r, c = coords()
    x, y_hi, z, y_lo, core = place(r, c)
    slot = core * 4 + x
    remote, peers = [], []
    for to in query_peers(r, c):
        there = lax.rem(to[1], 2) * 4 + lax.rem(to[0], 4)
        remote.append((dq.at[there], all_q.at[slot], to))
        peers.append(to)
    for to in key_peers(r, c):
        at = to[0] // 8
        remote += [(dk.at[at], all_k.at[z], to), (dv.at[at], all_v.at[z], to)]
        peers.append(to)
    local = [(dq.at[slot], all_q.at[slot]), (dk.at[z], all_k.at[z]), (dv.at[z], all_v.at[z])]
    return remote, local, peers


def grad_body(links, own, srcs, dsts):
    (g,), (mine, prev_g, next_g) = srcs, dsts
    r, c = coords()
    x, y_hi, z, y_lo, core = place(r, c)
    frame = y_hi * 2 + y_lo
    row = z * 8 + core * 4 + x
    row_low, row_high = near_rows(row)
    low, high = near_rows(r)
    targets = [(row, b) for b in range(CH)]
    around = [(i, b) for i in (row_low, row_high) for b in range(CH)]
    sources = [owner(f, i) for i in (r, low, high) for f in range(4)]
    greet_frames(links, (r, c), sources, targets + around)
    for b in range(CH):
        links.copy(g.at[b], mine.at[frame], (row, b), own=same((row, b), (r, c)), recv=frame)
    for b in range(CH):
        links.copy(g.at[b, 1], prev_g.at[frame], (row_high, b), recv=4 + frame)
        links.copy(g.at[b, 0], next_g.at[frame], (row_low, b), recv=8 + frame)
    for f in range(4):
        links.arrive(mine.at[f], f)
        links.arrive(prev_g.at[f], 4 + f)
        links.arrive(next_g.at[f], 8 + f)
    links.finish()


def sigmoid(v):
    return 1.0 / (1.0 + jnp.exp(-v))


def conv_kernel(feat, all_feat, prev_feat, next_feat, gains, w, cot, w_out, res, act, inv_in, grad_o, full):
    r = lax.axis_index("row")
    gain = jnp.concatenate([gains[b, 0] for b in range(CH)], 0).astype(F32)
    for f in range(4):
        for h in range(4):
            blocks = [
                prev_feat[b, f] if h == 0 else next_feat[b, f] if h == 3 else all_feat[b, f, h - 1]
                for b in range(CH)
            ]
            x = jnp.concatenate(blocks, 0).astype(F32)
            inv = lax.rsqrt(jnp.mean(x * x, 0, keepdims=True) + EPSILON)
            before = x * inv * gain
            a = before * sigmoid(before)
            if h == 0:
                a = jnp.where(r == 0, 0.0, a)
            elif h == 3:
                a = jnp.where(r == ROWS - 1, 0.0, a)
            else:
                inv_in[2 * f + h - 1, :] = inv[0]
            act[:, pl.ds((4 * f + h) * 128, 128)] = a.astype(BF16)
    for f in range(4):
        acc = jnp.zeros((288, 256), F32)
        for t in range(3):
            source = f + t - 2
            if source < 0:
                continue
            for h in range(3):
                acc += dot(w[3 * t + h], act[:, pl.ds((4 * source + h) * 128, 256)])
        for h in range(2):
            y = acc[:, 128 * h : 128 * h + 128]
            out = move(y[:96], 1) + y[96:192] + move(y[192:], -1)
            res[f, h] = (feat[f, h].astype(F32) + out).astype(BF16)
    for b in range(CH):
        for h in range(2):
            full[pl.ds(96 * b, 96), pl.ds(128 * h, 128)] = cot[b, h]
    grad_o[...] = dot(w_out[...], full[...]).astype(BF16)


def attn_norm(res_frame, full):
    for b in range(CH):
        for h in range(2):
            full[pl.ds(96 * b, 96), pl.ds(128 * h, 128)] = res_frame[b, h]
    x = full[...].astype(F32)
    return x, lax.rsqrt(jnp.mean(x * x, 0, keepdims=True) + EPSILON)


def project_kernel(res_frame, gains, w_qkv, q, k, v, full):
    gain = jnp.concatenate([gains[b, 1] for b in range(CH)], 0).astype(F32)
    gain = jnp.concatenate([gain, gain], 1)
    x, inv = attn_norm(res_frame, full)
    normed = (x * inv * gain).astype(BF16).astype(F32)
    out = dot(normed.T.astype(BF16), w_qkv[...])
    q[...] = out[:, :384].T.astype(BF16)
    k[...] = out[:, 384:768].astype(BF16)
    v[...] = out[:, 768:].astype(BF16)


def stats_kernel(scale, q, g, k, v, stats):
    keys, values = k[...].reshape(1024, 384), v[...].reshape(1024, 384)

    def step(b, carry):
        s = dot(keys, q[b]) * scale
        m = jnp.max(s, 0, keepdims=True)
        e = jnp.exp(s - m)
        stats[0, pl.ds(b, 1), :] = m
        stats[1, pl.ds(b, 1), :] = jnp.sum(e, 0, keepdims=True)
        stats[2, pl.ds(b, 1), :] = jnp.sum(e * dot(values, g[b]), 0, keepdims=True)
        return carry

    lax.fori_loop(0, 8, step, 0)


def attn_kernel(scale, q, g, k, v, stats, dq, dk, dv, acc_k, acc_v):
    keys, values = k[...].reshape(1024, 384), v[...].reshape(1024, 384)
    keys_t = keys.T
    acc_k[...] = jnp.zeros_like(acc_k)
    acc_v[...] = jnp.zeros_like(acc_v)

    def step(b, carry):
        part = [[stats[i, n, pl.ds(b, 1), :] for n in range(3)] for i in range(8)]
        top = functools.reduce(jnp.maximum, [p[0] for p in part])
        shift = [jnp.exp(p[0] - top) for p in part]
        total = sum(p[1] * w for p, w in zip(part, shift))
        delta = sum(p[2] * w for p, w in zip(part, shift)) / total
        offset = top + jnp.log(total)
        prob = jnp.exp(dot(keys, q[b]) * scale - offset)
        grad_s = (prob * (dot(values, g[b]) - delta)).astype(BF16)
        acc_v[...] += dot_t(prob.astype(BF16), g[b])
        acc_k[...] += dot_t(grad_s, q[b])
        dq[b] = (dot(keys_t, grad_s) * scale).astype(BF16)
        return carry

    lax.fori_loop(0, 8, step, 0)
    dk[...] = (acc_k[...] * scale).astype(BF16).reshape(4, 256, 384)
    dv[...] = acc_v[...].astype(BF16).reshape(4, 256, 384)


def total_of(ref, count):
    total = ref[0].astype(F32)
    for i in range(1, count):
        total += ref[i].astype(F32)
    return total


def residual_kernel(dq, dk, dv, res_frame, cot, gains, w_qkv, grad, full, cot_full):
    gain = jnp.concatenate([gains[b, 1] for b in range(CH)], 0).astype(F32)
    gain = jnp.concatenate([gain, gain], 1)
    x, inv = attn_norm(res_frame, full)
    for b in range(CH):
        for h in range(2):
            cot_full[pl.ds(96 * b, 96), pl.ds(128 * h, 128)] = cot[b, h]
    w = w_qkv[...]
    normed = (
        dot(w[:, :384], total_of(dq, 8).astype(BF16))
        + dot_t(w[:, 384:768], total_of(dk, 4).astype(BF16))
        + dot_t(w[:, 768:], total_of(dv, 4).astype(BF16))
    )
    scaled = normed.astype(BF16).astype(F32) * gain
    inner = jnp.mean(x * scaled, 0, keepdims=True)
    out = cot_full[...].astype(F32) + inv * scaled - x * (inv * inv * inv * inner)
    for b in range(CH):
        for h in range(2):
            grad[b, h] = out[96 * b : 96 * b + 96, 128 * h : 128 * h + 128].astype(BF16)


def tail_kernel(links, held, made, scratch):
    own, prev_g, next_g, act, w_t, all_feat, inv_in, gains, feat, gain_own = held
    out, flat = made
    rows, lines, weight, part, all_part, inner, all_inner, came1, came2, came3, sum1, sum2, sum3, mark = scratch
    r, c = coords()
    x, y_hi, z, y_lo, core = place(r, c)
    xs = [device(lax.rem(x + d, 4), y_hi, z, y_lo, core) for d in range(1, 4)]
    zs = [device(x, y_hi, lax.rem(z + d, 4), y_lo, core) for d in range(1, 4)]
    x_at = [lax.rem(x + d, 4) for d in range(1, 4)]
    z_at = [lax.rem(z + d, 4) for d in range(1, 4)]
    across = device(x, 1 - y_hi, z, y_lo, core)
    chs = ch_peers(r, c)
    halves = (
        (x, xs, x_at, z, zs, z_at),
        (z, zs, z_at, x, xs, x_at),
    )
    links.greet(xs + zs + [across] + chs, 10)
    moved = []
    for f in range(4):
        both = []
        for h in range(2):
            y = own[f, h].astype(F32)
            both.append(jnp.concatenate([move(y, -1), y, move(y, 1)], 0).astype(BF16))
        moved.append(jnp.concatenate(both, 1))
    for t in range(3):
        for h in range(3):
            acc = jnp.zeros((288, 384), F32)
            for f in range(4):
                source = f + t - 2
                if source < 0:
                    continue
                acc += dot_t(moved[f], act[:, pl.ds((4 * source + h) * 128, 256)])
            for lane in range(3):
                at = (3 * (3 * t + h) + lane) * 288
                weight[pl.ds(at, 288), :] = acc[:, 128 * lane : 128 * lane + 128].astype(BF16)
    weight[pl.ds(27 * 288, 416), :] = jnp.zeros((416, 128), BF16)
    first = []
    for half, (a, peers, ats, _, _, _) in enumerate(halves):
        for d in range(3):
            src = weight.at[pl.ds(4096 * half + 1024 * ats[d], 1024)]
            first.append(links.copy(src, came1.at[half, d], peers[d]))
    for f in range(4):
        rows[f, 0] = jnp.where(r == 0, 0.0, prev_g[f].astype(F32)).astype(BF16)
        rows[f, 1] = own[f, 0]
        rows[f, 2] = own[f, 1]
        rows[f, 3] = jnp.where(r == ROWS - 1, 0.0, next_g[f].astype(F32)).astype(BF16)
    for f in range(4):
        for h in range(3):
            for k in range(2):
                lines[f, pl.ds(96 * h, 96), pl.ds(128 * k, 128)] = rows[f, 2 - h + k]
    gain = jnp.concatenate([gains[b, 0] for b in range(CH)], 0).astype(F32)
    for f in range(4):
        acc = jnp.zeros((1152, 256), F32)
        for t in range(3):
            source = f + 2 - t
            if source > 3:
                continue
            acc += dot(w_t[t], lines[source])
        for h in range(2):
            y = acc[:, 128 * h : 128 * h + 128]
            total = move(y[:384], -1) + y[384:768] + move(y[768:], 1)
            v = jnp.concatenate([all_feat[b, f, h] for b in range(CH)], 0).astype(F32)
            before = v * inv_in[2 * f + h : 2 * f + h + 1, :] * gain
            sig = sigmoid(before)
            slope = sig * (1.0 + before * (1.0 - sig))
            inner[2 * f + h : 2 * f + h + 1, :] = jnp.sum(v * slope * gain * total, 0, keepdims=True)
            for b in range(CH):
                part[b, f, h] = total[96 * b : 96 * b + 96].astype(BF16)
    parts = []
    for d in range(3):
        parts.append(links.copy(part.at[chs[d][1]], all_part.at[d], chs[d]))
        parts.append(links.copy(inner, all_inner.at[d], chs[d]))
    for copy in first:
        copy.wait_recv()
    second = []
    for half, (a, _, _, b, peers, ats) in enumerate(halves):
        total = weight[pl.ds(4096 * half + 1024 * a, 1024), :].astype(F32)
        for d in range(3):
            total += came1[half, d].astype(F32)
        sum1[half] = total.astype(BF16)
        for d in range(3):
            src = sum1.at[half, pl.ds(256 * ats[d], 256)]
            second.append(links.copy(src, came2.at[half, d], peers[d]))
    for copy in second:
        copy.wait_recv()
    third = []
    for half, (a, _, _, b, _, _) in enumerate(halves):
        total = sum1[half, pl.ds(256 * b, 256), :].astype(F32)
        for d in range(3):
            total += came2[half, d].astype(F32)
        sum2[half] = total.astype(BF16)
        src = sum2.at[half, pl.ds(128 * (1 - y_hi), 128)]
        third.append(links.copy(src, came3.at[half], across))
    for copy in third:
        copy.wait_recv()
    fourth, kept = [], []
    for half, (a, _, _, b, _, _) in enumerate(halves):
        total = sum2[half, pl.ds(128 * y_hi, 128), :].astype(F32) + came3[half].astype(F32)
        sum3[half] = total.astype(BF16)
        at = flat.at[pl.ds(4096 * half + 1024 * a + 256 * b + 128 * y_hi, 128)]
        kept.append(pltpu.make_async_copy(sum3.at[half], at, mark.at[half]))
        kept[half].start()
        fourth.append(links.copy(sum3.at[half], at, across))
    fifth = []
    for half, (a, _, _, b, peers, _) in enumerate(halves):
        kept[half].wait()
        fourth[half].wait_recv()
        at = flat.at[pl.ds(4096 * half + 1024 * a + 256 * b, 256)]
        for d in range(3):
            fifth.append(links.copy(at, at, peers[d]))
    sixth = []
    for half, (a, peers, _, _, _, _) in enumerate(halves):
        for d in range(3):
            fifth[3 * half + d].wait_recv()
        at = flat.at[pl.ds(4096 * half + 1024 * a, 1024)]
        for d in range(3):
            sixth.append(links.copy(at, at, peers[d]))
    for copy in parts:
        copy.wait_recv()
    mean = (inner[...] + all_inner[0] + all_inner[1] + all_inner[2]) / 384.0
    gain = gain_own[0].astype(F32)
    for f in range(4):
        for h in range(2):
            v = feat[f, h].astype(F32)
            inv = inv_in[2 * f + h : 2 * f + h + 1, :]
            total = part[c, f, h].astype(F32)
            for d in range(3):
                total += all_part[d, f, h].astype(F32)
            before = v * inv * gain
            sig = sigmoid(before)
            scaled = total * (sig * (1.0 + before * (1.0 - sig))) * gain
            cube = inv * inv * inv * mean[2 * f + h : 2 * f + h + 1, :]
            out[f, h] = (own[f, h].astype(F32) + inv * scaled - v * cube).astype(BF16)
    for copy in sixth:
        copy.wait_recv()
    links.finish()


def widen_kernel(scale, flat, out):
    for lane in range(3):
        piece = flat[pl.ds(288 * lane, 288), :].astype(F32) * scale
        out[:, pl.ds(128 * lane, 128)] = piece


def on_device(features, gain_in, w_conv, gain_attn, w_qkv, w_out, cotangent):
    scale = 1.0 / math.sqrt(384)
    gain_own = jnp.broadcast_to(jnp.stack([gain_in, gain_attn])[:, :, None], (2, 96, 128))
    w_rows = w_conv.reshape(9, 288, 384)
    all_feat, prev_feat, next_feat, cot_frame, gains, w_t = exchange(
        0,
        start_body,
        (features, cotangent, gain_own),
        [
            ((4, 4, 2, 96, 128), BF16),
            ((4, 4, 96, 128), BF16),
            ((4, 4, 96, 128), BF16),
            ((4, 2, 96, 128), BF16),
            ((4, 2, 96, 128), BF16),
        ],
        18,
        local=2,
        held=(w_conv,),
        made=[((3, 1152, 288), BF16)],
    )
    res, act, inv_in, grad_o = compute(
        conv_kernel,
        [((4, 2, 96, 128), BF16), ((384, 2048), BF16), ((8, 128), F32), ((384, 256), BF16)],
        features,
        all_feat,
        prev_feat,
        next_feat,
        gains,
        w_rows,
        cot_frame,
        w_out,
        scratch=[pltpu.VMEM((384, 256), BF16)],
        name="conv",
    )
    (res_frame,) = exchange(1, frame_body, (res,), [((4, 2, 96, 128), BF16)], 4)
    q, k, v = compute(
        project_kernel,
        [((384, 256), BF16), ((256, 384), BF16), ((256, 384), BF16)],
        res_frame,
        gains,
        w_qkv,
        scratch=[pltpu.VMEM((384, 256), BF16)],
        name="project",
    )
    all_q, all_g, all_k, all_v = exchange(
        2,
        gather_body,
        (q, grad_o, k, v),
        [((8, 384, 256), BF16)] * 2 + [((4, 256, 384), BF16)] * 2,
        24,
        local=4,
    )
    (stats,) = compute(
        functools.partial(stats_kernel, scale),
        [((3, 8, 256), F32)],
        all_q,
        all_g,
        all_k,
        all_v,
        name="stats",
    )
    (all_stats,) = exchange(3, simple(stats_plan), (stats,), [((8, 3, 8, 256), F32)], 7, local=1)
    dq, dk, dv = compute(
        functools.partial(attn_kernel, scale),
        [((8, 384, 256), BF16)] + [((4, 256, 384), BF16)] * 2,
        all_q,
        all_g,
        all_k,
        all_v,
        all_stats,
        scratch=[pltpu.VMEM((1024, 384), F32)] * 2,
        name="attn",
    )
    all_dq, all_dk, all_dv = exchange(
        4,
        simple(back_plan),
        (dq, dk, dv),
        [((8, 384, 256), BF16)] + [((4, 256, 384), BF16)] * 2,
        13,
        local=3,
    )
    (grad,) = compute(
        residual_kernel,
        [((4, 2, 96, 128), BF16)],
        all_dq,
        all_dk,
        all_dv,
        res_frame,
        cot_frame,
        gains,
        w_qkv,
        scratch=[pltpu.VMEM((384, 256), BF16)] * 2,
        name="residual",
    )
    own, prev_g, next_g = exchange(
        5,
        grad_body,
        (grad,),
        [((4, 2, 96, 128), BF16), ((4, 96, 128), BF16), ((4, 96, 128), BF16)],
        12,
    )
    out, flat = fused(
        6,
        tail_kernel,
        (own, prev_g, next_g, act, w_t, all_feat, inv_in, gains, features, gain_own),
        [((4, 2, 96, 128), BF16, pltpu.VMEM), ((8192, 128), BF16, pl.ANY)],
        [
            pltpu.VMEM((4, 4, 96, 128), BF16),
            pltpu.VMEM((4, 288, 256), BF16),
            pltpu.VMEM((8192, 128), BF16),
            pltpu.VMEM((4, 4, 2, 96, 128), BF16),
            pltpu.VMEM((3, 4, 2, 96, 128), BF16),
            pltpu.VMEM((8, 128), F32),
            pltpu.VMEM((3, 8, 128), F32),
            pltpu.VMEM((2, 3, 1024, 128), BF16),
            pltpu.VMEM((2, 3, 256, 128), BF16),
            pltpu.VMEM((2, 128, 128), BF16),
            pltpu.VMEM((2, 1024, 128), BF16),
            pltpu.VMEM((2, 256, 128), BF16),
            pltpu.VMEM((2, 128, 128), BF16),
            pltpu.SemaphoreType.DMA((2,)),
        ],
        34,
    )
    cell_scale = 1.0 / math.sqrt(32768)
    grad_weights = pl.pallas_call(
        functools.partial(widen_kernel, cell_scale),
        grid=(9,),
        out_shape=jax.ShapeDtypeStruct((2592, 384), F32),
        in_specs=[pl.BlockSpec((864, 128), lambda i: (i, 0))],
        out_specs=pl.BlockSpec((288, 384), lambda i: (i, 0)),
        name="widen",
    )(flat)
    return out, grad_weights.reshape(27, 96, 384)


def solution(mesh):
    return jax.shard_map(
        on_device,
        mesh=mesh,
        in_specs=(
            P(None, "row", "ch", None),
            P("ch"),
            P(None, "ch", None),
            P("ch"),
            P(),
            P(),
            P(None, "row", "ch", None),
        ),
        out_specs=(P(None, "row", "ch", None), P(None, "ch", None)),
        check_vma=False,
    )
```

```python
import functools
import math

import jax
import jax.numpy as jnp
from jax import lax
from jax.experimental import pallas as pl
from jax.experimental.pallas import tpu as pltpu
from jax.sharding import PartitionSpec as P

EPSILON = 1e-06
MESH = pl.DeviceIdType.MESH
F32 = jnp.float32
BF16 = jnp.bfloat16
ROWS = 32
CH = 4
VMEM_BYTES = 56 * 1024 * 1024


def coords():
    return lax.axis_index("row"), lax.axis_index("ch")


def place(r, c):
    return lax.rem(r, 4), lax.rem(r // 4, 2), r // 8, c // 2, lax.rem(c, 2)


def device(x, y_hi, z, y_lo, core):
    return z * 8 + y_hi * 4 + x, y_lo * 2 + core


def owner(f, row):
    x, y_hi, z, _, _ = place(row, 0)
    return device(x, f // 2, z, f % 2, y_hi)


class Links:
    def __init__(self, send, recv):
        self.send, self.recv, self.sent, self.at = send, recv, [], 0

    def greet(self, peers, count):
        barrier = pltpu.get_barrier_semaphore()
        for peer in peers:
            pl.semaphore_signal(barrier, inc=1, device_id=peer, device_id_type=MESH)
        pl.semaphore_wait(barrier, count)

    def copy(self, src, dst, to, own=None, recv=None):
        k = self.at
        self.at += 1
        mark = self.recv.at[k if recv is None else recv]
        far = pltpu.make_async_remote_copy(
            src_ref=src,
            dst_ref=dst,
            send_sem=self.send.at[k],
            recv_sem=mark,
            device_id=to,
            device_id_type=MESH,
        )
        if own is None:
            far.start()
        else:
            pl.when(jnp.logical_not(own))(far.start)
            pl.when(own)(pltpu.make_async_copy(src, dst, mark).start)
        self.sent.append((far, own))
        return far

    def arrive(self, dst, k):
        pltpu.make_async_copy(dst, dst, self.recv.at[k]).wait()

    def finish(self):
        for far, own in self.sent:
            if own is None:
                far.wait_send()
            else:
                pl.when(jnp.logical_not(own))(far.wait_send)


def exchange(cid, body, ins, outs, count, local=0, held=(), made=()):
    def kernel(*refs):
        n_in, n_out = len(ins) + len(held), len(outs) + len(made)
        send, recv, own = refs[n_in + n_out :]
        body(Links(send, recv), own, refs[:n_in], refs[n_in : n_in + n_out])

    far = pl.BlockSpec(memory_space=pl.ANY)
    near = pl.BlockSpec(memory_space=pltpu.VMEM)
    return pl.pallas_call(
        kernel,
        out_shape=[jax.ShapeDtypeStruct(s, t) for s, t in list(outs) + list(made)],
        in_specs=[far] * len(ins) + [near] * len(held),
        out_specs=[far] * len(outs) + [near] * len(made),
        scratch_shapes=[
            pltpu.SemaphoreType.DMA((count,)),
            pltpu.SemaphoreType.DMA((count,)),
            pltpu.SemaphoreType.DMA((max(local, 1),)),
        ],
        compiler_params=pltpu.CompilerParams(
            collective_id=cid, has_side_effects=True, vmem_limit_bytes=VMEM_BYTES
        ),
        name="exchange_%d" % cid,
    )(*ins, *held)


def fused(cid, body, held, made, scratch, count):
    def kernel(*refs):
        n_in, n_out = len(held), len(held) + len(made)
        send, recv = refs[-2:]
        body(Links(send, recv), refs[:n_in], refs[n_in:n_out], refs[n_out:-2])

    return pl.pallas_call(
        kernel,
        out_shape=[jax.ShapeDtypeStruct(s, t) for s, t, _ in made],
        in_specs=[pl.BlockSpec(memory_space=pltpu.VMEM)] * len(held),
        out_specs=[pl.BlockSpec(memory_space=m) for _, _, m in made],
        scratch_shapes=list(scratch) + [pltpu.SemaphoreType.DMA((count,))] * 2,
        compiler_params=pltpu.CompilerParams(
            collective_id=cid, has_side_effects=True, vmem_limit_bytes=VMEM_BYTES
        ),
        name="fused_%d" % cid,
    )(*held)


def simple(plan):
    def body(links, own, srcs, dsts):
        remote, local, peers = plan(srcs, dsts)
        here = [pltpu.make_async_copy(s, d, own.at[k]) for k, (s, d) in enumerate(local)]
        for copy in here:
            copy.start()
        links.greet(peers, len(peers))
        there = [links.copy(s, d, to) for s, d, to in remote]
        for copy in here:
            copy.wait()
        for copy in there:
            copy.wait_recv()
        links.finish()

    return body


def compute(body, outs, *ins, scratch=(), name):
    return pl.pallas_call(
        body,
        out_shape=[jax.ShapeDtypeStruct(s, t) for s, t in outs],
        in_specs=[pl.BlockSpec(memory_space=pltpu.VMEM)] * len(ins),
        out_specs=[pl.BlockSpec(memory_space=pltpu.VMEM)] * len(outs),
        scratch_shapes=list(scratch),
        compiler_params=pltpu.CompilerParams(vmem_limit_bytes=VMEM_BYTES),
        name=name,
    )(*ins)


def dot(a, b):
    return lax.dot_general(a, b, (((1,), (0,)), ((), ())), preferred_element_type=F32)


def dot_t(a, b):
    return lax.dot_general(a, b, (((1,), (1,)), ((), ())), preferred_element_type=F32)


def move(block, by):
    lanes = block.shape[1]
    at = lax.broadcasted_iota(jnp.int32, block.shape, 1)
    if by > 0:
        return jnp.where(at == 0, 0.0, pltpu.roll(block, 1, axis=1))
    return jnp.where(at == lanes - 1, 0.0, pltpu.roll(block, lanes - 1, axis=1))


def ch_peers(r, c):
    return [(r, lax.rem(c + d, CH)) for d in range(1, CH)]


def near_rows(r):
    return lax.rem(r + ROWS - 1, ROWS), lax.rem(r + 1, ROWS)


def same(a, b):
    return jnp.logical_and(a[0] == b[0], a[1] == b[1])


def greet_frames(links, me, sources, targets):
    barrier = pltpu.get_barrier_semaphore()
    for peer in sources:
        def tell(peer=peer):
            pl.semaphore_signal(barrier, inc=1, device_id=peer, device_id_type=MESH)

        pl.when(jnp.logical_not(same(peer, me)))(tell)
    _, y_hi, _, _, core = place(*me)
    pl.semaphore_wait(barrier, len(targets) - 1 + (core - y_hi) * (core - y_hi))


def start_body(links, own, srcs, dsts):
    feat, cot, gain, w = srcs
    all_feat, prev_feat, next_feat, cot_frame, all_gain, w_t = dsts
    r, c = coords()
    low, high = near_rows(r)
    x, y_hi, z, y_lo, core = place(r, c)
    here = [
        pltpu.make_async_copy(feat, all_feat.at[c], own.at[0]),
        pltpu.make_async_copy(gain, all_gain.at[c], own.at[1]),
    ]
    for copy in here:
        copy.start()
    targets = [owner(f, r) for f in range(4)]
    sources = [(z * 8 + core * 4 + x, b) for b in range(4)]
    others = ch_peers(r, c) + [(row, b) for row in (low, high) for b in range(CH)]
    greet_frames(links, (r, c), sources + others, targets + others)
    for f in range(4):
        links.copy(cot.at[f], cot_frame.at[c], targets[f], own=same(targets[f], (r, c)), recv=c)
    there = []
    for to in ch_peers(r, c):
        there.append(links.copy(feat, all_feat.at[c], to))
        there.append(links.copy(gain, all_gain.at[c], to))
    for d in range(CH):
        c_to = lax.rem(c + d, CH)
        there.append(links.copy(feat.at[:, 1], prev_feat.at[c], (high, c_to)))
        there.append(links.copy(feat.at[:, 0], next_feat.at[c], (low, c_to)))
    for t in range(3):
        for k in range(3):
            piece = jnp.concatenate([w[9 * t + 3 * h + k] for h in range(3)], 0)
            w_t[t, pl.ds(384 * k, 384), :] = piece.T
    for copy in here:
        copy.wait()
    for b in range(CH):
        links.arrive(cot_frame.at[b], b)
    for copy in there:
        copy.wait_recv()
    links.finish()


def frame_body(links, own, srcs, dsts):
    (res,), (res_frame,) = srcs, dsts
    r, c = coords()
    x, y_hi, z, y_lo, core = place(r, c)
    targets = [owner(f, r) for f in range(4)]
    sources = [(z * 8 + core * 4 + x, b) for b in range(4)]
    greet_frames(links, (r, c), sources, targets)
    for f in range(4):
        links.copy(res.at[f], res_frame.at[c], targets[f], own=same(targets[f], (r, c)), recv=c)
    for b in range(CH):
        links.arrive(res_frame.at[b], b)
    links.finish()


def sigmoid(v):
    return 1.0 / (1.0 + jnp.exp(-v))


def conv_kernel(feat, all_feat, prev_feat, next_feat, gains, w, cot, w_out, res, act, inv_in, grad_o, full):
    r = lax.axis_index("row")
    gain = jnp.concatenate([gains[b, 0] for b in range(CH)], 0).astype(F32)
    for f in range(4):
        for h in range(4):
            blocks = [
                prev_feat[b, f] if h == 0 else next_feat[b, f] if h == 3 else all_feat[b, f, h - 1]
                for b in range(CH)
            ]
            x = jnp.concatenate(blocks, 0).astype(F32)
            inv = lax.rsqrt(jnp.mean(x * x, 0, keepdims=True) + EPSILON)
            before = x * inv * gain
            a = before * sigmoid(before)
            if h == 0:
                a = jnp.where(r == 0, 0.0, a)
            elif h == 3:
                a = jnp.where(r == ROWS - 1, 0.0, a)
            else:
                inv_in[2 * f + h - 1, :] = inv[0]
            act[:, pl.ds((4 * f + h) * 128, 128)] = a.astype(BF16)
    for f in range(4):
        acc = jnp.zeros((288, 256), F32)
        for t in range(3):
            source = f + t - 2
            if source < 0:
                continue
            for h in range(3):
                acc += dot(w[3 * t + h], act[:, pl.ds((4 * source + h) * 128, 256)])
        for h in range(2):
            y = acc[:, 128 * h : 128 * h + 128]
            out = move(y[:96], 1) + y[96:192] + move(y[192:], -1)
            res[f, h] = (feat[f, h].astype(F32) + out).astype(BF16)
    for b in range(CH):
        for h in range(2):
            full[pl.ds(96 * b, 96), pl.ds(128 * h, 128)] = cot[b, h]
    grad_o[...] = dot(w_out[...], full[...]).astype(BF16)


def attn_norm(res_frame, full):
    for b in range(CH):
        for h in range(2):
            full[pl.ds(96 * b, 96), pl.ds(128 * h, 128)] = res_frame[b, h]
    x = full[...].astype(F32)
    return x, lax.rsqrt(jnp.mean(x * x, 0, keepdims=True) + EPSILON)


def attn_body(scale, links, held, made, scratch):
    res_frame, cot, gains, w_qkv, grad_o = held
    mine, prev_g, next_g = made
    (full, cot_full, q, g, k, v, k_t, exps, grad_p, grad_s, prob_row, tops, sums, deltas, stats, all_stats, weights, delta,
     send_k, send_v, came_k, came_v, own_k, own_v, sib_out, sib_in, send_q, came_q, own_q, grad) = scratch
    r, c = coords()
    x, y_hi, z, y_lo, core = place(r, c)
    slot = core * 4 + x
    frame = y_hi * 2 + y_lo
    sibling = (r, y_lo * 2 + 1 - core)
    xs = [device(lax.rem(x + d, 4), y_hi, z, y_lo, core) for d in range(1, 4)]
    cross = [device(lax.rem(x + d, 4), y_hi, z, y_lo, 1 - core) for d in range(1, 4)]
    zs = [device(x, y_hi, lax.rem(z + d, 4), y_lo, core) for d in range(1, 4)]
    row = z * 8 + core * 4 + x
    row_low, row_high = near_rows(row)
    low, high = near_rows(r)
    around = [(i, b) for i in (row_low, row_high) for b in range(CH)]
    alike = xs + zs + cross + [sibling]
    sources = [owner(f, i) for i in (r, low, high) for f in range(4)]
    greet_frames(links, (r, c), sources + alike, [(row, b) for b in range(CH)] + around + alike)

    g[slot] = grad_o[...]
    g_first = [links.copy(g.at[slot], g.at[slot], to) for to in (xs[0], xs[2], sibling)]
    gain = jnp.concatenate([gains[b, 1] for b in range(CH)], 0).astype(F32)
    gain = jnp.concatenate([gain, gain], 1)
    centre, inv = attn_norm(res_frame, full)
    normed = (centre * inv * gain).astype(BF16).astype(F32).T.astype(BF16)
    k[z] = dot(normed, w_qkv[:, 384:768]).astype(BF16)
    k_first = [links.copy(k.at[z], k.at[z], to) for to in (zs[0], zs[2])]
    v[z] = dot(normed, w_qkv[:, 768:]).astype(BF16)
    v_first = [links.copy(v.at[z], v.at[z], to) for to in (zs[0], zs[2])]
    q[slot] = dot(normed, w_qkv[:, :384]).T.astype(BF16)
    q_first = [links.copy(q.at[slot], q.at[slot], to) for to in (xs[0], xs[2], sibling)]

    def turn(j):
        k_t[:, pl.ds(pl.multiple_of(256 * j, 256), 256)] = k[j].T

    def tile(b, j):
        s = dot(k[j], q[b]) * scale
        top = jnp.max(s, 0, keepdims=True)
        e = jnp.exp(s - top)
        p = dot(v[j], g[b])
        exps[j, b] = e
        grad_p[j, b] = p
        tops[j, pl.ds(b, 1), :] = top
        sums[j, pl.ds(b, 1), :] = jnp.sum(e, 0, keepdims=True)
        deltas[j, pl.ds(b, 1), :] = jnp.sum(e * p, 0, keepdims=True)

    def block(dk, dx):
        other = core + dk - 2 * core * dk
        return other * 4 + lax.rem(x + dx, 4)

    def key(dz):
        return lax.rem(z + dz, 4)

    def tiles(count, which):
        def step(n, carry):
            dk, dx, dz = which(n)
            tile(block(dk, dx), key(dz))
            return carry

        lax.fori_loop(0, count, step, 0)

    def relay_ring(first, ref, base, i, rows, peers, forward):
        on = []
        for side in range(2):
            first[side].wait_recv()
            came = base + lax.rem(i + 3 - 2 * side, 4)
            part = ref.at[came, pl.ds(rows * side, rows)]
            on.append(links.copy(part, part, peers[2 * side]))
            if forward:
                on.append(links.copy(ref.at[came], ref.at[came], sibling))
        return on

    turn(z)
    tile(slot, z)
    g_on = relay_ring(g_first, g, core * 4, x, 192, xs, True)
    k_on = relay_ring(k_first, k, 0, z, 128, zs, False)
    q_on = relay_ring(q_first, q, core * 4, x, 192, xs, True)
    v_on = relay_ring(v_first, v, 0, z, 128, zs, False)
    q_first[2].wait_recv()
    g_first[2].wait_recv()
    tiles(2, lambda n: (0, 0, 1 + 2 * n))
    tiles(3, lambda n: (1, 0, n + n // 2))
    turn(key(1))
    turn(key(3))
    q_on[1].wait_recv()
    q_on[3].wait_recv()
    g_on[1].wait_recv()
    g_on[3].wait_recv()

    def beside(n):
        dz = n // 4
        return lax.rem(n // 2, 2), 1 + 2 * lax.rem(n, 2), dz + dz // 2

    tiles(12, beside)
    for on in (g_on, q_on):
        on[0].wait_recv()
        on[2].wait_recv()
    at = core * 4 + lax.rem(x + 2, 4)
    last = [links.copy(ref.at[at], ref.at[at], sibling) for ref in (g, q)]
    for copy in k_on + v_on:
        copy.wait_recv()
    turn(key(2))

    def beyond(n):
        dx = n // 2
        return lax.rem(n, 2), dx + dx // 2, 2

    tiles(6, beyond)
    tiles(4, lambda n: (0, 2, n))
    for copy in last:
        copy.wait_recv()
    tiles(4, lambda n: (1, 2, n))

    top = functools.reduce(jnp.maximum, [tops[j] for j in range(4)])
    shift = [jnp.exp(tops[j] - top) for j in range(4)]
    stats[0] = top
    stats[1] = sum(sums[j] * shift[j] for j in range(4))
    stats[2] = sum(deltas[j] * shift[j] for j in range(4))
    shared = [links.copy(stats, all_stats.at[n], to) for n, to in enumerate(xs + cross + [sibling])]
    for copy in shared:
        copy.wait_recv()
    parts = [stats] + [all_stats.at[n] for n in range(7)]
    top = functools.reduce(jnp.maximum, [p[0] for p in parts])
    total = sum(p[1] * jnp.exp(p[0] - top) for p in parts)
    delta[...] = sum(p[2] * jnp.exp(p[0] - top) for p in parts) / total
    for j in range(4):
        weights[j] = jnp.exp(tops[j] - top) / total

    back = []
    for n, dz in enumerate((2, 1, 3, 0)):
        j = key(dz)
        rows = pl.ds(pl.multiple_of(256 * j, 256), 256)

        def step(b, carry, j=j, rows=rows):
            prob = exps[j, b] * weights[j, pl.ds(b, 1), :]
            prob_row[b] = prob.astype(BF16)
            grad_s[b, rows, :] = (prob * (grad_p[j, b] - delta[pl.ds(b, 1), :])).astype(BF16)
            return carry

        lax.fori_loop(0, 8, step, 0)
        for_k = sum(dot_t(grad_s[b, rows, :], q[b]) for b in range(8)) * scale
        for_v = sum(dot_t(prob_row[b], g[b]) for b in range(8))
        if dz:
            send_k[n] = for_k.astype(BF16)
            send_v[n] = for_v.astype(BF16)
            back.append(links.copy(send_k.at[n], came_k.at[n], zs[dz - 1]))
            back.append(links.copy(send_v.at[n], came_v.at[n], zs[dz - 1]))
        else:
            own_k[...] = for_k
            own_v[...] = for_v
    sib = []
    for dx in range(4):
        sib_out[dx] = (dot(k_t[...], grad_s[block(1, dx)]) * scale).astype(BF16)
        sib.append(links.copy(sib_out.at[dx], sib_in.at[dx], sibling))
    for n, dx in enumerate((2, 1, 3, 0)):
        for_q = dot(k_t[...], grad_s[block(0, dx)]) * scale
        sib[dx].wait_recv()
        for_q += sib_in[dx].astype(F32)
        if dx:
            send_q[n] = for_q.astype(BF16)
            back.append(links.copy(send_q.at[n], came_q.at[n], xs[dx - 1]))
        else:
            own_q[...] = for_q
    for b in range(CH):
        for h in range(2):
            cot_full[pl.ds(96 * b, 96), pl.ds(128 * h, 128)] = cot[b, h]
    for copy in back:
        copy.wait_recv()
    for n in range(3):
        own_k[...] += came_k[n].astype(F32)
        own_v[...] += came_v[n].astype(F32)
        own_q[...] += came_q[n].astype(F32)
    back_normed = (
        dot(w_qkv[:, :384], own_q[...].astype(BF16))
        + dot_t(w_qkv[:, 384:768], own_k[...].astype(BF16))
        + dot_t(w_qkv[:, 768:], own_v[...].astype(BF16))
    )
    scaled = back_normed.astype(BF16).astype(F32) * gain
    centre = full[...].astype(F32)
    inner = jnp.mean(centre * scaled, 0, keepdims=True)
    out = cot_full[...].astype(F32) + inv * scaled - centre * (inv * inv * inv * inner)
    for b in range(CH):
        for h in range(2):
            grad[b, h] = out[96 * b : 96 * b + 96, 128 * h : 128 * h + 128].astype(BF16)
    for b in range(CH):
        to = (row, b)
        links.copy(grad.at[b], mine.at[frame], to, own=same(to, (r, c)), recv=64 + frame)
    for b in range(CH):
        links.copy(grad.at[b, 1], prev_g.at[frame], (row_high, b), recv=68 + frame)
        links.copy(grad.at[b, 0], next_g.at[frame], (row_low, b), recv=72 + frame)
    for f in range(4):
        links.arrive(mine.at[f], 64 + f)
        links.arrive(prev_g.at[f], 68 + f)
        links.arrive(next_g.at[f], 72 + f)
    links.finish()


def tail_kernel(links, held, made, scratch):
    own, prev_g, next_g, act, w_t, all_feat, inv_in, gains, feat, gain_own = held
    out, flat = made
    rows, lines, weight, part, all_part, inner, all_inner, came1, came2, came3, sum1, sum2, sum3, mark = scratch
    r, c = coords()
    x, y_hi, z, y_lo, core = place(r, c)
    xs = [device(lax.rem(x + d, 4), y_hi, z, y_lo, core) for d in range(1, 4)]
    zs = [device(x, y_hi, lax.rem(z + d, 4), y_lo, core) for d in range(1, 4)]
    x_at = [lax.rem(x + d, 4) for d in range(1, 4)]
    z_at = [lax.rem(z + d, 4) for d in range(1, 4)]
    across = device(x, 1 - y_hi, z, y_lo, core)
    chs = ch_peers(r, c)
    halves = (
        (x, xs, x_at, z, zs, z_at),
        (z, zs, z_at, x, xs, x_at),
    )
    links.greet(xs + zs + [across] + chs, 10)
    moved = []
    for f in range(4):
        both = []
        for h in range(2):
            y = own[f, h].astype(F32)
            both.append(jnp.concatenate([move(y, -1), y, move(y, 1)], 0).astype(BF16))
        moved.append(jnp.concatenate(both, 1))
    for t in range(3):
        for h in range(3):
            acc = jnp.zeros((288, 384), F32)
            for f in range(4):
                source = f + t - 2
                if source < 0:
                    continue
                acc += dot_t(moved[f], act[:, pl.ds((4 * source + h) * 128, 256)])
            for lane in range(3):
                at = (3 * (3 * t + h) + lane) * 288
                weight[pl.ds(at, 288), :] = acc[:, 128 * lane : 128 * lane + 128].astype(BF16)
    weight[pl.ds(27 * 288, 416), :] = jnp.zeros((416, 128), BF16)
    first = []
    for half, (a, peers, ats, _, _, _) in enumerate(halves):
        for d in range(3):
            src = weight.at[pl.ds(4096 * half + 1024 * ats[d], 1024)]
            first.append(links.copy(src, came1.at[half, d], peers[d]))
    for f in range(4):
        rows[f, 0] = jnp.where(r == 0, 0.0, prev_g[f].astype(F32)).astype(BF16)
        rows[f, 1] = own[f, 0]
        rows[f, 2] = own[f, 1]
        rows[f, 3] = jnp.where(r == ROWS - 1, 0.0, next_g[f].astype(F32)).astype(BF16)
    for f in range(4):
        for h in range(3):
            for k in range(2):
                lines[f, pl.ds(96 * h, 96), pl.ds(128 * k, 128)] = rows[f, 2 - h + k]
    gain = jnp.concatenate([gains[b, 0] for b in range(CH)], 0).astype(F32)
    for f in range(4):
        acc = jnp.zeros((1152, 256), F32)
        for t in range(3):
            source = f + 2 - t
            if source > 3:
                continue
            acc += dot(w_t[t], lines[source])
        for h in range(2):
            y = acc[:, 128 * h : 128 * h + 128]
            total = move(y[:384], -1) + y[384:768] + move(y[768:], 1)
            v = jnp.concatenate([all_feat[b, f, h] for b in range(CH)], 0).astype(F32)
            before = v * inv_in[2 * f + h : 2 * f + h + 1, :] * gain
            sig = sigmoid(before)
            slope = sig * (1.0 + before * (1.0 - sig))
            inner[2 * f + h : 2 * f + h + 1, :] = jnp.sum(v * slope * gain * total, 0, keepdims=True)
            for b in range(CH):
                part[b, f, h] = total[96 * b : 96 * b + 96].astype(BF16)
    parts = []
    for d in range(3):
        parts.append(links.copy(part.at[chs[d][1]], all_part.at[d], chs[d]))
        parts.append(links.copy(inner, all_inner.at[d], chs[d]))
    for copy in first:
        copy.wait_recv()
    second = []
    for half, (a, _, _, b, peers, ats) in enumerate(halves):
        total = weight[pl.ds(4096 * half + 1024 * a, 1024), :].astype(F32)
        for d in range(3):
            total += came1[half, d].astype(F32)
        sum1[half] = total.astype(BF16)
        for d in range(3):
            src = sum1.at[half, pl.ds(256 * ats[d], 256)]
            second.append(links.copy(src, came2.at[half, d], peers[d]))
    for copy in second:
        copy.wait_recv()
    third = []
    for half, (a, _, _, b, _, _) in enumerate(halves):
        total = sum1[half, pl.ds(256 * b, 256), :].astype(F32)
        for d in range(3):
            total += came2[half, d].astype(F32)
        sum2[half] = total.astype(BF16)
        src = sum2.at[half, pl.ds(128 * (1 - y_hi), 128)]
        third.append(links.copy(src, came3.at[half], across))
    for copy in third:
        copy.wait_recv()
    fourth, kept = [], []
    for half, (a, _, _, b, _, _) in enumerate(halves):
        total = sum2[half, pl.ds(128 * y_hi, 128), :].astype(F32) + came3[half].astype(F32)
        sum3[half] = total.astype(BF16)
        at = flat.at[pl.ds(4096 * half + 1024 * a + 256 * b + 128 * y_hi, 128)]
        kept.append(pltpu.make_async_copy(sum3.at[half], at, mark.at[half]))
        kept[half].start()
        fourth.append(links.copy(sum3.at[half], at, across))
    fifth = []
    for half, (a, _, _, b, peers, _) in enumerate(halves):
        kept[half].wait()
        fourth[half].wait_recv()
        at = flat.at[pl.ds(4096 * half + 1024 * a + 256 * b, 256)]
        for d in range(3):
            fifth.append(links.copy(at, at, peers[d]))
    sixth = []
    for half, (a, peers, _, _, _, _) in enumerate(halves):
        for d in range(3):
            fifth[3 * half + d].wait_recv()
        at = flat.at[pl.ds(4096 * half + 1024 * a, 1024)]
        for d in range(3):
            sixth.append(links.copy(at, at, peers[d]))
    for copy in parts:
        copy.wait_recv()
    mean = (inner[...] + all_inner[0] + all_inner[1] + all_inner[2]) / 384.0
    gain = gain_own[0].astype(F32)
    for f in range(4):
        for h in range(2):
            v = feat[f, h].astype(F32)
            inv = inv_in[2 * f + h : 2 * f + h + 1, :]
            total = part[c, f, h].astype(F32)
            for d in range(3):
                total += all_part[d, f, h].astype(F32)
            before = v * inv * gain
            sig = sigmoid(before)
            scaled = total * (sig * (1.0 + before * (1.0 - sig))) * gain
            cube = inv * inv * inv * mean[2 * f + h : 2 * f + h + 1, :]
            out[f, h] = (own[f, h].astype(F32) + inv * scaled - v * cube).astype(BF16)
    for copy in sixth:
        copy.wait_recv()
    links.finish()


def widen_kernel(scale, flat, out):
    for k in range(9):
        for lane in range(3):
            piece = flat[pl.ds((3 * k + lane) * 288, 288), :].astype(F32) * scale
            out[pl.ds(288 * k, 288), pl.ds(128 * lane, 128)] = piece


def on_device(features, gain_in, w_conv, gain_attn, w_qkv, w_out, cotangent):
    scale = 1.0 / math.sqrt(384)
    gain_own = jnp.broadcast_to(jnp.stack([gain_in, gain_attn])[:, :, None], (2, 96, 128))
    w_rows = w_conv.reshape(9, 288, 384)
    all_feat, prev_feat, next_feat, cot_frame, gains, w_t = exchange(
        0,
        start_body,
        (features, cotangent, gain_own),
        [
            ((4, 4, 2, 96, 128), BF16),
            ((4, 4, 96, 128), BF16),
            ((4, 4, 96, 128), BF16),
            ((4, 2, 96, 128), BF16),
            ((4, 2, 96, 128), BF16),
        ],
        18,
        local=2,
        held=(w_conv,),
        made=[((3, 1152, 288), BF16)],
    )
    res, act, inv_in, grad_o = compute(
        conv_kernel,
        [((4, 2, 96, 128), BF16), ((384, 2048), BF16), ((8, 128), F32), ((384, 256), BF16)],
        features,
        all_feat,
        prev_feat,
        next_feat,
        gains,
        w_rows,
        cot_frame,
        w_out,
        scratch=[pltpu.VMEM((384, 256), BF16)],
        name="conv",
    )
    (res_frame,) = exchange(1, frame_body, (res,), [((4, 2, 96, 128), BF16)], 4)
    own, prev_g, next_g = fused(
        2,
        functools.partial(attn_body, scale),
        (res_frame, cot_frame, gains, w_qkv, grad_o),
        [
            ((4, 2, 96, 128), BF16, pl.ANY),
            ((4, 96, 128), BF16, pl.ANY),
            ((4, 96, 128), BF16, pl.ANY),
        ],
        [
            pltpu.VMEM((384, 256), BF16),
            pltpu.VMEM((384, 256), BF16),
            pltpu.VMEM((8, 384, 256), BF16),
            pltpu.VMEM((8, 384, 256), BF16),
            pltpu.VMEM((4, 256, 384), BF16),
            pltpu.VMEM((4, 256, 384), BF16),
            pltpu.VMEM((384, 1024), BF16),
            pltpu.VMEM((4, 8, 256, 256), F32),
            pltpu.VMEM((4, 8, 256, 256), F32),
            pltpu.VMEM((8, 1024, 256), BF16),
            pltpu.VMEM((8, 256, 256), BF16),
            pltpu.VMEM((4, 8, 256), F32),
            pltpu.VMEM((4, 8, 256), F32),
            pltpu.VMEM((4, 8, 256), F32),
            pltpu.VMEM((3, 8, 256), F32),
            pltpu.VMEM((7, 3, 8, 256), F32),
            pltpu.VMEM((4, 8, 256), F32),
            pltpu.VMEM((8, 256), F32),
            pltpu.VMEM((3, 256, 384), BF16),
            pltpu.VMEM((3, 256, 384), BF16),
            pltpu.VMEM((3, 256, 384), BF16),
            pltpu.VMEM((3, 256, 384), BF16),
            pltpu.VMEM((256, 384), F32),
            pltpu.VMEM((256, 384), F32),
            pltpu.VMEM((4, 384, 256), BF16),
            pltpu.VMEM((4, 384, 256), BF16),
            pltpu.VMEM((3, 384, 256), BF16),
            pltpu.VMEM((3, 384, 256), BF16),
            pltpu.VMEM((384, 256), F32),
            pltpu.VMEM((4, 2, 96, 128), BF16),
        ],
        76,
    )
    out, flat = fused(
        6,
        tail_kernel,
        (own, prev_g, next_g, act, w_t, all_feat, inv_in, gains, features, gain_own),
        [((4, 2, 96, 128), BF16, pltpu.VMEM), ((8192, 128), BF16, pl.ANY)],
        [
            pltpu.VMEM((4, 4, 96, 128), BF16),
            pltpu.VMEM((4, 288, 256), BF16),
            pltpu.VMEM((8192, 128), BF16),
            pltpu.VMEM((4, 4, 2, 96, 128), BF16),
            pltpu.VMEM((3, 4, 2, 96, 128), BF16),
            pltpu.VMEM((8, 128), F32),
            pltpu.VMEM((3, 8, 128), F32),
            pltpu.VMEM((2, 3, 1024, 128), BF16),
            pltpu.VMEM((2, 3, 256, 128), BF16),
            pltpu.VMEM((2, 128, 128), BF16),
            pltpu.VMEM((2, 1024, 128), BF16),
            pltpu.VMEM((2, 256, 128), BF16),
            pltpu.VMEM((2, 128, 128), BF16),
            pltpu.SemaphoreType.DMA((2,)),
        ],
        34,
    )
    cell_scale = 1.0 / math.sqrt(32768)
    (grad_weights,) = compute(
        functools.partial(widen_kernel, cell_scale),
        [((2592, 384), F32)],
        flat,
        name="widen",
    )
    return out, grad_weights.reshape(27, 96, 384)


def solution(mesh):
    return jax.shard_map(
        on_device,
        mesh=mesh,
        in_specs=(
            P(None, "row", "ch", None),
            P("ch"),
            P(None, "ch", None),
            P("ch"),
            P(),
            P(),
            P(None, "row", "ch", None),
        ),
        out_specs=(P(None, "row", "ch", None), P(None, "ch", None)),
        check_vma=False,
    )
```

```python
import functools
import math

import jax
import jax.numpy as jnp
from jax import lax
from jax.experimental import pallas as pl
from jax.experimental.pallas import tpu as pltpu
from jax.sharding import PartitionSpec as P

EPSILON = 1e-06
MESH = pl.DeviceIdType.MESH
F32 = jnp.float32
BF16 = jnp.bfloat16
ROWS = 32
CH = 4
VMEM_BYTES = 56 * 1024 * 1024


def coords():
    return lax.axis_index("row"), lax.axis_index("ch")


def place(r, c):
    return lax.rem(r, 4), lax.rem(r // 4, 2), r // 8, c // 2, lax.rem(c, 2)


def device(x, y_hi, z, y_lo, core):
    return z * 8 + y_hi * 4 + x, y_lo * 2 + core


def owner(f, row):
    x, y_hi, z, _, _ = place(row, 0)
    return device(x, f // 2, z, f % 2, y_hi)


class Links:
    def __init__(self, send, recv):
        self.send, self.recv, self.sent, self.at = send, recv, [], 0

    def greet(self, peers, count):
        barrier = pltpu.get_barrier_semaphore()
        for peer in peers:
            pl.semaphore_signal(barrier, inc=1, device_id=peer, device_id_type=MESH)
        pl.semaphore_wait(barrier, count)

    def copy(self, src, dst, to, own=None, recv=None):
        k = self.at
        self.at += 1
        mark = self.recv.at[k if recv is None else recv]
        far = pltpu.make_async_remote_copy(
            src_ref=src,
            dst_ref=dst,
            send_sem=self.send.at[k],
            recv_sem=mark,
            device_id=to,
            device_id_type=MESH,
        )
        if own is None:
            far.start()
        else:
            pl.when(jnp.logical_not(own))(far.start)
            pl.when(own)(pltpu.make_async_copy(src, dst, mark).start)
        self.sent.append((far, own))
        return far

    def arrive(self, dst, k):
        pltpu.make_async_copy(dst, dst, self.recv.at[k]).wait()

    def finish(self):
        for far, own in self.sent:
            if own is None:
                far.wait_send()
            else:
                pl.when(jnp.logical_not(own))(far.wait_send)


def fused(cid, body, held, made, scratch, count):
    def kernel(*refs):
        n_in, n_out = len(held), len(held) + len(made)
        send, recv = refs[-2:]
        body(Links(send, recv), refs[:n_in], refs[n_in:n_out], refs[n_out:-2])

    return pl.pallas_call(
        kernel,
        out_shape=[jax.ShapeDtypeStruct(s, t) for s, t, _ in made],
        in_specs=[pl.BlockSpec(memory_space=m) for _, m in held],
        out_specs=[pl.BlockSpec(memory_space=m) for _, _, m in made],
        scratch_shapes=list(scratch) + [pltpu.SemaphoreType.DMA((count,))] * 2,
        compiler_params=pltpu.CompilerParams(
            collective_id=cid, has_side_effects=True, vmem_limit_bytes=VMEM_BYTES
        ),
        name="fused_%d" % cid,
    )(*[array for array, _ in held])


def simple(plan):
    def body(links, own, srcs, dsts):
        remote, local, peers = plan(srcs, dsts)
        here = [pltpu.make_async_copy(s, d, own.at[k]) for k, (s, d) in enumerate(local)]
        for copy in here:
            copy.start()
        links.greet(peers, len(peers))
        there = [links.copy(s, d, to) for s, d, to in remote]
        for copy in here:
            copy.wait()
        for copy in there:
            copy.wait_recv()
        links.finish()

    return body


def compute(body, outs, *ins, scratch=(), name):
    return pl.pallas_call(
        body,
        out_shape=[jax.ShapeDtypeStruct(s, t) for s, t in outs],
        in_specs=[pl.BlockSpec(memory_space=pltpu.VMEM)] * len(ins),
        out_specs=[pl.BlockSpec(memory_space=pltpu.VMEM)] * len(outs),
        scratch_shapes=list(scratch),
        compiler_params=pltpu.CompilerParams(vmem_limit_bytes=VMEM_BYTES),
        name=name,
    )(*ins)


def dot(a, b):
    return lax.dot_general(a, b, (((1,), (0,)), ((), ())), preferred_element_type=F32)


def dot_t(a, b):
    return lax.dot_general(a, b, (((1,), (1,)), ((), ())), preferred_element_type=F32)


def move(block, by):
    lanes = block.shape[1]
    at = lax.broadcasted_iota(jnp.int32, block.shape, 1)
    if by > 0:
        return jnp.where(at == 0, 0.0, pltpu.roll(block, 1, axis=1))
    return jnp.where(at == lanes - 1, 0.0, pltpu.roll(block, lanes - 1, axis=1))


def ch_peers(r, c):
    return [(r, lax.rem(c + d, CH)) for d in range(1, CH)]


def near_rows(r):
    return lax.rem(r + ROWS - 1, ROWS), lax.rem(r + 1, ROWS)


def same(a, b):
    return jnp.logical_and(a[0] == b[0], a[1] == b[1])


def greet_frames(links, me, sources, targets):
    barrier = pltpu.get_barrier_semaphore()
    for peer in sources:
        def tell(peer=peer):
            pl.semaphore_signal(barrier, inc=1, device_id=peer, device_id_type=MESH)

        pl.when(jnp.logical_not(same(peer, me)))(tell)
    _, y_hi, _, _, core = place(*me)
    pl.semaphore_wait(barrier, len(targets) - 1 + (core - y_hi) * (core - y_hi))


def sigmoid(v):
    return 1.0 / (1.0 + jnp.exp(-v))


def gain_columns(rows, which):
    blocks = [jnp.broadcast_to(rows[b, which : which + 1, :], (128, 128)).T[:96] for b in range(CH)]
    return jnp.concatenate(blocks, 0)


def front_body(links, held, made, scratch):
    feat, cot, w_far, gain_in, gain_attn = held
    act_out, feat_out, cot_frame, res_frame, inv_in, gain_rows = made
    every, w, act, res, mark = scratch
    r, c = coords()
    x, y_hi, z, y_lo, core = place(r, c)
    low, high = near_rows(r)
    c_sib, c_near = y_lo * 2 + 1 - core, (1 - y_lo) * 2 + core
    sibling, near = (r, c_sib), (r, c_near)
    targets = [owner(f, r) for f in range(4)]
    sources = [(z * 8 + core * 4 + x, b) for b in range(4)]
    others = ch_peers(r, c) + [(low, c), (high, c)]
    own_rows = pl.ds(1, 2)
    here = pltpu.make_async_copy(feat, every.at[c, :, own_rows], mark.at[0])
    here.start()
    weights = pltpu.make_async_copy(w_far, w, mark.at[1])
    weights.start()
    gain_rows[c] = jnp.zeros((8, 128), F32)
    pad = jnp.zeros((1, 32), F32)
    gain_rows[c, 0:1, :] = jnp.concatenate([gain_in[...].astype(F32), pad], 1)
    gain_rows[c, 1:2, :] = jnp.concatenate([gain_attn[...].astype(F32), pad], 1)
    greet_frames(links, (r, c), sources + others, targets + others)
    edges = [
        links.copy(feat.at[:, 1], every.at[c, :, 0], (high, c)),
        links.copy(feat.at[:, 0], every.at[c, :, 3], (low, c)),
    ]
    to_near = links.copy(feat, every.at[c, :, own_rows], near)
    to_sib = links.copy(feat, every.at[c, :, own_rows], sibling)
    gains = [links.copy(gain_rows.at[c], gain_rows.at[c], to) for to in ch_peers(r, c)]
    near_edges, sib_edges = [], []
    for n, h in enumerate((0, 3)):
        edges[n].wait_recv()
        part = every.at[c, :, h]
        near_edges.append(links.copy(part, part, near))
        sib_edges.append(links.copy(part, part, sibling))
    to_near.wait_recv()
    part = every.at[c_near, :, own_rows]
    passed = links.copy(part, part, sibling)
    for f in range(4):
        links.copy(cot.at[f], cot_frame.at[c], targets[f], own=same(targets[f], (r, c)), recv=40 + c)
    for copy in gains:
        copy.wait_recv()
    gain = gain_columns(gain_rows, 0)
    here.wait()
    to_sib.wait_recv()
    passed.wait_recv()
    keep_feat = pltpu.make_async_copy(every.at[:, :, own_rows], feat_out, mark.at[0])
    keep_feat.start()

    def activate(f, h):
        v = jnp.concatenate([every[b, f, h] for b in range(CH)], 0).astype(F32)
        inv = lax.rsqrt(jnp.mean(v * v, 0, keepdims=True) + EPSILON)
        before = v * inv * gain
        a = before * sigmoid(before)
        if h == 0:
            a = jnp.where(r == 0, 0.0, a)
        elif h == 3:
            a = jnp.where(r == ROWS - 1, 0.0, a)
        else:
            inv_in[2 * f + h - 1 : 2 * f + h, :] = inv
        act[:, pl.ds((4 * f + h) * 128, 128)] = a.astype(BF16)

    for f in range(4):
        activate(f, 1)
        activate(f, 2)
    far_edges = []
    for n, h in enumerate((0, 3)):
        near_edges[n].wait_recv()
        part = every.at[c_near, :, h]
        far_edges.append(links.copy(part, part, sibling))
    for copy in sib_edges + far_edges:
        copy.wait_recv()
    for f in range(4):
        activate(f, 0)
        activate(f, 3)
    keep_act = pltpu.make_async_copy(act, act_out, mark.at[2])
    keep_act.start()
    weights.wait()
    for f in range(4):
        acc = jnp.zeros((288, 256), F32)
        for t in range(3):
            source = f + t - 2
            if source < 0:
                continue
            for h in range(3):
                taps = w[pl.ds(9 * t + 3 * h, 3)].reshape(288, 384)
                acc += dot(taps, act[:, pl.ds((4 * source + h) * 128, 256)])
        for h in range(2):
            y = acc[:, 128 * h : 128 * h + 128]
            out = move(y[:96], 1) + y[96:192] + move(y[192:], -1)
            res[f, h] = (every[c, f, h + 1].astype(F32) + out).astype(BF16)
        links.copy(res.at[f], res_frame.at[c], targets[f], own=same(targets[f], (r, c)), recv=44 + c)
    keep_feat.wait()
    keep_act.wait()
    for b in range(CH):
        links.arrive(cot_frame.at[b], 40 + b)
    for b in range(CH):
        links.arrive(res_frame.at[b], 44 + b)
    links.finish()


def attn_norm(res_frame, full):
    for b in range(CH):
        for h in range(2):
            full[pl.ds(96 * b, 96), pl.ds(128 * h, 128)] = res_frame[b, h]
    x = full[...].astype(F32)
    return x, lax.rsqrt(jnp.mean(x * x, 0, keepdims=True) + EPSILON)


def attn_body(scale, links, held, made, scratch):
    res_frame, cot, gain_rows, w_qkv, w_out, w_far = held
    mine, prev_g, next_g, w_t_out = made
    (full, cot_full, q, g, k, v, k_t, exps, grad_p, grad_s, prob_row, tops, sums, deltas, stats, all_stats, weights, delta,
     send_k, send_v, came_k, came_v, own_k, own_v, sib_out, sib_in, send_q, came_q, own_q, grad, w, w_t, mark) = scratch
    r, c = coords()
    x, y_hi, z, y_lo, core = place(r, c)
    slot = core * 4 + x
    frame = y_hi * 2 + y_lo
    sibling = (r, y_lo * 2 + 1 - core)
    xs = [device(lax.rem(x + d, 4), y_hi, z, y_lo, core) for d in range(1, 4)]
    cross = [device(lax.rem(x + d, 4), y_hi, z, y_lo, 1 - core) for d in range(1, 4)]
    zs = [device(x, y_hi, lax.rem(z + d, 4), y_lo, core) for d in range(1, 4)]
    row = z * 8 + core * 4 + x
    row_low, row_high = near_rows(row)
    low, high = near_rows(r)
    around = [(i, b) for i in (row_low, row_high) for b in range(CH)]
    alike = xs + zs + cross + [sibling]
    sources = [owner(f, i) for i in (r, low, high) for f in range(4)]
    greet_frames(links, (r, c), sources + alike, [(row, b) for b in range(CH)] + around + alike)

    weights_in = pltpu.make_async_copy(w_far, w, mark.at[0])
    weights_in.start()
    for b in range(CH):
        for h in range(2):
            cot_full[pl.ds(96 * b, 96), pl.ds(128 * h, 128)] = cot[b, h]
    g[slot] = dot(w_out[...], cot_full[...]).astype(BF16)
    g_first = [links.copy(g.at[slot], g.at[slot], to) for to in (xs[0], xs[2], sibling)]
    gain = gain_columns(gain_rows, 1)
    gain = jnp.concatenate([gain, gain], 1)
    centre, inv = attn_norm(res_frame, full)
    normed = (centre * inv * gain).astype(BF16).astype(F32).T.astype(BF16)
    k[z] = dot(normed, w_qkv[:, 384:768]).astype(BF16)
    k_first = [links.copy(k.at[z], k.at[z], to) for to in (zs[0], zs[2])]
    v[z] = dot(normed, w_qkv[:, 768:]).astype(BF16)
    v_first = [links.copy(v.at[z], v.at[z], to) for to in (zs[0], zs[2])]
    q[slot] = dot(normed, w_qkv[:, :384]).T.astype(BF16)
    q_first = [links.copy(q.at[slot], q.at[slot], to) for to in (xs[0], xs[2], sibling)]

    def turn(j):
        k_t[:, pl.ds(pl.multiple_of(256 * j, 256), 256)] = k[j].T

    def tile(b, j):
        s = dot(k[j], q[b]) * scale
        top = jnp.max(s, 0, keepdims=True)
        e = jnp.exp(s - top)
        p = dot(v[j], g[b])
        exps[j, b] = e
        grad_p[j, b] = p
        tops[j, pl.ds(b, 1), :] = top
        sums[j, pl.ds(b, 1), :] = jnp.sum(e, 0, keepdims=True)
        deltas[j, pl.ds(b, 1), :] = jnp.sum(e * p, 0, keepdims=True)

    def block(dk, dx):
        other = core + dk - 2 * core * dk
        return other * 4 + lax.rem(x + dx, 4)

    def key(dz):
        return lax.rem(z + dz, 4)

    def tiles(count, which):
        def step(n, carry):
            dk, dx, dz = which(n)
            tile(block(dk, dx), key(dz))
            return carry

        lax.fori_loop(0, count, step, 0)

    def relay_ring(first, ref, base, i, rows, peers, forward):
        on = []
        for side in range(2):
            first[side].wait_recv()
            came = base + lax.rem(i + 3 - 2 * side, 4)
            part = ref.at[came, pl.ds(rows * side, rows)]
            on.append(links.copy(part, part, peers[2 * side]))
            if forward:
                on.append(links.copy(ref.at[came], ref.at[came], sibling))
        return on

    turn(z)
    tile(slot, z)
    weights_in.wait()
    for t in range(3):
        for n in range(3):
            piece = jnp.concatenate([w[9 * t + 3 * h + n] for h in range(3)], 0)
            w_t[t, pl.ds(384 * n, 384), :] = piece.T
    weights_out = pltpu.make_async_copy(w_t, w_t_out, mark.at[0])
    weights_out.start()
    g_on = relay_ring(g_first, g, core * 4, x, 192, xs, True)
    k_on = relay_ring(k_first, k, 0, z, 128, zs, False)
    q_on = relay_ring(q_first, q, core * 4, x, 192, xs, True)
    v_on = relay_ring(v_first, v, 0, z, 128, zs, False)
    q_first[2].wait_recv()
    g_first[2].wait_recv()
    tiles(2, lambda n: (0, 0, 1 + 2 * n))
    tiles(3, lambda n: (1, 0, n + n // 2))
    turn(key(1))
    turn(key(3))
    q_on[1].wait_recv()
    q_on[3].wait_recv()
    g_on[1].wait_recv()
    g_on[3].wait_recv()

    def beside(n):
        dz = n // 4
        return lax.rem(n // 2, 2), 1 + 2 * lax.rem(n, 2), dz + dz // 2

    tiles(12, beside)
    for on in (g_on, q_on):
        on[0].wait_recv()
        on[2].wait_recv()
    at = core * 4 + lax.rem(x + 2, 4)
    last = [links.copy(ref.at[at], ref.at[at], sibling) for ref in (g, q)]
    for copy in k_on + v_on:
        copy.wait_recv()
    turn(key(2))

    def beyond(n):
        dx = n // 2
        return lax.rem(n, 2), dx + dx // 2, 2

    tiles(6, beyond)
    tiles(4, lambda n: (0, 2, n))
    for copy in last:
        copy.wait_recv()
    tiles(4, lambda n: (1, 2, n))

    top = functools.reduce(jnp.maximum, [tops[j] for j in range(4)])
    shift = [jnp.exp(tops[j] - top) for j in range(4)]
    stats[0] = top
    stats[1] = sum(sums[j] * shift[j] for j in range(4))
    stats[2] = sum(deltas[j] * shift[j] for j in range(4))
    shared = [links.copy(stats, all_stats.at[n], to) for n, to in enumerate(xs + cross + [sibling])]
    for copy in shared:
        copy.wait_recv()
    parts = [stats] + [all_stats.at[n] for n in range(7)]
    top = functools.reduce(jnp.maximum, [p[0] for p in parts])
    total = sum(p[1] * jnp.exp(p[0] - top) for p in parts)
    delta[...] = sum(p[2] * jnp.exp(p[0] - top) for p in parts) / total
    for j in range(4):
        weights[j] = jnp.exp(tops[j] - top) / total

    back = []
    for n, dz in enumerate((2, 1, 3, 0)):
        j = key(dz)
        rows = pl.ds(pl.multiple_of(256 * j, 256), 256)

        def step(b, carry, j=j, rows=rows):
            prob = exps[j, b] * weights[j, pl.ds(b, 1), :]
            prob_row[b] = prob.astype(BF16)
            grad_s[b, rows, :] = (prob * (grad_p[j, b] - delta[pl.ds(b, 1), :])).astype(BF16)
            return carry

        lax.fori_loop(0, 8, step, 0)
        for_k = sum(dot_t(grad_s[b, rows, :], q[b]) for b in range(8)) * scale
        for_v = sum(dot_t(prob_row[b], g[b]) for b in range(8))
        if dz:
            send_k[n] = for_k.astype(BF16)
            send_v[n] = for_v.astype(BF16)
            back.append(links.copy(send_k.at[n], came_k.at[n], zs[dz - 1]))
            back.append(links.copy(send_v.at[n], came_v.at[n], zs[dz - 1]))
        else:
            own_k[...] = for_k
            own_v[...] = for_v
    sib = []
    for dx in range(4):
        sib_out[dx] = (dot(k_t[...], grad_s[block(1, dx)]) * scale).astype(BF16)
        sib.append(links.copy(sib_out.at[dx], sib_in.at[dx], sibling))
    for n, dx in enumerate((2, 1, 3, 0)):
        for_q = dot(k_t[...], grad_s[block(0, dx)]) * scale
        sib[dx].wait_recv()
        for_q += sib_in[dx].astype(F32)
        if dx:
            send_q[n] = for_q.astype(BF16)
            back.append(links.copy(send_q.at[n], came_q.at[n], xs[dx - 1]))
        else:
            own_q[...] = for_q
    weights_out.wait()
    for copy in back:
        copy.wait_recv()
    for n in range(3):
        own_k[...] += came_k[n].astype(F32)
        own_v[...] += came_v[n].astype(F32)
        own_q[...] += came_q[n].astype(F32)
    back_normed = (
        dot(w_qkv[:, :384], own_q[...].astype(BF16))
        + dot_t(w_qkv[:, 384:768], own_k[...].astype(BF16))
        + dot_t(w_qkv[:, 768:], own_v[...].astype(BF16))
    )
    scaled = back_normed.astype(BF16).astype(F32) * gain
    centre = full[...].astype(F32)
    inner = jnp.mean(centre * scaled, 0, keepdims=True)
    out = cot_full[...].astype(F32) + inv * scaled - centre * (inv * inv * inv * inner)
    for b in range(CH):
        for h in range(2):
            grad[b, h] = out[96 * b : 96 * b + 96, 128 * h : 128 * h + 128].astype(BF16)
    for b in range(CH):
        to = (row, b)
        links.copy(grad.at[b], mine.at[frame], to, own=same(to, (r, c)), recv=64 + frame)
    for b in range(CH):
        links.copy(grad.at[b, 1], prev_g.at[frame], (row_high, b), recv=68 + frame)
        links.copy(grad.at[b, 0], next_g.at[frame], (row_low, b), recv=72 + frame)
    for f in range(4):
        links.arrive(mine.at[f], 64 + f)
        links.arrive(prev_g.at[f], 68 + f)
        links.arrive(next_g.at[f], 72 + f)
    links.finish()


def tail_kernel(links, held, made, scratch):
    own, prev_g, next_g, act_far, w_t_far, feat_far, inv_in, gain_rows = held
    out, flat = made
    rows, lines, weight, part, all_part, inner, all_inner, came1, came2, came3, sum1, sum2, sum3, act, w_t, all_feat, mark = scratch
    r, c = coords()
    x, y_hi, z, y_lo, core = place(r, c)
    xs = [device(lax.rem(x + d, 4), y_hi, z, y_lo, core) for d in range(1, 4)]
    zs = [device(x, y_hi, lax.rem(z + d, 4), y_lo, core) for d in range(1, 4)]
    x_at = [lax.rem(x + d, 4) for d in range(1, 4)]
    z_at = [lax.rem(z + d, 4) for d in range(1, 4)]
    across = device(x, 1 - y_hi, z, y_lo, core)
    chs = ch_peers(r, c)
    halves = (
        (x, xs, x_at, z, zs, z_at),
        (z, zs, z_at, x, xs, x_at),
    )
    inside = [
        pltpu.make_async_copy(src, dst, mark.at[2 + n])
        for n, (src, dst) in enumerate(((act_far, act), (w_t_far, w_t), (feat_far, all_feat)))
    ]
    for copy in inside:
        copy.start()
    links.greet(xs + zs + [across] + chs, 10)
    moved = []
    for f in range(4):
        both = []
        for h in range(2):
            y = own[f, h].astype(F32)
            both.append(jnp.concatenate([move(y, -1), y, move(y, 1)], 0).astype(BF16))
        moved.append(jnp.concatenate(both, 1))
    inside[0].wait()
    for t in range(3):
        for h in range(3):
            acc = jnp.zeros((288, 384), F32)
            for f in range(4):
                source = f + t - 2
                if source < 0:
                    continue
                acc += dot_t(moved[f], act[:, pl.ds((4 * source + h) * 128, 256)])
            for lane in range(3):
                at = (3 * (3 * t + h) + lane) * 288
                weight[pl.ds(at, 288), :] = acc[:, 128 * lane : 128 * lane + 128].astype(BF16)
    weight[pl.ds(27 * 288, 416), :] = jnp.zeros((416, 128), BF16)
    first = []
    for half, (a, peers, ats, _, _, _) in enumerate(halves):
        for d in range(3):
            src = weight.at[pl.ds(4096 * half + 1024 * ats[d], 1024)]
            first.append(links.copy(src, came1.at[half, d], peers[d]))
    for f in range(4):
        rows[f, 0] = jnp.where(r == 0, 0.0, prev_g[f].astype(F32)).astype(BF16)
        rows[f, 1] = own[f, 0]
        rows[f, 2] = own[f, 1]
        rows[f, 3] = jnp.where(r == ROWS - 1, 0.0, next_g[f].astype(F32)).astype(BF16)
    for f in range(4):
        for h in range(3):
            for k in range(2):
                lines[f, pl.ds(96 * h, 96), pl.ds(128 * k, 128)] = rows[f, 2 - h + k]
    gain = gain_columns(gain_rows, 0)
    inside[1].wait()
    inside[2].wait()
    for f in range(4):
        acc = jnp.zeros((1152, 256), F32)
        for t in range(3):
            source = f + 2 - t
            if source > 3:
                continue
            acc += dot(w_t[t], lines[source])
        for h in range(2):
            y = acc[:, 128 * h : 128 * h + 128]
            total = move(y[:384], -1) + y[384:768] + move(y[768:], 1)
            v = jnp.concatenate([all_feat[b, f, h] for b in range(CH)], 0).astype(F32)
            before = v * inv_in[2 * f + h : 2 * f + h + 1, :] * gain
            sig = sigmoid(before)
            slope = sig * (1.0 + before * (1.0 - sig))
            inner[2 * f + h : 2 * f + h + 1, :] = jnp.sum(v * slope * gain * total, 0, keepdims=True)
            for b in range(CH):
                part[b, f, h] = total[96 * b : 96 * b + 96].astype(BF16)
    parts = []
    for d in range(3):
        parts.append(links.copy(part.at[chs[d][1]], all_part.at[d], chs[d]))
        parts.append(links.copy(inner, all_inner.at[d], chs[d]))
    for copy in first:
        copy.wait_recv()
    second = []
    for half, (a, _, _, b, peers, ats) in enumerate(halves):
        total = weight[pl.ds(4096 * half + 1024 * a, 1024), :].astype(F32)
        for d in range(3):
            total += came1[half, d].astype(F32)
        sum1[half] = total.astype(BF16)
        for d in range(3):
            src = sum1.at[half, pl.ds(256 * ats[d], 256)]
            second.append(links.copy(src, came2.at[half, d], peers[d]))
    for copy in second:
        copy.wait_recv()
    third = []
    for half, (a, _, _, b, _, _) in enumerate(halves):
        total = sum1[half, pl.ds(256 * b, 256), :].astype(F32)
        for d in range(3):
            total += came2[half, d].astype(F32)
        sum2[half] = total.astype(BF16)
        src = sum2.at[half, pl.ds(128 * (1 - y_hi), 128)]
        third.append(links.copy(src, came3.at[half], across))
    for copy in third:
        copy.wait_recv()
    fourth, kept = [], []
    for half, (a, _, _, b, _, _) in enumerate(halves):
        total = sum2[half, pl.ds(128 * y_hi, 128), :].astype(F32) + came3[half].astype(F32)
        sum3[half] = total.astype(BF16)
        at = flat.at[pl.ds(4096 * half + 1024 * a + 256 * b + 128 * y_hi, 128)]
        kept.append(pltpu.make_async_copy(sum3.at[half], at, mark.at[half]))
        kept[half].start()
        fourth.append(links.copy(sum3.at[half], at, across))
    fifth = []
    for half, (a, _, _, b, peers, _) in enumerate(halves):
        kept[half].wait()
        fourth[half].wait_recv()
        at = flat.at[pl.ds(4096 * half + 1024 * a + 256 * b, 256)]
        for d in range(3):
            fifth.append(links.copy(at, at, peers[d]))
    sixth = []
    for half, (a, peers, _, _, _, _) in enumerate(halves):
        for d in range(3):
            fifth[3 * half + d].wait_recv()
        at = flat.at[pl.ds(4096 * half + 1024 * a, 1024)]
        for d in range(3):
            sixth.append(links.copy(at, at, peers[d]))
    for copy in parts:
        copy.wait_recv()
    mean = (inner[...] + all_inner[0] + all_inner[1] + all_inner[2]) / 384.0
    gain = jnp.broadcast_to(gain_rows[c, 0:1, :], (128, 128)).T[:96]
    for f in range(4):
        for h in range(2):
            v = all_feat[c, f, h].astype(F32)
            inv = inv_in[2 * f + h : 2 * f + h + 1, :]
            total = part[c, f, h].astype(F32)
            for d in range(3):
                total += all_part[d, f, h].astype(F32)
            before = v * inv * gain
            sig = sigmoid(before)
            scaled = total * (sig * (1.0 + before * (1.0 - sig))) * gain
            cube = inv * inv * inv * mean[2 * f + h : 2 * f + h + 1, :]
            out[f, h] = (own[f, h].astype(F32) + inv * scaled - v * cube).astype(BF16)
    for copy in sixth:
        copy.wait_recv()
    links.finish()


def widen_kernel(scale, flat, out):
    for k in range(9):
        for lane in range(3):
            piece = flat[pl.ds((3 * k + lane) * 288, 288), :].astype(F32) * scale
            out[pl.ds(288 * k, 288), pl.ds(128 * lane, 128)] = piece


def on_device(features, gain_in, w_conv, gain_attn, w_qkv, w_out, cotangent):
    scale = 1.0 / math.sqrt(384)
    near, far = pltpu.VMEM, pl.ANY
    act, all_feat, cot_frame, res_frame, inv_in, gain_rows = fused(
        0,
        front_body,
        [
            (features, far),
            (cotangent, far),
            (w_conv, far),
            (gain_in.reshape(1, 96), near),
            (gain_attn.reshape(1, 96), near),
        ],
        [
            ((384, 2048), BF16, far),
            ((4, 4, 2, 96, 128), BF16, far),
            ((4, 2, 96, 128), BF16, far),
            ((4, 2, 96, 128), BF16, far),
            ((8, 128), F32, near),
            ((4, 8, 128), F32, near),
        ],
        [
            pltpu.VMEM((4, 4, 4, 96, 128), BF16),
            pltpu.VMEM((27, 96, 384), BF16),
            pltpu.VMEM((384, 2048), BF16),
            pltpu.VMEM((4, 2, 96, 128), BF16),
            pltpu.SemaphoreType.DMA((3,)),
        ],
        48,
    )
    own, prev_g, next_g, w_t = fused(
        2,
        functools.partial(attn_body, scale),
        [(res_frame, near), (cot_frame, near), (gain_rows, near), (w_qkv, near), (w_out, near), (w_conv, far)],
        [
            ((4, 2, 96, 128), BF16, pl.ANY),
            ((4, 96, 128), BF16, pl.ANY),
            ((4, 96, 128), BF16, pl.ANY),
            ((3, 1152, 288), BF16, pl.ANY),
        ],
        [
            pltpu.VMEM((384, 256), BF16),
            pltpu.VMEM((384, 256), BF16),
            pltpu.VMEM((8, 384, 256), BF16),
            pltpu.VMEM((8, 384, 256), BF16),
            pltpu.VMEM((4, 256, 384), BF16),
            pltpu.VMEM((4, 256, 384), BF16),
            pltpu.VMEM((384, 1024), BF16),
            pltpu.VMEM((4, 8, 256, 256), F32),
            pltpu.VMEM((4, 8, 256, 256), F32),
            pltpu.VMEM((8, 1024, 256), BF16),
            pltpu.VMEM((8, 256, 256), BF16),
            pltpu.VMEM((4, 8, 256), F32),
            pltpu.VMEM((4, 8, 256), F32),
            pltpu.VMEM((4, 8, 256), F32),
            pltpu.VMEM((3, 8, 256), F32),
            pltpu.VMEM((7, 3, 8, 256), F32),
            pltpu.VMEM((4, 8, 256), F32),
            pltpu.VMEM((8, 256), F32),
            pltpu.VMEM((3, 256, 384), BF16),
            pltpu.VMEM((3, 256, 384), BF16),
            pltpu.VMEM((3, 256, 384), BF16),
            pltpu.VMEM((3, 256, 384), BF16),
            pltpu.VMEM((256, 384), F32),
            pltpu.VMEM((256, 384), F32),
            pltpu.VMEM((4, 384, 256), BF16),
            pltpu.VMEM((4, 384, 256), BF16),
            pltpu.VMEM((3, 384, 256), BF16),
            pltpu.VMEM((3, 384, 256), BF16),
            pltpu.VMEM((384, 256), F32),
            pltpu.VMEM((4, 2, 96, 128), BF16),
            pltpu.VMEM((27, 96, 384), BF16),
            pltpu.VMEM((3, 1152, 288), BF16),
            pltpu.SemaphoreType.DMA((1,)),
        ],
        76,
    )
    out, flat = fused(
        6,
        tail_kernel,
        [
            (own, near),
            (prev_g, near),
            (next_g, near),
            (act, far),
            (w_t, far),
            (all_feat, far),
            (inv_in, near),
            (gain_rows, near),
        ],
        [((4, 2, 96, 128), BF16, pltpu.VMEM), ((8192, 128), BF16, pl.ANY)],
        [
            pltpu.VMEM((4, 4, 96, 128), BF16),
            pltpu.VMEM((4, 288, 256), BF16),
            pltpu.VMEM((8192, 128), BF16),
            pltpu.VMEM((4, 4, 2, 96, 128), BF16),
            pltpu.VMEM((3, 4, 2, 96, 128), BF16),
            pltpu.VMEM((8, 128), F32),
            pltpu.VMEM((3, 8, 128), F32),
            pltpu.VMEM((2, 3, 1024, 128), BF16),
            pltpu.VMEM((2, 3, 256, 128), BF16),
            pltpu.VMEM((2, 128, 128), BF16),
            pltpu.VMEM((2, 1024, 128), BF16),
            pltpu.VMEM((2, 256, 128), BF16),
            pltpu.VMEM((2, 128, 128), BF16),
            pltpu.VMEM((384, 2048), BF16),
            pltpu.VMEM((3, 1152, 288), BF16),
            pltpu.VMEM((4, 4, 2, 96, 128), BF16),
            pltpu.SemaphoreType.DMA((5,)),
        ],
        34,
    )
    cell_scale = 1.0 / math.sqrt(32768)
    (grad_weights,) = compute(
        functools.partial(widen_kernel, cell_scale),
        [((2592, 384), F32)],
        flat,
        name="widen",
    )
    return out, grad_weights.reshape(27, 96, 384)


def solution(mesh):
    return jax.shard_map(
        on_device,
        mesh=mesh,
        in_specs=(
            P(None, "row", "ch", None),
            P("ch"),
            P(None, "ch", None),
            P("ch"),
            P(),
            P(),
            P(None, "row", "ch", None),
        ),
        out_specs=(P(None, "row", "ch", None), P(None, "ch", None)),
        check_vma=False,
    )
```

```python
import functools
import math
import types

import jax
import jax.numpy as jnp
from jax import lax
from jax.experimental import pallas as pl
from jax.experimental.pallas import tpu as pltpu
from jax.sharding import PartitionSpec as P

EPSILON = 1e-06
MESH = pl.DeviceIdType.MESH
F32 = jnp.float32
BF16 = jnp.bfloat16
ROWS = 32
SENDS = 128
COT, RES, OWN, PREV, NEXT = range(SENDS, SENDS + 20, 4)
CH = 4
VMEM_BYTES = 60 * 1024 * 1024


def coords():
    return lax.axis_index("row"), lax.axis_index("ch")


def place(r, c):
    return lax.rem(r, 4), lax.rem(r // 4, 2), r // 8, c // 2, lax.rem(c, 2)


def device(x, y_hi, z, y_lo, core):
    return z * 8 + y_hi * 4 + x, y_lo * 2 + core


def owner(f, row):
    x, y_hi, z, _, _ = place(row, 0)
    return device(x, f // 2, z, f % 2, y_hi)


class Links:
    def __init__(self, send, recv):
        self.send, self.recv, self.sent, self.at = send, recv, [], 0

    def greet(self, peers, count):
        barrier = pltpu.get_barrier_semaphore()
        for peer in peers:
            pl.semaphore_signal(barrier, inc=1, device_id=peer, device_id_type=MESH)
        pl.semaphore_wait(barrier, count)

    def copy(self, src, dst, to, own=None, recv=None):
        k = self.at
        self.at += 1
        mark = self.recv.at[k if recv is None else recv]
        far = pltpu.make_async_remote_copy(
            src_ref=src,
            dst_ref=dst,
            send_sem=self.send.at[k],
            recv_sem=mark,
            device_id=to,
            device_id_type=MESH,
        )
        if own is None:
            far.start()
        else:
            pl.when(jnp.logical_not(own))(far.start)
            pl.when(own)(pltpu.make_async_copy(src, dst, mark).start)
        self.sent.append((far, own))
        return far

    def arrive(self, dst, k):
        pltpu.make_async_copy(dst, dst, self.recv.at[k]).wait()

    def finish(self):
        for far, own in self.sent:
            if own is None:
                far.wait_send()
            else:
                pl.when(jnp.logical_not(own))(far.wait_send)


def fused(cid, body, held, made, scratch, count):
    names = [*held, *made, *scratch]

    def kernel(*refs):
        body(Links(*refs[-2:]), types.SimpleNamespace(**dict(zip(names, refs))))

    return pl.pallas_call(
        kernel,
        out_shape=[jax.ShapeDtypeStruct(s, t) for s, t, _ in made.values()],
        in_specs=[pl.BlockSpec(memory_space=m) for _, m in held.values()],
        out_specs=[pl.BlockSpec(memory_space=m) for _, _, m in made.values()],
        scratch_shapes=[*scratch.values()] + [pltpu.SemaphoreType.DMA((n,)) for n in count],
        compiler_params=pltpu.CompilerParams(
            collective_id=cid, has_side_effects=True, vmem_limit_bytes=VMEM_BYTES
        ),
        name="fused_%d" % cid,
    )(*[array for array, _ in held.values()])


def compute(body, outs, *ins, scratch=(), name):
    return pl.pallas_call(
        body,
        out_shape=[jax.ShapeDtypeStruct(s, t) for s, t in outs],
        in_specs=[pl.BlockSpec(memory_space=pltpu.VMEM)] * len(ins),
        out_specs=[pl.BlockSpec(memory_space=pltpu.VMEM)] * len(outs),
        scratch_shapes=list(scratch),
        compiler_params=pltpu.CompilerParams(vmem_limit_bytes=VMEM_BYTES),
        name=name,
    )(*ins)


def dot(a, b):
    return lax.dot_general(a, b, (((1,), (0,)), ((), ())), preferred_element_type=F32)


def dot_t(a, b):
    return lax.dot_general(a, b, (((1,), (1,)), ((), ())), preferred_element_type=F32)


def move(block, by):
    lanes = block.shape[1]
    at = lax.broadcasted_iota(jnp.int32, block.shape, 1)
    if by > 0:
        return jnp.where(at == 0, 0.0, pltpu.roll(block, 1, axis=1))
    return jnp.where(at == lanes - 1, 0.0, pltpu.roll(block, lanes - 1, axis=1))


def ch_peers(r, c):
    return [(r, lax.rem(c + d, CH)) for d in range(1, CH)]


def near_rows(r):
    return lax.rem(r + ROWS - 1, ROWS), lax.rem(r + 1, ROWS)


def same(a, b):
    return jnp.logical_and(a[0] == b[0], a[1] == b[1])


def greet_frames(me, sources, targets):
    barrier = pltpu.get_barrier_semaphore()
    for peer in sources:
        def tell(peer=peer):
            pl.semaphore_signal(barrier, inc=1, device_id=peer, device_id_type=MESH)

        pl.when(jnp.logical_not(same(peer, me)))(tell)
    _, y_hi, _, _, core = place(*me)
    pl.semaphore_wait(barrier, len(targets) - 2 + 2 * (core - y_hi) * (core - y_hi))


def sigmoid(v):
    return 1.0 / (1.0 + jnp.exp(-v))


def gain_columns(rows, which):
    blocks = [jnp.broadcast_to(rows[b, which : which + 1, :], (128, 128)).T[:96] for b in range(CH)]
    return jnp.concatenate(blocks, 0)


class Place:
    def __init__(self):
        r, c = self.r, self.c = self.me = coords()
        x, y_hi, z, y_lo, core = self.x, self.y_hi, self.z, self.y_lo, self.core = place(r, c)
        self.slot = core * 4 + x
        self.frame = y_hi * 2 + y_lo
        self.low, self.high = near_rows(r)
        self.c_near = (1 - y_lo) * 2 + core
        self.sibling = (r, y_lo * 2 + 1 - core)
        self.near = (r, self.c_near)
        self.chs = ch_peers(r, c)
        self.xs = [device(lax.rem(x + d, 4), y_hi, z, y_lo, core) for d in range(1, 4)]
        self.cross = [device(lax.rem(x + d, 4), y_hi, z, y_lo, 1 - core) for d in range(1, 4)]
        self.zs = [device(x, y_hi, lax.rem(z + d, 4), y_lo, core) for d in range(1, 4)]
        self.across = device(x, 1 - y_hi, z, y_lo, core)
        self.targets = [owner(f, r) for f in range(4)]
        self.row = z * 8 + core * 4 + x
        self.sources = [(self.row, b) for b in range(CH)]

    def greet(self):
        at = self
        alike = at.chs + at.xs + at.cross + at.zs + [at.across, (at.low, at.c), (at.high, at.c)]
        there = [(i, b) for i in near_rows(at.row) for b in range(CH)]
        whose = [owner(f, i) for i in (at.low, at.high) for f in range(4)]
        greet_frames(at.me, at.targets + at.sources + whose + alike, at.targets + at.sources + there + alike)


def front(links, at, m):
    r, c, near, sibling = at.r, at.c, at.near, at.sibling
    every, act = m.every, m.act
    here = pltpu.make_async_copy(m.feat, every.at[c, :, pl.ds(1, 2)], m.mark.at[0])
    here.start()
    weights = pltpu.make_async_copy(m.w_far, m.w, m.mark.at[1])
    weights.start()
    m.gain_rows[c] = jnp.zeros((8, 128), F32)
    pad = jnp.zeros((1, 32), F32)
    m.gain_rows[c, 0:1, :] = jnp.concatenate([m.gain_in[...].astype(F32), pad], 1)
    m.gain_rows[c, 1:2, :] = jnp.concatenate([m.gain_attn[...].astype(F32), pad], 1)
    at.greet()
    pairs = [pl.ds(2 * p, 2) for p in range(2)]
    to_near, edges = [], []
    for two in pairs:
        to_near.append(links.copy(m.feat.at[two], every.at[c, two, pl.ds(1, 2)], near))
        edges.append(links.copy(m.feat.at[two, 1], every.at[c, two, 0], (at.high, c)))
        edges.append(links.copy(m.feat.at[two, 0], every.at[c, two, 3], (at.low, c)))
    to_sib = links.copy(m.feat, every.at[c, :, pl.ds(1, 2)], sibling)
    gains = [links.copy(m.gain_rows.at[c], m.gain_rows.at[c], to) for to in at.chs]
    for f in range(4):
        own = same(at.targets[f], at.me)
        links.copy(m.cot.at[f], m.cot_frame.at[c], at.targets[f], own=own, recv=COT + c)
    passed, near_edges, sib_edges = [], [], []
    for p, two in enumerate(pairs):
        to_near[p].wait_recv()
        part = every.at[at.c_near, two, pl.ds(1, 2)]
        near_edges.append(links.copy(every.at[at.c_near, two, 2], every.at[at.c_near, two, 0], (at.high, c)))
        near_edges.append(links.copy(every.at[at.c_near, two, 1], every.at[at.c_near, two, 3], (at.low, c)))
        passed.append(links.copy(part, part, sibling))
        for n, h in enumerate((0, 3)):
            edges[2 * p + n].wait_recv()
            part = every.at[c, two, h]
            sib_edges.append(links.copy(part, part, sibling))
    for b in range(CH):
        links.arrive(m.cot_frame.at[b], COT + b)
    for b in range(CH):
        for h in range(2):
            m.cot_full[pl.ds(96 * b, 96), pl.ds(128 * h, 128)] = m.cot_frame[b, h]
    m.g[at.slot] = dot(m.w_out[...], m.cot_full[...]).astype(BF16)
    at.g_first = [links.copy(m.g.at[at.slot], m.g.at[at.slot], to) for to in (at.xs[0], at.xs[2], sibling)]
    for copy in gains:
        copy.wait_recv()
    gain = gain_columns(m.gain_rows, 0)

    def activate(f, h):
        v = jnp.concatenate([every[b, f, h] for b in range(CH)], 0).astype(F32)
        inv = lax.rsqrt(jnp.mean(v * v, 0, keepdims=True) + EPSILON)
        before = v * inv * gain
        a = before * sigmoid(before)
        if h == 0:
            a = jnp.where(r == 0, 0.0, a)
        elif h == 3:
            a = jnp.where(r == ROWS - 1, 0.0, a)
        else:
            m.inv_in[2 * f + h - 1 : 2 * f + h, :] = inv
        act[:, pl.ds((4 * f + h) * 128, 128)] = a.astype(BF16)

    here.wait()
    to_sib.wait_recv()
    passed[0].wait_recv()
    for f in range(2):
        activate(f, 1)
        activate(f, 2)
    far_edges = []
    for p, two in enumerate(pairs):
        for n, h in enumerate((0, 3)):
            near_edges[2 * p + n].wait_recv()
            part = every.at[at.c_near, two, h]
            far_edges.append(links.copy(part, part, sibling))
    passed[1].wait_recv()
    for f in range(2, 4):
        activate(f, 1)
        activate(f, 2)
    weights.wait()
    for p in range(2):
        for n in range(2):
            sib_edges[2 * p + n].wait_recv()
            far_edges[2 * p + n].wait_recv()
        for f in (2 * p, 2 * p + 1):
            activate(f, 0)
            activate(f, 3)
        for f in (2 * p, 2 * p + 1):
            acc = jnp.zeros((288, 256), F32)
            for t in range(3):
                source = f + t - 2
                if source < 0:
                    continue
                for h in range(3):
                    taps = m.w[pl.ds(9 * t + 3 * h, 3)].reshape(288, 384)
                    acc += dot(taps, act[:, pl.ds((4 * source + h) * 128, 256)])
            for h in range(2):
                y = acc[:, 128 * h : 128 * h + 128]
                out = move(y[:96], 1) + y[96:192] + move(y[192:], -1)
                m.res[f, h] = (every[c, f, h + 1].astype(F32) + out).astype(BF16)
            own = same(at.targets[f], at.me)
            links.copy(m.res.at[f], m.res_frame.at[c], at.targets[f], own=own, recv=RES + c)


def attention(links, at, m):
    scale = 1.0 / math.sqrt(384)
    x, z, core, slot, sibling = at.x, at.z, at.core, at.slot, at.sibling
    q, g, k, v, k_t = m.q, m.g, m.k, m.v, m.k_t
    w_qkv = m.w_qkv

    def relay_ring(first, ref, base, i, rows, peers, forward):
        on = []
        for side in range(2):
            first[side].wait_recv()
            came = base + lax.rem(i + 3 - 2 * side, 4)
            part = ref.at[came, pl.ds(rows * side, rows)]
            on.append(links.copy(part, part, peers[2 * side]))
            if forward:
                on.append(links.copy(ref.at[came], ref.at[came], sibling))
        return on

    g_on = relay_ring(at.g_first, g, core * 4, x, 192, at.xs, True)
    gain = gain_columns(m.gain_rows, 1)
    gain = jnp.concatenate([gain, gain], 1)
    for b in range(CH):
        links.arrive(m.res_frame.at[b], RES + b)
    for b in range(CH):
        for h in range(2):
            m.full[pl.ds(96 * b, 96), pl.ds(128 * h, 128)] = m.res_frame[b, h]
    centre = m.full[...].astype(F32)
    inv = lax.rsqrt(jnp.mean(centre * centre, 0, keepdims=True) + EPSILON)
    m.norm[z] = (centre * inv * gain).astype(BF16).astype(F32).T.astype(BF16)
    n_first = [links.copy(m.norm.at[z], m.norm.at[z], to) for to in (at.zs[0], at.zs[2])]
    q[slot] = dot(m.norm[z], w_qkv[:, :384]).T.astype(BF16)
    q_first = [links.copy(q.at[slot], q.at[slot], to) for to in (at.xs[0], at.xs[2], sibling)]

    def project(j):
        k[j] = dot(m.norm[j], w_qkv[:, 384:768]).astype(BF16)
        v[j] = dot(m.norm[j], w_qkv[:, 768:]).astype(BF16)
        k_t[:, pl.ds(pl.multiple_of(256 * j, 256), 256)] = k[j].T

    def tile(b, j):
        s = dot(k[j], q[b]) * scale
        top = jnp.max(s, 0, keepdims=True)
        e = jnp.exp(s - top)
        p = dot(v[j], g[b])
        m.exps[j, b] = e
        m.grad_p[j, b] = p
        m.tops[j, pl.ds(b, 1), :] = top
        m.sums[j, pl.ds(b, 1), :] = jnp.sum(e, 0, keepdims=True)
        m.deltas[j, pl.ds(b, 1), :] = jnp.sum(e * p, 0, keepdims=True)

    def block(dk, dx):
        other = core + dk - 2 * core * dk
        return other * 4 + lax.rem(x + dx, 4)

    def key(dz):
        return lax.rem(z + dz, 4)

    def tiles(count, unroll, which):
        def step(n, carry):
            dk, dx, dz = which(n)
            tile(block(dk, dx), key(dz))
            return carry

        lax.fori_loop(0, count, step, 0, unroll=unroll)

    project(z)
    g_on[1].wait_recv()
    g_on[3].wait_recv()
    g_on[0].wait_recv()
    g_on[2].wait_recv()
    far_x = core * 4 + lax.rem(x + 2, 4)
    g_last = links.copy(g.at[far_x], g.at[far_x], sibling)
    at.g_first[2].wait_recv()
    q_first[2].wait_recv()
    tiles(2, 2, lambda n: (n, 0, 0))
    for t in range(3):
        for n in range(3):
            piece = jnp.concatenate([m.w[9 * t + 3 * h + n] for h in range(3)], 0)
            m.w_t[t, pl.ds(384 * n, 384), :] = piece.T
    n_on = relay_ring(n_first, m.norm, 0, z, 128, at.zs, False)
    q_on = relay_ring(q_first, q, core * 4, x, 192, at.xs, True)
    project(key(1))
    project(key(3))
    tiles(4, 4, lambda n: (n // 2, 0, 1 + 2 * lax.rem(n, 2)))
    q_on[1].wait_recv()
    q_on[3].wait_recv()

    def beside(n):
        dz = n // 4
        return lax.rem(n // 2, 2), 1 + 2 * lax.rem(n, 2), dz + dz // 2

    tiles(12, 4, beside)
    q_on[0].wait_recv()
    q_on[2].wait_recv()
    q_last = links.copy(q.at[far_x], q.at[far_x], sibling)
    n_on[0].wait_recv()
    n_on[1].wait_recv()
    project(key(2))

    def beyond(n):
        dx = n // 2
        return lax.rem(n, 2), dx + dx // 2, 2

    tiles(6, 3, beyond)
    tiles(4, 4, lambda n: (0, 2, n))
    q_last.wait_recv()
    g_last.wait_recv()
    tiles(4, 4, lambda n: (1, 2, n))

    tops = [m.tops[j] for j in range(4)]
    top = functools.reduce(jnp.maximum, tops)
    shift = [jnp.exp(t - top) for t in tops]
    m.stats[0] = top
    m.stats[1] = sum(m.sums[j] * shift[j] for j in range(4))
    m.stats[2] = sum(m.deltas[j] * shift[j] for j in range(4))
    peers = at.xs + at.cross + [sibling]
    shared = [links.copy(m.stats, m.all_stats.at[n], to) for n, to in enumerate(peers)]
    for copy in shared:
        copy.wait_recv()
    parts = [m.stats] + [m.all_stats.at[n] for n in range(7)]
    top = functools.reduce(jnp.maximum, [p[0] for p in parts])
    total = sum(p[1] * jnp.exp(p[0] - top) for p in parts)
    m.delta[...] = sum(p[2] * jnp.exp(p[0] - top) for p in parts) / total
    for j in range(4):
        m.weights[j] = jnp.exp(m.tops[j] - top) / total

    def rows_of(j):
        return pl.ds(pl.multiple_of(256 * j, 256), 256)

    def weigh(b, j):
        prob = m.exps[j, b] * m.weights[j, pl.ds(b, 1), :]
        m.prob[b, rows_of(j), :] = prob.astype(BF16)
        m.grad_s[b, rows_of(j), :] = (prob * (m.grad_p[j, b] - m.delta[pl.ds(b, 1), :])).astype(BF16)

    def key_grad(j):
        for_k = sum(dot_t(m.grad_s[b, rows_of(j), :], q[b]) for b in range(8)) * scale
        for_v = sum(dot_t(m.prob[b, rows_of(j), :], g[b]) for b in range(8))
        return for_k, for_v

    for b in range(8):
        weigh(b, key(2))
    for n, grad in enumerate(key_grad(key(2))):
        m.far_kv[n] = grad.astype(BF16)
    halves = [pl.ds(0, 128), pl.ds(128, 128)]
    by = [at.zs[0], at.zs[2]]
    far = [[links.copy(m.far_kv.at[n, halves[i]], m.via_kv.at[i, n], by[i]) for n in range(2)] for i in range(2)]
    for dz in (0, 1, 3):
        for dx in range(4):
            weigh(block(1, dx), key(dz))
    sib = []
    for dx in range(4):
        m.sib_out[dx] = (dot(k_t[...], m.grad_s[block(1, dx)]) * scale).astype(BF16)
        sib.append(links.copy(m.sib_out.at[dx], m.sib_in.at[dx], sibling))
    for dz in (0, 1, 3):
        for dx in range(4):
            weigh(block(0, dx), key(dz))
    back = []
    for i, dz in enumerate((1, 3)):
        for n, grad in enumerate(key_grad(key(dz))):
            m.near_kv[i, n] = grad
            m.send_kv[i, n, halves[1 - i]] = grad[128 * (1 - i) : 128 * (2 - i)].astype(BF16)
            src, dst = m.send_kv.at[i, n, halves[1 - i]], m.came_kv.at[i, n, halves[1 - i]]
            back.append(links.copy(src, dst, by[i]))
    for n, dx in enumerate((2, 1, 3, 0)):
        for_q = dot(k_t[...], m.grad_s[block(0, dx)]) * scale
        sib[dx].wait_recv()
        for_q += m.sib_in[dx].astype(F32)
        if dx:
            m.send_q[n] = for_q.astype(BF16)
            back.append(links.copy(m.send_q.at[n], m.came_q.at[n], at.xs[dx - 1]))
        else:
            m.own_q[...] = for_q
    for i in range(2):
        for n in range(2):
            far[i][n].wait_recv()
            grad = m.near_kv[i, n, halves[i], :] + m.via_kv[i, n].astype(F32)
            m.send_kv[i, n, halves[i]] = grad.astype(BF16)
            back.append(links.copy(m.send_kv.at[i, n, halves[i]], m.came_kv.at[i, n, halves[i]], by[i]))
    for n, grad in enumerate(key_grad(z)):
        m.own_kv[n] = grad
    for copy in back:
        copy.wait_recv()
    for_q = m.own_q[...] + sum(m.came_q[n].astype(F32) for n in range(3))
    for_k, for_v = [m.own_kv[n] + m.came_kv[0, n].astype(F32) + m.came_kv[1, n].astype(F32) for n in range(2)]
    back_normed = (
        dot(w_qkv[:, :384], for_q.astype(BF16))
        + dot_t(w_qkv[:, 384:768], for_k.astype(BF16))
        + dot_t(w_qkv[:, 768:], for_v.astype(BF16))
    )
    scaled = back_normed.astype(BF16).astype(F32) * gain
    centre = m.full[...].astype(F32)
    inner = jnp.mean(centre * scaled, 0, keepdims=True)
    out = m.cot_full[...].astype(F32) + inv * scaled - centre * (inv * inv * inv * inner)
    for b in range(CH):
        for h in range(2):
            m.grad[b, h] = out[96 * b : 96 * b + 96, 128 * h : 128 * h + 128].astype(BF16)
    row_low, row_high = near_rows(at.row)
    for b in range(CH):
        to = at.sources[b]
        links.copy(m.grad.at[b], m.own.at[at.frame], to, own=same(to, at.me), recv=OWN + at.frame)
    for b in range(CH):
        links.copy(m.grad.at[b, 1], m.prev_g.at[at.frame], (row_high, b), recv=PREV + at.frame)
        links.copy(m.grad.at[b, 0], m.next_g.at[at.frame], (row_low, b), recv=NEXT + at.frame)


def tail(links, at, m):
    r, c, x, y_hi, z = at.r, at.c, at.x, at.y_hi, at.z
    xs, zs, across, chs = at.xs, at.zs, at.across, at.chs
    own, act, w_t, every, inv_in, gain_rows = m.own, m.act, m.w_t, m.every, m.inv_in, m.gain_rows
    rows, lines, weight, part, all_part, inner, all_inner = m.rows, m.lines, m.weight, m.part, m.all_part, m.inner, m.all_inner
    came1, came2, came3, sum1, sum2, sum3 = m.came1, m.came2, m.came3, m.sum1, m.sum2, m.sum3
    mark, flat, out = m.mark, m.flat, m.out
    x_at = [lax.rem(x + d, 4) for d in range(1, 4)]
    z_at = [lax.rem(z + d, 4) for d in range(1, 4)]
    halves = (
        (x, xs, x_at, z, zs, z_at),
        (z, zs, z_at, x, xs, x_at),
    )
    for f in range(4):
        links.arrive(own.at[f], OWN + f)
    moved = []
    for f in range(4):
        both = []
        for h in range(2):
            y = own[f, h].astype(F32)
            both.append(jnp.concatenate([move(y, -1), y, move(y, 1)], 0).astype(BF16))
        moved.append(jnp.concatenate(both, 1))
    for t in range(3):
        for h in range(3):
            acc = jnp.zeros((288, 384), F32)
            for f in range(4):
                source = f + t - 2
                if source < 0:
                    continue
                acc += dot_t(moved[f], act[:, pl.ds((4 * source + h) * 128, 256)])
            for lane in range(3):
                at = (3 * (3 * t + h) + lane) * 288
                weight[pl.ds(at, 288), :] = acc[:, 128 * lane : 128 * lane + 128].astype(BF16)
    weight[pl.ds(27 * 288, 416), :] = jnp.zeros((416, 128), BF16)
    first = []
    for half, (a, peers, ats, _, _, _) in enumerate(halves):
        for d in range(3):
            src = weight.at[pl.ds(4096 * half + 1024 * ats[d], 1024)]
            first.append(links.copy(src, came1.at[half, d], peers[d]))
    for f in range(4):
        links.arrive(m.prev_g.at[f], PREV + f)
        links.arrive(m.next_g.at[f], NEXT + f)
    for f in range(4):
        rows[f, 0] = jnp.where(r == 0, 0.0, m.prev_g[f].astype(F32)).astype(BF16)
        rows[f, 1] = own[f, 0]
        rows[f, 2] = own[f, 1]
        rows[f, 3] = jnp.where(r == ROWS - 1, 0.0, m.next_g[f].astype(F32)).astype(BF16)
    for f in range(4):
        for h in range(3):
            for k in range(2):
                lines[f, pl.ds(96 * h, 96), pl.ds(128 * k, 128)] = rows[f, 2 - h + k]
    gain = gain_columns(gain_rows, 0)
    for f in range(4):
        acc = jnp.zeros((1152, 256), F32)
        for t in range(3):
            source = f + 2 - t
            if source > 3:
                continue
            acc += dot(w_t[t], lines[source])
        for h in range(2):
            y = acc[:, 128 * h : 128 * h + 128]
            total = move(y[:384], -1) + y[384:768] + move(y[768:], 1)
            v = jnp.concatenate([every[b, f, h + 1] for b in range(CH)], 0).astype(F32)
            before = v * inv_in[2 * f + h : 2 * f + h + 1, :] * gain
            sig = sigmoid(before)
            slope = sig * (1.0 + before * (1.0 - sig))
            inner[2 * f + h : 2 * f + h + 1, :] = jnp.sum(v * slope * gain * total, 0, keepdims=True)
            for b in range(CH):
                part[b, f, h] = total[96 * b : 96 * b + 96].astype(BF16)
    parts = []
    for d in range(3):
        parts.append(links.copy(part.at[chs[d][1]], all_part.at[d], chs[d]))
        parts.append(links.copy(inner, all_inner.at[d], chs[d]))
    for copy in first:
        copy.wait_recv()
    second = []
    for half, (a, _, _, b, peers, ats) in enumerate(halves):
        total = weight[pl.ds(4096 * half + 1024 * a, 1024), :].astype(F32)
        for d in range(3):
            total += came1[half, d].astype(F32)
        sum1[half] = total.astype(BF16)
        for d in range(3):
            src = sum1.at[half, pl.ds(256 * ats[d], 256)]
            second.append(links.copy(src, came2.at[half, d], peers[d]))
    for copy in second:
        copy.wait_recv()
    third = []
    for half, (a, _, _, b, _, _) in enumerate(halves):
        total = sum1[half, pl.ds(256 * b, 256), :].astype(F32)
        for d in range(3):
            total += came2[half, d].astype(F32)
        sum2[half] = total.astype(BF16)
        src = sum2.at[half, pl.ds(128 * (1 - y_hi), 128)]
        third.append(links.copy(src, came3.at[half], across))
    for copy in third:
        copy.wait_recv()
    fourth, kept = [], []
    for half, (a, _, _, b, _, _) in enumerate(halves):
        total = sum2[half, pl.ds(128 * y_hi, 128), :].astype(F32) + came3[half].astype(F32)
        sum3[half] = total.astype(BF16)
        at = flat.at[pl.ds(4096 * half + 1024 * a + 256 * b + 128 * y_hi, 128)]
        kept.append(pltpu.make_async_copy(sum3.at[half], at, mark.at[half]))
        kept[half].start()
        fourth.append(links.copy(sum3.at[half], at, across))
    fifth = []
    for half, (a, _, _, b, peers, _) in enumerate(halves):
        kept[half].wait()
        fourth[half].wait_recv()
        at = flat.at[pl.ds(4096 * half + 1024 * a + 256 * b, 256)]
        for d in range(3):
            fifth.append(links.copy(at, at, peers[d]))
    sixth = []
    for half, (a, peers, _, _, _, _) in enumerate(halves):
        for d in range(3):
            fifth[3 * half + d].wait_recv()
        at = flat.at[pl.ds(4096 * half + 1024 * a, 1024)]
        for d in range(3):
            sixth.append(links.copy(at, at, peers[d]))
    for copy in parts:
        copy.wait_recv()
    mean = (inner[...] + all_inner[0] + all_inner[1] + all_inner[2]) / 384.0
    gain = jnp.broadcast_to(gain_rows[c, 0:1, :], (128, 128)).T[:96]
    for f in range(4):
        for h in range(2):
            v = every[c, f, h + 1].astype(F32)
            inv = inv_in[2 * f + h : 2 * f + h + 1, :]
            total = part[c, f, h].astype(F32)
            for d in range(3):
                total += all_part[d, f, h].astype(F32)
            before = v * inv * gain
            sig = sigmoid(before)
            scaled = total * (sig * (1.0 + before * (1.0 - sig))) * gain
            cube = inv * inv * inv * mean[2 * f + h : 2 * f + h + 1, :]
            out[f, h] = (own[f, h].astype(F32) + inv * scaled - v * cube).astype(BF16)
    for copy in sixth:
        copy.wait_recv()


def whole(links, m):
    at = Place()
    front(links, at, m)
    attention(links, at, m)
    tail(links, at, m)
    links.finish()


def widen_kernel(scale, flat, out):
    for k in range(9):
        for lane in range(3):
            piece = flat[pl.ds((3 * k + lane) * 288, 288), :].astype(F32) * scale
            out[pl.ds(288 * k, 288), pl.ds(128 * lane, 128)] = piece


def on_device(features, gain_in, w_conv, gain_attn, w_qkv, w_out, cotangent):
    near, far = pltpu.VMEM, pl.ANY
    held = {
        "feat": (features, far),
        "cot": (cotangent, far),
        "w_far": (w_conv, far),
        "gain_in": (gain_in.reshape(1, 96), near),
        "gain_attn": (gain_attn.reshape(1, 96), near),
        "w_qkv": (w_qkv, near),
        "w_out": (w_out, near),
    }
    made = {"out": ((4, 2, 96, 128), BF16, near), "flat": ((8192, 128), BF16, far)}
    b16 = {
        "every": (4, 4, 4, 96, 128),
        "w": (27, 96, 384),
        "act": (384, 2048),
        "res": (4, 2, 96, 128),
        "cot_frame": (4, 2, 96, 128),
        "res_frame": (4, 2, 96, 128),
        "full": (384, 256),
        "cot_full": (384, 256),
        "norm": (4, 256, 384),
        "q": (8, 384, 256),
        "g": (8, 384, 256),
        "k": (4, 256, 384),
        "v": (4, 256, 384),
        "k_t": (384, 1024),
        "prob": (8, 1024, 256),
        "grad_s": (8, 1024, 256),
        "far_kv": (2, 256, 384),
        "via_kv": (2, 2, 128, 384),
        "send_kv": (2, 2, 256, 384),
        "came_kv": (2, 2, 256, 384),
        "sib_out": (4, 384, 256),
        "sib_in": (4, 384, 256),
        "send_q": (3, 384, 256),
        "came_q": (3, 384, 256),
        "grad": (4, 2, 96, 128),
        "own": (4, 2, 96, 128),
        "prev_g": (4, 96, 128),
        "next_g": (4, 96, 128),
        "w_t": (3, 1152, 288),
        "rows": (4, 4, 96, 128),
        "lines": (4, 288, 256),
        "weight": (8192, 128),
        "part": (4, 4, 2, 96, 128),
        "all_part": (3, 4, 2, 96, 128),
        "came1": (2, 3, 1024, 128),
        "came2": (2, 3, 256, 128),
        "came3": (2, 128, 128),
        "sum1": (2, 1024, 128),
        "sum2": (2, 256, 128),
        "sum3": (2, 128, 128),
    }
    f32 = {
        "inv_in": (8, 128),
        "gain_rows": (4, 8, 128),
        "exps": (4, 8, 256, 256),
        "grad_p": (4, 8, 256, 256),
        "tops": (4, 8, 256),
        "sums": (4, 8, 256),
        "deltas": (4, 8, 256),
        "stats": (3, 8, 256),
        "all_stats": (7, 3, 8, 256),
        "weights": (4, 8, 256),
        "delta": (8, 256),
        "near_kv": (2, 2, 256, 384),
        "own_kv": (2, 256, 384),
        "own_q": (384, 256),
        "inner": (8, 128),
        "all_inner": (3, 8, 128),
    }
    scratch = {n: pltpu.VMEM(s, BF16) for n, s in b16.items()}
    scratch |= {n: pltpu.VMEM(s, F32) for n, s in f32.items()}
    scratch["mark"] = pltpu.SemaphoreType.DMA((2,))
    out, flat = fused(0, whole, held, made, scratch, (SENDS, NEXT + 4))
    cell_scale = 1.0 / math.sqrt(32768)
    (grad_weights,) = compute(
        functools.partial(widen_kernel, cell_scale),
        [((2592, 384), F32)],
        flat,
        name="widen",
    )
    return out, grad_weights.reshape(27, 96, 384)


def solution(mesh):
    return jax.shard_map(
        on_device,
        mesh=mesh,
        in_specs=(
            P(None, "row", "ch", None),
            P("ch"),
            P(None, "ch", None),
            P("ch"),
            P(),
            P(),
            P(None, "row", "ch", None),
        ),
        out_specs=(P(None, "row", "ch", None), P(None, "ch", None)),
        check_vma=False,
    )
```

```python
import functools
import math
import types

import jax
import jax.numpy as jnp
from jax import lax
from jax.experimental import pallas as pl
from jax.experimental.pallas import tpu as pltpu
from jax.sharding import PartitionSpec as P

EPSILON = 1e-06
MESH = pl.DeviceIdType.MESH
F32 = jnp.float32
BF16 = jnp.bfloat16
ROWS = 32
SENDS = 128
COT, RES, OWN, PREV, NEXT = range(SENDS, SENDS + 20, 4)
CH = 4
VMEM_BYTES = 60 * 1024 * 1024


def coords():
    return lax.axis_index("row"), lax.axis_index("ch")


def place(r, c):
    return lax.rem(r, 4), lax.rem(r // 4, 2), r // 8, c // 2, lax.rem(c, 2)


def device(x, y_hi, z, y_lo, core):
    return z * 8 + y_hi * 4 + x, y_lo * 2 + core


def owner(f, row):
    x, y_hi, z, _, _ = place(row, 0)
    return device(x, f // 2, z, f % 2, y_hi)


class Links:
    def __init__(self, send, recv):
        self.send, self.recv, self.sent, self.at = send, recv, [], 0

    def greet(self, peers, count):
        barrier = pltpu.get_barrier_semaphore()
        for peer in peers:
            pl.semaphore_signal(barrier, inc=1, device_id=peer, device_id_type=MESH)
        pl.semaphore_wait(barrier, count)

    def copy(self, src, dst, to, own=None, recv=None):
        k = self.at
        self.at += 1
        mark = self.recv.at[k if recv is None else recv]
        far = pltpu.make_async_remote_copy(
            src_ref=src,
            dst_ref=dst,
            send_sem=self.send.at[k],
            recv_sem=mark,
            device_id=to,
            device_id_type=MESH,
        )
        if own is None:
            far.start()
        else:
            pl.when(jnp.logical_not(own))(far.start)
            pl.when(own)(pltpu.make_async_copy(src, dst, mark).start)
        self.sent.append((far, own))
        return far

    def arrive(self, dst, k):
        pltpu.make_async_copy(dst, dst, self.recv.at[k]).wait()

    def finish(self):
        for far, own in self.sent:
            if own is None:
                far.wait_send()
            else:
                pl.when(jnp.logical_not(own))(far.wait_send)


def fused(cid, body, held, made, scratch, count):
    names = [*held, *made, *scratch]

    def kernel(*refs):
        body(Links(*refs[-2:]), types.SimpleNamespace(**dict(zip(names, refs))))

    return pl.pallas_call(
        kernel,
        out_shape=[jax.ShapeDtypeStruct(s, t) for s, t, _ in made.values()],
        in_specs=[pl.BlockSpec(memory_space=m) for _, m in held.values()],
        out_specs=[pl.BlockSpec(memory_space=m) for _, _, m in made.values()],
        scratch_shapes=[*scratch.values()] + [pltpu.SemaphoreType.DMA((n,)) for n in count],
        compiler_params=pltpu.CompilerParams(
            collective_id=cid, has_side_effects=True, vmem_limit_bytes=VMEM_BYTES
        ),
        name="fused_%d" % cid,
    )(*[array for array, _ in held.values()])


def dot(a, b):
    return lax.dot_general(a, b, (((1,), (0,)), ((), ())), preferred_element_type=F32)


def dot_t(a, b):
    return lax.dot_general(a, b, (((1,), (1,)), ((), ())), preferred_element_type=F32)


def move(block, by):
    lanes = block.shape[1]
    at = lax.broadcasted_iota(jnp.int32, block.shape, 1)
    if by > 0:
        return jnp.where(at == 0, 0.0, pltpu.roll(block, 1, axis=1))
    return jnp.where(at == lanes - 1, 0.0, pltpu.roll(block, lanes - 1, axis=1))


def ch_peers(r, c):
    return [(r, lax.rem(c + d, CH)) for d in range(1, CH)]


def near_rows(r):
    return lax.rem(r + ROWS - 1, ROWS), lax.rem(r + 1, ROWS)


def same(a, b):
    return jnp.logical_and(a[0] == b[0], a[1] == b[1])


def greet_frames(me, sources, targets):
    barrier = pltpu.get_barrier_semaphore()
    for peer in sources:
        def tell(peer=peer):
            pl.semaphore_signal(barrier, inc=1, device_id=peer, device_id_type=MESH)

        pl.when(jnp.logical_not(same(peer, me)))(tell)
    _, y_hi, _, _, core = place(*me)
    pl.semaphore_wait(barrier, len(targets) - 2 + 2 * (core - y_hi) * (core - y_hi))


def sigmoid(v):
    return 1.0 / (1.0 + jnp.exp(-v))


def gain_columns(rows, which):
    blocks = [jnp.broadcast_to(rows[b, which : which + 1, :], (128, 128)).T[:96] for b in range(CH)]
    return jnp.concatenate(blocks, 0)


class Place:
    def __init__(self):
        r, c = self.r, self.c = self.me = coords()
        x, y_hi, z, y_lo, core = self.x, self.y_hi, self.z, self.y_lo, self.core = place(r, c)
        self.slot = core * 4 + x
        self.frame = y_hi * 2 + y_lo
        self.low, self.high = near_rows(r)
        self.c_near = (1 - y_lo) * 2 + core
        self.sibling = (r, y_lo * 2 + 1 - core)
        self.near = (r, self.c_near)
        self.chs = ch_peers(r, c)
        self.xs = [device(lax.rem(x + d, 4), y_hi, z, y_lo, core) for d in range(1, 4)]
        self.cross = [device(lax.rem(x + d, 4), y_hi, z, y_lo, 1 - core) for d in range(1, 4)]
        self.zs = [device(x, y_hi, lax.rem(z + d, 4), y_lo, core) for d in range(1, 4)]
        self.across = device(x, 1 - y_hi, z, y_lo, core)
        self.targets = [owner(f, r) for f in range(4)]
        self.row = z * 8 + core * 4 + x
        self.sources = [(self.row, b) for b in range(CH)]

    def greet(self):
        at = self
        alike = at.chs + at.xs + at.cross + at.zs + [at.across, (at.low, at.c), (at.high, at.c)]
        there = [(i, b) for i in near_rows(at.row) for b in range(CH)]
        whose = [owner(f, i) for i in (at.low, at.high) for f in range(4)]
        greet_frames(at.me, at.targets + at.sources + whose + alike, at.targets + at.sources + there + alike)


def front(links, at, m):
    r, c, near, sibling = at.r, at.c, at.near, at.sibling
    every, act = m.every, m.act
    here = pltpu.make_async_copy(m.feat, every.at[c], m.mark.at[0])
    here.start()
    weights = pltpu.make_async_copy(m.w_far, m.w, m.mark.at[1])
    weights.start()
    m.gain_rows[c] = jnp.zeros((8, 128), F32)
    pad = jnp.zeros((1, 32), F32)
    m.gain_rows[c, 0:1, :] = jnp.concatenate([m.gain_in[...].astype(F32), pad], 1)
    m.gain_rows[c, 1:2, :] = jnp.concatenate([m.gain_attn[...].astype(F32), pad], 1)
    at.greet()
    pairs = [pl.ds(2 * p, 2) for p in range(2)]
    gains = [links.copy(m.gain_rows.at[c], m.gain_rows.at[c], to) for to in at.chs]
    to_near = [links.copy(m.feat.at[two], every.at[c, two], near) for two in pairs]
    to_sib = links.copy(m.feat, every.at[c], sibling)
    for copy in gains:
        copy.wait_recv()
    gain = gain_columns(m.gain_rows, 0)
    passed = []
    for p, two in enumerate(pairs):
        to_near[p].wait_recv()
        part = every.at[at.c_near, two]
        passed.append(links.copy(part, part, sibling))
    for f in range(4):
        own = same(at.targets[f], at.me)
        links.copy(m.cot.at[f], m.cot_frame.at[c], at.targets[f], own=own, recv=COT + c)

    def activate(f, h):
        v = jnp.concatenate([every[b, f, h] for b in range(CH)], 0).astype(F32)
        inv = lax.rsqrt(jnp.mean(v * v, 0, keepdims=True) + EPSILON)
        before = v * inv * gain
        m.inv_in[2 * f + h : 2 * f + h + 1, :] = inv
        act[:, pl.ds((2 * f + h) * 128, 128)] = (before * sigmoid(before)).astype(BF16)

    here.wait()
    to_sib.wait_recv()
    weights.wait()
    edges = []
    for p, two in enumerate(pairs):
        passed[p].wait_recv()
        for f in (2 * p, 2 * p + 1):
            activate(f, 0)
            activate(f, 1)
        for f in (2 * p, 2 * p + 1):
            by_tap = []
            for h in range(3):
                acc = jnp.zeros((288, 256), F32)
                for t in range(3):
                    source = f + t - 2
                    if source >= 0:
                        taps = m.w[pl.ds(9 * t + 3 * h, 3)].reshape(288, 384)
                        acc += dot(taps, act[:, pl.ds(256 * source, 256)])
                by_tap.append((acc[:, :128], acc[:, 128:]))
            lines = (
                by_tap[2][0],
                by_tap[2][1] + by_tap[1][0],
                by_tap[1][1] + by_tap[0][0],
                by_tap[0][1],
            )
            lines = [move(y[:96], 1) + y[96:192] + move(y[192:], -1) for y in lines]
            m.edge_out[0, f] = lines[0].astype(BF16)
            m.edge_out[1, f] = lines[3].astype(BF16)
            m.conv_own[f, 0] = lines[1]
            m.conv_own[f, 1] = lines[2]
        edges.append(links.copy(m.edge_out.at[0, two], m.edge_in.at[0, two], (at.low, c)))
        edges.append(links.copy(m.edge_out.at[1, two], m.edge_in.at[1, two], (at.high, c)))
    for b in range(CH):
        links.arrive(m.cot_frame.at[b], COT + b)
    for b in range(CH):
        for h in range(2):
            m.cot_full[pl.ds(96 * b, 96), pl.ds(128 * h, 128)] = m.cot_frame[b, h]
    m.g[at.slot] = dot(m.w_out[...], m.cot_full[...]).astype(BF16)
    at.g_first = [links.copy(m.g.at[at.slot], m.g.at[at.slot], to) for to in (at.xs[0], at.xs[2], sibling)]
    for p in range(2):
        edges[2 * p].wait_recv()
        edges[2 * p + 1].wait_recv()
        for f in (2 * p, 2 * p + 1):
            before = jnp.where(r == 0, 0.0, m.edge_in[1, f].astype(F32))
            after = jnp.where(r == ROWS - 1, 0.0, m.edge_in[0, f].astype(F32))
            m.res[f, 0] = (every[c, f, 0].astype(F32) + (m.conv_own[f, 0] + before)).astype(BF16)
            m.res[f, 1] = (every[c, f, 1].astype(F32) + (m.conv_own[f, 1] + after)).astype(BF16)
            own = same(at.targets[f], at.me)
            links.copy(m.res.at[f], m.res_frame.at[c], at.targets[f], own=own, recv=RES + c)


def attention(links, at, m):
    scale = 1.0 / math.sqrt(384)
    x, z, core, slot, sibling = at.x, at.z, at.core, at.slot, at.sibling
    q, g, k, v, k_t = m.q, m.g, m.k, m.v, m.k_t
    w_qkv = m.w_qkv

    def relay_ring(first, ref, base, i, rows, peers, forward):
        on = []
        for side in range(2):
            first[side].wait_recv()
            came = base + lax.rem(i + 3 - 2 * side, 4)
            part = ref.at[came, pl.ds(rows * side, rows)]
            on.append(links.copy(part, part, peers[2 * side]))
            if forward:
                on.append(links.copy(ref.at[came], ref.at[came], sibling))
        return on

    g_on = relay_ring(at.g_first, g, core * 4, x, 192, at.xs, True)
    gain = gain_columns(m.gain_rows, 1)
    gain = jnp.concatenate([gain, gain], 1)
    for b in range(CH):
        links.arrive(m.res_frame.at[b], RES + b)
    for b in range(CH):
        for h in range(2):
            m.full[pl.ds(96 * b, 96), pl.ds(128 * h, 128)] = m.res_frame[b, h]
    centre = m.full[...].astype(F32)
    inv = lax.rsqrt(jnp.mean(centre * centre, 0, keepdims=True) + EPSILON)
    m.norm[z] = (centre * inv * gain).astype(BF16).astype(F32).T.astype(BF16)
    n_first = [links.copy(m.norm.at[z], m.norm.at[z], to) for to in (at.zs[0], at.zs[2])]
    q[slot] = dot(m.norm[z], w_qkv[:, :384]).T.astype(BF16)
    q_first = [links.copy(q.at[slot], q.at[slot], to) for to in (at.xs[0], at.xs[2], sibling)]

    def project(j):
        k[j] = dot(m.norm[j], w_qkv[:, 384:768]).astype(BF16)
        v[j] = dot(m.norm[j], w_qkv[:, 768:]).astype(BF16)
        k_t[:, pl.ds(pl.multiple_of(256 * j, 256), 256)] = k[j].T

    def tile(b, j):
        s = dot(k[j], q[b]) * scale
        top = jnp.max(s, 0, keepdims=True)
        e = jnp.exp(s - top)
        p = dot(v[j], g[b])
        m.exps[j, b] = e
        m.grad_p[j, b] = p
        m.tops[j, pl.ds(b, 1), :] = top
        m.sums[j, pl.ds(b, 1), :] = jnp.sum(e, 0, keepdims=True)
        m.deltas[j, pl.ds(b, 1), :] = jnp.sum(e * p, 0, keepdims=True)

    def block(dk, dx):
        other = core + dk - 2 * core * dk
        return other * 4 + lax.rem(x + dx, 4)

    def key(dz):
        return lax.rem(z + dz, 4)

    def tiles(count, unroll, which):
        def step(n, carry):
            dk, dx, dz = which(n)
            tile(block(dk, dx), key(dz))
            return carry

        lax.fori_loop(0, count, step, 0, unroll=unroll)

    project(z)
    g_on[1].wait_recv()
    g_on[3].wait_recv()
    g_on[0].wait_recv()
    g_on[2].wait_recv()
    far_x = core * 4 + lax.rem(x + 2, 4)
    g_last = links.copy(g.at[far_x], g.at[far_x], sibling)
    at.g_first[2].wait_recv()
    q_first[2].wait_recv()
    tiles(2, 2, lambda n: (n, 0, 0))
    for t in range(3):
        for n in range(3):
            piece = jnp.concatenate([m.w[9 * t + 3 * h + n] for h in range(3)], 0)
            m.w_t[t, pl.ds(384 * n, 384), :] = piece.T
    n_on = relay_ring(n_first, m.norm, 0, z, 128, at.zs, False)
    q_on = relay_ring(q_first, q, core * 4, x, 192, at.xs, True)
    project(key(1))
    project(key(3))
    tiles(4, 4, lambda n: (n // 2, 0, 1 + 2 * lax.rem(n, 2)))
    q_on[1].wait_recv()
    q_on[3].wait_recv()

    def beside(n):
        dz = n // 4
        return lax.rem(n // 2, 2), 1 + 2 * lax.rem(n, 2), dz + dz // 2

    tiles(12, 4, beside)
    q_on[0].wait_recv()
    q_on[2].wait_recv()
    q_last = links.copy(q.at[far_x], q.at[far_x], sibling)
    n_on[0].wait_recv()
    n_on[1].wait_recv()
    project(key(2))

    def beyond(n):
        dx = n // 2
        return lax.rem(n, 2), dx + dx // 2, 2

    tiles(6, 3, beyond)
    tiles(4, 4, lambda n: (0, 2, n))
    q_last.wait_recv()
    g_last.wait_recv()
    tiles(4, 4, lambda n: (1, 2, n))

    tops = [m.tops[j] for j in range(4)]
    top = functools.reduce(jnp.maximum, tops)
    shift = [jnp.exp(t - top) for t in tops]
    m.stats[0] = top
    m.stats[1] = sum(m.sums[j] * shift[j] for j in range(4))
    m.stats[2] = sum(m.deltas[j] * shift[j] for j in range(4))
    peers = at.xs + at.cross + [sibling]
    shared = [links.copy(m.stats, m.all_stats.at[n], to) for n, to in enumerate(peers)]
    for copy in shared:
        copy.wait_recv()
    parts = [m.stats] + [m.all_stats.at[n] for n in range(7)]
    top = functools.reduce(jnp.maximum, [p[0] for p in parts])
    total = sum(p[1] * jnp.exp(p[0] - top) for p in parts)
    m.delta[...] = sum(p[2] * jnp.exp(p[0] - top) for p in parts) / total
    for j in range(4):
        m.weights[j] = jnp.exp(m.tops[j] - top) / total

    def rows_of(j):
        return pl.ds(pl.multiple_of(256 * j, 256), 256)

    def weigh(b, j):
        prob = m.exps[j, b] * m.weights[j, pl.ds(b, 1), :]
        m.prob[b, rows_of(j), :] = prob.astype(BF16)
        m.grad_s[b, rows_of(j), :] = (prob * (m.grad_p[j, b] - m.delta[pl.ds(b, 1), :])).astype(BF16)

    def key_grad(j):
        for_k = sum(dot_t(m.grad_s[b, rows_of(j), :], q[b]) for b in range(8)) * scale
        for_v = sum(dot_t(m.prob[b, rows_of(j), :], g[b]) for b in range(8))
        return for_k, for_v

    for b in range(8):
        weigh(b, key(2))
    for n, grad in enumerate(key_grad(key(2))):
        m.far_kv[n] = grad.astype(BF16)
    halves = [pl.ds(0, 128), pl.ds(128, 128)]
    by = [at.zs[0], at.zs[2]]
    far = [[links.copy(m.far_kv.at[n, halves[i]], m.via_kv.at[i, n], by[i]) for n in range(2)] for i in range(2)]
    for dz in (0, 1, 3):
        for dx in range(4):
            weigh(block(1, dx), key(dz))
    sib = []
    for dx in range(4):
        m.sib_out[dx] = (dot(k_t[...], m.grad_s[block(1, dx)]) * scale).astype(BF16)
        sib.append(links.copy(m.sib_out.at[dx], m.sib_in.at[dx], sibling))
    for dz in (0, 1, 3):
        for dx in range(4):
            weigh(block(0, dx), key(dz))
    back = []
    for i, dz in enumerate((1, 3)):
        for n, grad in enumerate(key_grad(key(dz))):
            m.near_kv[i, n] = grad
            m.send_kv[i, n, halves[1 - i]] = grad[128 * (1 - i) : 128 * (2 - i)].astype(BF16)
            src, dst = m.send_kv.at[i, n, halves[1 - i]], m.came_kv.at[i, n, halves[1 - i]]
            back.append(links.copy(src, dst, by[i]))
    for n, dx in enumerate((2, 1, 3, 0)):
        for_q = dot(k_t[...], m.grad_s[block(0, dx)]) * scale
        sib[dx].wait_recv()
        for_q += m.sib_in[dx].astype(F32)
        if dx:
            m.send_q[n] = for_q.astype(BF16)
            back.append(links.copy(m.send_q.at[n], m.came_q.at[n], at.xs[dx - 1]))
        else:
            m.own_q[...] = for_q
    for i in range(2):
        for n in range(2):
            far[i][n].wait_recv()
            grad = m.near_kv[i, n, halves[i], :] + m.via_kv[i, n].astype(F32)
            m.send_kv[i, n, halves[i]] = grad.astype(BF16)
            back.append(links.copy(m.send_kv.at[i, n, halves[i]], m.came_kv.at[i, n, halves[i]], by[i]))
    for n, grad in enumerate(key_grad(z)):
        m.own_kv[n] = grad
    for copy in back:
        copy.wait_recv()
    for_q = m.own_q[...] + sum(m.came_q[n].astype(F32) for n in range(3))
    for_k, for_v = [m.own_kv[n] + m.came_kv[0, n].astype(F32) + m.came_kv[1, n].astype(F32) for n in range(2)]
    back_normed = (
        dot(w_qkv[:, :384], for_q.astype(BF16))
        + dot_t(w_qkv[:, 384:768], for_k.astype(BF16))
        + dot_t(w_qkv[:, 768:], for_v.astype(BF16))
    )
    scaled = back_normed.astype(BF16).astype(F32) * gain
    centre = m.full[...].astype(F32)
    inner = jnp.mean(centre * scaled, 0, keepdims=True)
    out = m.cot_full[...].astype(F32) + inv * scaled - centre * (inv * inv * inv * inner)
    for b in range(CH):
        for h in range(2):
            m.grad[b, h] = out[96 * b : 96 * b + 96, 128 * h : 128 * h + 128].astype(BF16)
    row_low, row_high = near_rows(at.row)
    for b in range(CH):
        to = at.sources[b]
        links.copy(m.grad.at[b], m.own.at[at.frame], to, own=same(to, at.me), recv=OWN + at.frame)
    for b in range(CH):
        links.copy(m.grad.at[b, 1], m.prev_g.at[at.frame], (row_high, b), recv=PREV + at.frame)
        links.copy(m.grad.at[b, 0], m.next_g.at[at.frame], (row_low, b), recv=NEXT + at.frame)


def tail(links, at, m):
    r, c, x, y_hi, z = at.r, at.c, at.x, at.y_hi, at.z
    xs, zs, across, chs = at.xs, at.zs, at.across, at.chs
    own, act, w_t, every, inv_in, gain_rows = m.own, m.act, m.w_t, m.every, m.inv_in, m.gain_rows
    rows, lines, weight, part, all_part, inner, all_inner = m.rows, m.lines, m.weight, m.part, m.all_part, m.inner, m.all_inner
    came1, came2, came3, sum1, sum2, sum3 = m.came1, m.came2, m.came3, m.sum1, m.sum2, m.sum3
    mark, flat, out = m.mark, m.flat, m.out
    x_at = [lax.rem(x + d, 4) for d in range(1, 4)]
    z_at = [lax.rem(z + d, 4) for d in range(1, 4)]
    halves = (
        (x, xs, x_at, z, zs, z_at),
        (z, zs, z_at, x, xs, x_at),
    )
    for f in range(4):
        links.arrive(own.at[f], OWN + f)
        links.arrive(m.prev_g.at[f], PREV + f)
        links.arrive(m.next_g.at[f], NEXT + f)
    for f in range(4):
        rows[f, 0] = jnp.where(r == 0, 0.0, m.prev_g[f].astype(F32)).astype(BF16)
        rows[f, 1] = own[f, 0]
        rows[f, 2] = own[f, 1]
        rows[f, 3] = jnp.where(r == ROWS - 1, 0.0, m.next_g[f].astype(F32)).astype(BF16)
        for h in range(4):
            y = rows[f, h].astype(F32)
            at_lanes = pl.ds(128 * h, 128)
            m.moved[f, :, at_lanes] = jnp.concatenate([move(y, -1), y, move(y, 1)], 0).astype(BF16)
    for t in range(3):
        for h in range(3):
            acc = jnp.zeros((288, 384), F32)
            for f in range(4):
                source = f + t - 2
                if source < 0:
                    continue
                acc += dot_t(m.moved[f, :, pl.ds(128 * (2 - h), 256)], act[:, pl.ds(256 * source, 256)])
            for lane in range(3):
                at = (3 * (3 * t + h) + lane) * 288
                weight[pl.ds(at, 288), :] = acc[:, 128 * lane : 128 * lane + 128].astype(BF16)
    weight[pl.ds(27 * 288, 416), :] = jnp.zeros((416, 128), BF16)
    first = []
    for half, (a, peers, ats, _, _, _) in enumerate(halves):
        for d in range(3):
            src = weight.at[pl.ds(4096 * half + 1024 * ats[d], 1024)]
            first.append(links.copy(src, came1.at[half, d], peers[d]))
    for f in range(4):
        for h in range(3):
            for k in range(2):
                lines[f, pl.ds(96 * h, 96), pl.ds(128 * k, 128)] = rows[f, 2 - h + k]
    gain = gain_columns(gain_rows, 0)
    for f in range(4):
        acc = jnp.zeros((1152, 256), F32)
        for t in range(3):
            source = f + 2 - t
            if source > 3:
                continue
            acc += dot(w_t[t], lines[source])
        for h in range(2):
            y = acc[:, 128 * h : 128 * h + 128]
            total = move(y[:384], -1) + y[384:768] + move(y[768:], 1)
            v = jnp.concatenate([every[b, f, h] for b in range(CH)], 0).astype(F32)
            before = v * inv_in[2 * f + h : 2 * f + h + 1, :] * gain
            sig = sigmoid(before)
            slope = sig * (1.0 + before * (1.0 - sig))
            inner[2 * f + h : 2 * f + h + 1, :] = jnp.sum(v * slope * gain * total, 0, keepdims=True)
            for b in range(CH):
                part[b, f, h] = total[96 * b : 96 * b + 96].astype(BF16)
    parts = []
    for d in range(3):
        parts.append(links.copy(part.at[chs[d][1]], all_part.at[d], chs[d]))
        parts.append(links.copy(inner, all_inner.at[d], chs[d]))
    for copy in first:
        copy.wait_recv()
    second = []
    for half, (a, _, _, b, peers, ats) in enumerate(halves):
        total = weight[pl.ds(4096 * half + 1024 * a, 1024), :].astype(F32)
        for d in range(3):
            total += came1[half, d].astype(F32)
        sum1[half] = total.astype(BF16)
        for d in range(3):
            src = sum1.at[half, pl.ds(256 * ats[d], 256)]
            second.append(links.copy(src, came2.at[half, d], peers[d]))
    for copy in second:
        copy.wait_recv()
    third = []
    for half, (a, _, _, b, _, _) in enumerate(halves):
        total = sum1[half, pl.ds(256 * b, 256), :].astype(F32)
        for d in range(3):
            total += came2[half, d].astype(F32)
        sum2[half] = total.astype(BF16)
        src = sum2.at[half, pl.ds(128 * (1 - y_hi), 128)]
        third.append(links.copy(src, came3.at[half], across))
    for copy in third:
        copy.wait_recv()
    fourth, kept = [], []
    for half, (a, _, _, b, _, _) in enumerate(halves):
        total = sum2[half, pl.ds(128 * y_hi, 128), :].astype(F32) + came3[half].astype(F32)
        sum3[half] = total.astype(BF16)
        at = flat.at[pl.ds(4096 * half + 1024 * a + 256 * b + 128 * y_hi, 128)]
        kept.append(pltpu.make_async_copy(sum3.at[half], at, mark.at[half]))
        kept[half].start()
        fourth.append(links.copy(sum3.at[half], at, across))
    fifth = []
    for half, (a, _, _, b, peers, _) in enumerate(halves):
        kept[half].wait()
        fourth[half].wait_recv()
        at = flat.at[pl.ds(4096 * half + 1024 * a + 256 * b, 256)]
        for d in range(3):
            fifth.append(links.copy(at, at, peers[d]))
    sixth = []
    for half, (a, peers, _, _, _, _) in enumerate(halves):
        for d in range(3):
            fifth[3 * half + d].wait_recv()
        at = flat.at[pl.ds(4096 * half + 1024 * a, 1024)]
        for d in range(3):
            sixth.append(links.copy(at, at, peers[d]))
    for copy in parts:
        copy.wait_recv()
    mean = (inner[...] + all_inner[0] + all_inner[1] + all_inner[2]) / 384.0
    gain = jnp.broadcast_to(gain_rows[c, 0:1, :], (128, 128)).T[:96]
    for f in range(4):
        for h in range(2):
            v = every[c, f, h].astype(F32)
            inv = inv_in[2 * f + h : 2 * f + h + 1, :]
            total = part[c, f, h].astype(F32)
            for d in range(3):
                total += all_part[d, f, h].astype(F32)
            before = v * inv * gain
            sig = sigmoid(before)
            scaled = total * (sig * (1.0 + before * (1.0 - sig))) * gain
            cube = inv * inv * inv * mean[2 * f + h : 2 * f + h + 1, :]
            out[f, h] = (own[f, h].astype(F32) + inv * scaled - v * cube).astype(BF16)
    for copy in sixth:
        copy.wait_recv()


def whole(links, m):
    at = Place()
    front(links, at, m)
    attention(links, at, m)
    tail(links, at, m)
    links.finish()


def widen_kernel(scale, flat, out, near, wide, into, back):
    come = [
        pltpu.make_async_copy(flat.at[pl.ds(864 * k, 864)], near.at[k], into.at[k]) for k in range(9)
    ]
    go = [
        pltpu.make_async_copy(wide.at[k], out.at[pl.ds(288 * k, 288)], back.at[k]) for k in range(9)
    ]
    for copy in come:
        copy.start()
    for k in range(9):
        come[k].wait()
        for lane in range(3):
            piece = near[k, pl.ds(288 * lane, 288), :].astype(F32) * scale
            wide[k, :, pl.ds(128 * lane, 128)] = piece
        go[k].start()
    for copy in go:
        copy.wait()


def on_device(features, gain_in, w_conv, gain_attn, w_qkv, w_out, cotangent):
    near, far = pltpu.VMEM, pl.ANY
    held = {
        "feat": (features, far),
        "cot": (cotangent, far),
        "w_far": (w_conv, far),
        "gain_in": (gain_in.reshape(1, 96), near),
        "gain_attn": (gain_attn.reshape(1, 96), near),
        "w_qkv": (w_qkv, near),
        "w_out": (w_out, near),
    }
    made = {"out": ((4, 2, 96, 128), BF16, near), "flat": ((8192, 128), BF16, far)}
    b16 = {
        "every": (4, 4, 2, 96, 128),
        "w": (27, 96, 384),
        "act": (384, 1024),
        "edge_out": (2, 4, 96, 128),
        "edge_in": (2, 4, 96, 128),
        "moved": (4, 288, 512),
        "res": (4, 2, 96, 128),
        "cot_frame": (4, 2, 96, 128),
        "res_frame": (4, 2, 96, 128),
        "full": (384, 256),
        "cot_full": (384, 256),
        "norm": (4, 256, 384),
        "q": (8, 384, 256),
        "g": (8, 384, 256),
        "k": (4, 256, 384),
        "v": (4, 256, 384),
        "k_t": (384, 1024),
        "prob": (8, 1024, 256),
        "grad_s": (8, 1024, 256),
        "far_kv": (2, 256, 384),
        "via_kv": (2, 2, 128, 384),
        "send_kv": (2, 2, 256, 384),
        "came_kv": (2, 2, 256, 384),
        "sib_out": (4, 384, 256),
        "sib_in": (4, 384, 256),
        "send_q": (3, 384, 256),
        "came_q": (3, 384, 256),
        "grad": (4, 2, 96, 128),
        "own": (4, 2, 96, 128),
        "prev_g": (4, 96, 128),
        "next_g": (4, 96, 128),
        "w_t": (3, 1152, 288),
        "rows": (4, 4, 96, 128),
        "lines": (4, 288, 256),
        "weight": (8192, 128),
        "part": (4, 4, 2, 96, 128),
        "all_part": (3, 4, 2, 96, 128),
        "came1": (2, 3, 1024, 128),
        "came2": (2, 3, 256, 128),
        "came3": (2, 128, 128),
        "sum1": (2, 1024, 128),
        "sum2": (2, 256, 128),
        "sum3": (2, 128, 128),
    }
    f32 = {
        "inv_in": (8, 128),
        "conv_own": (4, 2, 96, 128),
        "gain_rows": (4, 8, 128),
        "exps": (4, 8, 256, 256),
        "grad_p": (4, 8, 256, 256),
        "tops": (4, 8, 256),
        "sums": (4, 8, 256),
        "deltas": (4, 8, 256),
        "stats": (3, 8, 256),
        "all_stats": (7, 3, 8, 256),
        "weights": (4, 8, 256),
        "delta": (8, 256),
        "near_kv": (2, 2, 256, 384),
        "own_kv": (2, 256, 384),
        "own_q": (384, 256),
        "inner": (8, 128),
        "all_inner": (3, 8, 128),
    }
    scratch = {n: pltpu.VMEM(s, BF16) for n, s in b16.items()}
    scratch |= {n: pltpu.VMEM(s, F32) for n, s in f32.items()}
    scratch["mark"] = pltpu.SemaphoreType.DMA((2,))
    out, flat = fused(0, whole, held, made, scratch, (SENDS, NEXT + 4))
    cell_scale = 1.0 / math.sqrt(32768)
    grad_weights = pl.pallas_call(
        functools.partial(widen_kernel, cell_scale),
        out_shape=jax.ShapeDtypeStruct((2592, 384), F32),
        in_specs=[pl.BlockSpec(memory_space=pl.ANY)],
        out_specs=pl.BlockSpec(memory_space=pl.ANY),
        scratch_shapes=[
            pltpu.VMEM((9, 864, 128), BF16),
            pltpu.VMEM((9, 288, 384), F32),
            pltpu.SemaphoreType.DMA((9,)),
            pltpu.SemaphoreType.DMA((9,)),
        ],
        compiler_params=pltpu.CompilerParams(vmem_limit_bytes=VMEM_BYTES),
        name="widen",
    )(flat)
    return out, grad_weights.reshape(27, 96, 384)


def solution(mesh):
    return jax.shard_map(
        on_device,
        mesh=mesh,
        in_specs=(
            P(None, "row", "ch", None),
            P("ch"),
            P(None, "ch", None),
            P("ch"),
            P(),
            P(),
            P(None, "row", "ch", None),
        ),
        out_specs=(P(None, "row", "ch", None), P(None, "ch", None)),
        check_vma=False,
    )
```

```python
import functools
import math
import types

import jax
import jax.numpy as jnp
from jax import lax
from jax.experimental import pallas as pl
from jax.experimental.pallas import tpu as pltpu
from jax.sharding import PartitionSpec as P

EPSILON = 1e-06
MESH = pl.DeviceIdType.MESH
F32 = jnp.float32
BF16 = jnp.bfloat16
ROWS = 32
SENDS = 128
COT, RES, OWN, PREV, NEXT = range(SENDS, SENDS + 20, 4)
CH = 4
VMEM_BYTES = 60 * 1024 * 1024


def coords():
    return lax.axis_index("row"), lax.axis_index("ch")


def place(r, c):
    return lax.rem(r, 4), lax.rem(r // 4, 2), r // 8, c // 2, lax.rem(c, 2)


def device(x, y_hi, z, y_lo, core):
    return z * 8 + y_hi * 4 + x, y_lo * 2 + core


def owner(f, row):
    x, y_hi, z, _, _ = place(row, 0)
    return device(x, f // 2, z, f % 2, y_hi)


class Links:
    def __init__(self, send, recv):
        self.send, self.recv, self.sent, self.at = send, recv, [], 0

    def greet(self, peers, count):
        barrier = pltpu.get_barrier_semaphore()
        for peer in peers:
            pl.semaphore_signal(barrier, inc=1, device_id=peer, device_id_type=MESH)
        pl.semaphore_wait(barrier, count)

    def copy(self, src, dst, to, own=None, recv=None):
        k = self.at
        self.at += 1
        mark = self.recv.at[k if recv is None else recv]
        far = pltpu.make_async_remote_copy(
            src_ref=src,
            dst_ref=dst,
            send_sem=self.send.at[k],
            recv_sem=mark,
            device_id=to,
            device_id_type=MESH,
        )
        if own is None:
            far.start()
        else:
            pl.when(jnp.logical_not(own))(far.start)
            pl.when(own)(pltpu.make_async_copy(src, dst, mark).start)
        self.sent.append((far, own))
        return far

    def arrive(self, dst, k):
        pltpu.make_async_copy(dst, dst, self.recv.at[k]).wait()

    def finish(self):
        for far, own in self.sent:
            if own is None:
                far.wait_send()
            else:
                pl.when(jnp.logical_not(own))(far.wait_send)


def fused(cid, body, held, made, scratch, count):
    names = [*held, *made, *scratch]

    def kernel(*refs):
        body(Links(*refs[-2:]), types.SimpleNamespace(**dict(zip(names, refs))))

    return pl.pallas_call(
        kernel,
        out_shape=[jax.ShapeDtypeStruct(s, t) for s, t, _ in made.values()],
        in_specs=[pl.BlockSpec(memory_space=m) for _, m in held.values()],
        out_specs=[pl.BlockSpec(memory_space=m) for _, _, m in made.values()],
        scratch_shapes=[*scratch.values()] + [pltpu.SemaphoreType.DMA((n,)) for n in count],
        compiler_params=pltpu.CompilerParams(
            collective_id=cid, has_side_effects=True, vmem_limit_bytes=VMEM_BYTES
        ),
        name="fused_%d" % cid,
    )(*[array for array, _ in held.values()])


def dot(a, b):
    return lax.dot_general(a, b, (((1,), (0,)), ((), ())), preferred_element_type=F32)


def dot_t(a, b):
    return lax.dot_general(a, b, (((1,), (1,)), ((), ())), preferred_element_type=F32)


def move(block, by):
    lanes = block.shape[1]
    at = lax.broadcasted_iota(jnp.int32, block.shape, 1)
    if by > 0:
        return jnp.where(at == 0, 0.0, pltpu.roll(block, 1, axis=1))
    return jnp.where(at == lanes - 1, 0.0, pltpu.roll(block, lanes - 1, axis=1))


def ch_peers(r, c):
    return [(r, lax.rem(c + d, CH)) for d in range(1, CH)]


def near_rows(r):
    return lax.rem(r + ROWS - 1, ROWS), lax.rem(r + 1, ROWS)


def same(a, b):
    return jnp.logical_and(a[0] == b[0], a[1] == b[1])


def greet_frames(me, sources, targets):
    barrier = pltpu.get_barrier_semaphore()
    for peer in sources:
        def tell(peer=peer):
            pl.semaphore_signal(barrier, inc=1, device_id=peer, device_id_type=MESH)

        pl.when(jnp.logical_not(same(peer, me)))(tell)
    _, y_hi, _, _, core = place(*me)
    pl.semaphore_wait(barrier, len(targets) - 2 + 2 * (core - y_hi) * (core - y_hi))


def sigmoid(v):
    return 1.0 / (1.0 + jnp.exp(-v))


def gain_columns(rows, which):
    blocks = [jnp.broadcast_to(rows[b, which : which + 1, :], (128, 128)).T[:96] for b in range(CH)]
    return jnp.concatenate(blocks, 0)


class Place:
    def __init__(self):
        r, c = self.r, self.c = self.me = coords()
        x, y_hi, z, y_lo, core = self.x, self.y_hi, self.z, self.y_lo, self.core = place(r, c)
        self.slot = core * 4 + x
        self.frame = y_hi * 2 + y_lo
        self.low, self.high = near_rows(r)
        self.c_near = (1 - y_lo) * 2 + core
        self.sibling = (r, y_lo * 2 + 1 - core)
        self.near = (r, self.c_near)
        self.chs = ch_peers(r, c)
        self.xs = [device(lax.rem(x + d, 4), y_hi, z, y_lo, core) for d in range(1, 4)]
        self.cross = [device(lax.rem(x + d, 4), y_hi, z, y_lo, 1 - core) for d in range(1, 4)]
        self.zs = [device(x, y_hi, lax.rem(z + d, 4), y_lo, core) for d in range(1, 4)]
        self.across = device(x, 1 - y_hi, z, y_lo, core)
        self.targets = [owner(f, r) for f in range(4)]
        self.row = z * 8 + core * 4 + x
        self.sources = [(self.row, b) for b in range(CH)]

    def greet(self):
        at = self
        alike = at.chs + at.xs + at.cross + at.zs + [at.across, (at.low, at.c), (at.high, at.c)]
        there = [(i, b) for i in near_rows(at.row) for b in range(CH)]
        whose = [owner(f, i) for i in (at.low, at.high) for f in range(4)]
        greet_frames(at.me, at.targets + at.sources + whose + alike, at.targets + at.sources + there + alike)


def front(links, at, m):
    r, c, near, sibling = at.r, at.c, at.near, at.sibling
    every, act = m.every, m.act
    here = pltpu.make_async_copy(m.feat, every.at[c], m.mark.at[0])
    here.start()
    weights = pltpu.make_async_copy(m.w_far, m.w, m.mark.at[1])
    weights.start()
    m.gain_rows[c] = jnp.zeros((8, 128), F32)
    pad = jnp.zeros((1, 32), F32)
    m.gain_rows[c, 0:1, :] = jnp.concatenate([m.gain_in[...].astype(F32), pad], 1)
    m.gain_rows[c, 1:2, :] = jnp.concatenate([m.gain_attn[...].astype(F32), pad], 1)
    at.greet()
    pairs = [pl.ds(2 * p, 2) for p in range(2)]
    gains = [links.copy(m.gain_rows.at[c], m.gain_rows.at[c], to) for to in at.chs]
    to_near = [links.copy(m.feat.at[two], every.at[c, two], near) for two in pairs]
    to_sib = links.copy(m.feat, every.at[c], sibling)
    for copy in gains:
        copy.wait_recv()
    gain = gain_columns(m.gain_rows, 0)
    passed = []
    for p, two in enumerate(pairs):
        to_near[p].wait_recv()
        part = every.at[at.c_near, two]
        passed.append(links.copy(part, part, sibling))
    for f in range(4):
        own = same(at.targets[f], at.me)
        links.copy(m.cot.at[f], m.cot_frame.at[c], at.targets[f], own=own, recv=COT + c)

    def activate(f, h):
        v = jnp.concatenate([every[b, f, h] for b in range(CH)], 0).astype(F32)
        inv = lax.rsqrt(jnp.mean(v * v, 0, keepdims=True) + EPSILON)
        before = v * inv * gain
        m.inv_in[2 * f + h : 2 * f + h + 1, :] = inv
        act[:, pl.ds((2 * f + h) * 128, 128)] = (before * sigmoid(before)).astype(BF16)

    here.wait()
    to_sib.wait_recv()
    weights.wait()
    edges = []
    for p, two in enumerate(pairs):
        passed[p].wait_recv()
        for f in (2 * p, 2 * p + 1):
            activate(f, 0)
            activate(f, 1)
        for f in (2 * p, 2 * p + 1):
            by_tap = []
            for h in range(3):
                acc = jnp.zeros((288, 256), F32)
                for t in range(3):
                    source = f + t - 2
                    if source >= 0:
                        taps = m.w[pl.ds(9 * t + 3 * h, 3)].reshape(288, 384)
                        acc += dot(taps, act[:, pl.ds(256 * source, 256)])
                by_tap.append((acc[:, :128], acc[:, 128:]))
            lines = (
                by_tap[2][0],
                by_tap[2][1] + by_tap[1][0],
                by_tap[1][1] + by_tap[0][0],
                by_tap[0][1],
            )
            lines = [move(y[:96], 1) + y[96:192] + move(y[192:], -1) for y in lines]
            m.edge_out[0, f] = lines[0].astype(BF16)
            m.edge_out[1, f] = lines[3].astype(BF16)
            m.conv_own[f, 0] = lines[1]
            m.conv_own[f, 1] = lines[2]
        edges.append(links.copy(m.edge_out.at[0, two], m.edge_in.at[0, two], (at.low, c)))
        edges.append(links.copy(m.edge_out.at[1, two], m.edge_in.at[1, two], (at.high, c)))
    for b in range(CH):
        links.arrive(m.cot_frame.at[b], COT + b)
    for b in range(CH):
        for h in range(2):
            m.cot_full[pl.ds(96 * b, 96), pl.ds(128 * h, 128)] = m.cot_frame[b, h]
    m.g[at.slot] = dot(m.w_out[...], m.cot_full[...]).astype(BF16)
    at.g_first = [links.copy(m.g.at[at.slot], m.g.at[at.slot], to) for to in (at.xs[0], at.xs[2], sibling)]
    for p in range(2):
        edges[2 * p].wait_recv()
        edges[2 * p + 1].wait_recv()
        for f in (2 * p, 2 * p + 1):
            before = jnp.where(r == 0, 0.0, m.edge_in[1, f].astype(F32))
            after = jnp.where(r == ROWS - 1, 0.0, m.edge_in[0, f].astype(F32))
            m.res[f, 0] = (every[c, f, 0].astype(F32) + (m.conv_own[f, 0] + before)).astype(BF16)
            m.res[f, 1] = (every[c, f, 1].astype(F32) + (m.conv_own[f, 1] + after)).astype(BF16)
            own = same(at.targets[f], at.me)
            links.copy(m.res.at[f], m.res_frame.at[c], at.targets[f], own=own, recv=RES + c)


def attention(links, at, m):
    scale = 1.0 / math.sqrt(384)
    x, z, core, slot, sibling = at.x, at.z, at.core, at.slot, at.sibling
    q, g, k, v, k_t = m.q, m.g, m.k, m.v, m.k_t
    w_qkv = m.w_qkv

    def relay_ring(first, ref, base, i, rows, peers, forward):
        on = []
        for side in range(2):
            first[side].wait_recv()
            came = base + lax.rem(i + 3 - 2 * side, 4)
            part = ref.at[came, pl.ds(rows * side, rows)]
            on.append(links.copy(part, part, peers[2 * side]))
            if forward:
                on.append(links.copy(ref.at[came], ref.at[came], sibling))
        return on

    g_on = relay_ring(at.g_first, g, core * 4, x, 192, at.xs, True)
    gain = gain_columns(m.gain_rows, 1)
    gain = jnp.concatenate([gain, gain], 1)
    for b in range(CH):
        links.arrive(m.res_frame.at[b], RES + b)
    for b in range(CH):
        for h in range(2):
            m.full[pl.ds(96 * b, 96), pl.ds(128 * h, 128)] = m.res_frame[b, h]
    centre = m.full[...].astype(F32)
    inv = lax.rsqrt(jnp.mean(centre * centre, 0, keepdims=True) + EPSILON)
    m.norm[z] = (centre * inv * gain).astype(BF16).astype(F32).T.astype(BF16)
    n_first = [links.copy(m.norm.at[z], m.norm.at[z], to) for to in (at.zs[0], at.zs[2])]
    q[slot] = dot(m.norm[z], w_qkv[:, :384]).T.astype(BF16)
    q_first = [links.copy(q.at[slot], q.at[slot], to) for to in (at.xs[0], at.xs[2], sibling)]

    def project(j):
        k[j] = dot(m.norm[j], w_qkv[:, 384:768]).astype(BF16)
        v[j] = dot(m.norm[j], w_qkv[:, 768:]).astype(BF16)
        k_t[:, pl.ds(pl.multiple_of(256 * j, 256), 256)] = k[j].T

    def tile(b, j):
        s = dot(k[j], q[b]) * scale
        top = jnp.max(s, 0, keepdims=True)
        e = jnp.exp(s - top)
        p = dot(v[j], g[b])
        m.exps[j, b] = e
        m.grad_p[j, b] = p
        m.tops[j, pl.ds(b, 1), :] = top
        m.sums[j, pl.ds(b, 1), :] = jnp.sum(e, 0, keepdims=True)
        m.deltas[j, pl.ds(b, 1), :] = jnp.sum(e * p, 0, keepdims=True)

    def block(dk, dx):
        other = core + dk - 2 * core * dk
        return other * 4 + lax.rem(x + dx, 4)

    def key(dz):
        return lax.rem(z + dz, 4)

    def tiles(count, unroll, which):
        def step(n, carry):
            dk, dx, dz = which(n)
            tile(block(dk, dx), key(dz))
            return carry

        lax.fori_loop(0, count, step, 0, unroll=unroll)

    project(z)
    g_on[1].wait_recv()
    g_on[3].wait_recv()
    g_on[0].wait_recv()
    g_on[2].wait_recv()
    far_x = core * 4 + lax.rem(x + 2, 4)
    g_last = links.copy(g.at[far_x], g.at[far_x], sibling)
    at.g_first[2].wait_recv()
    q_first[2].wait_recv()
    tiles(2, 2, lambda n: (n, 0, 0))
    for t in range(3):
        for n in range(3):
            piece = jnp.concatenate([m.w[9 * t + 3 * h + n] for h in range(3)], 0)
            m.w_t[t, pl.ds(384 * n, 384), :] = piece.T
    n_on = relay_ring(n_first, m.norm, 0, z, 128, at.zs, False)
    q_on = relay_ring(q_first, q, core * 4, x, 192, at.xs, True)
    project(key(1))
    project(key(3))
    tiles(4, 4, lambda n: (n // 2, 0, 1 + 2 * lax.rem(n, 2)))
    q_on[1].wait_recv()
    q_on[3].wait_recv()

    def beside(n):
        dz = n // 4
        return lax.rem(n // 2, 2), 1 + 2 * lax.rem(n, 2), dz + dz // 2

    tiles(12, 4, beside)
    q_on[0].wait_recv()
    q_on[2].wait_recv()
    q_last = links.copy(q.at[far_x], q.at[far_x], sibling)
    n_on[0].wait_recv()
    n_on[1].wait_recv()
    project(key(2))

    def beyond(n):
        dx = n // 2
        return lax.rem(n, 2), dx + dx // 2, 2

    tiles(6, 3, beyond)
    tiles(4, 4, lambda n: (0, 2, n))
    q_last.wait_recv()
    g_last.wait_recv()
    tiles(4, 4, lambda n: (1, 2, n))

    tops = [m.tops[j] for j in range(4)]
    top = functools.reduce(jnp.maximum, tops)
    shift = [jnp.exp(t - top) for t in tops]
    m.stats[0] = top
    m.stats[1] = sum(m.sums[j] * shift[j] for j in range(4))
    m.stats[2] = sum(m.deltas[j] * shift[j] for j in range(4))
    peers = at.xs + at.cross + [sibling]
    shared = [links.copy(m.stats, m.all_stats.at[n], to) for n, to in enumerate(peers)]
    for copy in shared:
        copy.wait_recv()
    parts = [m.stats] + [m.all_stats.at[n] for n in range(7)]
    top = functools.reduce(jnp.maximum, [p[0] for p in parts])
    total = sum(p[1] * jnp.exp(p[0] - top) for p in parts)
    m.delta[...] = sum(p[2] * jnp.exp(p[0] - top) for p in parts) / total
    for j in range(4):
        m.weights[j] = jnp.exp(m.tops[j] - top) / total

    def rows_of(j):
        return pl.ds(pl.multiple_of(256 * j, 256), 256)

    def weigh(b, j):
        prob = m.exps[j, b] * m.weights[j, pl.ds(b, 1), :]
        m.prob[b, rows_of(j), :] = prob.astype(BF16)
        m.grad_s[b, rows_of(j), :] = (prob * (m.grad_p[j, b] - m.delta[pl.ds(b, 1), :])).astype(BF16)

    def key_grad(j):
        for_k = sum(dot_t(m.grad_s[b, rows_of(j), :], q[b]) for b in range(8)) * scale
        for_v = sum(dot_t(m.prob[b, rows_of(j), :], g[b]) for b in range(8))
        return for_k, for_v

    for b in range(8):
        weigh(b, key(2))
    for n, grad in enumerate(key_grad(key(2))):
        m.far_kv[n] = grad.astype(BF16)
    halves = [pl.ds(0, 128), pl.ds(128, 128)]
    by = [at.zs[0], at.zs[2]]
    far = [[links.copy(m.far_kv.at[n, halves[i]], m.via_kv.at[i, n], by[i]) for n in range(2)] for i in range(2)]
    for dz in (0, 1, 3):
        for dx in range(4):
            weigh(block(1, dx), key(dz))
    sib = []
    for dx in range(4):
        m.sib_out[dx] = (dot(k_t[...], m.grad_s[block(1, dx)]) * scale).astype(BF16)
        sib.append(links.copy(m.sib_out.at[dx], m.sib_in.at[dx], sibling))
    for dz in (0, 1, 3):
        for dx in range(4):
            weigh(block(0, dx), key(dz))
    back = []
    for i, dz in enumerate((1, 3)):
        for n, grad in enumerate(key_grad(key(dz))):
            m.near_kv[i, n] = grad
            m.send_kv[i, n, halves[1 - i]] = grad[128 * (1 - i) : 128 * (2 - i)].astype(BF16)
            src, dst = m.send_kv.at[i, n, halves[1 - i]], m.came_kv.at[i, n, halves[1 - i]]
            back.append(links.copy(src, dst, by[i]))
    for n, dx in enumerate((2, 1, 3, 0)):
        for_q = dot(k_t[...], m.grad_s[block(0, dx)]) * scale
        sib[dx].wait_recv()
        for_q += m.sib_in[dx].astype(F32)
        if dx:
            m.send_q[n] = for_q.astype(BF16)
            back.append(links.copy(m.send_q.at[n], m.came_q.at[n], at.xs[dx - 1]))
        else:
            m.own_q[...] = for_q
    for i in range(2):
        for n in range(2):
            far[i][n].wait_recv()
            grad = m.near_kv[i, n, halves[i], :] + m.via_kv[i, n].astype(F32)
            m.send_kv[i, n, halves[i]] = grad.astype(BF16)
            back.append(links.copy(m.send_kv.at[i, n, halves[i]], m.came_kv.at[i, n, halves[i]], by[i]))
    for n, grad in enumerate(key_grad(z)):
        m.own_kv[n] = grad
    for copy in back:
        copy.wait_recv()
    for_q = m.own_q[...] + sum(m.came_q[n].astype(F32) for n in range(3))
    for_k, for_v = [m.own_kv[n] + m.came_kv[0, n].astype(F32) + m.came_kv[1, n].astype(F32) for n in range(2)]
    back_normed = (
        dot(w_qkv[:, :384], for_q.astype(BF16))
        + dot_t(w_qkv[:, 384:768], for_k.astype(BF16))
        + dot_t(w_qkv[:, 768:], for_v.astype(BF16))
    )
    scaled = back_normed.astype(BF16).astype(F32) * gain
    centre = m.full[...].astype(F32)
    inner = jnp.mean(centre * scaled, 0, keepdims=True)
    out = m.cot_full[...].astype(F32) + inv * scaled - centre * (inv * inv * inv * inner)
    for b in range(CH):
        for h in range(2):
            m.grad[b, h] = out[96 * b : 96 * b + 96, 128 * h : 128 * h + 128].astype(BF16)
    row_low, row_high = near_rows(at.row)
    for b in range(CH):
        to = at.sources[b]
        links.copy(m.grad.at[b], m.own.at[at.frame], to, own=same(to, at.me), recv=OWN + at.frame)
    for b in range(CH):
        links.copy(m.grad.at[b, 1], m.prev_g.at[at.frame], (row_high, b), recv=PREV + at.frame)
        links.copy(m.grad.at[b, 0], m.next_g.at[at.frame], (row_low, b), recv=NEXT + at.frame)


def tail(links, at, m):
    r, c, x, y_hi, z = at.r, at.c, at.x, at.y_hi, at.z
    xs, zs, across, chs = at.xs, at.zs, at.across, at.chs
    own, act, w_t, every, inv_in, gain_rows = m.own, m.act, m.w_t, m.every, m.inv_in, m.gain_rows
    rows, lines, weight, part, all_part, inner, all_inner = m.rows, m.lines, m.weight, m.part, m.all_part, m.inner, m.all_inner
    mark, flat, out = m.mark, m.flat, m.out
    ring_x = (x, [lax.rem(x + d, 4) for d in range(1, 4)], xs)
    ring_z = (z, [lax.rem(z + d, 4) for d in range(1, 4)], zs)
    ring_y = (y_hi, [1 - y_hi], [across])
    stripes = []
    for n, (base, size, rings) in enumerate(
        (
            (0, 2048, (ring_y, ring_x, ring_z)),
            (2048, 3072, (ring_x, ring_z, ring_y)),
            (5120, 3072, (ring_z, ring_y, ring_x)),
        )
    ):
        steps, at_row = [], base
        for p, (place_on, places, peers) in enumerate(rings):
            size //= len(peers) + 1
            start = at_row
            at_row = at_row + place_on * size
            came, total = getattr(m, "came_%d_%d" % (n, p)), getattr(m, "total_%d_%d" % (n, p))
            steps.append((start, size, places, peers, at_row, came, total))
        stripes.append(steps)

    def rows_at(start, size):
        return pl.ds(pl.multiple_of(start, 16), size)

    def give(steps, p):
        start, size, places, peers, _, came, _ = steps[p]
        sent = []
        for d, peer in enumerate(peers):
            if p == 0:
                src = weight.at[rows_at(start + places[d] * size, size)]
            else:
                src = steps[p - 1][6].at[rows_at(places[d] * size, size)]
            sent.append(links.copy(src, came.at[d], peer))
        return sent

    def take(steps, p, sent):
        start, size, _, peers, mine, came, total = steps[p]
        for copy in sent:
            copy.wait_recv()
        if p == 0:
            value = weight[rows_at(mine, size), :].astype(F32)
        else:
            value = steps[p - 1][6][rows_at(mine - start, size), :].astype(F32)
        for d in range(len(peers)):
            value += came[d].astype(F32)
        total[...] = value.astype(BF16)

    for f in range(4):
        links.arrive(own.at[f], OWN + f)
        links.arrive(m.prev_g.at[f], PREV + f)
        links.arrive(m.next_g.at[f], NEXT + f)
    for f in range(4):
        rows[f, 0] = jnp.where(r == 0, 0.0, m.prev_g[f].astype(F32)).astype(BF16)
        rows[f, 1] = own[f, 0]
        rows[f, 2] = own[f, 1]
        rows[f, 3] = jnp.where(r == ROWS - 1, 0.0, m.next_g[f].astype(F32)).astype(BF16)
        for h in range(4):
            y = rows[f, h].astype(F32)
            at_lanes = pl.ds(128 * h, 128)
            m.moved[f, :, at_lanes] = jnp.concatenate([move(y, -1), y, move(y, 1)], 0).astype(BF16)
    first = []
    for t in range(3):
        for h in range(3):
            acc = jnp.zeros((288, 384), F32)
            for f in range(4):
                source = f + t - 2
                if source < 0:
                    continue
                acc += dot_t(m.moved[f, :, pl.ds(128 * (2 - h), 256)], act[:, pl.ds(256 * source, 256)])
            for lane in range(3):
                at = (3 * (3 * t + h) + lane) * 288
                weight[pl.ds(at, 288), :] = acc[:, 128 * lane : 128 * lane + 128].astype(BF16)
        if t == 2:
            weight[pl.ds(27 * 288, 416), :] = jnp.zeros((416, 128), BF16)
        first.append(give(stripes[t], 0))
    for f in range(4):
        for h in range(3):
            for k in range(2):
                lines[f, pl.ds(96 * h, 96), pl.ds(128 * k, 128)] = rows[f, 2 - h + k]
    gain = gain_columns(gain_rows, 0)
    for f in range(4):
        acc = jnp.zeros((1152, 256), F32)
        for t in range(3):
            source = f + 2 - t
            if source > 3:
                continue
            acc += dot(w_t[t], lines[source])
        for h in range(2):
            y = acc[:, 128 * h : 128 * h + 128]
            total = move(y[:384], -1) + y[384:768] + move(y[768:], 1)
            v = jnp.concatenate([every[b, f, h] for b in range(CH)], 0).astype(F32)
            before = v * inv_in[2 * f + h : 2 * f + h + 1, :] * gain
            sig = sigmoid(before)
            slope = sig * (1.0 + before * (1.0 - sig))
            inner[2 * f + h : 2 * f + h + 1, :] = jnp.sum(v * slope * gain * total, 0, keepdims=True)
            for b in range(CH):
                part[b, f, h] = total[96 * b : 96 * b + 96].astype(BF16)
    second, third, parts = [], [], []
    for n, steps in enumerate(stripes):
        take(steps, 0, first[n])
        second.append(give(steps, 1))
    for d in range(3):
        parts.append(links.copy(part.at[chs[d][1]], all_part.at[d], chs[d]))
        parts.append(links.copy(inner, all_inner.at[d], chs[d]))
    for n, steps in enumerate(stripes):
        take(steps, 1, second[n])
        third.append(give(steps, 2))
    spread, kept = [], []
    for n, steps in enumerate(stripes):
        take(steps, 2, third[n])
        _, size, _, peers, mine, _, total = steps[2]
        at_flat = flat.at[rows_at(mine, size)]
        kept.append(pltpu.make_async_copy(total, at_flat, mark.at[n]))
        kept[n].start()
        spread.append([links.copy(total, at_flat, peer) for peer in peers])
    for p in (1, 0):
        for n, steps in enumerate(stripes):
            if p == 1:
                kept[n].wait()
            for copy in spread[n]:
                copy.wait_recv()
            _, size, _, peers, mine, _, _ = steps[p]
            at_flat = flat.at[rows_at(mine, size)]
            spread[n] = [links.copy(at_flat, at_flat, peer) for peer in peers]
    for copy in parts:
        copy.wait_recv()
    mean = (inner[...] + all_inner[0] + all_inner[1] + all_inner[2]) / 384.0
    gain = jnp.broadcast_to(gain_rows[c, 0:1, :], (128, 128)).T[:96]
    for f in range(4):
        for h in range(2):
            v = every[c, f, h].astype(F32)
            inv = inv_in[2 * f + h : 2 * f + h + 1, :]
            total = part[c, f, h].astype(F32)
            for d in range(3):
                total += all_part[d, f, h].astype(F32)
            before = v * inv * gain
            sig = sigmoid(before)
            scaled = total * (sig * (1.0 + before * (1.0 - sig))) * gain
            cube = inv * inv * inv * mean[2 * f + h : 2 * f + h + 1, :]
            out[f, h] = (own[f, h].astype(F32) + inv * scaled - v * cube).astype(BF16)
    for copy in spread[0] + spread[1] + spread[2]:
        copy.wait_recv()


def whole(links, m):
    at = Place()
    front(links, at, m)
    attention(links, at, m)
    tail(links, at, m)
    links.finish()


def widen_kernel(scale, flat, out, near, wide, into, back):
    come = [
        pltpu.make_async_copy(flat.at[pl.ds(864 * k, 864)], near.at[k], into.at[k]) for k in range(9)
    ]
    go = [
        pltpu.make_async_copy(wide.at[k], out.at[pl.ds(288 * k, 288)], back.at[k]) for k in range(9)
    ]
    for copy in come:
        copy.start()
    for k in range(9):
        come[k].wait()
        for lane in range(3):
            piece = near[k, pl.ds(288 * lane, 288), :].astype(F32) * scale
            wide[k, :, pl.ds(128 * lane, 128)] = piece
        go[k].start()
    for copy in go:
        copy.wait()


def on_device(features, gain_in, w_conv, gain_attn, w_qkv, w_out, cotangent):
    near, far = pltpu.VMEM, pl.ANY
    held = {
        "feat": (features, far),
        "cot": (cotangent, far),
        "w_far": (w_conv, far),
        "gain_in": (gain_in.reshape(1, 96), near),
        "gain_attn": (gain_attn.reshape(1, 96), near),
        "w_qkv": (w_qkv, near),
        "w_out": (w_out, near),
    }
    made = {"out": ((4, 2, 96, 128), BF16, near), "flat": ((8192, 128), BF16, far)}
    b16 = {
        "every": (4, 4, 2, 96, 128),
        "w": (27, 96, 384),
        "act": (384, 1024),
        "edge_out": (2, 4, 96, 128),
        "edge_in": (2, 4, 96, 128),
        "moved": (4, 288, 512),
        "res": (4, 2, 96, 128),
        "cot_frame": (4, 2, 96, 128),
        "res_frame": (4, 2, 96, 128),
        "full": (384, 256),
        "cot_full": (384, 256),
        "norm": (4, 256, 384),
        "q": (8, 384, 256),
        "g": (8, 384, 256),
        "k": (4, 256, 384),
        "v": (4, 256, 384),
        "k_t": (384, 1024),
        "prob": (8, 1024, 256),
        "grad_s": (8, 1024, 256),
        "far_kv": (2, 256, 384),
        "via_kv": (2, 2, 128, 384),
        "send_kv": (2, 2, 256, 384),
        "came_kv": (2, 2, 256, 384),
        "sib_out": (4, 384, 256),
        "sib_in": (4, 384, 256),
        "send_q": (3, 384, 256),
        "came_q": (3, 384, 256),
        "grad": (4, 2, 96, 128),
        "own": (4, 2, 96, 128),
        "prev_g": (4, 96, 128),
        "next_g": (4, 96, 128),
        "w_t": (3, 1152, 288),
        "rows": (4, 4, 96, 128),
        "lines": (4, 288, 256),
        "weight": (8192, 128),
        "part": (4, 4, 2, 96, 128),
        "all_part": (3, 4, 2, 96, 128),
    }
    for n, (size, counts) in enumerate(((2048, (2, 4, 4)), (3072, (4, 4, 2)), (3072, (4, 2, 4)))):
        for p, count in enumerate(counts):
            size //= count
            b16["came_%d_%d" % (n, p)] = (count - 1, size, 128)
            b16["total_%d_%d" % (n, p)] = (size, 128)
    f32 = {
        "inv_in": (8, 128),
        "conv_own": (4, 2, 96, 128),
        "gain_rows": (4, 8, 128),
        "exps": (4, 8, 256, 256),
        "grad_p": (4, 8, 256, 256),
        "tops": (4, 8, 256),
        "sums": (4, 8, 256),
        "deltas": (4, 8, 256),
        "stats": (3, 8, 256),
        "all_stats": (7, 3, 8, 256),
        "weights": (4, 8, 256),
        "delta": (8, 256),
        "near_kv": (2, 2, 256, 384),
        "own_kv": (2, 256, 384),
        "own_q": (384, 256),
        "inner": (8, 128),
        "all_inner": (3, 8, 128),
    }
    scratch = {n: pltpu.VMEM(s, BF16) for n, s in b16.items()}
    scratch |= {n: pltpu.VMEM(s, F32) for n, s in f32.items()}
    scratch["mark"] = pltpu.SemaphoreType.DMA((3,))
    out, flat = fused(0, whole, held, made, scratch, (SENDS, NEXT + 4))
    cell_scale = 1.0 / math.sqrt(32768)
    grad_weights = pl.pallas_call(
        functools.partial(widen_kernel, cell_scale),
        out_shape=jax.ShapeDtypeStruct((2592, 384), F32),
        in_specs=[pl.BlockSpec(memory_space=pl.ANY)],
        out_specs=pl.BlockSpec(memory_space=pl.ANY),
        scratch_shapes=[
            pltpu.VMEM((9, 864, 128), BF16),
            pltpu.VMEM((9, 288, 384), F32),
            pltpu.SemaphoreType.DMA((9,)),
            pltpu.SemaphoreType.DMA((9,)),
        ],
        compiler_params=pltpu.CompilerParams(vmem_limit_bytes=VMEM_BYTES),
        name="widen",
    )(flat)
    return out, grad_weights.reshape(27, 96, 384)


def solution(mesh):
    return jax.shard_map(
        on_device,
        mesh=mesh,
        in_specs=(
            P(None, "row", "ch", None),
            P("ch"),
            P(None, "ch", None),
            P("ch"),
            P(),
            P(),
            P(None, "row", "ch", None),
        ),
        out_specs=(P(None, "row", "ch", None), P(None, "ch", None)),
        check_vma=False,
    )
```

```python
import functools
import math
import types

import jax
import jax.numpy as jnp
from jax import lax
from jax.experimental import pallas as pl
from jax.experimental.pallas import tpu as pltpu
from jax.sharding import PartitionSpec as P

EPSILON = 1e-06
MESH = pl.DeviceIdType.MESH
F32 = jnp.float32
BF16 = jnp.bfloat16
ROWS = 32
SENDS = 128
COT, RES, OWN, PREV, NEXT = range(SENDS, SENDS + 20, 4)
CH = 4
VMEM_BYTES = 60 * 1024 * 1024


def coords():
    return lax.axis_index("row"), lax.axis_index("ch")


def place(r, c):
    return lax.rem(r, 4), lax.rem(r // 4, 2), r // 8, c // 2, lax.rem(c, 2)


def device(x, y_hi, z, y_lo, core):
    return z * 8 + y_hi * 4 + x, y_lo * 2 + core


def owner(f, row):
    x, y_hi, z, _, _ = place(row, 0)
    return device(x, f // 2, z, f % 2, y_hi)


class Links:
    def __init__(self, send, recv):
        self.send, self.recv, self.sent, self.at = send, recv, [], 0

    def greet(self, peers, count):
        barrier = pltpu.get_barrier_semaphore()
        for peer in peers:
            pl.semaphore_signal(barrier, inc=1, device_id=peer, device_id_type=MESH)
        pl.semaphore_wait(barrier, count)

    def copy(self, src, dst, to, own=None, recv=None):
        k = self.at
        self.at += 1
        mark = self.recv.at[k if recv is None else recv]
        far = pltpu.make_async_remote_copy(
            src_ref=src,
            dst_ref=dst,
            send_sem=self.send.at[k],
            recv_sem=mark,
            device_id=to,
            device_id_type=MESH,
        )
        if own is None:
            far.start()
        else:
            pl.when(jnp.logical_not(own))(far.start)
            pl.when(own)(pltpu.make_async_copy(src, dst, mark).start)
        self.sent.append((far, own))
        return far

    def arrive(self, dst, k):
        pltpu.make_async_copy(dst, dst, self.recv.at[k]).wait()

    def finish(self):
        for far, own in self.sent:
            if own is None:
                far.wait_send()
            else:
                pl.when(jnp.logical_not(own))(far.wait_send)


def fused(cid, body, held, made, scratch, count):
    names = [*held, *made, *scratch]

    def kernel(*refs):
        body(Links(*refs[-2:]), types.SimpleNamespace(**dict(zip(names, refs))))

    return pl.pallas_call(
        kernel,
        out_shape=[jax.ShapeDtypeStruct(s, t) for s, t, _ in made.values()],
        in_specs=[pl.BlockSpec(memory_space=m) for _, m in held.values()],
        out_specs=[pl.BlockSpec(memory_space=m) for _, _, m in made.values()],
        scratch_shapes=[*scratch.values()] + [pltpu.SemaphoreType.DMA((n,)) for n in count],
        compiler_params=pltpu.CompilerParams(
            collective_id=cid, has_side_effects=True, vmem_limit_bytes=VMEM_BYTES
        ),
        name="fused_%d" % cid,
    )(*[array for array, _ in held.values()])


def dot(a, b):
    return lax.dot_general(a, b, (((1,), (0,)), ((), ())), preferred_element_type=F32)


def dot_t(a, b):
    return lax.dot_general(a, b, (((1,), (1,)), ((), ())), preferred_element_type=F32)


def move(block, by):
    lanes = block.shape[1]
    at = lax.broadcasted_iota(jnp.int32, block.shape, 1)
    if by > 0:
        return jnp.where(at == 0, 0.0, pltpu.roll(block, 1, axis=1))
    return jnp.where(at == lanes - 1, 0.0, pltpu.roll(block, lanes - 1, axis=1))


def ch_peers(r, c):
    return [(r, lax.rem(c + d, CH)) for d in range(1, CH)]


def near_rows(r):
    return lax.rem(r + ROWS - 1, ROWS), lax.rem(r + 1, ROWS)


def same(a, b):
    return jnp.logical_and(a[0] == b[0], a[1] == b[1])


def greet_frames(me, sources, targets):
    barrier = pltpu.get_barrier_semaphore()
    for peer in sources:
        def tell(peer=peer):
            pl.semaphore_signal(barrier, inc=1, device_id=peer, device_id_type=MESH)

        pl.when(jnp.logical_not(same(peer, me)))(tell)
    _, y_hi, _, _, core = place(*me)
    pl.semaphore_wait(barrier, len(targets) - 2 + 2 * (core - y_hi) * (core - y_hi))


def sigmoid(v):
    return 1.0 / (1.0 + jnp.exp(-v))


def gain_columns(rows, which):
    blocks = [jnp.broadcast_to(rows[b, which : which + 1, :], (128, 128)).T[:96] for b in range(CH)]
    return jnp.concatenate(blocks, 0)


class Place:
    def __init__(self):
        r, c = self.r, self.c = self.me = coords()
        x, y_hi, z, y_lo, core = self.x, self.y_hi, self.z, self.y_lo, self.core = place(r, c)
        self.slot = core * 4 + x
        self.frame = y_hi * 2 + y_lo
        self.low, self.high = near_rows(r)
        self.c_near = (1 - y_lo) * 2 + core
        self.sibling = (r, y_lo * 2 + 1 - core)
        self.near = (r, self.c_near)
        self.chs = ch_peers(r, c)
        self.xs = [device(lax.rem(x + d, 4), y_hi, z, y_lo, core) for d in range(1, 4)]
        self.cross = [device(lax.rem(x + d, 4), y_hi, z, y_lo, 1 - core) for d in range(1, 4)]
        self.zs = [device(x, y_hi, lax.rem(z + d, 4), y_lo, core) for d in range(1, 4)]
        self.across = device(x, 1 - y_hi, z, y_lo, core)
        self.targets = [owner(f, r) for f in range(4)]
        self.row = z * 8 + core * 4 + x
        self.sources = [(self.row, b) for b in range(CH)]

    def greet(self):
        at = self
        alike = at.chs + at.xs + at.cross + at.zs + [at.across, (at.low, at.c), (at.high, at.c)]
        there = [(i, b) for i in near_rows(at.row) for b in range(CH)]
        whose = [owner(f, i) for i in (at.low, at.high) for f in range(4)]
        greet_frames(at.me, at.targets + at.sources + whose + alike, at.targets + at.sources + there + alike)


def front(links, at, m):
    r, c, near, sibling = at.r, at.c, at.near, at.sibling
    every, act = m.every, m.act
    here = pltpu.make_async_copy(m.feat, every.at[c], m.mark.at[0])
    here.start()
    weights = pltpu.make_async_copy(m.w_far, m.w, m.mark.at[1])
    weights.start()
    m.gain_rows[c] = jnp.zeros((8, 128), F32)
    pad = jnp.zeros((1, 32), F32)
    m.gain_rows[c, 0:1, :] = jnp.concatenate([m.gain_in[...].astype(F32), pad], 1)
    m.gain_rows[c, 1:2, :] = jnp.concatenate([m.gain_attn[...].astype(F32), pad], 1)
    at.greet()
    pairs = [pl.ds(2 * p, 2) for p in range(2)]
    gains = [links.copy(m.gain_rows.at[c], m.gain_rows.at[c], to) for to in at.chs]
    to_near = [links.copy(m.feat.at[two], every.at[c, two], near) for two in pairs]
    to_sib = links.copy(m.feat, every.at[c], sibling)
    for copy in gains:
        copy.wait_recv()
    gain = gain_columns(m.gain_rows, 0)
    passed = []
    for p, two in enumerate(pairs):
        to_near[p].wait_recv()
        part = every.at[at.c_near, two]
        passed.append(links.copy(part, part, sibling))
    for f in range(4):
        own = same(at.targets[f], at.me)
        links.copy(m.cot.at[f], m.cot_frame.at[c], at.targets[f], own=own, recv=COT + c)

    def activate(f, h):
        v = jnp.concatenate([every[b, f, h] for b in range(CH)], 0).astype(F32)
        inv = lax.rsqrt(jnp.mean(v * v, 0, keepdims=True) + EPSILON)
        before = v * inv * gain
        m.inv_in[2 * f + h : 2 * f + h + 1, :] = inv
        act[:, pl.ds((2 * f + h) * 128, 128)] = (before * sigmoid(before)).astype(BF16)

    here.wait()
    to_sib.wait_recv()
    weights.wait()
    edges = []
    for p, two in enumerate(pairs):
        passed[p].wait_recv()
        for f in (2 * p, 2 * p + 1):
            activate(f, 0)
            activate(f, 1)
        for f in (2 * p, 2 * p + 1):
            by_tap = []
            for h in range(3):
                acc = jnp.zeros((288, 256), F32)
                for t in range(3):
                    source = f + t - 2
                    if source >= 0:
                        taps = m.w[pl.ds(9 * t + 3 * h, 3)].reshape(288, 384)
                        acc += dot(taps, act[:, pl.ds(256 * source, 256)])
                by_tap.append((acc[:, :128], acc[:, 128:]))
            lines = (
                by_tap[2][0],
                by_tap[2][1] + by_tap[1][0],
                by_tap[1][1] + by_tap[0][0],
                by_tap[0][1],
            )
            lines = [move(y[:96], 1) + y[96:192] + move(y[192:], -1) for y in lines]
            m.edge_out[0, f] = lines[0].astype(BF16)
            m.edge_out[1, f] = lines[3].astype(BF16)
            m.conv_own[f, 0] = lines[1]
            m.conv_own[f, 1] = lines[2]
        edges.append(links.copy(m.edge_out.at[0, two], m.edge_in.at[0, two], (at.low, c)))
        edges.append(links.copy(m.edge_out.at[1, two], m.edge_in.at[1, two], (at.high, c)))
    for b in range(CH):
        links.arrive(m.cot_frame.at[b], COT + b)
    for b in range(CH):
        for h in range(2):
            m.cot_full[pl.ds(96 * b, 96), pl.ds(128 * h, 128)] = m.cot_frame[b, h]
    m.g[at.slot] = dot(m.w_out[...], m.cot_full[...]).astype(BF16)
    at.g_first = [links.copy(m.g.at[at.slot], m.g.at[at.slot], to) for to in (at.xs[0], at.xs[2], sibling)]
    for p in range(2):
        edges[2 * p].wait_recv()
        edges[2 * p + 1].wait_recv()
        for f in (2 * p, 2 * p + 1):
            before = jnp.where(r == 0, 0.0, m.edge_in[1, f].astype(F32))
            after = jnp.where(r == ROWS - 1, 0.0, m.edge_in[0, f].astype(F32))
            m.res[f, 0] = (every[c, f, 0].astype(F32) + (m.conv_own[f, 0] + before)).astype(BF16)
            m.res[f, 1] = (every[c, f, 1].astype(F32) + (m.conv_own[f, 1] + after)).astype(BF16)
            own = same(at.targets[f], at.me)
            links.copy(m.res.at[f], m.res_frame.at[c], at.targets[f], own=own, recv=RES + c)


def attention(links, at, m):
    scale = 1.0 / math.sqrt(384)
    x, z, core, slot, sibling = at.x, at.z, at.core, at.slot, at.sibling
    q, g, k, v, k_t = m.q, m.g, m.k, m.v, m.k_t
    w_qkv = m.w_qkv

    def relay_ring(first, ref, base, i, rows, peers, forward):
        on = []
        for side in range(2):
            first[side].wait_recv()
            came = base + lax.rem(i + 3 - 2 * side, 4)
            part = ref.at[came, pl.ds(rows * side, rows)]
            on.append(links.copy(part, part, peers[2 * side]))
            if forward:
                on.append(links.copy(ref.at[came], ref.at[came], sibling))
        return on

    g_on = relay_ring(at.g_first, g, core * 4, x, 192, at.xs, True)
    gain = gain_columns(m.gain_rows, 1)
    gain = jnp.concatenate([gain, gain], 1)
    for b in range(CH):
        links.arrive(m.res_frame.at[b], RES + b)
    for b in range(CH):
        for h in range(2):
            m.full[pl.ds(96 * b, 96), pl.ds(128 * h, 128)] = m.res_frame[b, h]
    centre = m.full[...].astype(F32)
    inv = lax.rsqrt(jnp.mean(centre * centre, 0, keepdims=True) + EPSILON)
    m.norm[z] = (centre * inv * gain).astype(BF16).astype(F32).T.astype(BF16)
    n_first = [links.copy(m.norm.at[z], m.norm.at[z], to) for to in (at.zs[0], at.zs[2])]
    q[slot] = dot(m.norm[z], w_qkv[:, :384]).T.astype(BF16)
    q_first = [links.copy(q.at[slot], q.at[slot], to) for to in (at.xs[0], at.xs[2], sibling)]

    def project(j):
        k[j] = dot(m.norm[j], w_qkv[:, 384:768]).astype(BF16)
        v[j] = dot(m.norm[j], w_qkv[:, 768:]).astype(BF16)
        k_t[:, pl.ds(pl.multiple_of(256 * j, 256), 256)] = k[j].T

    def tile(b, j):
        s = dot(k[j], q[b]) * scale
        top = jnp.max(s, 0, keepdims=True)
        e = jnp.exp(s - top)
        p = dot(v[j], g[b])
        m.exps[j, b] = e
        m.grad_p[j, b] = p
        m.tops[j, pl.ds(b, 1), :] = top
        m.sums[j, pl.ds(b, 1), :] = jnp.sum(e, 0, keepdims=True)
        m.deltas[j, pl.ds(b, 1), :] = jnp.sum(e * p, 0, keepdims=True)

    def block(dk, dx):
        other = core + dk - 2 * core * dk
        return other * 4 + lax.rem(x + dx, 4)

    def key(dz):
        return lax.rem(z + dz, 4)

    def tiles(count, unroll, which):
        def step(n, carry):
            dk, dx, dz = which(n)
            tile(block(dk, dx), key(dz))
            return carry

        lax.fori_loop(0, count, step, 0, unroll=unroll)

    project(z)
    g_on[1].wait_recv()
    g_on[3].wait_recv()
    far_x = core * 4 + lax.rem(x + 2, 4)
    at.g_first[2].wait_recv()
    q_first[2].wait_recv()
    tiles(2, 2, lambda n: (n, 0, 0))
    for t in range(3):
        for n in range(3):
            piece = jnp.concatenate([m.w[9 * t + 3 * h + n] for h in range(3)], 0)
            m.w_t[t, pl.ds(384 * n, 384), :] = piece.T
    n_on = relay_ring(n_first, m.norm, 0, z, 128, at.zs, False)
    q_on = relay_ring(q_first, q, core * 4, x, 192, at.xs, True)
    g_on[0].wait_recv()
    g_on[2].wait_recv()
    g_last = links.copy(g.at[far_x], g.at[far_x], sibling)
    project(key(1))
    project(key(3))
    tiles(4, 4, lambda n: (n // 2, 0, 1 + 2 * lax.rem(n, 2)))
    q_on[1].wait_recv()
    q_on[3].wait_recv()

    def beside(n):
        dz = n // 4
        return lax.rem(n // 2, 2), 1 + 2 * lax.rem(n, 2), dz + dz // 2

    tiles(12, 4, beside)
    q_on[0].wait_recv()
    q_on[2].wait_recv()
    q_last = links.copy(q.at[far_x], q.at[far_x], sibling)
    n_on[0].wait_recv()
    n_on[1].wait_recv()
    project(key(2))

    def beyond(n):
        dx = n // 2
        return lax.rem(n, 2), dx + dx // 2, 2

    tiles(6, 3, beyond)
    tiles(4, 4, lambda n: (0, 2, n))
    q_last.wait_recv()
    g_last.wait_recv()
    tiles(4, 4, lambda n: (1, 2, n))

    tops = [m.tops[j] for j in range(4)]
    top = functools.reduce(jnp.maximum, tops)
    shift = [jnp.exp(t - top) for t in tops]
    m.stats[0] = top
    m.stats[1] = sum(m.sums[j] * shift[j] for j in range(4))
    m.stats[2] = sum(m.deltas[j] * shift[j] for j in range(4))
    peers = at.xs + at.cross + [sibling]
    shared = [links.copy(m.stats, m.all_stats.at[n], to) for n, to in enumerate(peers)]
    for copy in shared:
        copy.wait_recv()
    parts = [m.stats] + [m.all_stats.at[n] for n in range(7)]
    top = functools.reduce(jnp.maximum, [p[0] for p in parts])
    total = sum(p[1] * jnp.exp(p[0] - top) for p in parts)
    m.delta[...] = sum(p[2] * jnp.exp(p[0] - top) for p in parts) / total
    for j in range(4):
        m.weights[j] = jnp.exp(m.tops[j] - top) / total

    def rows_of(j):
        return pl.ds(pl.multiple_of(256 * j, 256), 256)

    def weigh(b, j):
        prob = m.exps[j, b] * m.weights[j, pl.ds(b, 1), :]
        m.prob[b, rows_of(j), :] = prob.astype(BF16)
        m.grad_s[b, rows_of(j), :] = (prob * (m.grad_p[j, b] - m.delta[pl.ds(b, 1), :])).astype(BF16)

    def key_grad(j):
        for_k = sum(dot_t(m.grad_s[b, rows_of(j), :], q[b]) for b in range(8)) * scale
        for_v = sum(dot_t(m.prob[b, rows_of(j), :], g[b]) for b in range(8))
        return dot_t(w_qkv[:, 384:768], for_k.astype(BF16)) + dot_t(w_qkv[:, 768:], for_v.astype(BF16))

    halves = [pl.ds(0, 192), pl.ds(192, 192)]
    rings = ((at.zs[0], at.zs[2]), (at.xs[0], at.xs[2]))
    by_way, back = {}, []

    def send_far(kind, value):
        m.far[kind] = value.astype(BF16)
        for i in range(2):
            by_way[kind, i] = links.copy(m.far.at[kind, halves[i]], m.via.at[kind, i], rings[kind][i])

    def send_half(kind, i, half, value):
        m.send[kind, i, halves[half]] = value.astype(BF16)
        src, dst = m.send.at[kind, i, halves[half]], m.came.at[kind, i, halves[half]]
        back.append(links.copy(src, dst, rings[kind][i]))

    def send_near(kind, i, value):
        m.nearest[kind, i] = value
        send_half(kind, i, 1 - i, value[192 * (1 - i) : 192 * (2 - i)])

    def send_added(kind):
        for i in range(2):
            by_way[kind, i].wait_recv()
            send_half(kind, i, i, m.nearest[kind, i, halves[i], :] + m.via[kind, i].astype(F32))

    for dz in range(4):
        for dx in range(4):
            weigh(block(1, dx), key(dz))
    sib = []
    for dx in range(4):
        m.sib_out[dx] = (dot(k_t[...], m.grad_s[block(1, dx)]) * scale).astype(BF16)
        sib.append(links.copy(m.sib_out.at[dx], m.sib_in.at[dx], sibling))
    for dz in range(4):
        for dx in range(4):
            weigh(block(0, dx), key(dz))

    def query_grad(dx):
        value = dot(k_t[...], m.grad_s[block(0, dx)]) * scale
        sib[dx].wait_recv()
        return value + m.sib_in[dx].astype(F32)

    send_far(0, key_grad(key(2)))
    send_far(1, query_grad(2))
    send_near(1, 0, query_grad(1))
    send_near(1, 1, query_grad(3))
    send_near(0, 0, key_grad(key(1)))
    send_near(0, 1, key_grad(key(3)))
    send_added(1)
    send_added(0)
    m.own_sum[0] = key_grad(z)
    m.own_sum[1] = query_grad(0)
    for copy in back:
        copy.wait_recv()
    by_key, by_query = [
        m.own_sum[n] + m.came[n, 0].astype(F32) + m.came[n, 1].astype(F32) for n in range(2)
    ]
    back_normed = dot(w_qkv[:, :384], by_query.astype(BF16)) + by_key
    scaled = back_normed.astype(BF16).astype(F32) * gain
    centre = m.full[...].astype(F32)
    inner = jnp.mean(centre * scaled, 0, keepdims=True)
    out = m.cot_full[...].astype(F32) + inv * scaled - centre * (inv * inv * inv * inner)
    for b in range(CH):
        for h in range(2):
            m.grad[b, h] = out[96 * b : 96 * b + 96, 128 * h : 128 * h + 128].astype(BF16)
    row_low, row_high = near_rows(at.row)
    for b in range(CH):
        to = at.sources[b]
        links.copy(m.grad.at[b], m.own.at[at.frame], to, own=same(to, at.me), recv=OWN + at.frame)
    for b in range(CH):
        links.copy(m.grad.at[b, 1], m.prev_g.at[at.frame], (row_high, b), recv=PREV + at.frame)
        links.copy(m.grad.at[b, 0], m.next_g.at[at.frame], (row_low, b), recv=NEXT + at.frame)


def tail(links, at, m):
    r, c, x, y_hi, z = at.r, at.c, at.x, at.y_hi, at.z
    xs, zs, across, chs = at.xs, at.zs, at.across, at.chs
    own, act, w_t, every, inv_in, gain_rows = m.own, m.act, m.w_t, m.every, m.inv_in, m.gain_rows
    rows, lines, weight, part, all_part, inner, all_inner = m.rows, m.lines, m.weight, m.part, m.all_part, m.inner, m.all_inner
    mark, flat, out = m.mark, m.flat, m.out
    ring_x = (x, [lax.rem(x + d, 4) for d in range(1, 4)], xs)
    ring_z = (z, [lax.rem(z + d, 4) for d in range(1, 4)], zs)
    ring_y = (y_hi, [1 - y_hi], [across])
    stripes = []
    for n, (base, size, rings) in enumerate(
        (
            (0, 2048, (ring_y, ring_x, ring_z)),
            (2048, 3072, (ring_x, ring_z, ring_y)),
            (5120, 3072, (ring_z, ring_y, ring_x)),
        )
    ):
        steps, at_row = [], base
        for p, (place_on, places, peers) in enumerate(rings):
            size //= len(peers) + 1
            start = at_row
            at_row = at_row + place_on * size
            came, total = getattr(m, "came_%d_%d" % (n, p)), getattr(m, "total_%d_%d" % (n, p))
            steps.append((start, size, places, peers, at_row, came, total))
        stripes.append(steps)

    def rows_at(start, size):
        return pl.ds(pl.multiple_of(start, 16), size)

    def give(steps, p):
        start, size, places, peers, _, came, _ = steps[p]
        sent = []
        for d, peer in enumerate(peers):
            if p == 0:
                src = weight.at[rows_at(start + places[d] * size, size)]
            else:
                src = steps[p - 1][6].at[rows_at(places[d] * size, size)]
            sent.append(links.copy(src, came.at[d], peer))
        return sent

    def take(steps, p, sent):
        start, size, _, peers, mine, came, total = steps[p]
        for copy in sent:
            copy.wait_recv()
        if p == 0:
            value = weight[rows_at(mine, size), :].astype(F32)
        else:
            value = steps[p - 1][6][rows_at(mine - start, size), :].astype(F32)
        for d in range(len(peers)):
            value += came[d].astype(F32)
        total[...] = value.astype(BF16)

    for f in range(4):
        links.arrive(own.at[f], OWN + f)
        links.arrive(m.prev_g.at[f], PREV + f)
        links.arrive(m.next_g.at[f], NEXT + f)
    for f in range(4):
        rows[f, 0] = jnp.where(r == 0, 0.0, m.prev_g[f].astype(F32)).astype(BF16)
        rows[f, 1] = own[f, 0]
        rows[f, 2] = own[f, 1]
        rows[f, 3] = jnp.where(r == ROWS - 1, 0.0, m.next_g[f].astype(F32)).astype(BF16)
        for h in range(4):
            y = rows[f, h].astype(F32)
            at_lanes = pl.ds(128 * h, 128)
            m.moved[f, :, at_lanes] = jnp.concatenate([move(y, -1), y, move(y, 1)], 0).astype(BF16)
    first = []
    for t in range(3):
        for h in range(3):
            acc = jnp.zeros((288, 384), F32)
            for f in range(4):
                source = f + t - 2
                if source < 0:
                    continue
                acc += dot_t(m.moved[f, :, pl.ds(128 * (2 - h), 256)], act[:, pl.ds(256 * source, 256)])
            for lane in range(3):
                at = (3 * (3 * t + h) + lane) * 288
                weight[pl.ds(at, 288), :] = acc[:, 128 * lane : 128 * lane + 128].astype(BF16)
        if t == 2:
            weight[pl.ds(27 * 288, 416), :] = jnp.zeros((416, 128), BF16)
        first.append(give(stripes[t], 0))
    for f in range(4):
        for h in range(3):
            for k in range(2):
                lines[f, pl.ds(96 * h, 96), pl.ds(128 * k, 128)] = rows[f, 2 - h + k]
    gain = gain_columns(gain_rows, 0)
    for f in range(4):
        acc = jnp.zeros((1152, 256), F32)
        for t in range(3):
            source = f + 2 - t
            if source > 3:
                continue
            acc += dot(w_t[t], lines[source])
        for h in range(2):
            y = acc[:, 128 * h : 128 * h + 128]
            total = move(y[:384], -1) + y[384:768] + move(y[768:], 1)
            v = jnp.concatenate([every[b, f, h] for b in range(CH)], 0).astype(F32)
            before = v * inv_in[2 * f + h : 2 * f + h + 1, :] * gain
            sig = sigmoid(before)
            slope = sig * (1.0 + before * (1.0 - sig))
            inner[2 * f + h : 2 * f + h + 1, :] = jnp.sum(v * slope * gain * total, 0, keepdims=True)
            for b in range(CH):
                part[b, f, h] = total[96 * b : 96 * b + 96].astype(BF16)
    second, third, parts = [], [], []
    for n, steps in enumerate(stripes):
        take(steps, 0, first[n])
        second.append(give(steps, 1))
    for d in range(3):
        parts.append(links.copy(part.at[chs[d][1]], all_part.at[d], chs[d]))
        parts.append(links.copy(inner, all_inner.at[d], chs[d]))
    for n, steps in enumerate(stripes):
        take(steps, 1, second[n])
        third.append(give(steps, 2))
    spread, kept = [], []
    for n, steps in enumerate(stripes):
        take(steps, 2, third[n])
        _, size, _, peers, mine, _, total = steps[2]
        at_flat = flat.at[rows_at(mine, size)]
        kept.append(pltpu.make_async_copy(total, at_flat, mark.at[n]))
        kept[n].start()
        spread.append([links.copy(total, at_flat, peer) for peer in peers])
    for p in (1, 0):
        for n, steps in enumerate(stripes):
            if p == 1:
                kept[n].wait()
            for copy in spread[n]:
                copy.wait_recv()
            _, size, _, peers, mine, _, _ = steps[p]
            at_flat = flat.at[rows_at(mine, size)]
            spread[n] = [links.copy(at_flat, at_flat, peer) for peer in peers]
    for copy in parts:
        copy.wait_recv()
    mean = (inner[...] + all_inner[0] + all_inner[1] + all_inner[2]) / 384.0
    gain = jnp.broadcast_to(gain_rows[c, 0:1, :], (128, 128)).T[:96]
    for f in range(4):
        for h in range(2):
            v = every[c, f, h].astype(F32)
            inv = inv_in[2 * f + h : 2 * f + h + 1, :]
            total = part[c, f, h].astype(F32)
            for d in range(3):
                total += all_part[d, f, h].astype(F32)
            before = v * inv * gain
            sig = sigmoid(before)
            scaled = total * (sig * (1.0 + before * (1.0 - sig))) * gain
            cube = inv * inv * inv * mean[2 * f + h : 2 * f + h + 1, :]
            out[f, h] = (own[f, h].astype(F32) + inv * scaled - v * cube).astype(BF16)
    for copy in spread[0] + spread[1] + spread[2]:
        copy.wait_recv()


def whole(links, m):
    at = Place()
    front(links, at, m)
    attention(links, at, m)
    tail(links, at, m)
    links.finish()


def widen_kernel(scale, flat, out, near, wide, into, back):
    come = [
        pltpu.make_async_copy(flat.at[pl.ds(864 * k, 864)], near.at[k], into.at[k]) for k in range(9)
    ]
    go = [
        pltpu.make_async_copy(wide.at[k], out.at[pl.ds(288 * k, 288)], back.at[k]) for k in range(9)
    ]
    for copy in come:
        copy.start()
    for k in range(9):
        come[k].wait()
        for lane in range(3):
            piece = near[k, pl.ds(288 * lane, 288), :].astype(F32) * scale
            wide[k, :, pl.ds(128 * lane, 128)] = piece
        go[k].start()
    for copy in go:
        copy.wait()


def on_device(features, gain_in, w_conv, gain_attn, w_qkv, w_out, cotangent):
    near, far = pltpu.VMEM, pl.ANY
    held = {
        "feat": (features, far),
        "cot": (cotangent, far),
        "w_far": (w_conv, far),
        "gain_in": (gain_in.reshape(1, 96), near),
        "gain_attn": (gain_attn.reshape(1, 96), near),
        "w_qkv": (w_qkv, near),
        "w_out": (w_out, near),
    }
    made = {"out": ((4, 2, 96, 128), BF16, near), "flat": ((8192, 128), BF16, far)}
    b16 = {
        "every": (4, 4, 2, 96, 128),
        "w": (27, 96, 384),
        "act": (384, 1024),
        "edge_out": (2, 4, 96, 128),
        "edge_in": (2, 4, 96, 128),
        "moved": (4, 288, 512),
        "res": (4, 2, 96, 128),
        "cot_frame": (4, 2, 96, 128),
        "res_frame": (4, 2, 96, 128),
        "full": (384, 256),
        "cot_full": (384, 256),
        "norm": (4, 256, 384),
        "q": (8, 384, 256),
        "g": (8, 384, 256),
        "k": (4, 256, 384),
        "v": (4, 256, 384),
        "k_t": (384, 1024),
        "prob": (8, 1024, 256),
        "grad_s": (8, 1024, 256),
        "far": (2, 384, 256),
        "via": (2, 2, 192, 256),
        "send": (2, 2, 384, 256),
        "came": (2, 2, 384, 256),
        "sib_out": (4, 384, 256),
        "sib_in": (4, 384, 256),
        "grad": (4, 2, 96, 128),
        "own": (4, 2, 96, 128),
        "prev_g": (4, 96, 128),
        "next_g": (4, 96, 128),
        "w_t": (3, 1152, 288),
        "rows": (4, 4, 96, 128),
        "lines": (4, 288, 256),
        "weight": (8192, 128),
        "part": (4, 4, 2, 96, 128),
        "all_part": (3, 4, 2, 96, 128),
    }
    for n, (size, counts) in enumerate(((2048, (2, 4, 4)), (3072, (4, 4, 2)), (3072, (4, 2, 4)))):
        for p, count in enumerate(counts):
            size //= count
            b16["came_%d_%d" % (n, p)] = (count - 1, size, 128)
            b16["total_%d_%d" % (n, p)] = (size, 128)
    f32 = {
        "inv_in": (8, 128),
        "conv_own": (4, 2, 96, 128),
        "gain_rows": (4, 8, 128),
        "exps": (4, 8, 256, 256),
        "grad_p": (4, 8, 256, 256),
        "tops": (4, 8, 256),
        "sums": (4, 8, 256),
        "deltas": (4, 8, 256),
        "stats": (3, 8, 256),
        "all_stats": (7, 3, 8, 256),
        "weights": (4, 8, 256),
        "delta": (8, 256),
        "nearest": (2, 2, 384, 256),
        "own_sum": (2, 384, 256),
        "inner": (8, 128),
        "all_inner": (3, 8, 128),
    }
    scratch = {n: pltpu.VMEM(s, BF16) for n, s in b16.items()}
    scratch |= {n: pltpu.VMEM(s, F32) for n, s in f32.items()}
    scratch["mark"] = pltpu.SemaphoreType.DMA((3,))
    out, flat = fused(0, whole, held, made, scratch, (SENDS, NEXT + 4))
    cell_scale = 1.0 / math.sqrt(32768)
    grad_weights = pl.pallas_call(
        functools.partial(widen_kernel, cell_scale),
        out_shape=jax.ShapeDtypeStruct((2592, 384), F32),
        in_specs=[pl.BlockSpec(memory_space=pl.ANY)],
        out_specs=pl.BlockSpec(memory_space=pl.ANY),
        scratch_shapes=[
            pltpu.VMEM((9, 864, 128), BF16),
            pltpu.VMEM((9, 288, 384), F32),
            pltpu.SemaphoreType.DMA((9,)),
            pltpu.SemaphoreType.DMA((9,)),
        ],
        compiler_params=pltpu.CompilerParams(vmem_limit_bytes=VMEM_BYTES),
        name="widen",
    )(flat)
    return out, grad_weights.reshape(27, 96, 384)


def solution(mesh):
    return jax.shard_map(
        on_device,
        mesh=mesh,
        in_specs=(
            P(None, "row", "ch", None),
            P("ch"),
            P(None, "ch", None),
            P("ch"),
            P(),
            P(),
            P(None, "row", "ch", None),
        ),
        out_specs=(P(None, "row", "ch", None), P(None, "ch", None)),
        check_vma=False,
    )
```

```python
import functools
import math
import types

import jax
import jax.numpy as jnp
from jax import lax
from jax.experimental import pallas as pl
from jax.experimental.pallas import tpu as pltpu
from jax.sharding import PartitionSpec as P

EPSILON = 1e-06
MESH = pl.DeviceIdType.MESH
F32 = jnp.float32
BF16 = jnp.bfloat16
ROWS = 32
SENDS = 168
COT, RES, OWN, PREV, NEXT = range(SENDS, SENDS + 20, 4)
CH = 4
VMEM_BYTES = 60 * 1024 * 1024


def coords():
    return lax.axis_index("row"), lax.axis_index("ch")


def place(r, c):
    return lax.rem(r, 4), lax.rem(r // 4, 2), r // 8, c // 2, lax.rem(c, 2)


def device(x, y_hi, z, y_lo, core):
    return z * 8 + y_hi * 4 + x, y_lo * 2 + core


def owner(f, row):
    x, y_hi, z, _, _ = place(row, 0)
    return device(x, f // 2, z, f % 2, y_hi)


class Links:
    def __init__(self, send, recv):
        self.send, self.recv, self.sent, self.at = send, recv, [], 0

    def greet(self, peers, count):
        barrier = pltpu.get_barrier_semaphore()
        for peer in peers:
            pl.semaphore_signal(barrier, inc=1, device_id=peer, device_id_type=MESH)
        pl.semaphore_wait(barrier, count)

    def copy(self, src, dst, to, own=None, recv=None):
        k = self.at
        self.at += 1
        mark = self.recv.at[k if recv is None else recv]
        far = pltpu.make_async_remote_copy(
            src_ref=src,
            dst_ref=dst,
            send_sem=self.send.at[k],
            recv_sem=mark,
            device_id=to,
            device_id_type=MESH,
        )
        if own is None:
            far.start()
        else:
            pl.when(jnp.logical_not(own))(far.start)
            pl.when(own)(pltpu.make_async_copy(src, dst, mark).start)
        self.sent.append((far, own))
        return far

    def arrive(self, dst, k):
        pltpu.make_async_copy(dst, dst, self.recv.at[k]).wait()

    def finish(self):
        for far, own in self.sent:
            if own is None:
                far.wait_send()
            else:
                pl.when(jnp.logical_not(own))(far.wait_send)


def fused(cid, body, held, made, scratch, count):
    names = [*held, *made, *scratch]

    def kernel(*refs):
        body(Links(*refs[-2:]), types.SimpleNamespace(**dict(zip(names, refs))))

    return pl.pallas_call(
        kernel,
        out_shape=[jax.ShapeDtypeStruct(s, t) for s, t, _ in made.values()],
        in_specs=[pl.BlockSpec(memory_space=m) for _, m in held.values()],
        out_specs=[pl.BlockSpec(memory_space=m) for _, _, m in made.values()],
        scratch_shapes=[*scratch.values()] + [pltpu.SemaphoreType.DMA((n,)) for n in count],
        compiler_params=pltpu.CompilerParams(
            collective_id=cid, has_side_effects=True, vmem_limit_bytes=VMEM_BYTES
        ),
        name="fused_%d" % cid,
    )(*[array for array, _ in held.values()])


def dot(a, b):
    return lax.dot_general(a, b, (((1,), (0,)), ((), ())), preferred_element_type=F32)


def dot_t(a, b):
    return lax.dot_general(a, b, (((1,), (1,)), ((), ())), preferred_element_type=F32)


def move(block, by):
    lanes = block.shape[1]
    at = lax.broadcasted_iota(jnp.int32, block.shape, 1)
    if by > 0:
        return jnp.where(at == 0, 0.0, pltpu.roll(block, 1, axis=1))
    return jnp.where(at == lanes - 1, 0.0, pltpu.roll(block, lanes - 1, axis=1))


def ch_peers(r, c):
    return [(r, lax.rem(c + d, CH)) for d in range(1, CH)]


def near_rows(r):
    return lax.rem(r + ROWS - 1, ROWS), lax.rem(r + 1, ROWS)


def same(a, b):
    return jnp.logical_and(a[0] == b[0], a[1] == b[1])


def greet_frames(me, sources, targets):
    barrier = pltpu.get_barrier_semaphore()
    for peer in sources:
        def tell(peer=peer):
            pl.semaphore_signal(barrier, inc=1, device_id=peer, device_id_type=MESH)

        pl.when(jnp.logical_not(same(peer, me)))(tell)
    _, y_hi, _, _, core = place(*me)
    pl.semaphore_wait(barrier, len(targets) - 2 + 2 * (core - y_hi) * (core - y_hi))


def sigmoid(v):
    return 1.0 / (1.0 + jnp.exp(-v))


def gain_columns(rows, which):
    blocks = [jnp.broadcast_to(rows[b, which : which + 1, :], (128, 128)).T[:96] for b in range(CH)]
    return jnp.concatenate(blocks, 0)


class Place:
    def __init__(self):
        r, c = self.r, self.c = self.me = coords()
        x, y_hi, z, y_lo, core = self.x, self.y_hi, self.z, self.y_lo, self.core = place(r, c)
        self.slot = core * 4 + x
        self.frame = y_hi * 2 + y_lo
        self.low, self.high = near_rows(r)
        self.c_near = (1 - y_lo) * 2 + core
        self.sibling = (r, y_lo * 2 + 1 - core)
        self.near = (r, self.c_near)
        self.chs = ch_peers(r, c)
        self.xs = [device(lax.rem(x + d, 4), y_hi, z, y_lo, core) for d in range(1, 4)]
        self.cross = [device(lax.rem(x + d, 4), y_hi, z, y_lo, 1 - core) for d in range(1, 4)]
        self.zs = [device(x, y_hi, lax.rem(z + d, 4), y_lo, core) for d in range(1, 4)]
        self.across = device(x, 1 - y_hi, z, y_lo, core)
        self.targets = [owner(f, r) for f in range(4)]
        self.row = z * 8 + core * 4 + x
        self.sources = [(self.row, b) for b in range(CH)]

    def greet(self):
        at = self
        alike = at.chs + at.xs + at.cross + at.zs + [at.across, (at.low, at.c), (at.high, at.c)]
        there = [(i, b) for i in near_rows(at.row) for b in range(CH)]
        whose = [owner(f, i) for i in (at.low, at.high) for f in range(4)]
        greet_frames(at.me, at.targets + at.sources + whose + alike, at.targets + at.sources + there + alike)


def front(links, at, m):
    r, c, near, sibling = at.r, at.c, at.near, at.sibling
    every, act = m.every, m.act
    here = pltpu.make_async_copy(m.feat, every.at[c], m.mark.at[0])
    here.start()
    weights = pltpu.make_async_copy(m.w_far, m.w, m.mark.at[1])
    weights.start()
    m.gain_rows[c] = jnp.zeros((8, 128), F32)
    pad = jnp.zeros((1, 32), F32)
    m.gain_rows[c, 0:1, :] = jnp.concatenate([m.gain_in[...].astype(F32), pad], 1)
    m.gain_rows[c, 1:2, :] = jnp.concatenate([m.gain_attn[...].astype(F32), pad], 1)
    at.greet()
    pairs = [pl.ds(2 * p, 2) for p in range(2)]
    gains = [links.copy(m.gain_rows.at[c], m.gain_rows.at[c], to) for to in at.chs]
    to_near = [links.copy(m.feat.at[two], every.at[c, two], near) for two in pairs]
    to_sib = links.copy(m.feat, every.at[c], sibling)
    for copy in gains:
        copy.wait_recv()
    gain = gain_columns(m.gain_rows, 0)
    passed = []
    for p, two in enumerate(pairs):
        to_near[p].wait_recv()
        part = every.at[at.c_near, two]
        passed.append(links.copy(part, part, sibling))
    for f in range(4):
        own = same(at.targets[f], at.me)
        links.copy(m.cot.at[f], m.cot_frame.at[c], at.targets[f], own=own, recv=COT + c)

    def activate(f, h):
        v = jnp.concatenate([every[b, f, h] for b in range(CH)], 0).astype(F32)
        inv = lax.rsqrt(jnp.mean(v * v, 0, keepdims=True) + EPSILON)
        before = v * inv * gain
        m.inv_in[2 * f + h : 2 * f + h + 1, :] = inv
        act[:, pl.ds((2 * f + h) * 128, 128)] = (before * sigmoid(before)).astype(BF16)

    here.wait()
    to_sib.wait_recv()
    weights.wait()
    edges = []
    for p, two in enumerate(pairs):
        passed[p].wait_recv()
        for f in (2 * p, 2 * p + 1):
            activate(f, 0)
            activate(f, 1)
        for f in (2 * p, 2 * p + 1):
            by_tap = []
            for h in range(3):
                acc = jnp.zeros((288, 256), F32)
                for t in range(3):
                    source = f + t - 2
                    if source >= 0:
                        taps = m.w[pl.ds(9 * t + 3 * h, 3)].reshape(288, 384)
                        acc += dot(taps, act[:, pl.ds(256 * source, 256)])
                by_tap.append((acc[:, :128], acc[:, 128:]))
            lines = (
                by_tap[2][0],
                by_tap[2][1] + by_tap[1][0],
                by_tap[1][1] + by_tap[0][0],
                by_tap[0][1],
            )
            lines = [move(y[:96], 1) + y[96:192] + move(y[192:], -1) for y in lines]
            m.edge_out[0, f] = lines[0].astype(BF16)
            m.edge_out[1, f] = lines[3].astype(BF16)
            m.conv_own[f, 0] = lines[1]
            m.conv_own[f, 1] = lines[2]
        edges.append(links.copy(m.edge_out.at[0, two], m.edge_in.at[0, two], (at.low, c)))
        edges.append(links.copy(m.edge_out.at[1, two], m.edge_in.at[1, two], (at.high, c)))
    for b in range(CH):
        links.arrive(m.cot_frame.at[b], COT + b)
    for b in range(CH):
        for h in range(2):
            m.cot_full[pl.ds(96 * b, 96), pl.ds(128 * h, 128)] = m.cot_frame[b, h]
    m.g[at.slot] = dot(m.w_out[...], m.cot_full[...]).astype(BF16)
    at.g_first = [links.copy(m.g.at[at.slot], m.g.at[at.slot], to) for to in (at.xs[0], at.xs[2], sibling)]
    for p in range(2):
        edges[2 * p].wait_recv()
        edges[2 * p + 1].wait_recv()
        for f in (2 * p, 2 * p + 1):
            before = jnp.where(r == 0, 0.0, m.edge_in[1, f].astype(F32))
            after = jnp.where(r == ROWS - 1, 0.0, m.edge_in[0, f].astype(F32))
            m.res[f, 0] = (every[c, f, 0].astype(F32) + (m.conv_own[f, 0] + before)).astype(BF16)
            m.res[f, 1] = (every[c, f, 1].astype(F32) + (m.conv_own[f, 1] + after)).astype(BF16)
            own = same(at.targets[f], at.me)
            links.copy(m.res.at[f], m.res_frame.at[c], at.targets[f], own=own, recv=RES + c)


def attention(links, at, m):
    scale = 1.0 / math.sqrt(384)
    x, z, core, slot, sibling = at.x, at.z, at.core, at.slot, at.sibling
    q, g, k, v, k_t = m.q, m.g, m.k, m.v, m.k_t
    w_qkv = m.w_qkv

    def relay_ring(first, ref, base, i, rows, peers, forward):
        on = []
        for side in range(2):
            first[side].wait_recv()
            came = base + lax.rem(i + 3 - 2 * side, 4)
            part = ref.at[came, pl.ds(rows * side, rows)]
            on.append(links.copy(part, part, peers[2 * side]))
            if forward:
                on.append(links.copy(ref.at[came], ref.at[came], sibling))
        return on

    g_on = relay_ring(at.g_first, g, core * 4, x, 192, at.xs, True)
    gain = gain_columns(m.gain_rows, 1)
    gain = jnp.concatenate([gain, gain], 1)
    for b in range(CH):
        links.arrive(m.res_frame.at[b], RES + b)
    for b in range(CH):
        for h in range(2):
            m.full[pl.ds(96 * b, 96), pl.ds(128 * h, 128)] = m.res_frame[b, h]
    centre = m.full[...].astype(F32)
    inv = lax.rsqrt(jnp.mean(centre * centre, 0, keepdims=True) + EPSILON)
    m.norm[z] = (centre * inv * gain).astype(BF16).astype(F32).T.astype(BF16)
    n_first = [links.copy(m.norm.at[z], m.norm.at[z], to) for to in (at.zs[0], at.zs[2])]
    q[slot] = dot(m.norm[z], w_qkv[:, :384]).T.astype(BF16)
    q_first = [links.copy(q.at[slot], q.at[slot], to) for to in (at.xs[0], at.xs[2], sibling)]

    def project(j):
        k[j] = dot(m.norm[j], w_qkv[:, 384:768]).astype(BF16)
        v[j] = dot(m.norm[j], w_qkv[:, 768:]).astype(BF16)
        k_t[:, pl.ds(pl.multiple_of(256 * j, 256), 256)] = k[j].T

    def tile(b, j):
        s = dot(k[j], q[b]) * scale
        top = jnp.max(s, 0, keepdims=True)
        e = jnp.exp(s - top)
        p = dot(v[j], g[b])
        m.exps[j, b] = e
        m.grad_p[j, b] = p
        m.tops[j, pl.ds(b, 1), :] = top
        m.sums[j, pl.ds(b, 1), :] = jnp.sum(e, 0, keepdims=True)
        m.deltas[j, pl.ds(b, 1), :] = jnp.sum(e * p, 0, keepdims=True)

    def block(dk, dx):
        other = core + dk - 2 * core * dk
        return other * 4 + lax.rem(x + dx, 4)

    def key(dz):
        return lax.rem(z + dz, 4)

    def tiles(count, unroll, which):
        def step(n, carry):
            dk, dx, dz = which(n)
            tile(block(dk, dx), key(dz))
            return carry

        lax.fori_loop(0, count, step, 0, unroll=unroll)

    project(z)
    g_on[1].wait_recv()
    g_on[3].wait_recv()
    far_x = core * 4 + lax.rem(x + 2, 4)
    at.g_first[2].wait_recv()
    q_first[2].wait_recv()
    tiles(2, 2, lambda n: (n, 0, 0))
    for t in range(3):
        for n in range(3):
            piece = jnp.concatenate([m.w[9 * t + 3 * h + n] for h in range(3)], 0)
            m.w_t[t, pl.ds(384 * n, 384), :] = piece.T
    n_on = relay_ring(n_first, m.norm, 0, z, 128, at.zs, False)
    q_on = relay_ring(q_first, q, core * 4, x, 192, at.xs, True)
    g_on[0].wait_recv()
    g_on[2].wait_recv()
    g_last = links.copy(g.at[far_x], g.at[far_x], sibling)
    project(key(1))
    project(key(3))
    tiles(4, 4, lambda n: (n // 2, 0, 1 + 2 * lax.rem(n, 2)))
    q_on[1].wait_recv()
    q_on[3].wait_recv()

    def beside(n):
        dz = n // 4
        return lax.rem(n // 2, 2), 1 + 2 * lax.rem(n, 2), dz + dz // 2

    tiles(12, 4, beside)
    q_on[0].wait_recv()
    q_on[2].wait_recv()
    q_last = links.copy(q.at[far_x], q.at[far_x], sibling)
    n_on[0].wait_recv()
    n_on[1].wait_recv()
    project(key(2))

    def beyond(n):
        dx = n // 2
        return lax.rem(n, 2), dx + dx // 2, 2

    tiles(6, 3, beyond)
    tiles(4, 4, lambda n: (0, 2, n))
    q_last.wait_recv()
    g_last.wait_recv()
    tiles(4, 4, lambda n: (1, 2, n))

    tops = [m.tops[j] for j in range(4)]
    top = functools.reduce(jnp.maximum, tops)
    shift = [jnp.exp(t - top) for t in tops]
    m.stats[0] = top
    m.stats[1] = sum(m.sums[j] * shift[j] for j in range(4))
    m.stats[2] = sum(m.deltas[j] * shift[j] for j in range(4))
    peers = at.xs + at.cross + [sibling]
    shared = [links.copy(m.stats, m.all_stats.at[n], to) for n, to in enumerate(peers)]
    for copy in shared:
        copy.wait_recv()
    parts = [m.stats] + [m.all_stats.at[n] for n in range(7)]
    top = functools.reduce(jnp.maximum, [p[0] for p in parts])
    total = sum(p[1] * jnp.exp(p[0] - top) for p in parts)
    m.delta[...] = sum(p[2] * jnp.exp(p[0] - top) for p in parts) / total
    for j in range(4):
        m.weights[j] = jnp.exp(m.tops[j] - top) / total

    def rows_of(j):
        return pl.ds(pl.multiple_of(256 * j, 256), 256)

    def weigh(b, j):
        prob = m.exps[j, b] * m.weights[j, pl.ds(b, 1), :]
        m.prob[b, rows_of(j), :] = prob.astype(BF16)
        m.grad_s[b, rows_of(j), :] = (prob * (m.grad_p[j, b] - m.delta[pl.ds(b, 1), :])).astype(BF16)

    def key_grad(j):
        for_k = sum(dot_t(m.grad_s[b, rows_of(j), :], q[b]) for b in range(8)) * scale
        for_v = sum(dot_t(m.prob[b, rows_of(j), :], g[b]) for b in range(8))
        return dot_t(w_qkv[:, 384:768], for_k.astype(BF16)) + dot_t(w_qkv[:, 768:], for_v.astype(BF16))

    halves = [pl.ds(0, 192), pl.ds(192, 192)]
    rings = ((at.zs[0], at.zs[2]), (at.xs[0], at.xs[2]))
    by_way, back = {}, []

    def send_far(kind, value):
        m.far[kind] = value.astype(BF16)
        for i in range(2):
            by_way[kind, i] = links.copy(m.far.at[kind, halves[i]], m.via.at[kind, i], rings[kind][i])

    def send_half(kind, i, half, value):
        m.send[kind, i, halves[half]] = value.astype(BF16)
        src, dst = m.send.at[kind, i, halves[half]], m.came.at[kind, i, halves[half]]
        back.append(links.copy(src, dst, rings[kind][i]))

    def send_near(kind, i, value):
        m.nearest[kind, i] = value
        send_half(kind, i, 1 - i, value[192 * (1 - i) : 192 * (2 - i)])

    def send_added(kind):
        for i in range(2):
            by_way[kind, i].wait_recv()
            send_half(kind, i, i, m.nearest[kind, i, halves[i], :] + m.via[kind, i].astype(F32))

    for dz in range(4):
        for dx in range(4):
            weigh(block(1, dx), key(dz))
    sib = []
    for dx in range(4):
        m.sib_out[dx] = (dot(k_t[...], m.grad_s[block(1, dx)]) * scale).astype(BF16)
        sib.append(links.copy(m.sib_out.at[dx], m.sib_in.at[dx], sibling))
    for dz in range(4):
        for dx in range(4):
            weigh(block(0, dx), key(dz))

    def query_grad(dx):
        value = dot(k_t[...], m.grad_s[block(0, dx)]) * scale
        sib[dx].wait_recv()
        return value + m.sib_in[dx].astype(F32)

    send_far(0, key_grad(key(2)))
    send_far(1, query_grad(2))
    send_near(1, 0, query_grad(1))
    send_near(1, 1, query_grad(3))
    send_near(0, 0, key_grad(key(1)))
    send_near(0, 1, key_grad(key(3)))
    send_added(1)
    send_added(0)
    m.own_sum[0] = key_grad(z)
    m.own_sum[1] = query_grad(0)
    for copy in back:
        copy.wait_recv()
    by_key, by_query = [
        m.own_sum[n] + m.came[n, 0].astype(F32) + m.came[n, 1].astype(F32) for n in range(2)
    ]
    back_normed = dot(w_qkv[:, :384], by_query.astype(BF16)) + by_key
    scaled = back_normed.astype(BF16).astype(F32) * gain
    centre = m.full[...].astype(F32)
    inner = jnp.mean(centre * scaled, 0, keepdims=True)
    out = m.cot_full[...].astype(F32) + inv * scaled - centre * (inv * inv * inv * inner)
    for b in range(CH):
        for h in range(2):
            m.grad[b, h] = out[96 * b : 96 * b + 96, 128 * h : 128 * h + 128].astype(BF16)
    row_low, row_high = near_rows(at.row)
    for b in range(CH):
        to = at.sources[b]
        links.copy(m.grad.at[b], m.own.at[at.frame], to, own=same(to, at.me), recv=OWN + at.frame)
    for b in range(CH):
        links.copy(m.grad.at[b, 1], m.prev_g.at[at.frame], (row_high, b), recv=PREV + at.frame)
        links.copy(m.grad.at[b, 0], m.next_g.at[at.frame], (row_low, b), recv=NEXT + at.frame)


def tail(links, at, m):
    r, c, x, y_hi, z = at.r, at.c, at.x, at.y_hi, at.z
    xs, zs, across, chs = at.xs, at.zs, at.across, at.chs
    own, act, w_t, every, inv_in, gain_rows = m.own, m.act, m.w_t, m.every, m.inv_in, m.gain_rows
    rows, lines, weight, part, all_part, inner, all_inner = m.rows, m.lines, m.weight, m.part, m.all_part, m.inner, m.all_inner
    mark, flat, out = m.mark, m.flat, m.out
    ring_x = (x, [lax.rem(x + d, 4) for d in range(1, 4)], xs)
    ring_z = (z, [lax.rem(z + d, 4) for d in range(1, 4)], zs)
    ring_y = (y_hi, [1 - y_hi], [across])
    by_y, by_x, by_z = (ring_y, ring_x, ring_z), (ring_x, ring_z, ring_y), (ring_z, ring_y, ring_x)
    stripes = []
    for n, (base, size, rings) in enumerate(
        (
            (0, 1024, by_y),
            (2048, 1536, by_x),
            (5120, 1536, by_z),
            (1024, 1024, by_y),
            (3584, 1536, by_x),
            (6656, 1536, by_z),
        )
    ):
        steps, at_row = [], base
        for p, (place_on, places, peers) in enumerate(rings):
            size //= len(peers) + 1
            start = at_row
            at_row = at_row + place_on * size
            came, total = getattr(m, "came_%d_%d" % (n, p)), getattr(m, "total_%d_%d" % (n, p))
            steps.append((start, size, places, peers, at_row, came, total))
        stripes.append(steps)

    def rows_at(start, size):
        return pl.ds(pl.multiple_of(start, 16), size)

    def give(steps, p):
        start, size, places, peers, _, came, _ = steps[p]
        sent = []
        for d, peer in enumerate(peers):
            if p == 0:
                src = weight.at[rows_at(start + places[d] * size, size)]
            else:
                src = steps[p - 1][6].at[rows_at(places[d] * size, size)]
            sent.append(links.copy(src, came.at[d], peer))
        return sent

    def take(steps, p, sent):
        start, size, _, peers, mine, came, total = steps[p]
        for copy in sent:
            copy.wait_recv()
        if p == 0:
            value = weight[rows_at(mine, size), :].astype(F32)
        else:
            value = steps[p - 1][6][rows_at(mine - start, size), :].astype(F32)
        for d in range(len(peers)):
            value += came[d].astype(F32)
        total[...] = value.astype(BF16)

    for f in range(4):
        links.arrive(own.at[f], OWN + f)
        links.arrive(m.prev_g.at[f], PREV + f)
        links.arrive(m.next_g.at[f], NEXT + f)
    for f in range(4):
        rows[f, 0] = jnp.where(r == 0, 0.0, m.prev_g[f].astype(F32)).astype(BF16)
        rows[f, 1] = own[f, 0]
        rows[f, 2] = own[f, 1]
        rows[f, 3] = jnp.where(r == ROWS - 1, 0.0, m.next_g[f].astype(F32)).astype(BF16)
        for h in range(4):
            y = rows[f, h].astype(F32)
            at_lanes = pl.ds(128 * h, 128)
            m.moved[f, :, at_lanes] = jnp.concatenate([move(y, -1), y, move(y, 1)], 0).astype(BF16)
    flying = [None] * 6
    for t in range(3):
        for h in range(3):
            acc = jnp.zeros((288, 384), F32)
            for f in range(4):
                source = f + t - 2
                if source < 0:
                    continue
                acc += dot_t(m.moved[f, :, pl.ds(128 * (2 - h), 256)], act[:, pl.ds(256 * source, 256)])
            for lane in range(3):
                at = (3 * (3 * t + h) + lane) * 288
                weight[pl.ds(at, 288), :] = acc[:, 128 * lane : 128 * lane + 128].astype(BF16)
        if t == 2:
            weight[pl.ds(27 * 288, 416), :] = jnp.zeros((416, 128), BF16)
        flying[t] = give(stripes[t], 0)
        flying[t + 3] = give(stripes[t + 3], 0)
    for f in range(4):
        for h in range(3):
            for k in range(2):
                lines[f, pl.ds(96 * h, 96), pl.ds(128 * k, 128)] = rows[f, 2 - h + k]
    gain = gain_columns(gain_rows, 0)
    for f in range(4):
        acc = jnp.zeros((1152, 256), F32)
        for t in range(3):
            source = f + 2 - t
            if source > 3:
                continue
            acc += dot(w_t[t], lines[source])
        for h in range(2):
            y = acc[:, 128 * h : 128 * h + 128]
            total = move(y[:384], -1) + y[384:768] + move(y[768:], 1)
            v = jnp.concatenate([every[b, f, h] for b in range(CH)], 0).astype(F32)
            before = v * inv_in[2 * f + h : 2 * f + h + 1, :] * gain
            sig = sigmoid(before)
            slope = sig * (1.0 + before * (1.0 - sig))
            inner[2 * f + h : 2 * f + h + 1, :] = jnp.sum(v * slope * gain * total, 0, keepdims=True)
            for b in range(CH):
                part[b, f, h] = total[96 * b : 96 * b + 96].astype(BF16)
    parts, kept = [], [None] * 6

    def advance(group, p):
        for n in range(3 * group, 3 * group + 3):
            steps = stripes[n]
            if p < 3:
                take(steps, p, flying[n])
            else:
                for copy in flying[n]:
                    copy.wait_recv()
            if p < 2:
                flying[n] = give(steps, p + 1)
                continue
            _, size, _, peers, mine, _, total = steps[4 - p]
            src = dst = flat.at[rows_at(mine, size)]
            if p == 2:
                src = total
                kept[n] = pltpu.make_async_copy(total, dst, mark.at[n])
                kept[n].start()
            elif p == 3:
                kept[n].wait()
            flying[n] = [links.copy(src, dst, peer) for peer in peers]

    advance(0, 0)
    advance(0, 1)
    advance(1, 0)
    for d in range(3):
        parts.append(links.copy(part.at[chs[d][1]], all_part.at[d], chs[d]))
        parts.append(links.copy(inner, all_inner.at[d], chs[d]))
    for group, p in ((0, 2), (1, 1), (0, 3), (1, 2), (0, 4), (1, 3), (1, 4)):
        advance(group, p)
    for copy in parts:
        copy.wait_recv()
    mean = (inner[...] + all_inner[0] + all_inner[1] + all_inner[2]) / 384.0
    gain = jnp.broadcast_to(gain_rows[c, 0:1, :], (128, 128)).T[:96]
    for f in range(4):
        for h in range(2):
            v = every[c, f, h].astype(F32)
            inv = inv_in[2 * f + h : 2 * f + h + 1, :]
            total = part[c, f, h].astype(F32)
            for d in range(3):
                total += all_part[d, f, h].astype(F32)
            before = v * inv * gain
            sig = sigmoid(before)
            scaled = total * (sig * (1.0 + before * (1.0 - sig))) * gain
            cube = inv * inv * inv * mean[2 * f + h : 2 * f + h + 1, :]
            out[f, h] = (own[f, h].astype(F32) + inv * scaled - v * cube).astype(BF16)
    for sent in flying:
        for copy in sent:
            copy.wait_recv()


def whole(links, m):
    at = Place()
    front(links, at, m)
    attention(links, at, m)
    tail(links, at, m)
    links.finish()


def widen_kernel(scale, flat, out, near, wide, into, back):
    come = [
        pltpu.make_async_copy(flat.at[pl.ds(864 * k, 864)], near.at[k], into.at[k]) for k in range(9)
    ]
    go = [
        pltpu.make_async_copy(wide.at[k], out.at[pl.ds(288 * k, 288)], back.at[k]) for k in range(9)
    ]
    for copy in come:
        copy.start()
    for k in range(9):
        come[k].wait()
        for lane in range(3):
            piece = near[k, pl.ds(288 * lane, 288), :].astype(F32) * scale
            wide[k, :, pl.ds(128 * lane, 128)] = piece
        go[k].start()
    for copy in go:
        copy.wait()


def on_device(features, gain_in, w_conv, gain_attn, w_qkv, w_out, cotangent):
    near, far = pltpu.VMEM, pl.ANY
    held = {
        "feat": (features, far),
        "cot": (cotangent, far),
        "w_far": (w_conv, far),
        "gain_in": (gain_in.reshape(1, 96), near),
        "gain_attn": (gain_attn.reshape(1, 96), near),
        "w_qkv": (w_qkv, near),
        "w_out": (w_out, near),
    }
    made = {"out": ((4, 2, 96, 128), BF16, near), "flat": ((8192, 128), BF16, far)}
    b16 = {
        "every": (4, 4, 2, 96, 128),
        "w": (27, 96, 384),
        "act": (384, 1024),
        "edge_out": (2, 4, 96, 128),
        "edge_in": (2, 4, 96, 128),
        "moved": (4, 288, 512),
        "res": (4, 2, 96, 128),
        "cot_frame": (4, 2, 96, 128),
        "res_frame": (4, 2, 96, 128),
        "full": (384, 256),
        "cot_full": (384, 256),
        "norm": (4, 256, 384),
        "q": (8, 384, 256),
        "g": (8, 384, 256),
        "k": (4, 256, 384),
        "v": (4, 256, 384),
        "k_t": (384, 1024),
        "prob": (8, 1024, 256),
        "grad_s": (8, 1024, 256),
        "far": (2, 384, 256),
        "via": (2, 2, 192, 256),
        "send": (2, 2, 384, 256),
        "came": (2, 2, 384, 256),
        "sib_out": (4, 384, 256),
        "sib_in": (4, 384, 256),
        "grad": (4, 2, 96, 128),
        "own": (4, 2, 96, 128),
        "prev_g": (4, 96, 128),
        "next_g": (4, 96, 128),
        "w_t": (3, 1152, 288),
        "rows": (4, 4, 96, 128),
        "lines": (4, 288, 256),
        "weight": (8192, 128),
        "part": (4, 4, 2, 96, 128),
        "all_part": (3, 4, 2, 96, 128),
    }
    for n, (size, counts) in enumerate(2 * ((1024, (2, 4, 4)), (1536, (4, 4, 2)), (1536, (4, 2, 4)))):
        for p, count in enumerate(counts):
            size //= count
            b16["came_%d_%d" % (n, p)] = (count - 1, size, 128)
            b16["total_%d_%d" % (n, p)] = (size, 128)
    f32 = {
        "inv_in": (8, 128),
        "conv_own": (4, 2, 96, 128),
        "gain_rows": (4, 8, 128),
        "exps": (4, 8, 256, 256),
        "grad_p": (4, 8, 256, 256),
        "tops": (4, 8, 256),
        "sums": (4, 8, 256),
        "deltas": (4, 8, 256),
        "stats": (3, 8, 256),
        "all_stats": (7, 3, 8, 256),
        "weights": (4, 8, 256),
        "delta": (8, 256),
        "nearest": (2, 2, 384, 256),
        "own_sum": (2, 384, 256),
        "inner": (8, 128),
        "all_inner": (3, 8, 128),
    }
    scratch = {n: pltpu.VMEM(s, BF16) for n, s in b16.items()}
    scratch |= {n: pltpu.VMEM(s, F32) for n, s in f32.items()}
    scratch["mark"] = pltpu.SemaphoreType.DMA((6,))
    out, flat = fused(0, whole, held, made, scratch, (SENDS, NEXT + 4))
    cell_scale = 1.0 / math.sqrt(32768)
    grad_weights = pl.pallas_call(
        functools.partial(widen_kernel, cell_scale),
        out_shape=jax.ShapeDtypeStruct((2592, 384), F32),
        in_specs=[pl.BlockSpec(memory_space=pl.ANY)],
        out_specs=pl.BlockSpec(memory_space=pl.ANY),
        scratch_shapes=[
            pltpu.VMEM((9, 864, 128), BF16),
            pltpu.VMEM((9, 288, 384), F32),
            pltpu.SemaphoreType.DMA((9,)),
            pltpu.SemaphoreType.DMA((9,)),
        ],
        compiler_params=pltpu.CompilerParams(vmem_limit_bytes=VMEM_BYTES),
        name="widen",
    )(flat)
    return out, grad_weights.reshape(27, 96, 384)


def solution(mesh):
    return jax.shard_map(
        on_device,
        mesh=mesh,
        in_specs=(
            P(None, "row", "ch", None),
            P("ch"),
            P(None, "ch", None),
            P("ch"),
            P(),
            P(),
            P(None, "row", "ch", None),
        ),
        out_specs=(P(None, "row", "ch", None), P(None, "ch", None)),
        check_vma=False,
    )
```

```python
import functools
import math
import types

import jax
import jax.numpy as jnp
from jax import lax
from jax.experimental import pallas as pl
from jax.experimental.pallas import tpu as pltpu
from jax.sharding import PartitionSpec as P

EPSILON = 1e-06
MESH = pl.DeviceIdType.MESH
F32 = jnp.float32
BF16 = jnp.bfloat16
ROWS = 32
SENDS = 128
COT, RES, OWN, PREV, NEXT = range(SENDS, SENDS + 20, 4)
CH = 4
VMEM_BYTES = 60 * 1024 * 1024


def coords():
    return lax.axis_index("row"), lax.axis_index("ch")


def place(r, c):
    return lax.rem(r, 4), lax.rem(r // 4, 2), r // 8, c // 2, lax.rem(c, 2)


def device(x, y_hi, z, y_lo, core):
    return z * 8 + y_hi * 4 + x, y_lo * 2 + core


def owner(f, row):
    x, y_hi, z, _, _ = place(row, 0)
    return device(x, f // 2, z, f % 2, y_hi)


class Links:
    def __init__(self, send, recv):
        self.send, self.recv, self.sent, self.at = send, recv, [], 0

    def greet(self, peers, count):
        barrier = pltpu.get_barrier_semaphore()
        for peer in peers:
            pl.semaphore_signal(barrier, inc=1, device_id=peer, device_id_type=MESH)
        pl.semaphore_wait(barrier, count)

    def copy(self, src, dst, to, own=None, recv=None):
        k = self.at
        self.at += 1
        mark = self.recv.at[k if recv is None else recv]
        far = pltpu.make_async_remote_copy(
            src_ref=src,
            dst_ref=dst,
            send_sem=self.send.at[k],
            recv_sem=mark,
            device_id=to,
            device_id_type=MESH,
        )
        if own is None:
            far.start()
        else:
            pl.when(jnp.logical_not(own))(far.start)
            pl.when(own)(pltpu.make_async_copy(src, dst, mark).start)
        self.sent.append((far, own))
        return far

    def arrive(self, dst, k):
        pltpu.make_async_copy(dst, dst, self.recv.at[k]).wait()

    def finish(self):
        for far, own in self.sent:
            if own is None:
                far.wait_send()
            else:
                pl.when(jnp.logical_not(own))(far.wait_send)


def fused(cid, body, held, made, scratch, count):
    names = [*held, *made, *scratch]

    def kernel(*refs):
        body(Links(*refs[-2:]), types.SimpleNamespace(**dict(zip(names, refs))))

    return pl.pallas_call(
        kernel,
        out_shape=[jax.ShapeDtypeStruct(s, t) for s, t, _ in made.values()],
        in_specs=[pl.BlockSpec(memory_space=m) for _, m in held.values()],
        out_specs=[pl.BlockSpec(memory_space=m) for _, _, m in made.values()],
        scratch_shapes=[*scratch.values()] + [pltpu.SemaphoreType.DMA((n,)) for n in count],
        compiler_params=pltpu.CompilerParams(
            collective_id=cid, has_side_effects=True, vmem_limit_bytes=VMEM_BYTES
        ),
        name="fused_%d" % cid,
    )(*[array for array, _ in held.values()])


def dot(a, b):
    return lax.dot_general(a, b, (((1,), (0,)), ((), ())), preferred_element_type=F32)


def dot_t(a, b):
    return lax.dot_general(a, b, (((1,), (1,)), ((), ())), preferred_element_type=F32)


def move(block, by):
    lanes = block.shape[1]
    at = lax.broadcasted_iota(jnp.int32, block.shape, 1)
    if by > 0:
        return jnp.where(at == 0, 0.0, pltpu.roll(block, 1, axis=1))
    return jnp.where(at == lanes - 1, 0.0, pltpu.roll(block, lanes - 1, axis=1))


def ch_peers(r, c):
    return [(r, lax.rem(c + d, CH)) for d in range(1, CH)]


def near_rows(r):
    return lax.rem(r + ROWS - 1, ROWS), lax.rem(r + 1, ROWS)


def same(a, b):
    return jnp.logical_and(a[0] == b[0], a[1] == b[1])


def greet_frames(me, sources, targets):
    barrier = pltpu.get_barrier_semaphore()
    for peer in sources:
        def tell(peer=peer):
            pl.semaphore_signal(barrier, inc=1, device_id=peer, device_id_type=MESH)

        pl.when(jnp.logical_not(same(peer, me)))(tell)
    _, y_hi, _, _, core = place(*me)
    pl.semaphore_wait(barrier, len(targets) - 2 + 2 * (core - y_hi) * (core - y_hi))


def sigmoid(v):
    return 1.0 / (1.0 + jnp.exp(-v))


def gain_columns(rows, which):
    blocks = [jnp.broadcast_to(rows[b, which : which + 1, :], (128, 128)).T[:96] for b in range(CH)]
    return jnp.concatenate(blocks, 0)


class Place:
    def __init__(self):
        r, c = self.r, self.c = self.me = coords()
        x, y_hi, z, y_lo, core = self.x, self.y_hi, self.z, self.y_lo, self.core = place(r, c)
        self.slot = core * 4 + x
        self.frame = y_hi * 2 + y_lo
        self.low, self.high = near_rows(r)
        self.c_near = (1 - y_lo) * 2 + core
        self.sibling = (r, y_lo * 2 + 1 - core)
        self.near = (r, self.c_near)
        self.chs = ch_peers(r, c)
        self.xs = [device(lax.rem(x + d, 4), y_hi, z, y_lo, core) for d in range(1, 4)]
        self.cross = [device(lax.rem(x + d, 4), y_hi, z, y_lo, 1 - core) for d in range(1, 4)]
        self.zs = [device(x, y_hi, lax.rem(z + d, 4), y_lo, core) for d in range(1, 4)]
        self.across = device(x, 1 - y_hi, z, y_lo, core)
        self.targets = [owner(f, r) for f in range(4)]
        self.row = z * 8 + core * 4 + x
        self.sources = [(self.row, b) for b in range(CH)]

    def greet(self):
        at = self
        alike = at.chs + at.xs + at.cross + at.zs + [at.across, (at.low, at.c), (at.high, at.c)]
        there = [(i, b) for i in near_rows(at.row) for b in range(CH)]
        whose = [owner(f, i) for i in (at.low, at.high) for f in range(4)]
        greet_frames(at.me, at.targets + at.sources + whose + alike, at.targets + at.sources + there + alike)


def front(links, at, m):
    r, c, near, sibling = at.r, at.c, at.near, at.sibling
    every, act = m.every, m.act
    here = pltpu.make_async_copy(m.feat, every.at[c], m.mark.at[0])
    here.start()
    weights = pltpu.make_async_copy(m.w_far, m.w, m.mark.at[1])
    weights.start()
    projections = [
        pltpu.make_async_copy(m.w_out_far, m.w_out, m.mark.at[2]),
        pltpu.make_async_copy(m.w_qkv_far, m.w_qkv, m.mark.at[3]),
    ]
    for copy in projections:
        copy.start()
    m.gain_rows[c] = jnp.zeros((8, 128), F32)
    pad = jnp.zeros((1, 32), F32)
    m.gain_rows[c, 0:1, :] = jnp.concatenate([m.gain_in[...].astype(F32), pad], 1)
    m.gain_rows[c, 1:2, :] = jnp.concatenate([m.gain_attn[...].astype(F32), pad], 1)
    at.greet()
    pairs = [pl.ds(2 * p, 2) for p in range(2)]
    gains = [links.copy(m.gain_rows.at[c], m.gain_rows.at[c], to) for to in at.chs]
    to_near = [links.copy(m.feat.at[two], every.at[c, two], near) for two in pairs]
    to_sib = links.copy(m.feat, every.at[c], sibling)
    for copy in gains:
        copy.wait_recv()
    gain = gain_columns(m.gain_rows, 0)
    passed = []
    for p, two in enumerate(pairs):
        to_near[p].wait_recv()
        part = every.at[at.c_near, two]
        passed.append(links.copy(part, part, sibling))
    for f in range(4):
        own = same(at.targets[f], at.me)
        links.copy(m.cot.at[f], m.cot_frame.at[c], at.targets[f], own=own, recv=COT + c)

    def activate(n):
        v = jnp.concatenate([every[b, n // 2, lax.rem(n, 2)] for b in range(CH)], 0).astype(F32)
        inv = lax.rsqrt(jnp.mean(v * v, 0, keepdims=True) + EPSILON)
        before = v * inv * gain
        m.inv_in[pl.ds(n, 1), :] = inv
        act[:, pl.ds(pl.multiple_of(128 * n, 128), 128)] = (before * sigmoid(before)).astype(BF16)

    here.wait()
    to_sib.wait_recv()
    weights.wait()
    edges = []
    for p, two in enumerate(pairs):
        passed[p].wait_recv()

        def step(n, carry, p=p):
            activate(4 * p + n)
            return carry

        lax.fori_loop(0, 4, step, 0, unroll=2)
        for f in (2 * p, 2 * p + 1):
            by_tap = []
            for h in range(3):
                acc = jnp.zeros((288, 256), F32)
                for t in range(3):
                    source = f + t - 2
                    if source >= 0:
                        taps = m.w[pl.ds(9 * t + 3 * h, 3)].reshape(288, 384)
                        acc += dot(taps, act[:, pl.ds(256 * source, 256)])
                by_tap.append((acc[:, :128], acc[:, 128:]))
            lines = (
                by_tap[2][0],
                by_tap[2][1] + by_tap[1][0],
                by_tap[1][1] + by_tap[0][0],
                by_tap[0][1],
            )
            lines = [move(y[:96], 1) + y[96:192] + move(y[192:], -1) for y in lines]
            m.edge_out[0, f] = lines[0].astype(BF16)
            m.edge_out[1, f] = lines[3].astype(BF16)
            m.conv_own[f, 0] = lines[1]
            m.conv_own[f, 1] = lines[2]
        edges.append(links.copy(m.edge_out.at[0, two], m.edge_in.at[0, two], (at.low, c)))
        edges.append(links.copy(m.edge_out.at[1, two], m.edge_in.at[1, two], (at.high, c)))
    for b in range(CH):
        links.arrive(m.cot_frame.at[b], COT + b)
    for b in range(CH):
        for h in range(2):
            m.cot_full[pl.ds(96 * b, 96), pl.ds(128 * h, 128)] = m.cot_frame[b, h]
    for copy in projections:
        copy.wait()
    m.g[at.slot] = dot(m.w_out[...], m.cot_full[...]).astype(BF16)
    at.g_first = [links.copy(m.g.at[at.slot], m.g.at[at.slot], to) for to in (at.xs[0], at.xs[2], sibling)]
    for p in range(2):
        edges[2 * p].wait_recv()
        edges[2 * p + 1].wait_recv()
        for f in (2 * p, 2 * p + 1):
            before = jnp.where(r == 0, 0.0, m.edge_in[1, f].astype(F32))
            after = jnp.where(r == ROWS - 1, 0.0, m.edge_in[0, f].astype(F32))
            m.res[f, 0] = (every[c, f, 0].astype(F32) + (m.conv_own[f, 0] + before)).astype(BF16)
            m.res[f, 1] = (every[c, f, 1].astype(F32) + (m.conv_own[f, 1] + after)).astype(BF16)
            own = same(at.targets[f], at.me)
            links.copy(m.res.at[f], m.res_frame.at[c], at.targets[f], own=own, recv=RES + c)


def attention(links, at, m):
    scale = 1.0 / math.sqrt(384)
    x, z, core, slot, sibling = at.x, at.z, at.core, at.slot, at.sibling
    q, g, k, v, k_t = m.q, m.g, m.k, m.v, m.k_t
    w_qkv = m.w_qkv

    def relay_ring(first, ref, base, i, rows, peers, forward):
        on = []
        for side in range(2):
            first[side].wait_recv()
            came = base + lax.rem(i + 3 - 2 * side, 4)
            part = ref.at[came, pl.ds(rows * side, rows)]
            on.append(links.copy(part, part, peers[2 * side]))
            if forward:
                on.append(links.copy(ref.at[came], ref.at[came], sibling))
        return on

    g_on = relay_ring(at.g_first, g, core * 4, x, 192, at.xs, True)
    gain = gain_columns(m.gain_rows, 1)
    gain = jnp.concatenate([gain, gain], 1)
    for b in range(CH):
        links.arrive(m.res_frame.at[b], RES + b)
    for b in range(CH):
        for h in range(2):
            m.full[pl.ds(96 * b, 96), pl.ds(128 * h, 128)] = m.res_frame[b, h]
    centre = m.full[...].astype(F32)
    inv = lax.rsqrt(jnp.mean(centre * centre, 0, keepdims=True) + EPSILON)
    m.norm[z] = (centre * inv * gain).astype(BF16).astype(F32).T.astype(BF16)
    n_first = [links.copy(m.norm.at[z], m.norm.at[z], to) for to in (at.zs[0], at.zs[2])]
    q[slot] = dot(m.norm[z], w_qkv[:, :384]).T.astype(BF16)
    q_first = [links.copy(q.at[slot], q.at[slot], to) for to in (at.xs[0], at.xs[2], sibling)]

    def project(j):
        k[j] = dot(m.norm[j], w_qkv[:, 384:768]).astype(BF16)
        v[j] = dot(m.norm[j], w_qkv[:, 768:]).astype(BF16)
        k_t[:, pl.ds(pl.multiple_of(256 * j, 256), 256)] = k[j].T

    def tile(b, j):
        s = dot(k[j], q[b]) * scale
        top = jnp.max(s, 0, keepdims=True)
        e = jnp.exp(s - top)
        p = dot(v[j], g[b])
        m.exps[j, b] = e
        m.grad_p[j, b] = p
        m.tops[j, pl.ds(b, 1), :] = top
        m.sums[j, pl.ds(b, 1), :] = jnp.sum(e, 0, keepdims=True)
        m.deltas[j, pl.ds(b, 1), :] = jnp.sum(e * p, 0, keepdims=True)

    def block(dk, dx):
        other = core + dk - 2 * core * dk
        return other * 4 + lax.rem(x + dx, 4)

    def key(dz):
        return lax.rem(z + dz, 4)

    def tiles(count, unroll, which):
        def step(n, carry):
            dk, dx, dz = which(n)
            tile(block(dk, dx), key(dz))
            return carry

        lax.fori_loop(0, count, step, 0, unroll=unroll)

    project(z)
    g_on[1].wait_recv()
    g_on[3].wait_recv()
    far_x = core * 4 + lax.rem(x + 2, 4)
    at.g_first[2].wait_recv()
    q_first[2].wait_recv()
    tiles(2, 2, lambda n: (n, 0, 0))
    for t in range(3):
        for n in range(3):
            piece = jnp.concatenate([m.w[9 * t + 3 * h + n] for h in range(3)], 0)
            m.w_t[t, pl.ds(384 * n, 384), :] = piece.T
    n_on = relay_ring(n_first, m.norm, 0, z, 128, at.zs, False)
    q_on = relay_ring(q_first, q, core * 4, x, 192, at.xs, True)
    g_on[0].wait_recv()
    g_on[2].wait_recv()
    g_last = links.copy(g.at[far_x], g.at[far_x], sibling)
    project(key(1))
    project(key(3))
    tiles(4, 4, lambda n: (n // 2, 0, 1 + 2 * lax.rem(n, 2)))
    q_on[1].wait_recv()
    q_on[3].wait_recv()

    def beside(n):
        dz = n // 4
        return lax.rem(n // 2, 2), 1 + 2 * lax.rem(n, 2), dz + dz // 2

    tiles(12, 4, beside)
    q_on[0].wait_recv()
    q_on[2].wait_recv()
    q_last = links.copy(q.at[far_x], q.at[far_x], sibling)
    n_on[0].wait_recv()
    n_on[1].wait_recv()
    project(key(2))

    def beyond(n):
        dx = n // 2
        return lax.rem(n, 2), dx + dx // 2, 2

    tiles(6, 3, beyond)
    tiles(4, 4, lambda n: (0, 2, n))
    q_last.wait_recv()
    g_last.wait_recv()
    tiles(4, 4, lambda n: (1, 2, n))

    tops = [m.tops[j] for j in range(4)]
    top = functools.reduce(jnp.maximum, tops)
    shift = [jnp.exp(t - top) for t in tops]
    m.stats[0] = top
    m.stats[1] = sum(m.sums[j] * shift[j] for j in range(4))
    m.stats[2] = sum(m.deltas[j] * shift[j] for j in range(4))
    peers = at.xs + at.cross + [sibling]
    shared = [links.copy(m.stats, m.all_stats.at[n], to) for n, to in enumerate(peers)]
    for copy in shared:
        copy.wait_recv()
    parts = [m.stats] + [m.all_stats.at[n] for n in range(7)]
    top = functools.reduce(jnp.maximum, [p[0] for p in parts])
    total = sum(p[1] * jnp.exp(p[0] - top) for p in parts)
    m.delta[...] = sum(p[2] * jnp.exp(p[0] - top) for p in parts) / total
    for j in range(4):
        m.weights[j] = jnp.exp(m.tops[j] - top) / total

    def rows_of(j):
        return pl.ds(pl.multiple_of(256 * j, 256), 256)

    def weigh(b, j):
        prob = m.exps[j, b] * m.weights[j, pl.ds(b, 1), :]
        m.prob[b, rows_of(j), :] = prob.astype(BF16)
        m.grad_s[b, rows_of(j), :] = (prob * (m.grad_p[j, b] - m.delta[pl.ds(b, 1), :])).astype(BF16)

    def key_grad(j):
        for_k = sum(dot_t(m.grad_s[b, rows_of(j), :], q[b]) for b in range(8)) * scale
        for_v = sum(dot_t(m.prob[b, rows_of(j), :], g[b]) for b in range(8))
        return dot_t(w_qkv[:, 384:768], for_k.astype(BF16)) + dot_t(w_qkv[:, 768:], for_v.astype(BF16))

    halves = [pl.ds(0, 192), pl.ds(192, 192)]
    rings = ((at.zs[0], at.zs[2]), (at.xs[0], at.xs[2]))
    by_way, back = {}, []

    def send_far(kind, value):
        m.far[kind] = value.astype(BF16)
        for i in range(2):
            by_way[kind, i] = links.copy(m.far.at[kind, halves[i]], m.via.at[kind, i], rings[kind][i])

    def send_half(kind, i, half, value):
        m.send[kind, i, halves[half]] = value.astype(BF16)
        src, dst = m.send.at[kind, i, halves[half]], m.came.at[kind, i, halves[half]]
        back.append(links.copy(src, dst, rings[kind][i]))

    def send_near(kind, i, value):
        m.nearest[kind, i] = value
        send_half(kind, i, 1 - i, value[192 * (1 - i) : 192 * (2 - i)])

    def send_added(kind):
        for i in range(2):
            by_way[kind, i].wait_recv()
            send_half(kind, i, i, m.nearest[kind, i, halves[i], :] + m.via[kind, i].astype(F32))

    def weigh_all(dk):
        def step(n, carry):
            weigh(block(dk, lax.rem(n, 4)), key(n // 4))
            return carry

        lax.fori_loop(0, 16, step, 0, unroll=4)

    def query_grads(dk, put):
        def step(dx, carry):
            put(dx, dot(k_t[...], m.grad_s[block(dk, dx)]) * scale)
            return carry

        lax.fori_loop(0, 4, step, 0)

    def for_sibling(dx, value):
        m.sib_out[dx] = value.astype(BF16)

    def for_own(dx, value):
        m.own_q[dx] = value

    weigh_all(1)
    query_grads(1, for_sibling)
    sib = links.copy(m.sib_out, m.sib_in, sibling)
    weigh_all(0)
    send_far(0, key_grad(key(2)))
    query_grads(0, for_own)
    sib.wait_recv()

    def query_grad(dx):
        return m.own_q[dx] + m.sib_in[dx].astype(F32)

    send_far(1, query_grad(2))
    send_near(1, 0, query_grad(1))
    send_near(1, 1, query_grad(3))

    def near_keys(i, carry):
        m.nearest[0, i] = key_grad(key(1 + 2 * i))
        return carry

    lax.fori_loop(0, 2, near_keys, 0)
    for i in range(2):
        send_half(0, i, 1 - i, m.nearest[0, i, halves[1 - i], :])
    send_added(0)
    send_added(1)
    m.own_sum[0] = key_grad(z)
    m.own_sum[1] = query_grad(0)
    for copy in back:
        copy.wait_recv()
    by_key, by_query = [
        m.own_sum[n] + m.came[n, 0].astype(F32) + m.came[n, 1].astype(F32) for n in range(2)
    ]
    back_normed = dot(w_qkv[:, :384], by_query.astype(BF16)) + by_key
    scaled = back_normed.astype(BF16).astype(F32) * gain
    centre = m.full[...].astype(F32)
    inner = jnp.mean(centre * scaled, 0, keepdims=True)
    out = m.cot_full[...].astype(F32) + inv * scaled - centre * (inv * inv * inv * inner)
    for b in range(CH):
        for h in range(2):
            m.grad[b, h] = out[96 * b : 96 * b + 96, 128 * h : 128 * h + 128].astype(BF16)
    row_low, row_high = near_rows(at.row)
    for b in range(CH):
        to = at.sources[b]
        links.copy(m.grad.at[b], m.own.at[at.frame], to, own=same(to, at.me), recv=OWN + at.frame)
    for b in range(CH):
        links.copy(m.grad.at[b, 1], m.prev_g.at[at.frame], (row_high, b), recv=PREV + at.frame)
        links.copy(m.grad.at[b, 0], m.next_g.at[at.frame], (row_low, b), recv=NEXT + at.frame)


def tail(links, at, m):
    r, c, x, y_hi, z = at.r, at.c, at.x, at.y_hi, at.z
    xs, zs, across, chs = at.xs, at.zs, at.across, at.chs
    own, act, w_t, every, inv_in, gain_rows = m.own, m.act, m.w_t, m.every, m.inv_in, m.gain_rows
    rows, lines, weight, part, all_part, inner, all_inner = m.rows, m.lines, m.weight, m.part, m.all_part, m.inner, m.all_inner
    mark, flat, out = m.mark, m.flat, m.out
    ring_x = (x, [lax.rem(x + d, 4) for d in range(1, 4)], xs)
    ring_z = (z, [lax.rem(z + d, 4) for d in range(1, 4)], zs)
    ring_y = (y_hi, [1 - y_hi], [across])
    stripes = []
    for n, (base, size, rings) in enumerate(
        (
            (0, 2048, (ring_y, ring_x, ring_z)),
            (2048, 3072, (ring_x, ring_z, ring_y)),
            (5120, 3072, (ring_z, ring_y, ring_x)),
        )
    ):
        steps, at_row = [], base
        for p, (place_on, places, peers) in enumerate(rings):
            size //= len(peers) + 1
            start = at_row
            at_row = at_row + place_on * size
            came, total = getattr(m, "came_%d_%d" % (n, p)), getattr(m, "total_%d_%d" % (n, p))
            steps.append((start, size, places, peers, at_row, came, total))
        stripes.append(steps)

    def rows_at(start, size):
        return pl.ds(pl.multiple_of(start, 16), size)

    def give(steps, p):
        start, size, places, peers, _, came, _ = steps[p]
        sent = []
        for d, peer in enumerate(peers):
            if p == 0:
                src = weight.at[rows_at(start + places[d] * size, size)]
            else:
                src = steps[p - 1][6].at[rows_at(places[d] * size, size)]
            sent.append(links.copy(src, came.at[d], peer))
        return sent

    def take(steps, p, sent):
        start, size, _, peers, mine, came, total = steps[p]
        for copy in sent:
            copy.wait_recv()
        if p == 0:
            value = weight[rows_at(mine, size), :].astype(F32)
        else:
            value = steps[p - 1][6][rows_at(mine - start, size), :].astype(F32)
        for d in range(len(peers)):
            value += came[d].astype(F32)
        total[...] = value.astype(BF16)

    for f in range(4):
        links.arrive(own.at[f], OWN + f)
        links.arrive(m.prev_g.at[f], PREV + f)
        links.arrive(m.next_g.at[f], NEXT + f)
    for f in range(4):
        rows[f, 0] = jnp.where(r == 0, 0.0, m.prev_g[f].astype(F32)).astype(BF16)
        rows[f, 1] = own[f, 0]
        rows[f, 2] = own[f, 1]
        rows[f, 3] = jnp.where(r == ROWS - 1, 0.0, m.next_g[f].astype(F32)).astype(BF16)
        for h in range(4):
            y = rows[f, h].astype(F32)
            at_lanes = pl.ds(128 * h, 128)
            m.moved[f, :, at_lanes] = jnp.concatenate([move(y, -1), y, move(y, 1)], 0).astype(BF16)
    first = []
    for t in range(3):
        for h in range(3):
            acc = jnp.zeros((288, 384), F32)
            for f in range(4):
                source = f + t - 2
                if source < 0:
                    continue
                acc += dot_t(m.moved[f, :, pl.ds(128 * (2 - h), 256)], act[:, pl.ds(256 * source, 256)])
            for lane in range(3):
                at = (3 * (3 * t + h) + lane) * 288
                weight[pl.ds(at, 288), :] = acc[:, 128 * lane : 128 * lane + 128].astype(BF16)
        if t == 2:
            weight[pl.ds(27 * 288, 416), :] = jnp.zeros((416, 128), BF16)
        first.append(give(stripes[t], 0))
    for f in range(4):
        for h in range(3):
            for k in range(2):
                lines[f, pl.ds(96 * h, 96), pl.ds(128 * k, 128)] = rows[f, 2 - h + k]
    gain = gain_columns(gain_rows, 0)
    for f in range(4):
        acc = jnp.zeros((1152, 256), F32)
        for t in range(3):
            source = f + 2 - t
            if source > 3:
                continue
            acc += dot(w_t[t], lines[source])
        for h in range(2):
            y = acc[:, 128 * h : 128 * h + 128]
            total = move(y[:384], -1) + y[384:768] + move(y[768:], 1)
            v = jnp.concatenate([every[b, f, h] for b in range(CH)], 0).astype(F32)
            before = v * inv_in[2 * f + h : 2 * f + h + 1, :] * gain
            sig = sigmoid(before)
            slope = sig * (1.0 + before * (1.0 - sig))
            inner[2 * f + h : 2 * f + h + 1, :] = jnp.sum(v * slope * gain * total, 0, keepdims=True)
            for b in range(CH):
                part[b, f, h] = total[96 * b : 96 * b + 96].astype(BF16)
    second, third, parts = [], [], []
    for n, steps in enumerate(stripes):
        take(steps, 0, first[n])
        second.append(give(steps, 1))
    for d in range(3):
        parts.append(links.copy(part.at[chs[d][1]], all_part.at[d], chs[d]))
        parts.append(links.copy(inner, all_inner.at[d], chs[d]))
    for n, steps in enumerate(stripes):
        take(steps, 1, second[n])
        third.append(give(steps, 2))
    spread, kept = [], []
    for n, steps in enumerate(stripes):
        take(steps, 2, third[n])
        _, size, _, peers, mine, _, total = steps[2]
        at_flat = flat.at[rows_at(mine, size)]
        kept.append(pltpu.make_async_copy(total, at_flat, mark.at[n]))
        kept[n].start()
        spread.append([links.copy(total, at_flat, peer) for peer in peers])
    for p in (1, 0):
        for n, steps in enumerate(stripes):
            if p == 1:
                kept[n].wait()
            for copy in spread[n]:
                copy.wait_recv()
            _, size, _, peers, mine, _, _ = steps[p]
            at_flat = flat.at[rows_at(mine, size)]
            spread[n] = [links.copy(at_flat, at_flat, peer) for peer in peers]
    for copy in parts:
        copy.wait_recv()
    mean = (inner[...] + all_inner[0] + all_inner[1] + all_inner[2]) / 384.0
    gain = jnp.broadcast_to(gain_rows[c, 0:1, :], (128, 128)).T[:96]
    for f in range(4):
        for h in range(2):
            v = every[c, f, h].astype(F32)
            inv = inv_in[2 * f + h : 2 * f + h + 1, :]
            total = part[c, f, h].astype(F32)
            for d in range(3):
                total += all_part[d, f, h].astype(F32)
            before = v * inv * gain
            sig = sigmoid(before)
            scaled = total * (sig * (1.0 + before * (1.0 - sig))) * gain
            cube = inv * inv * inv * mean[2 * f + h : 2 * f + h + 1, :]
            out[f, h] = (own[f, h].astype(F32) + inv * scaled - v * cube).astype(BF16)
    for copy in spread[0] + spread[1] + spread[2]:
        copy.wait_recv()


def whole(links, m):
    at = Place()
    front(links, at, m)
    attention(links, at, m)
    tail(links, at, m)
    links.finish()


def widen_kernel(scale, flat, grad, out, grad_out, near, wide, into, back):
    come = [
        pltpu.make_async_copy(flat.at[pl.ds(864 * k, 864)], near.at[k], into.at[k]) for k in range(9)
    ]
    go = [
        pltpu.make_async_copy(wide.at[k], out.at[pl.ds(288 * k, 288)], back.at[k]) for k in range(9)
    ]
    passing = pltpu.make_async_copy(grad, grad_out, into.at[9])
    for copy in come:
        copy.start()
    passing.start()
    for k in range(9):
        come[k].wait()
        for lane in range(3):
            piece = near[k, pl.ds(288 * lane, 288), :].astype(F32) * scale
            wide[k, :, pl.ds(128 * lane, 128)] = piece
        go[k].start()
    for copy in go:
        copy.wait()
    passing.wait()


def on_device(features, gain_in, w_conv, gain_attn, w_qkv, w_out, cotangent):
    near, far = pltpu.VMEM, pl.ANY
    held = {
        "feat": (features, far),
        "cot": (cotangent, far),
        "w_far": (w_conv, far),
        "gain_in": (gain_in.reshape(1, 96), near),
        "gain_attn": (gain_attn.reshape(1, 96), near),
        "w_qkv_far": (w_qkv, far),
        "w_out_far": (w_out, far),
    }
    made = {"out": ((4, 2, 96, 128), BF16, near), "flat": ((8192, 128), BF16, far)}
    b16 = {
        "every": (4, 4, 2, 96, 128),
        "w": (27, 96, 384),
        "w_qkv": (384, 1152),
        "w_out": (384, 384),
        "act": (384, 1024),
        "edge_out": (2, 4, 96, 128),
        "edge_in": (2, 4, 96, 128),
        "moved": (4, 288, 512),
        "res": (4, 2, 96, 128),
        "cot_frame": (4, 2, 96, 128),
        "res_frame": (4, 2, 96, 128),
        "full": (384, 256),
        "cot_full": (384, 256),
        "norm": (4, 256, 384),
        "q": (8, 384, 256),
        "g": (8, 384, 256),
        "k": (4, 256, 384),
        "v": (4, 256, 384),
        "k_t": (384, 1024),
        "prob": (8, 1024, 256),
        "grad_s": (8, 1024, 256),
        "far": (2, 384, 256),
        "via": (2, 2, 192, 256),
        "send": (2, 2, 384, 256),
        "came": (2, 2, 384, 256),
        "sib_out": (4, 384, 256),
        "sib_in": (4, 384, 256),
        "grad": (4, 2, 96, 128),
        "own": (4, 2, 96, 128),
        "prev_g": (4, 96, 128),
        "next_g": (4, 96, 128),
        "w_t": (3, 1152, 288),
        "rows": (4, 4, 96, 128),
        "lines": (4, 288, 256),
        "weight": (8192, 128),
        "part": (4, 4, 2, 96, 128),
        "all_part": (3, 4, 2, 96, 128),
    }
    for n, (size, counts) in enumerate(((2048, (2, 4, 4)), (3072, (4, 4, 2)), (3072, (4, 2, 4)))):
        for p, count in enumerate(counts):
            size //= count
            b16["came_%d_%d" % (n, p)] = (count - 1, size, 128)
            b16["total_%d_%d" % (n, p)] = (size, 128)
    f32 = {
        "inv_in": (8, 128),
        "conv_own": (4, 2, 96, 128),
        "gain_rows": (4, 8, 128),
        "exps": (4, 8, 256, 256),
        "grad_p": (4, 8, 256, 256),
        "tops": (4, 8, 256),
        "sums": (4, 8, 256),
        "deltas": (4, 8, 256),
        "stats": (3, 8, 256),
        "all_stats": (7, 3, 8, 256),
        "weights": (4, 8, 256),
        "delta": (8, 256),
        "nearest": (2, 2, 384, 256),
        "own_sum": (2, 384, 256),
        "own_q": (4, 384, 256),
        "inner": (8, 128),
        "all_inner": (3, 8, 128),
    }
    scratch = {n: pltpu.VMEM(s, BF16) for n, s in b16.items()}
    scratch |= {n: pltpu.VMEM(s, F32) for n, s in f32.items()}
    scratch["mark"] = pltpu.SemaphoreType.DMA((4,))
    out, flat = fused(0, whole, held, made, scratch, (SENDS, NEXT + 4))
    cell_scale = 1.0 / math.sqrt(32768)
    grad_weights, out = pl.pallas_call(
        functools.partial(widen_kernel, cell_scale),
        out_shape=[jax.ShapeDtypeStruct((2592, 384), F32), jax.ShapeDtypeStruct(out.shape, BF16)],
        in_specs=[pl.BlockSpec(memory_space=pl.ANY)] * 2,
        out_specs=[pl.BlockSpec(memory_space=pl.ANY)] * 2,
        scratch_shapes=[
            pltpu.VMEM((9, 864, 128), BF16),
            pltpu.VMEM((9, 288, 384), F32),
            pltpu.SemaphoreType.DMA((10,)),
            pltpu.SemaphoreType.DMA((9,)),
        ],
        compiler_params=pltpu.CompilerParams(vmem_limit_bytes=VMEM_BYTES),
        name="widen",
    )(flat, out)
    return out, grad_weights.reshape(27, 96, 384)


def solution(mesh):
    return jax.shard_map(
        on_device,
        mesh=mesh,
        in_specs=(
            P(None, "row", "ch", None),
            P("ch"),
            P(None, "ch", None),
            P("ch"),
            P(),
            P(),
            P(None, "row", "ch", None),
        ),
        out_specs=(P(None, "row", "ch", None), P(None, "ch", None)),
        check_vma=False,
    )
```

```python
import functools
import math
import types

import jax
import jax.numpy as jnp
from jax import lax
from jax.experimental import pallas as pl
from jax.experimental.pallas import tpu as pltpu
from jax.sharding import PartitionSpec as P

EPSILON = 1e-06
MESH = pl.DeviceIdType.MESH
F32 = jnp.float32
BF16 = jnp.bfloat16
ROWS = 32
SENDS = 128
COT, RES, OWN, PREV, NEXT = range(SENDS, SENDS + 20, 4)
CH = 4
VMEM_BYTES = 60 * 1024 * 1024


def coords():
    return lax.axis_index("row"), lax.axis_index("ch")


def place(r, c):
    return lax.rem(r, 4), lax.rem(r // 4, 2), r // 8, c // 2, lax.rem(c, 2)


def device(x, y_hi, z, y_lo, core):
    return z * 8 + y_hi * 4 + x, y_lo * 2 + core


def owner(f, row):
    x, y_hi, z, _, _ = place(row, 0)
    return device(x, f // 2, z, f % 2, y_hi)


class Links:
    def __init__(self, send, recv):
        self.send, self.recv, self.sent, self.at = send, recv, [], 0

    def greet(self, peers, count):
        barrier = pltpu.get_barrier_semaphore()
        for peer in peers:
            pl.semaphore_signal(barrier, inc=1, device_id=peer, device_id_type=MESH)
        pl.semaphore_wait(barrier, count)

    def copy(self, src, dst, to, own=None, recv=None):
        k = self.at
        self.at += 1
        mark = self.recv.at[k if recv is None else recv]
        far = pltpu.make_async_remote_copy(
            src_ref=src,
            dst_ref=dst,
            send_sem=self.send.at[k],
            recv_sem=mark,
            device_id=to,
            device_id_type=MESH,
        )
        if own is None:
            far.start()
        else:
            pl.when(jnp.logical_not(own))(far.start)
            pl.when(own)(pltpu.make_async_copy(src, dst, mark).start)
        self.sent.append((far, own))
        return far

    def arrive(self, dst, k):
        pltpu.make_async_copy(dst, dst, self.recv.at[k]).wait()

    def finish(self):
        for far, own in self.sent:
            if own is None:
                far.wait_send()
            else:
                pl.when(jnp.logical_not(own))(far.wait_send)


def fused(cid, body, held, made, scratch, count):
    names = [*held, *made, *scratch]

    def kernel(*refs):
        body(Links(*refs[-2:]), types.SimpleNamespace(**dict(zip(names, refs))))

    return pl.pallas_call(
        kernel,
        out_shape=[jax.ShapeDtypeStruct(s, t) for s, t, _ in made.values()],
        in_specs=[pl.BlockSpec(memory_space=m) for _, m in held.values()],
        out_specs=[pl.BlockSpec(memory_space=m) for _, _, m in made.values()],
        scratch_shapes=[*scratch.values()] + [pltpu.SemaphoreType.DMA((n,)) for n in count],
        compiler_params=pltpu.CompilerParams(
            collective_id=cid, has_side_effects=True, vmem_limit_bytes=VMEM_BYTES
        ),
        name="fused_%d" % cid,
    )(*[array for array, _ in held.values()])


def dot(a, b):
    return lax.dot_general(a, b, (((1,), (0,)), ((), ())), preferred_element_type=F32)


def dot_t(a, b):
    return lax.dot_general(a, b, (((1,), (1,)), ((), ())), preferred_element_type=F32)


def move(block, by):
    lanes = block.shape[1]
    at = lax.broadcasted_iota(jnp.int32, block.shape, 1)
    if by > 0:
        return jnp.where(at == 0, 0.0, pltpu.roll(block, 1, axis=1))
    return jnp.where(at == lanes - 1, 0.0, pltpu.roll(block, lanes - 1, axis=1))


def ch_peers(r, c):
    return [(r, lax.rem(c + d, CH)) for d in range(1, CH)]


def near_rows(r):
    return lax.rem(r + ROWS - 1, ROWS), lax.rem(r + 1, ROWS)


def same(a, b):
    return jnp.logical_and(a[0] == b[0], a[1] == b[1])


def greet_frames(me, sources, targets):
    barrier = pltpu.get_barrier_semaphore()
    for peer in sources:
        def tell(peer=peer):
            pl.semaphore_signal(barrier, inc=1, device_id=peer, device_id_type=MESH)

        pl.when(jnp.logical_not(same(peer, me)))(tell)
    _, y_hi, _, _, core = place(*me)
    pl.semaphore_wait(barrier, len(targets) - 2 + 2 * (core - y_hi) * (core - y_hi))


def sigmoid(v):
    return 1.0 / (1.0 + jnp.exp(-v))


def gain_columns(rows, which):
    blocks = [jnp.broadcast_to(rows[b, which : which + 1, :], (128, 128)).T[:96] for b in range(CH)]
    return jnp.concatenate(blocks, 0)


class Place:
    def __init__(self):
        r, c = self.r, self.c = self.me = coords()
        x, y_hi, z, y_lo, core = self.x, self.y_hi, self.z, self.y_lo, self.core = place(r, c)
        self.slot = core * 4 + x
        self.frame = y_hi * 2 + y_lo
        self.low, self.high = near_rows(r)
        self.c_near = (1 - y_lo) * 2 + core
        self.sibling = (r, y_lo * 2 + 1 - core)
        self.near = (r, self.c_near)
        self.chs = ch_peers(r, c)
        self.xs = [device(lax.rem(x + d, 4), y_hi, z, y_lo, core) for d in range(1, 4)]
        self.cross = [device(lax.rem(x + d, 4), y_hi, z, y_lo, 1 - core) for d in range(1, 4)]
        self.zs = [device(x, y_hi, lax.rem(z + d, 4), y_lo, core) for d in range(1, 4)]
        self.across = device(x, 1 - y_hi, z, y_lo, core)
        self.targets = [owner(f, r) for f in range(4)]
        self.row = z * 8 + core * 4 + x
        self.sources = [(self.row, b) for b in range(CH)]

    def greet(self):
        at = self
        alike = at.chs + at.xs + at.cross + at.zs + [at.across, (at.low, at.c), (at.high, at.c)]
        there = [(i, b) for i in near_rows(at.row) for b in range(CH)]
        whose = [owner(f, i) for i in (at.low, at.high) for f in range(4)]
        greet_frames(at.me, at.targets + at.sources + whose + alike, at.targets + at.sources + there + alike)


def front(links, at, m):
    r, c, near, sibling = at.r, at.c, at.near, at.sibling
    every, act = m.every, m.act
    here = pltpu.make_async_copy(m.feat, every.at[c], m.mark.at[0])
    here.start()
    weights = pltpu.make_async_copy(m.w_far, m.w, m.mark.at[1])
    weights.start()
    projections = [
        pltpu.make_async_copy(m.w_out_far, m.w_out, m.mark.at[2]),
        pltpu.make_async_copy(m.w_qkv_far, m.w_qkv, m.mark.at[3]),
    ]
    for copy in projections:
        copy.start()
    m.gain_rows[c] = jnp.zeros((8, 128), F32)
    pad = jnp.zeros((1, 32), F32)
    m.gain_rows[c, 0:1, :] = jnp.concatenate([m.gain_in[...].astype(F32), pad], 1)
    m.gain_rows[c, 1:2, :] = jnp.concatenate([m.gain_attn[...].astype(F32), pad], 1)
    at.greet()
    pairs = [pl.ds(2 * p, 2) for p in range(2)]
    gains = [links.copy(m.gain_rows.at[c], m.gain_rows.at[c], to) for to in at.chs]
    to_near = [links.copy(m.feat.at[two], every.at[c, two], near) for two in pairs]
    to_sib = links.copy(m.feat, every.at[c], sibling)
    for copy in gains:
        copy.wait_recv()
    gain = gain_columns(m.gain_rows, 0)
    passed = []
    for p, two in enumerate(pairs):
        to_near[p].wait_recv()
        part = every.at[at.c_near, two]
        passed.append(links.copy(part, part, sibling))
    for f in range(4):
        own = same(at.targets[f], at.me)
        links.copy(m.cot.at[f], m.cot_frame.at[c], at.targets[f], own=own, recv=COT + c)

    def activate(n):
        v = jnp.concatenate([every[b, n // 2, lax.rem(n, 2)] for b in range(CH)], 0).astype(F32)
        inv = lax.rsqrt(jnp.mean(v * v, 0, keepdims=True) + EPSILON)
        before = v * inv * gain
        m.inv_in[pl.ds(n, 1), :] = inv
        act[:, pl.ds(pl.multiple_of(128 * n, 128), 128)] = (before * sigmoid(before)).astype(BF16)

    here.wait()
    to_sib.wait_recv()
    weights.wait()
    edges = []
    for p, two in enumerate(pairs):
        passed[p].wait_recv()

        def step(n, carry, p=p):
            activate(4 * p + n)
            return carry

        lax.fori_loop(0, 4, step, 0, unroll=2)
        for f in (2 * p, 2 * p + 1):
            by_tap = []
            for h in range(3):
                acc = jnp.zeros((288, 256), F32)
                for t in range(3):
                    source = f + t - 2
                    if source >= 0:
                        taps = m.w[pl.ds(9 * t + 3 * h, 3)].reshape(288, 384)
                        acc += dot(taps, act[:, pl.ds(256 * source, 256)])
                by_tap.append((acc[:, :128], acc[:, 128:]))
            lines = (
                by_tap[2][0],
                by_tap[2][1] + by_tap[1][0],
                by_tap[1][1] + by_tap[0][0],
                by_tap[0][1],
            )
            lines = [move(y[:96], 1) + y[96:192] + move(y[192:], -1) for y in lines]
            m.edge_out[0, f] = lines[0].astype(BF16)
            m.edge_out[1, f] = lines[3].astype(BF16)
            m.conv_own[f, 0] = lines[1]
            m.conv_own[f, 1] = lines[2]
        edges.append(links.copy(m.edge_out.at[0, two], m.edge_in.at[0, two], (at.low, c)))
        edges.append(links.copy(m.edge_out.at[1, two], m.edge_in.at[1, two], (at.high, c)))
    for b in range(CH):
        links.arrive(m.cot_frame.at[b], COT + b)
    for b in range(CH):
        for h in range(2):
            m.cot_full[pl.ds(96 * b, 96), pl.ds(128 * h, 128)] = m.cot_frame[b, h]
    for copy in projections:
        copy.wait()
    m.g[at.slot] = dot(m.w_out[...], m.cot_full[...]).astype(BF16)
    at.g_first = [links.copy(m.g.at[at.slot], m.g.at[at.slot], to) for to in (at.xs[0], at.xs[2], sibling)]
    for p in range(2):
        edges[2 * p].wait_recv()
        edges[2 * p + 1].wait_recv()
        for f in (2 * p, 2 * p + 1):
            before = jnp.where(r == 0, 0.0, m.edge_in[1, f].astype(F32))
            after = jnp.where(r == ROWS - 1, 0.0, m.edge_in[0, f].astype(F32))
            m.res[f, 0] = (every[c, f, 0].astype(F32) + (m.conv_own[f, 0] + before)).astype(BF16)
            m.res[f, 1] = (every[c, f, 1].astype(F32) + (m.conv_own[f, 1] + after)).astype(BF16)
            own = same(at.targets[f], at.me)
            links.copy(m.res.at[f], m.res_frame.at[c], at.targets[f], own=own, recv=RES + c)


def attention(links, at, m):
    scale = 1.0 / math.sqrt(384)
    x, z, core, slot, sibling = at.x, at.z, at.core, at.slot, at.sibling
    q, g, k, v, k_t = m.q, m.g, m.k, m.v, m.k_t
    w_qkv = m.w_qkv

    def relay_ring(first, ref, base, i, rows, peers, forward):
        on = []
        for side in range(2):
            first[side].wait_recv()
            came = base + lax.rem(i + 3 - 2 * side, 4)
            part = ref.at[came, pl.ds(rows * side, rows)]
            on.append(links.copy(part, part, peers[2 * side]))
            if forward:
                on.append(links.copy(ref.at[came], ref.at[came], sibling))
        return on

    g_on = relay_ring(at.g_first, g, core * 4, x, 192, at.xs, True)
    gain = gain_columns(m.gain_rows, 1)
    gain = jnp.concatenate([gain, gain], 1)
    for b in range(CH):
        links.arrive(m.res_frame.at[b], RES + b)
    for b in range(CH):
        for h in range(2):
            m.full[pl.ds(96 * b, 96), pl.ds(128 * h, 128)] = m.res_frame[b, h]
    centre = m.full[...].astype(F32)
    inv = lax.rsqrt(jnp.mean(centre * centre, 0, keepdims=True) + EPSILON)
    m.norm[z] = (centre * inv * gain).astype(BF16).astype(F32).T.astype(BF16)
    n_first = [links.copy(m.norm.at[z], m.norm.at[z], to) for to in (at.zs[0], at.zs[2])]
    q[slot] = dot(m.norm[z], w_qkv[:, :384]).T.astype(BF16)
    q_first = [links.copy(q.at[slot], q.at[slot], to) for to in (at.xs[0], at.xs[2], sibling)]

    def project(j):
        k[j] = dot(m.norm[j], w_qkv[:, 384:768]).astype(BF16)
        v[j] = dot(m.norm[j], w_qkv[:, 768:]).astype(BF16)
        k_t[:, pl.ds(pl.multiple_of(256 * j, 256), 256)] = k[j].T

    def tile(b, j):
        s = dot(k[j], q[b]) * scale
        top = jnp.max(s, 0, keepdims=True)
        e = jnp.exp(s - top)
        p = dot(v[j], g[b])
        m.exps[j, b] = e
        m.grad_p[j, b] = p
        m.tops[j, pl.ds(b, 1), :] = top
        m.sums[j, pl.ds(b, 1), :] = jnp.sum(e, 0, keepdims=True)
        m.deltas[j, pl.ds(b, 1), :] = jnp.sum(e * p, 0, keepdims=True)

    def block(dk, dx):
        other = core + dk - 2 * core * dk
        return other * 4 + lax.rem(x + dx, 4)

    def key(dz):
        return lax.rem(z + dz, 4)

    def tiles(count, unroll, which):
        def step(n, carry):
            dk, dx, dz = which(n)
            tile(block(dk, dx), key(dz))
            return carry

        lax.fori_loop(0, count, step, 0, unroll=unroll)

    project(z)
    g_on[1].wait_recv()
    g_on[3].wait_recv()
    far_x = core * 4 + lax.rem(x + 2, 4)
    at.g_first[2].wait_recv()
    q_first[2].wait_recv()
    tiles(2, 2, lambda n: (n, 0, 0))
    for t in range(3):
        for n in range(3):
            piece = jnp.concatenate([m.w[9 * t + 3 * h + n] for h in range(3)], 0)
            m.w_t[t, pl.ds(384 * n, 384), :] = piece.T
    n_on = relay_ring(n_first, m.norm, 0, z, 128, at.zs, False)
    q_on = relay_ring(q_first, q, core * 4, x, 192, at.xs, True)
    g_on[0].wait_recv()
    g_on[2].wait_recv()
    g_last = links.copy(g.at[far_x], g.at[far_x], sibling)
    project(key(1))
    project(key(3))
    tiles(4, 4, lambda n: (n // 2, 0, 1 + 2 * lax.rem(n, 2)))
    q_on[1].wait_recv()
    q_on[3].wait_recv()

    def beside(n):
        dz = n // 4
        return lax.rem(n // 2, 2), 1 + 2 * lax.rem(n, 2), dz + dz // 2

    tiles(12, 4, beside)
    q_on[0].wait_recv()
    q_on[2].wait_recv()
    q_last = links.copy(q.at[far_x], q.at[far_x], sibling)
    n_on[0].wait_recv()
    n_on[1].wait_recv()
    project(key(2))

    def beyond(n):
        dx = n // 2
        return lax.rem(n, 2), dx + dx // 2, 2

    tiles(6, 3, beyond)
    tiles(4, 4, lambda n: (0, 2, n))
    q_last.wait_recv()
    g_last.wait_recv()
    tiles(4, 4, lambda n: (1, 2, n))

    tops = [m.tops[j] for j in range(4)]
    top = functools.reduce(jnp.maximum, tops)
    shift = [jnp.exp(t - top) for t in tops]
    m.stats[0] = top
    m.stats[1] = sum(m.sums[j] * shift[j] for j in range(4))
    m.stats[2] = sum(m.deltas[j] * shift[j] for j in range(4))
    peers = at.xs + at.cross + [sibling]
    shared = [links.copy(m.stats, m.all_stats.at[n], to) for n, to in enumerate(peers)]
    for copy in shared:
        copy.wait_recv()
    parts = [m.stats] + [m.all_stats.at[n] for n in range(7)]
    top = functools.reduce(jnp.maximum, [p[0] for p in parts])
    total = sum(p[1] * jnp.exp(p[0] - top) for p in parts)
    m.delta[...] = sum(p[2] * jnp.exp(p[0] - top) for p in parts) / total
    for j in range(4):
        m.weights[j] = jnp.exp(m.tops[j] - top) / total

    def rows_of(j):
        return pl.ds(pl.multiple_of(256 * j, 256), 256)

    def weigh(b, j):
        prob = m.exps[j, b] * m.weights[j, pl.ds(b, 1), :]
        m.prob[b, rows_of(j), :] = prob.astype(BF16)
        m.grad_s[b, rows_of(j), :] = (prob * (m.grad_p[j, b] - m.delta[pl.ds(b, 1), :])).astype(BF16)

    def key_grad(j):
        for_k = sum(dot_t(m.grad_s[b, rows_of(j), :], q[b]) for b in range(8)) * scale
        for_v = sum(dot_t(m.prob[b, rows_of(j), :], g[b]) for b in range(8))
        return dot_t(w_qkv[:, 384:768], for_k.astype(BF16)) + dot_t(w_qkv[:, 768:], for_v.astype(BF16))

    halves = [pl.ds(0, 192), pl.ds(192, 192)]
    rings = ((at.zs[0], at.zs[2]), (at.xs[0], at.xs[2]))
    by_way, back = {}, []

    def send_far(kind, value):
        m.far[kind] = value.astype(BF16)
        for i in range(2):
            by_way[kind, i] = links.copy(m.far.at[kind, halves[i]], m.via.at[kind, i], rings[kind][i])

    def send_half(kind, i, half, value):
        m.send[kind, i, halves[half]] = value.astype(BF16)
        src, dst = m.send.at[kind, i, halves[half]], m.came.at[kind, i, halves[half]]
        back.append(links.copy(src, dst, rings[kind][i]))

    def send_near(kind, i, value):
        m.nearest[kind, i] = value
        send_half(kind, i, 1 - i, value[192 * (1 - i) : 192 * (2 - i)])

    def send_added(kind):
        for i in range(2):
            by_way[kind, i].wait_recv()
            send_half(kind, i, i, m.nearest[kind, i, halves[i], :] + m.via[kind, i].astype(F32))

    def weigh_all(dk):
        def step(n, carry):
            weigh(block(dk, lax.rem(n, 4)), key(n // 4))
            return carry

        lax.fori_loop(0, 16, step, 0, unroll=4)

    def query_grads(dk, put):
        def step(dx, carry):
            put(dx, dot(k_t[...], m.grad_s[block(dk, dx)]) * scale)
            return carry

        lax.fori_loop(0, 4, step, 0)

    def for_sibling(dx, value):
        m.sib_out[dx] = value.astype(BF16)

    def for_own(dx, value):
        m.own_q[dx] = value

    weigh_all(1)
    query_grads(1, for_sibling)
    sib = links.copy(m.sib_out, m.sib_in, sibling)
    weigh_all(0)
    send_far(0, key_grad(key(2)))
    query_grads(0, for_own)
    sib.wait_recv()

    def query_grad(dx):
        return m.own_q[dx] + m.sib_in[dx].astype(F32)

    send_far(1, query_grad(2))
    send_near(1, 0, query_grad(1))
    send_near(1, 1, query_grad(3))

    def near_keys(i, carry):
        m.nearest[0, i] = key_grad(key(1 + 2 * i))
        return carry

    lax.fori_loop(0, 2, near_keys, 0)
    for i in range(2):
        send_half(0, i, 1 - i, m.nearest[0, i, halves[1 - i], :])
    send_added(0)
    send_added(1)
    m.own_sum[0] = key_grad(z)
    m.own_sum[1] = query_grad(0)
    for copy in back:
        copy.wait_recv()
    by_key, by_query = [
        m.own_sum[n] + m.came[n, 0].astype(F32) + m.came[n, 1].astype(F32) for n in range(2)
    ]
    back_normed = dot(w_qkv[:, :384], by_query.astype(BF16)) + by_key
    scaled = back_normed.astype(BF16).astype(F32) * gain
    centre = m.full[...].astype(F32)
    inner = jnp.mean(centre * scaled, 0, keepdims=True)
    out = m.cot_full[...].astype(F32) + inv * scaled - centre * (inv * inv * inv * inner)
    for b in range(CH):
        for h in range(2):
            m.grad[b, h] = out[96 * b : 96 * b + 96, 128 * h : 128 * h + 128].astype(BF16)
    row_low, row_high = near_rows(at.row)
    for b in range(CH):
        to = at.sources[b]
        links.copy(m.grad.at[b], m.own.at[at.frame], to, own=same(to, at.me), recv=OWN + at.frame)
    for b in range(CH):
        links.copy(m.grad.at[b, 1], m.prev_g.at[at.frame], (row_high, b), recv=PREV + at.frame)
        links.copy(m.grad.at[b, 0], m.next_g.at[at.frame], (row_low, b), recv=NEXT + at.frame)


def tail(links, at, m):
    r, c, x, y_hi, z = at.r, at.c, at.x, at.y_hi, at.z
    xs, zs, across, chs = at.xs, at.zs, at.across, at.chs
    own, act, w_t, every, inv_in, gain_rows = m.own, m.act, m.w_t, m.every, m.inv_in, m.gain_rows
    rows, lines, weight, part, all_part, inner, all_inner = m.rows, m.lines, m.weight, m.part, m.all_part, m.inner, m.all_inner
    mark, flat, out = m.mark, m.flat, m.out
    ring_x = (x, [lax.rem(x + d, 4) for d in range(1, 4)], xs)
    ring_z = (z, [lax.rem(z + d, 4) for d in range(1, 4)], zs)
    ring_y = (y_hi, [1 - y_hi], [across])
    stripes = []
    for n, (base, size, rings) in enumerate(
        (
            (0, 2048, (ring_y, ring_x, ring_z)),
            (2048, 3072, (ring_x, ring_z, ring_y)),
            (5120, 3072, (ring_z, ring_y, ring_x)),
        )
    ):
        steps, at_row = [], base
        for p, (place_on, places, peers) in enumerate(rings):
            size //= len(peers) + 1
            start = at_row
            at_row = at_row + place_on * size
            came, total = getattr(m, "came_%d_%d" % (n, p)), getattr(m, "total_%d_%d" % (n, p))
            steps.append((start, size, places, peers, at_row, came, total))
        stripes.append(steps)

    def rows_at(start, size):
        return pl.ds(pl.multiple_of(start, 16), size)

    def give(steps, p):
        start, size, places, peers, _, came, _ = steps[p]
        sent = []
        for d, peer in enumerate(peers):
            if p == 0:
                src = weight.at[rows_at(start + places[d] * size, size)]
            else:
                src = steps[p - 1][6].at[rows_at(places[d] * size, size)]
            sent.append(links.copy(src, came.at[d], peer))
        return sent

    def take(steps, p, sent):
        start, size, _, peers, mine, came, total = steps[p]
        for copy in sent:
            copy.wait_recv()
        if p == 0:
            value = weight[rows_at(mine, size), :].astype(F32)
        else:
            value = steps[p - 1][6][rows_at(mine - start, size), :].astype(F32)
        for d in range(len(peers)):
            value += came[d].astype(F32)
        total[...] = value.astype(BF16)

    def prepare(f, h):
        y = rows[f, h].astype(F32)
        m.moved[f, :, pl.ds(128 * h, 128)] = jnp.concatenate([move(y, -1), y, move(y, 1)], 0).astype(BF16)

    for f in range(4):
        links.arrive(own.at[f], OWN + f)
    for f in range(4):
        for h in range(2):
            rows[f, h + 1] = own[f, h]
            prepare(f, h + 1)
    for f in range(4):
        links.arrive(m.prev_g.at[f], PREV + f)
        links.arrive(m.next_g.at[f], NEXT + f)
    for f in range(4):
        rows[f, 0] = jnp.where(r == 0, 0.0, m.prev_g[f].astype(F32)).astype(BF16)
        rows[f, 3] = jnp.where(r == ROWS - 1, 0.0, m.next_g[f].astype(F32)).astype(BF16)
        prepare(f, 0)
        prepare(f, 3)
    first = []
    for t in range(3):
        for h in range(3):
            acc = jnp.zeros((288, 384), F32)
            for f in range(4):
                source = f + t - 2
                if source < 0:
                    continue
                acc += dot_t(m.moved[f, :, pl.ds(128 * (2 - h), 256)], act[:, pl.ds(256 * source, 256)])
            for lane in range(3):
                at = (3 * (3 * t + h) + lane) * 288
                weight[pl.ds(at, 288), :] = acc[:, 128 * lane : 128 * lane + 128].astype(BF16)
        if t == 2:
            weight[pl.ds(27 * 288, 416), :] = jnp.zeros((416, 128), BF16)
        first.append(give(stripes[t], 0))
    for f in range(4):
        for h in range(3):
            for k in range(2):
                lines[f, pl.ds(96 * h, 96), pl.ds(128 * k, 128)] = rows[f, 2 - h + k]
    gain = gain_columns(gain_rows, 0)
    for f in range(4):
        acc = jnp.zeros((1152, 256), F32)
        for t in range(3):
            source = f + 2 - t
            if source > 3:
                continue
            acc += dot(w_t[t], lines[source])
        for h in range(2):
            y = acc[:, 128 * h : 128 * h + 128]
            total = move(y[:384], -1) + y[384:768] + move(y[768:], 1)
            v = jnp.concatenate([every[b, f, h] for b in range(CH)], 0).astype(F32)
            before = v * inv_in[2 * f + h : 2 * f + h + 1, :] * gain
            sig = sigmoid(before)
            slope = sig * (1.0 + before * (1.0 - sig))
            inner[2 * f + h : 2 * f + h + 1, :] = jnp.sum(v * slope * gain * total, 0, keepdims=True)
            for b in range(CH):
                part[b, f, h] = total[96 * b : 96 * b + 96].astype(BF16)
    second, third, parts = [], [], []
    for n, steps in enumerate(stripes):
        take(steps, 0, first[n])
        second.append(give(steps, 1))
    for d in range(3):
        parts.append(links.copy(part.at[chs[d][1]], all_part.at[d], chs[d]))
        parts.append(links.copy(inner, all_inner.at[d], chs[d]))
    for n, steps in enumerate(stripes):
        take(steps, 1, second[n])
        third.append(give(steps, 2))
    spread, kept = [], []
    for n, steps in enumerate(stripes):
        take(steps, 2, third[n])
        _, size, _, peers, mine, _, total = steps[2]
        m.spread[rows_at(mine, size), :] = total[...]
        spread.append([links.copy(total, m.spread.at[rows_at(mine, size)], peer) for peer in peers])
    for p in (1, 0):
        for n, steps in enumerate(stripes):
            for copy in spread[n]:
                copy.wait_recv()
            _, size, _, peers, mine, _, _ = steps[p]
            src = dst = m.spread.at[rows_at(mine, size)]
            if p == 0:
                dst = flat.at[rows_at(mine, size)]
                kept.append(pltpu.make_async_copy(src, dst, mark.at[n]))
                kept[n].start()
            spread[n] = [links.copy(src, dst, peer) for peer in peers]
    for copy in parts:
        copy.wait_recv()
    mean = (inner[...] + all_inner[0] + all_inner[1] + all_inner[2]) / 384.0
    gain = jnp.broadcast_to(gain_rows[c, 0:1, :], (128, 128)).T[:96]
    for f in range(4):
        for h in range(2):
            v = every[c, f, h].astype(F32)
            inv = inv_in[2 * f + h : 2 * f + h + 1, :]
            total = part[c, f, h].astype(F32)
            for d in range(3):
                total += all_part[d, f, h].astype(F32)
            before = v * inv * gain
            sig = sigmoid(before)
            scaled = total * (sig * (1.0 + before * (1.0 - sig))) * gain
            cube = inv * inv * inv * mean[2 * f + h : 2 * f + h + 1, :]
            out[f, h] = (own[f, h].astype(F32) + inv * scaled - v * cube).astype(BF16)
    for copy in kept:
        copy.wait()
    for copy in spread[0] + spread[1] + spread[2]:
        copy.wait_recv()


def whole(links, m):
    at = Place()
    front(links, at, m)
    attention(links, at, m)
    tail(links, at, m)
    links.finish()


def widen_kernel(scale, flat, grad, out, grad_out, near, wide, through, into, back):
    come = [
        pltpu.make_async_copy(flat.at[pl.ds(864 * k, 864)], near.at[k], into.at[k]) for k in range(9)
    ]
    go = [
        pltpu.make_async_copy(wide.at[k], out.at[pl.ds(288 * k, 288)], back.at[k]) for k in range(9)
    ]
    enter = pltpu.make_async_copy(grad, through, into.at[9])
    leave = pltpu.make_async_copy(through, grad_out, back.at[9])
    for copy in come:
        copy.start()
    enter.start()
    for k in range(9):
        if k == 4:
            enter.wait()
            leave.start()
        come[k].wait()
        for lane in range(3):
            piece = near[k, pl.ds(288 * lane, 288), :].astype(F32) * scale
            wide[k, :, pl.ds(128 * lane, 128)] = piece
        go[k].start()
    for copy in go:
        copy.wait()
    leave.wait()


def on_device(features, gain_in, w_conv, gain_attn, w_qkv, w_out, cotangent):
    near, far = pltpu.VMEM, pl.ANY
    held = {
        "feat": (features, far),
        "cot": (cotangent, far),
        "w_far": (w_conv, far),
        "gain_in": (gain_in.reshape(1, 96), near),
        "gain_attn": (gain_attn.reshape(1, 96), near),
        "w_qkv_far": (w_qkv, far),
        "w_out_far": (w_out, far),
    }
    made = {"out": ((4, 2, 96, 128), BF16, near), "flat": ((8192, 128), BF16, far)}
    b16 = {
        "every": (4, 4, 2, 96, 128),
        "w": (27, 96, 384),
        "w_qkv": (384, 1152),
        "w_out": (384, 384),
        "act": (384, 1024),
        "edge_out": (2, 4, 96, 128),
        "edge_in": (2, 4, 96, 128),
        "moved": (4, 288, 512),
        "res": (4, 2, 96, 128),
        "cot_frame": (4, 2, 96, 128),
        "res_frame": (4, 2, 96, 128),
        "full": (384, 256),
        "cot_full": (384, 256),
        "norm": (4, 256, 384),
        "q": (8, 384, 256),
        "g": (8, 384, 256),
        "k": (4, 256, 384),
        "v": (4, 256, 384),
        "k_t": (384, 1024),
        "prob": (8, 1024, 256),
        "grad_s": (8, 1024, 256),
        "far": (2, 384, 256),
        "via": (2, 2, 192, 256),
        "send": (2, 2, 384, 256),
        "came": (2, 2, 384, 256),
        "sib_out": (4, 384, 256),
        "sib_in": (4, 384, 256),
        "grad": (4, 2, 96, 128),
        "own": (4, 2, 96, 128),
        "prev_g": (4, 96, 128),
        "next_g": (4, 96, 128),
        "w_t": (3, 1152, 288),
        "rows": (4, 4, 96, 128),
        "lines": (4, 288, 256),
        "weight": (8192, 128),
        "spread": (8192, 128),
        "part": (4, 4, 2, 96, 128),
        "all_part": (3, 4, 2, 96, 128),
    }
    for n, (size, counts) in enumerate(((2048, (2, 4, 4)), (3072, (4, 4, 2)), (3072, (4, 2, 4)))):
        for p, count in enumerate(counts):
            size //= count
            b16["came_%d_%d" % (n, p)] = (count - 1, size, 128)
            b16["total_%d_%d" % (n, p)] = (size, 128)
    f32 = {
        "inv_in": (8, 128),
        "conv_own": (4, 2, 96, 128),
        "gain_rows": (4, 8, 128),
        "exps": (4, 8, 256, 256),
        "grad_p": (4, 8, 256, 256),
        "tops": (4, 8, 256),
        "sums": (4, 8, 256),
        "deltas": (4, 8, 256),
        "stats": (3, 8, 256),
        "all_stats": (7, 3, 8, 256),
        "weights": (4, 8, 256),
        "delta": (8, 256),
        "nearest": (2, 2, 384, 256),
        "own_sum": (2, 384, 256),
        "own_q": (4, 384, 256),
        "inner": (8, 128),
        "all_inner": (3, 8, 128),
    }
    scratch = {n: pltpu.VMEM(s, BF16) for n, s in b16.items()}
    scratch |= {n: pltpu.VMEM(s, F32) for n, s in f32.items()}
    scratch["mark"] = pltpu.SemaphoreType.DMA((4,))
    out, flat = fused(0, whole, held, made, scratch, (SENDS, NEXT + 4))
    cell_scale = 1.0 / math.sqrt(32768)
    grad_weights, out = pl.pallas_call(
        functools.partial(widen_kernel, cell_scale),
        out_shape=[jax.ShapeDtypeStruct((2592, 384), F32), jax.ShapeDtypeStruct(out.shape, BF16)],
        in_specs=[pl.BlockSpec(memory_space=pl.ANY)] * 2,
        out_specs=[pl.BlockSpec(memory_space=pl.ANY)] * 2,
        scratch_shapes=[
            pltpu.VMEM((9, 864, 128), BF16),
            pltpu.VMEM((9, 288, 384), F32),
            pltpu.VMEM((4, 2, 96, 128), BF16),
            pltpu.SemaphoreType.DMA((10,)),
            pltpu.SemaphoreType.DMA((10,)),
        ],
        compiler_params=pltpu.CompilerParams(vmem_limit_bytes=VMEM_BYTES),
        name="widen",
    )(flat, out)
    return out, grad_weights.reshape(27, 96, 384)


def solution(mesh):
    return jax.shard_map(
        on_device,
        mesh=mesh,
        in_specs=(
            P(None, "row", "ch", None),
            P("ch"),
            P(None, "ch", None),
            P("ch"),
            P(),
            P(),
            P(None, "row", "ch", None),
        ),
        out_specs=(P(None, "row", "ch", None), P(None, "ch", None)),
        check_vma=False,
    )
```

```python
import functools
import math
import types

import jax
import jax.numpy as jnp
from jax import lax
from jax.experimental import pallas as pl
from jax.experimental.pallas import tpu as pltpu
from jax.sharding import PartitionSpec as P

EPSILON = 1e-06
MESH = pl.DeviceIdType.MESH
F32 = jnp.float32
BF16 = jnp.bfloat16
ROWS = 32
SENDS = 128
COT, RES, OWN, PREV, NEXT = range(SENDS, SENDS + 20, 4)
CH = 4
VMEM_BYTES = 60 * 1024 * 1024


def coords():
    return lax.axis_index("row"), lax.axis_index("ch")


def place(r, c):
    return lax.rem(r, 4), lax.rem(r // 4, 2), r // 8, c // 2, lax.rem(c, 2)


def device(x, y_hi, z, y_lo, core):
    return z * 8 + y_hi * 4 + x, y_lo * 2 + core


def owner(f, row):
    x, y_hi, z, _, _ = place(row, 0)
    return device(x, f // 2, z, f % 2, y_hi)


class Links:
    def __init__(self, send, recv):
        self.send, self.recv, self.sent, self.at = send, recv, [], 0

    def greet(self, peers, count):
        barrier = pltpu.get_barrier_semaphore()
        for peer in peers:
            pl.semaphore_signal(barrier, inc=1, device_id=peer, device_id_type=MESH)
        pl.semaphore_wait(barrier, count)

    def copy(self, src, dst, to, own=None, recv=None):
        k = self.at
        self.at += 1
        mark = self.recv.at[k if recv is None else recv]
        far = pltpu.make_async_remote_copy(
            src_ref=src,
            dst_ref=dst,
            send_sem=self.send.at[k],
            recv_sem=mark,
            device_id=to,
            device_id_type=MESH,
        )
        if own is None:
            far.start()
        else:
            pl.when(jnp.logical_not(own))(far.start)
            pl.when(own)(pltpu.make_async_copy(src, dst, mark).start)
        self.sent.append((far, own))
        return far

    def arrive(self, dst, k):
        pltpu.make_async_copy(dst, dst, self.recv.at[k]).wait()

    def finish(self):
        for far, own in self.sent:
            if own is None:
                far.wait_send()
            else:
                pl.when(jnp.logical_not(own))(far.wait_send)


def fused(cid, body, held, made, scratch, count):
    names = [*held, *made, *scratch]

    def kernel(*refs):
        body(Links(*refs[-2:]), types.SimpleNamespace(**dict(zip(names, refs))))

    return pl.pallas_call(
        kernel,
        out_shape=[jax.ShapeDtypeStruct(s, t) for s, t, _ in made.values()],
        in_specs=[pl.BlockSpec(memory_space=m) for _, m in held.values()],
        out_specs=[pl.BlockSpec(memory_space=m) for _, _, m in made.values()],
        scratch_shapes=[*scratch.values()] + [pltpu.SemaphoreType.DMA((n,)) for n in count],
        compiler_params=pltpu.CompilerParams(
            collective_id=cid, has_side_effects=True, vmem_limit_bytes=VMEM_BYTES
        ),
        name="fused_%d" % cid,
    )(*[array for array, _ in held.values()])


def dot(a, b):
    return lax.dot_general(a, b, (((1,), (0,)), ((), ())), preferred_element_type=F32)


def dot_t(a, b):
    return lax.dot_general(a, b, (((1,), (1,)), ((), ())), preferred_element_type=F32)


def move(block, by):
    lanes = block.shape[1]
    at = lax.broadcasted_iota(jnp.int32, block.shape, 1)
    if by > 0:
        return jnp.where(at == 0, 0.0, pltpu.roll(block, 1, axis=1))
    return jnp.where(at == lanes - 1, 0.0, pltpu.roll(block, lanes - 1, axis=1))


def ch_peers(r, c):
    return [(r, lax.rem(c + d, CH)) for d in range(1, CH)]


def near_rows(r):
    return lax.rem(r + ROWS - 1, ROWS), lax.rem(r + 1, ROWS)


def same(a, b):
    return jnp.logical_and(a[0] == b[0], a[1] == b[1])


def greet_frames(me, sources, targets):
    barrier = pltpu.get_barrier_semaphore()
    for peer in sources:
        def tell(peer=peer):
            pl.semaphore_signal(barrier, inc=1, device_id=peer, device_id_type=MESH)

        pl.when(jnp.logical_not(same(peer, me)))(tell)
    _, y_hi, _, _, core = place(*me)
    pl.semaphore_wait(barrier, len(targets) - 2 + 2 * (core - y_hi) * (core - y_hi))


def sigmoid(v):
    return 1.0 / (1.0 + jnp.exp(-v))


def gain_columns(rows, which):
    blocks = [jnp.broadcast_to(rows[b, which : which + 1, :], (128, 128)).T[:96] for b in range(CH)]
    return jnp.concatenate(blocks, 0)


class Place:
    def __init__(self):
        r, c = self.r, self.c = self.me = coords()
        x, y_hi, z, y_lo, core = self.x, self.y_hi, self.z, self.y_lo, self.core = place(r, c)
        self.slot = core * 4 + x
        self.frame = y_hi * 2 + y_lo
        self.low, self.high = near_rows(r)
        self.c_near = (1 - y_lo) * 2 + core
        self.sibling = (r, y_lo * 2 + 1 - core)
        self.near = (r, self.c_near)
        self.chs = ch_peers(r, c)
        self.xs = [device(lax.rem(x + d, 4), y_hi, z, y_lo, core) for d in range(1, 4)]
        self.cross = [device(lax.rem(x + d, 4), y_hi, z, y_lo, 1 - core) for d in range(1, 4)]
        self.zs = [device(x, y_hi, lax.rem(z + d, 4), y_lo, core) for d in range(1, 4)]
        self.across = device(x, 1 - y_hi, z, y_lo, core)
        self.targets = [owner(f, r) for f in range(4)]
        self.row = z * 8 + core * 4 + x
        self.sources = [(self.row, b) for b in range(CH)]

    def greet(self):
        at = self
        alike = at.chs + at.xs + at.cross + at.zs + [at.across, (at.low, at.c), (at.high, at.c)]
        there = [(i, b) for i in near_rows(at.row) for b in range(CH)]
        whose = [owner(f, i) for i in (at.low, at.high) for f in range(4)]
        greet_frames(at.me, at.targets + at.sources + whose + alike, at.targets + at.sources + there + alike)


def front(links, at, m):
    r, c, near, sibling = at.r, at.c, at.near, at.sibling
    every, act = m.every, m.act
    here = pltpu.make_async_copy(m.feat, every.at[c], m.mark.at[0])
    here.start()
    weights = pltpu.make_async_copy(m.w_far, m.w, m.mark.at[1])
    weights.start()
    projections = [
        pltpu.make_async_copy(m.w_out_far, m.w_out, m.mark.at[2]),
        pltpu.make_async_copy(m.w_qkv_far, m.w_qkv, m.mark.at[3]),
    ]
    for copy in projections:
        copy.start()
    m.gain_rows[c] = jnp.zeros((8, 128), F32)
    pad = jnp.zeros((1, 32), F32)
    m.gain_rows[c, 0:1, :] = jnp.concatenate([m.gain_in[...].astype(F32), pad], 1)
    m.gain_rows[c, 1:2, :] = jnp.concatenate([m.gain_attn[...].astype(F32), pad], 1)
    at.greet()
    pairs = [pl.ds(2 * p, 2) for p in range(2)]
    gains = [links.copy(m.gain_rows.at[c], m.gain_rows.at[c], to) for to in at.chs]
    to_near = [links.copy(m.feat.at[two], every.at[c, two], near) for two in pairs]
    to_sib = links.copy(m.feat, every.at[c], sibling)
    for copy in gains:
        copy.wait_recv()
    gain = gain_columns(m.gain_rows, 0)
    passed = []
    for p, two in enumerate(pairs):
        to_near[p].wait_recv()
        part = every.at[at.c_near, two]
        passed.append(links.copy(part, part, sibling))
    for f in range(4):
        own = same(at.targets[f], at.me)
        links.copy(m.cot.at[f], m.cot_frame.at[c], at.targets[f], own=own, recv=COT + c)

    def activate(n):
        v = jnp.concatenate([every[b, n // 2, lax.rem(n, 2)] for b in range(CH)], 0).astype(F32)
        inv = lax.rsqrt(jnp.mean(v * v, 0, keepdims=True) + EPSILON)
        before = v * inv * gain
        m.inv_in[pl.ds(n, 1), :] = inv
        act[:, pl.ds(pl.multiple_of(128 * n, 128), 128)] = (before * sigmoid(before)).astype(BF16)

    here.wait()
    to_sib.wait_recv()
    weights.wait()
    edges = []
    for p, two in enumerate(pairs):
        passed[p].wait_recv()

        def step(n, carry, p=p):
            activate(4 * p + n)
            return carry

        lax.fori_loop(0, 4, step, 0, unroll=2)
        for f in (2 * p, 2 * p + 1):
            by_tap = []
            for h in range(3):
                acc = jnp.zeros((288, 256), F32)
                for t in range(3):
                    source = f + t - 2
                    if source >= 0:
                        taps = m.w[pl.ds(9 * t + 3 * h, 3)].reshape(288, 384)
                        acc += dot(taps, act[:, pl.ds(256 * source, 256)])
                by_tap.append((acc[:, :128], acc[:, 128:]))
            lines = (
                by_tap[2][0],
                by_tap[2][1] + by_tap[1][0],
                by_tap[1][1] + by_tap[0][0],
                by_tap[0][1],
            )
            lines = [move(y[:96], 1) + y[96:192] + move(y[192:], -1) for y in lines]
            m.edge_out[0, f] = lines[0].astype(BF16)
            m.edge_out[1, f] = lines[3].astype(BF16)
            m.conv_own[f, 0] = lines[1]
            m.conv_own[f, 1] = lines[2]
        edges.append(links.copy(m.edge_out.at[0, two], m.edge_in.at[0, two], (at.low, c)))
        edges.append(links.copy(m.edge_out.at[1, two], m.edge_in.at[1, two], (at.high, c)))
    for b in range(CH):
        links.arrive(m.cot_frame.at[b], COT + b)
    for b in range(CH):
        for h in range(2):
            m.cot_full[pl.ds(96 * b, 96), pl.ds(128 * h, 128)] = m.cot_frame[b, h]
    for copy in projections:
        copy.wait()
    m.g[at.slot] = dot(m.w_out[...], m.cot_full[...]).astype(BF16)
    at.g_first = [links.copy(m.g.at[at.slot], m.g.at[at.slot], to) for to in (at.xs[0], at.xs[2], sibling)]
    for p in range(2):
        edges[2 * p].wait_recv()
        edges[2 * p + 1].wait_recv()
        for f in (2 * p, 2 * p + 1):
            before = jnp.where(r == 0, 0.0, m.edge_in[1, f].astype(F32))
            after = jnp.where(r == ROWS - 1, 0.0, m.edge_in[0, f].astype(F32))
            m.res[f, 0] = (every[c, f, 0].astype(F32) + (m.conv_own[f, 0] + before)).astype(BF16)
            m.res[f, 1] = (every[c, f, 1].astype(F32) + (m.conv_own[f, 1] + after)).astype(BF16)
            own = same(at.targets[f], at.me)
            links.copy(m.res.at[f], m.res_frame.at[c], at.targets[f], own=own, recv=RES + c)


def attention(links, at, m):
    scale = 1.0 / math.sqrt(384)
    x, z, core, slot, sibling = at.x, at.z, at.core, at.slot, at.sibling
    q, g, k, v, k_t = m.q, m.g, m.k, m.v, m.k_t
    w_qkv = m.w_qkv

    def relay_ring(first, ref, base, i, rows, peers, forward):
        on = []
        for side in range(2):
            first[side].wait_recv()
            came = base + lax.rem(i + 3 - 2 * side, 4)
            part = ref.at[came, pl.ds(rows * side, rows)]
            on.append(links.copy(part, part, peers[2 * side]))
            if forward:
                on.append(links.copy(ref.at[came], ref.at[came], sibling))
        return on

    g_on = relay_ring(at.g_first, g, core * 4, x, 192, at.xs, True)
    gain = gain_columns(m.gain_rows, 1)
    gain = jnp.concatenate([gain, gain], 1)
    for b in range(CH):
        links.arrive(m.res_frame.at[b], RES + b)
    for b in range(CH):
        for h in range(2):
            m.full[pl.ds(96 * b, 96), pl.ds(128 * h, 128)] = m.res_frame[b, h]
    centre = m.full[...].astype(F32)
    inv = lax.rsqrt(jnp.mean(centre * centre, 0, keepdims=True) + EPSILON)
    m.norm[z] = (centre * inv * gain).astype(BF16).astype(F32).T.astype(BF16)
    n_first = [links.copy(m.norm.at[z], m.norm.at[z], to) for to in (at.zs[0], at.zs[2])]
    q[slot] = dot(m.norm[z], w_qkv[:, :384]).T.astype(BF16)
    q_first = [links.copy(q.at[slot], q.at[slot], to) for to in (at.xs[0], at.xs[2], sibling)]

    def project(j):
        k[j] = dot(m.norm[j], w_qkv[:, 384:768]).astype(BF16)
        v[j] = dot(m.norm[j], w_qkv[:, 768:]).astype(BF16)
        k_t[:, pl.ds(pl.multiple_of(256 * j, 256), 256)] = k[j].T

    def tile(b, j):
        s = dot(k[j], q[b]) * scale
        top = jnp.max(s, 0, keepdims=True)
        e = jnp.exp(s - top)
        p = dot(v[j], g[b])
        m.exps[j, b] = e
        m.grad_p[j, b] = p
        m.tops[j, pl.ds(b, 1), :] = top
        m.sums[j, pl.ds(b, 1), :] = jnp.sum(e, 0, keepdims=True)
        m.deltas[j, pl.ds(b, 1), :] = jnp.sum(e * p, 0, keepdims=True)

    def block(dk, dx):
        other = core + dk - 2 * core * dk
        return other * 4 + lax.rem(x + dx, 4)

    def key(dz):
        return lax.rem(z + dz, 4)

    def tiles(count, unroll, which):
        def step(n, carry):
            dk, dx, dz = which(n)
            tile(block(dk, dx), key(dz))
            return carry

        lax.fori_loop(0, count, step, 0, unroll=unroll)

    project(z)
    g_on[1].wait_recv()
    g_on[3].wait_recv()
    far_x = core * 4 + lax.rem(x + 2, 4)
    at.g_first[2].wait_recv()
    q_first[2].wait_recv()
    tiles(2, 2, lambda n: (n, 0, 0))
    for t in range(3):
        for n in range(3):
            piece = jnp.concatenate([m.w[9 * t + 3 * h + n] for h in range(3)], 0)
            m.w_t[t, pl.ds(384 * n, 384), :] = piece.T
    n_on = relay_ring(n_first, m.norm, 0, z, 128, at.zs, False)
    q_on = relay_ring(q_first, q, core * 4, x, 192, at.xs, True)
    g_on[0].wait_recv()
    g_on[2].wait_recv()
    g_last = links.copy(g.at[far_x], g.at[far_x], sibling)
    project(key(1))
    project(key(3))
    tiles(4, 4, lambda n: (n // 2, 0, 1 + 2 * lax.rem(n, 2)))
    q_on[1].wait_recv()
    q_on[3].wait_recv()

    def beside(n):
        dz = n // 4
        return lax.rem(n // 2, 2), 1 + 2 * lax.rem(n, 2), dz + dz // 2

    tiles(12, 4, beside)
    q_on[0].wait_recv()
    q_on[2].wait_recv()
    q_last = links.copy(q.at[far_x], q.at[far_x], sibling)
    n_on[0].wait_recv()
    n_on[1].wait_recv()
    project(key(2))

    def beyond(n):
        dx = n // 2
        return lax.rem(n, 2), dx + dx // 2, 2

    tiles(6, 3, beyond)
    tiles(4, 4, lambda n: (0, 2, n))
    q_last.wait_recv()
    g_last.wait_recv()
    tiles(4, 4, lambda n: (1, 2, n))

    tops = [m.tops[j] for j in range(4)]
    top = functools.reduce(jnp.maximum, tops)
    shift = [jnp.exp(t - top) for t in tops]
    m.stats[0] = top
    m.stats[1] = sum(m.sums[j] * shift[j] for j in range(4))
    m.stats[2] = sum(m.deltas[j] * shift[j] for j in range(4))
    peers = at.xs + at.cross + [sibling]
    shared = [links.copy(m.stats, m.all_stats.at[n], to) for n, to in enumerate(peers)]
    for copy in shared:
        copy.wait_recv()
    parts = [m.stats] + [m.all_stats.at[n] for n in range(7)]
    top = functools.reduce(jnp.maximum, [p[0] for p in parts])
    total = sum(p[1] * jnp.exp(p[0] - top) for p in parts)
    m.delta[...] = sum(p[2] * jnp.exp(p[0] - top) for p in parts) / total
    for j in range(4):
        m.weights[j] = jnp.exp(m.tops[j] - top) / total

    def rows_of(j):
        return pl.ds(pl.multiple_of(256 * j, 256), 256)

    def weigh(b, j):
        prob = m.exps[j, b] * m.weights[j, pl.ds(b, 1), :]
        m.prob[b, rows_of(j), :] = prob.astype(BF16)
        m.grad_s[b, rows_of(j), :] = (prob * (m.grad_p[j, b] - m.delta[pl.ds(b, 1), :])).astype(BF16)

    def key_grad(j):
        for_k = sum(dot_t(m.grad_s[b, rows_of(j), :], q[b]) for b in range(8)) * scale
        for_v = sum(dot_t(m.prob[b, rows_of(j), :], g[b]) for b in range(8))
        return dot_t(w_qkv[:, 384:768], for_k.astype(BF16)) + dot_t(w_qkv[:, 768:], for_v.astype(BF16))

    halves = [pl.ds(0, 192), pl.ds(192, 192)]
    rings = ((at.zs[0], at.zs[2]), (at.xs[0], at.xs[2]))
    by_way, back = {}, []

    def send_far(kind, value):
        m.far[kind] = value.astype(BF16)
        for i in range(2):
            by_way[kind, i] = links.copy(m.far.at[kind, halves[i]], m.via.at[kind, i], rings[kind][i])

    def send_half(kind, i, half, value):
        m.send[kind, i, halves[half]] = value.astype(BF16)
        src, dst = m.send.at[kind, i, halves[half]], m.came.at[kind, i, halves[half]]
        back.append(links.copy(src, dst, rings[kind][i]))

    def send_near(kind, i, value):
        m.nearest[kind, i] = value
        send_half(kind, i, 1 - i, value[192 * (1 - i) : 192 * (2 - i)])

    def send_added(kind):
        for i in range(2):
            by_way[kind, i].wait_recv()
            send_half(kind, i, i, m.nearest[kind, i, halves[i], :] + m.via[kind, i].astype(F32))

    def weigh_all(dk):
        def step(n, carry):
            weigh(block(dk, lax.rem(n, 4)), key(n // 4))
            return carry

        lax.fori_loop(0, 16, step, 0, unroll=4)

    def query_grads(dk, put):
        def step(dx, carry):
            put(dx, dot(k_t[...], m.grad_s[block(dk, dx)]) * scale)
            return carry

        lax.fori_loop(0, 4, step, 0)

    def for_sibling(dx, value):
        m.sib_out[dx] = value.astype(BF16)

    def for_own(dx, value):
        m.own_q[dx] = value

    weigh_all(1)
    query_grads(1, for_sibling)
    sib = links.copy(m.sib_out, m.sib_in, sibling)
    weigh_all(0)
    send_far(0, key_grad(key(2)))
    query_grads(0, for_own)
    sib.wait_recv()

    def query_grad(dx):
        return m.own_q[dx] + m.sib_in[dx].astype(F32)

    send_far(1, query_grad(2))
    send_near(1, 0, query_grad(1))
    send_near(1, 1, query_grad(3))

    def near_keys(i, carry):
        m.nearest[0, i] = key_grad(key(1 + 2 * i))
        return carry

    lax.fori_loop(0, 2, near_keys, 0)
    for i in range(2):
        send_half(0, i, 1 - i, m.nearest[0, i, halves[1 - i], :])
    send_added(0)
    send_added(1)
    m.own_sum[0] = key_grad(z)
    m.own_sum[1] = query_grad(0)
    for copy in back:
        copy.wait_recv()
    by_key, by_query = [
        m.own_sum[n] + m.came[n, 0].astype(F32) + m.came[n, 1].astype(F32) for n in range(2)
    ]
    back_normed = dot(w_qkv[:, :384], by_query.astype(BF16)) + by_key
    scaled = back_normed.astype(BF16).astype(F32) * gain
    centre = m.full[...].astype(F32)
    inner = jnp.mean(centre * scaled, 0, keepdims=True)
    out = m.cot_full[...].astype(F32) + inv * scaled - centre * (inv * inv * inv * inner)
    for b in range(CH):
        for h in range(2):
            m.grad[b, h] = out[96 * b : 96 * b + 96, 128 * h : 128 * h + 128].astype(BF16)
    row_low, row_high = near_rows(at.row)
    for b in range(CH):
        to = at.sources[b]
        links.copy(m.grad.at[b], m.own.at[at.frame], to, own=same(to, at.me), recv=OWN + at.frame)
    for b in range(CH):
        links.copy(m.grad.at[b, 1], m.prev_g.at[at.frame], (row_high, b), recv=PREV + at.frame)
        links.copy(m.grad.at[b, 0], m.next_g.at[at.frame], (row_low, b), recv=NEXT + at.frame)


def tail(links, at, m):
    r, c, x, y_hi, z = at.r, at.c, at.x, at.y_hi, at.z
    xs, zs, across, chs = at.xs, at.zs, at.across, at.chs
    own, act, w_t, every, inv_in, gain_rows = m.own, m.act, m.w_t, m.every, m.inv_in, m.gain_rows
    rows, lines, weight, part, all_part, inner, all_inner = m.rows, m.lines, m.weight, m.part, m.all_part, m.inner, m.all_inner
    mark, flat, out = m.mark, m.flat, m.out
    ring_x = (x, [lax.rem(x + d, 4) for d in range(1, 4)], xs)
    ring_z = (z, [lax.rem(z + d, 4) for d in range(1, 4)], zs)
    ring_y = (y_hi, [1 - y_hi], [across])
    stripes = []
    for n, (base, size, rings) in enumerate(
        (
            (0, 2048, (ring_y, ring_x, ring_z)),
            (2048, 3072, (ring_x, ring_z, ring_y)),
            (5120, 3072, (ring_z, ring_y, ring_x)),
        )
    ):
        steps, at_row = [], base
        for p, (place_on, places, peers) in enumerate(rings):
            size //= len(peers) + 1
            start = at_row
            at_row = at_row + place_on * size
            came, total = getattr(m, "came_%d_%d" % (n, p)), getattr(m, "total_%d_%d" % (n, p))
            steps.append((start, size, places, peers, at_row, came, total))
        stripes.append(steps)

    def rows_at(start, size):
        return pl.ds(pl.multiple_of(start, 16), size)

    def give(steps, p):
        start, size, places, peers, _, came, _ = steps[p]
        sent = []
        for d, peer in enumerate(peers):
            if p == 0:
                src = weight.at[rows_at(start + places[d] * size, size)]
            else:
                src = steps[p - 1][6].at[rows_at(places[d] * size, size)]
            sent.append(links.copy(src, came.at[d], peer))
        return sent

    def take(steps, p, sent):
        start, size, _, peers, mine, came, total = steps[p]
        for copy in sent:
            copy.wait_recv()
        if p == 0:
            value = weight[rows_at(mine, size), :].astype(F32)
        else:
            value = steps[p - 1][6][rows_at(mine - start, size), :].astype(F32)
        for d in range(len(peers)):
            value += came[d].astype(F32)
        total[...] = value.astype(BF16)

    def prepare(f, h):
        y = rows[f, h].astype(F32)
        m.moved[f, :, pl.ds(128 * h, 128)] = jnp.concatenate([move(y, -1), y, move(y, 1)], 0).astype(BF16)

    for f in range(4):
        links.arrive(own.at[f], OWN + f)
    for f in range(4):
        for h in range(2):
            rows[f, h + 1] = own[f, h]
            prepare(f, h + 1)
    for f in range(4):
        links.arrive(m.prev_g.at[f], PREV + f)
        links.arrive(m.next_g.at[f], NEXT + f)
    for f in range(4):
        rows[f, 0] = jnp.where(r == 0, 0.0, m.prev_g[f].astype(F32)).astype(BF16)
        rows[f, 3] = jnp.where(r == ROWS - 1, 0.0, m.next_g[f].astype(F32)).astype(BF16)
        prepare(f, 0)
        prepare(f, 3)
    first = []
    for t in range(3):
        for h in range(3):
            acc = jnp.zeros((288, 384), F32)
            for f in range(4):
                source = f + t - 2
                if source < 0:
                    continue
                acc += dot_t(m.moved[f, :, pl.ds(128 * (2 - h), 256)], act[:, pl.ds(256 * source, 256)])
            for lane in range(3):
                line = (3 * (3 * t + h) + lane) * 288
                weight[pl.ds(line, 288), :] = acc[:, 128 * lane : 128 * lane + 128].astype(BF16)
        if t == 2:
            weight[pl.ds(27 * 288, 416), :] = jnp.zeros((416, 128), BF16)
        first.append(give(stripes[t], 0))
    for f in range(4):
        for h in range(3):
            for k in range(2):
                lines[f, pl.ds(96 * h, 96), pl.ds(128 * k, 128)] = rows[f, 2 - h + k]
    gain = gain_columns(gain_rows, 0)
    for f in range(4):
        acc = jnp.zeros((1152, 256), F32)
        for t in range(3):
            source = f + 2 - t
            if source > 3:
                continue
            acc += dot(w_t[t], lines[source])
        for h in range(2):
            y = acc[:, 128 * h : 128 * h + 128]
            total = move(y[:384], -1) + y[384:768] + move(y[768:], 1)
            v = jnp.concatenate([every[b, f, h] for b in range(CH)], 0).astype(F32)
            before = v * inv_in[2 * f + h : 2 * f + h + 1, :] * gain
            sig = sigmoid(before)
            slope = sig * (1.0 + before * (1.0 - sig))
            inner[2 * f + h : 2 * f + h + 1, :] = jnp.sum(v * slope * gain * total, 0, keepdims=True)
            for b in range(CH):
                part[b, f, h] = total[96 * b : 96 * b + 96].astype(BF16)
    second, third, parts = [], [], []
    parts.append(links.copy(part.at[at.sibling[1]], all_part.at[0], at.sibling))
    joined = links.copy(part.at[(1 - at.y_lo) * 2 + 1 - at.core], m.assist, at.sibling)
    for d in range(3):
        parts.append(links.copy(inner, all_inner.at[d], chs[d]))
    for n, steps in enumerate(stripes):
        take(steps, 0, first[n])
        second.append(give(steps, 1))
    joined.wait_recv()
    for f in range(4):
        both = part[at.c_near, f].astype(F32) + m.assist[f].astype(F32)
        m.near_part[f] = both.astype(BF16)
    parts.append(links.copy(m.near_part, all_part.at[1], at.near))
    for n, steps in enumerate(stripes):
        take(steps, 1, second[n])
        third.append(give(steps, 2))
    spread, kept = [], []
    for n, steps in enumerate(stripes):
        take(steps, 2, third[n])
        _, size, _, peers, mine, _, total = steps[2]
        m.spread[rows_at(mine, size), :] = total[...]
        spread.append([links.copy(total, m.spread.at[rows_at(mine, size)], peer) for peer in peers])
    for p in (1, 0):
        for n, steps in enumerate(stripes):
            for copy in spread[n]:
                copy.wait_recv()
            _, size, _, peers, mine, _, _ = steps[p]
            src = dst = m.spread.at[rows_at(mine, size)]
            if p == 0:
                dst = flat.at[rows_at(mine, size)]
                kept.append(pltpu.make_async_copy(src, dst, mark.at[n]))
                kept[n].start()
            spread[n] = [links.copy(src, dst, peer) for peer in peers]
    for copy in parts:
        copy.wait_recv()
    mean = (inner[...] + all_inner[0] + all_inner[1] + all_inner[2]) / 384.0
    gain = jnp.broadcast_to(gain_rows[c, 0:1, :], (128, 128)).T[:96]
    for f in range(4):
        for h in range(2):
            v = every[c, f, h].astype(F32)
            inv = inv_in[2 * f + h : 2 * f + h + 1, :]
            total = part[c, f, h].astype(F32)
            for d in range(2):
                total += all_part[d, f, h].astype(F32)
            before = v * inv * gain
            sig = sigmoid(before)
            scaled = total * (sig * (1.0 + before * (1.0 - sig))) * gain
            cube = inv * inv * inv * mean[2 * f + h : 2 * f + h + 1, :]
            out[f, h] = (own[f, h].astype(F32) + inv * scaled - v * cube).astype(BF16)
    for copy in kept:
        copy.wait()
    for copy in spread[0] + spread[1] + spread[2]:
        copy.wait_recv()


def whole(links, m):
    at = Place()
    front(links, at, m)
    attention(links, at, m)
    tail(links, at, m)
    links.finish()


def widen_kernel(scale, flat, grad, out, grad_out, near, wide, through, into, back):
    come = [
        pltpu.make_async_copy(flat.at[pl.ds(864 * k, 864)], near.at[k], into.at[k]) for k in range(9)
    ]
    go = [
        pltpu.make_async_copy(wide.at[k], out.at[pl.ds(288 * k, 288)], back.at[k]) for k in range(9)
    ]
    enter = pltpu.make_async_copy(grad, through, into.at[9])
    leave = pltpu.make_async_copy(through, grad_out, back.at[9])
    for copy in come:
        copy.start()
    enter.start()
    for k in range(9):
        if k == 4:
            enter.wait()
            leave.start()
        come[k].wait()
        for lane in range(3):
            piece = near[k, pl.ds(288 * lane, 288), :].astype(F32) * scale
            wide[k, :, pl.ds(128 * lane, 128)] = piece
        go[k].start()
    for copy in go:
        copy.wait()
    leave.wait()


def on_device(features, gain_in, w_conv, gain_attn, w_qkv, w_out, cotangent):
    near, far = pltpu.VMEM, pl.ANY
    held = {
        "feat": (features, far),
        "cot": (cotangent, far),
        "w_far": (w_conv, far),
        "gain_in": (gain_in.reshape(1, 96), near),
        "gain_attn": (gain_attn.reshape(1, 96), near),
        "w_qkv_far": (w_qkv, far),
        "w_out_far": (w_out, far),
    }
    made = {"out": ((4, 2, 96, 128), BF16, near), "flat": ((8192, 128), BF16, far)}
    b16 = {
        "every": (4, 4, 2, 96, 128),
        "w": (27, 96, 384),
        "w_qkv": (384, 1152),
        "w_out": (384, 384),
        "act": (384, 1024),
        "edge_out": (2, 4, 96, 128),
        "edge_in": (2, 4, 96, 128),
        "moved": (4, 288, 512),
        "res": (4, 2, 96, 128),
        "cot_frame": (4, 2, 96, 128),
        "res_frame": (4, 2, 96, 128),
        "full": (384, 256),
        "cot_full": (384, 256),
        "norm": (4, 256, 384),
        "q": (8, 384, 256),
        "g": (8, 384, 256),
        "k": (4, 256, 384),
        "v": (4, 256, 384),
        "k_t": (384, 1024),
        "prob": (8, 1024, 256),
        "grad_s": (8, 1024, 256),
        "far": (2, 384, 256),
        "via": (2, 2, 192, 256),
        "send": (2, 2, 384, 256),
        "came": (2, 2, 384, 256),
        "sib_out": (4, 384, 256),
        "sib_in": (4, 384, 256),
        "grad": (4, 2, 96, 128),
        "own": (4, 2, 96, 128),
        "prev_g": (4, 96, 128),
        "next_g": (4, 96, 128),
        "w_t": (3, 1152, 288),
        "rows": (4, 4, 96, 128),
        "lines": (4, 288, 256),
        "weight": (8192, 128),
        "spread": (8192, 128),
        "part": (4, 4, 2, 96, 128),
        "all_part": (2, 4, 2, 96, 128),
        "assist": (4, 2, 96, 128),
        "near_part": (4, 2, 96, 128),
    }
    for n, (size, counts) in enumerate(((2048, (2, 4, 4)), (3072, (4, 4, 2)), (3072, (4, 2, 4)))):
        for p, count in enumerate(counts):
            size //= count
            b16["came_%d_%d" % (n, p)] = (count - 1, size, 128)
            b16["total_%d_%d" % (n, p)] = (size, 128)
    f32 = {
        "inv_in": (8, 128),
        "conv_own": (4, 2, 96, 128),
        "gain_rows": (4, 8, 128),
        "exps": (4, 8, 256, 256),
        "grad_p": (4, 8, 256, 256),
        "tops": (4, 8, 256),
        "sums": (4, 8, 256),
        "deltas": (4, 8, 256),
        "stats": (3, 8, 256),
        "all_stats": (7, 3, 8, 256),
        "weights": (4, 8, 256),
        "delta": (8, 256),
        "nearest": (2, 2, 384, 256),
        "own_sum": (2, 384, 256),
        "own_q": (4, 384, 256),
        "inner": (8, 128),
        "all_inner": (3, 8, 128),
    }
    scratch = {n: pltpu.VMEM(s, BF16) for n, s in b16.items()}
    scratch |= {n: pltpu.VMEM(s, F32) for n, s in f32.items()}
    scratch["mark"] = pltpu.SemaphoreType.DMA((4,))
    out, flat = fused(0, whole, held, made, scratch, (SENDS, NEXT + 4))
    cell_scale = 1.0 / math.sqrt(32768)
    grad_weights, out = pl.pallas_call(
        functools.partial(widen_kernel, cell_scale),
        out_shape=[jax.ShapeDtypeStruct((2592, 384), F32), jax.ShapeDtypeStruct(out.shape, BF16)],
        in_specs=[pl.BlockSpec(memory_space=pl.ANY)] * 2,
        out_specs=[pl.BlockSpec(memory_space=pl.ANY)] * 2,
        scratch_shapes=[
            pltpu.VMEM((9, 864, 128), BF16),
            pltpu.VMEM((9, 288, 384), F32),
            pltpu.VMEM((4, 2, 96, 128), BF16),
            pltpu.SemaphoreType.DMA((10,)),
            pltpu.SemaphoreType.DMA((10,)),
        ],
        compiler_params=pltpu.CompilerParams(vmem_limit_bytes=VMEM_BYTES),
        name="widen",
    )(flat, out)
    return out, grad_weights.reshape(27, 96, 384)


def solution(mesh):
    return jax.shard_map(
        on_device,
        mesh=mesh,
        in_specs=(
            P(None, "row", "ch", None),
            P("ch"),
            P(None, "ch", None),
            P("ch"),
            P(),
            P(),
            P(None, "row", "ch", None),
        ),
        out_specs=(P(None, "row", "ch", None), P(None, "ch", None)),
        check_vma=False,
    )
```

```python
import functools
import math
import types

import jax
import jax.numpy as jnp
from jax import lax
from jax.experimental import pallas as pl
from jax.experimental.pallas import tpu as pltpu
from jax.sharding import PartitionSpec as P

EPSILON = 1e-06
MESH = pl.DeviceIdType.MESH
F32 = jnp.float32
BF16 = jnp.bfloat16
ROWS = 32
SENDS = 128
COT, RES, OWN, PREV, NEXT = range(SENDS, SENDS + 20, 4)
CH = 4
VMEM_BYTES = 60 * 1024 * 1024


def coords():
    return lax.axis_index("row"), lax.axis_index("ch")


def place(r, c):
    return lax.rem(r, 4), lax.rem(r // 4, 2), r // 8, c // 2, lax.rem(c, 2)


def device(x, y_hi, z, y_lo, core):
    return z * 8 + y_hi * 4 + x, y_lo * 2 + core


def owner(f, row):
    x, y_hi, z, _, _ = place(row, 0)
    return device(x, f // 2, z, f % 2, y_hi)


class Links:
    def __init__(self, send, recv):
        self.send, self.recv, self.sent, self.at = send, recv, [], 0

    def greet(self, peers, count):
        barrier = pltpu.get_barrier_semaphore()
        for peer in peers:
            pl.semaphore_signal(barrier, inc=1, device_id=peer, device_id_type=MESH)
        pl.semaphore_wait(barrier, count)

    def copy(self, src, dst, to, own=None, recv=None):
        k = self.at
        self.at += 1
        mark = self.recv.at[k if recv is None else recv]
        far = pltpu.make_async_remote_copy(
            src_ref=src,
            dst_ref=dst,
            send_sem=self.send.at[k],
            recv_sem=mark,
            device_id=to,
            device_id_type=MESH,
        )
        if own is None:
            far.start()
        else:
            pl.when(jnp.logical_not(own))(far.start)
            pl.when(own)(pltpu.make_async_copy(src, dst, mark).start)
        self.sent.append((far, own))
        return far

    def arrive(self, dst, k):
        pltpu.make_async_copy(dst, dst, self.recv.at[k]).wait()

    def finish(self):
        for far, own in self.sent:
            if own is None:
                far.wait_send()
            else:
                pl.when(jnp.logical_not(own))(far.wait_send)


def fused(cid, body, held, made, scratch, count):
    names = [*held, *made, *scratch]

    def kernel(*refs):
        body(Links(*refs[-2:]), types.SimpleNamespace(**dict(zip(names, refs))))

    return pl.pallas_call(
        kernel,
        out_shape=[jax.ShapeDtypeStruct(s, t) for s, t, _ in made.values()],
        in_specs=[pl.BlockSpec(memory_space=m) for _, m in held.values()],
        out_specs=[pl.BlockSpec(memory_space=m) for _, _, m in made.values()],
        scratch_shapes=[*scratch.values()] + [pltpu.SemaphoreType.DMA((n,)) for n in count],
        compiler_params=pltpu.CompilerParams(
            collective_id=cid, has_side_effects=True, vmem_limit_bytes=VMEM_BYTES
        ),
        name="fused_%d" % cid,
    )(*[array for array, _ in held.values()])


def dot(a, b):
    return lax.dot_general(a, b, (((1,), (0,)), ((), ())), preferred_element_type=F32)


def dot_t(a, b):
    return lax.dot_general(a, b, (((1,), (1,)), ((), ())), preferred_element_type=F32)


def move(block, by):
    lanes = block.shape[1]
    at = lax.broadcasted_iota(jnp.int32, block.shape, 1)
    if by > 0:
        return jnp.where(at == 0, 0.0, pltpu.roll(block, 1, axis=1))
    return jnp.where(at == lanes - 1, 0.0, pltpu.roll(block, lanes - 1, axis=1))


def ch_peers(r, c):
    return [(r, lax.rem(c + d, CH)) for d in range(1, CH)]


def near_rows(r):
    return lax.rem(r + ROWS - 1, ROWS), lax.rem(r + 1, ROWS)


def same(a, b):
    return jnp.logical_and(a[0] == b[0], a[1] == b[1])


def greet_frames(me, sources, targets):
    barrier = pltpu.get_barrier_semaphore()
    for peer in sources:
        def tell(peer=peer):
            pl.semaphore_signal(barrier, inc=1, device_id=peer, device_id_type=MESH)

        pl.when(jnp.logical_not(same(peer, me)))(tell)
    _, y_hi, _, _, core = place(*me)
    pl.semaphore_wait(barrier, len(targets) - 2 + 2 * (core - y_hi) * (core - y_hi))


def sigmoid(v):
    return 1.0 / (1.0 + jnp.exp(-v))


def gain_columns(rows, which):
    blocks = [jnp.broadcast_to(rows[b, which : which + 1, :], (128, 128)).T[:96] for b in range(CH)]
    return jnp.concatenate(blocks, 0)


class Place:
    def __init__(self):
        r, c = self.r, self.c = self.me = coords()
        x, y_hi, z, y_lo, core = self.x, self.y_hi, self.z, self.y_lo, self.core = place(r, c)
        self.slot = core * 4 + x
        self.frame = y_hi * 2 + y_lo
        self.low, self.high = near_rows(r)
        self.c_near = (1 - y_lo) * 2 + core
        self.sibling = (r, y_lo * 2 + 1 - core)
        self.near = (r, self.c_near)
        self.chs = ch_peers(r, c)
        self.xs = [device(lax.rem(x + d, 4), y_hi, z, y_lo, core) for d in range(1, 4)]
        self.cross = [device(lax.rem(x + d, 4), y_hi, z, y_lo, 1 - core) for d in range(1, 4)]
        self.zs = [device(x, y_hi, lax.rem(z + d, 4), y_lo, core) for d in range(1, 4)]
        self.across = device(x, 1 - y_hi, z, y_lo, core)
        self.targets = [owner(f, r) for f in range(4)]
        self.row = z * 8 + core * 4 + x
        self.sources = [(self.row, b) for b in range(CH)]

    def greet(self):
        at = self
        alike = at.chs + at.xs + at.cross + at.zs + [at.across, (at.low, at.c), (at.high, at.c)]
        there = [(i, b) for i in near_rows(at.row) for b in range(CH)]
        whose = [owner(f, i) for i in (at.low, at.high) for f in range(4)]
        greet_frames(at.me, at.targets + at.sources + whose + alike, at.targets + at.sources + there + alike)


def relay_ring(links, sibling, first, ref, base, i, rows, peers, forward):
    on = []
    for side in range(2):
        first[side].wait_recv()
        came = base + lax.rem(i + 3 - 2 * side, 4)
        part = ref.at[came, pl.ds(rows * side, rows)]
        on.append(links.copy(part, part, peers[2 * side]))
        if forward:
            on.append(links.copy(ref.at[came], ref.at[came], sibling))
    return on


def front(links, at, m):
    r, c, near, sibling = at.r, at.c, at.near, at.sibling
    every, act = m.every, m.act
    here = pltpu.make_async_copy(m.feat, every.at[c], m.mark.at[0])
    here.start()
    weights = pltpu.make_async_copy(m.w_far, m.w, m.mark.at[1])
    weights.start()
    projections = [
        pltpu.make_async_copy(m.w_out_far, m.w_out, m.mark.at[2]),
        pltpu.make_async_copy(m.w_qkv_far, m.w_qkv, m.mark.at[3]),
    ]
    for copy in projections:
        copy.start()
    m.gain_rows[c] = jnp.zeros((8, 128), F32)
    pad = jnp.zeros((1, 32), F32)
    m.gain_rows[c, 0:1, :] = jnp.concatenate([m.gain_in[...].astype(F32), pad], 1)
    m.gain_rows[c, 1:2, :] = jnp.concatenate([m.gain_attn[...].astype(F32), pad], 1)
    at.greet()
    pairs = [pl.ds(2 * p, 2) for p in range(2)]
    gains = [links.copy(m.gain_rows.at[c], m.gain_rows.at[c], to) for to in at.chs]
    to_near = [links.copy(m.feat.at[two], every.at[c, two], near) for two in pairs]
    to_sib = links.copy(m.feat, every.at[c], sibling)
    for f in range(4):
        own = same(at.targets[f], at.me)
        links.copy(m.cot.at[f], m.cot_frame.at[c], at.targets[f], own=own, recv=COT + c)
    for copy in gains:
        copy.wait_recv()
    gain = gain_columns(m.gain_rows, 0)
    passed = []
    for p, two in enumerate(pairs):
        to_near[p].wait_recv()
        part = every.at[at.c_near, two]
        passed.append(links.copy(part, part, sibling))

    def activate(n):
        v = jnp.concatenate([every[b, n // 2, lax.rem(n, 2)] for b in range(CH)], 0).astype(F32)
        inv = lax.rsqrt(jnp.mean(v * v, 0, keepdims=True) + EPSILON)
        before = v * inv * gain
        m.inv_in[pl.ds(n, 1), :] = inv
        act[:, pl.ds(pl.multiple_of(128 * n, 128), 128)] = (before * sigmoid(before)).astype(BF16)

    for b in range(CH):
        links.arrive(m.cot_frame.at[b], COT + b)
    for b in range(CH):
        for h in range(2):
            m.cot_full[pl.ds(96 * b, 96), pl.ds(128 * h, 128)] = m.cot_frame[b, h]
    for copy in projections:
        copy.wait()
    m.g[at.slot] = dot(m.w_out[...], m.cot_full[...]).astype(BF16)
    at.g_first = [links.copy(m.g.at[at.slot], m.g.at[at.slot], to) for to in (at.xs[0], at.xs[2], sibling)]
    here.wait()
    to_sib.wait_recv()
    weights.wait()
    edges = []
    for p, two in enumerate(pairs):
        passed[p].wait_recv()

        def step(n, carry, p=p):
            activate(4 * p + n)
            return carry

        lax.fori_loop(0, 4, step, 0, unroll=2)
        for f in (2 * p, 2 * p + 1):
            by_tap = []
            for h in range(3):
                acc = jnp.zeros((288, 256), F32)
                for t in range(3):
                    source = f + t - 2
                    if source >= 0:
                        taps = m.w[pl.ds(9 * t + 3 * h, 3)].reshape(288, 384)
                        acc += dot(taps, act[:, pl.ds(256 * source, 256)])
                by_tap.append((acc[:, :128], acc[:, 128:]))
            lines = (
                by_tap[2][0],
                by_tap[2][1] + by_tap[1][0],
                by_tap[1][1] + by_tap[0][0],
                by_tap[0][1],
            )
            lines = [move(y[:96], 1) + y[96:192] + move(y[192:], -1) for y in lines]
            m.edge_out[0, f] = lines[0].astype(BF16)
            m.edge_out[1, f] = lines[3].astype(BF16)
            m.conv_own[f, 0] = lines[1]
            m.conv_own[f, 1] = lines[2]
        edges.append(links.copy(m.edge_out.at[0, two], m.edge_in.at[0, two], (at.low, c)))
        edges.append(links.copy(m.edge_out.at[1, two], m.edge_in.at[1, two], (at.high, c)))
    at.g_on = relay_ring(links, sibling, at.g_first, m.g, at.core * 4, at.x, 192, at.xs, True)
    for p in range(2):
        edges[2 * p].wait_recv()
        edges[2 * p + 1].wait_recv()
        for f in (2 * p, 2 * p + 1):
            before = jnp.where(r == 0, 0.0, m.edge_in[1, f].astype(F32))
            after = jnp.where(r == ROWS - 1, 0.0, m.edge_in[0, f].astype(F32))
            m.res[f, 0] = (every[c, f, 0].astype(F32) + (m.conv_own[f, 0] + before)).astype(BF16)
            m.res[f, 1] = (every[c, f, 1].astype(F32) + (m.conv_own[f, 1] + after)).astype(BF16)
            own = same(at.targets[f], at.me)
            links.copy(m.res.at[f], m.res_frame.at[c], at.targets[f], own=own, recv=RES + c)


def attention(links, at, m):
    scale = 1.0 / math.sqrt(384)
    x, z, core, slot, sibling = at.x, at.z, at.core, at.slot, at.sibling
    q, g, k, v, k_t = m.q, m.g, m.k, m.v, m.k_t
    w_qkv = m.w_qkv

    g_on = at.g_on
    gain = gain_columns(m.gain_rows, 1)
    gain = jnp.concatenate([gain, gain], 1)
    for b in range(CH):
        links.arrive(m.res_frame.at[b], RES + b)
    for b in range(CH):
        for h in range(2):
            m.full[pl.ds(96 * b, 96), pl.ds(128 * h, 128)] = m.res_frame[b, h]
    centre = m.full[...].astype(F32)
    inv = lax.rsqrt(jnp.mean(centre * centre, 0, keepdims=True) + EPSILON)
    m.norm[z] = (centre * inv * gain).astype(BF16).astype(F32).T.astype(BF16)
    n_first = [links.copy(m.norm.at[z], m.norm.at[z], to) for to in (at.zs[0], at.zs[2])]
    q[slot] = dot(m.norm[z], w_qkv[:, :384]).T.astype(BF16)
    q_first = [links.copy(q.at[slot], q.at[slot], to) for to in (at.xs[0], at.xs[2], sibling)]

    def project(j):
        k[j] = dot(m.norm[j], w_qkv[:, 384:768]).astype(BF16)
        v[j] = dot(m.norm[j], w_qkv[:, 768:]).astype(BF16)
        k_t[:, pl.ds(pl.multiple_of(256 * j, 256), 256)] = k[j].T

    def tile(b, j):
        s = dot(k[j], q[b]) * scale
        top = jnp.max(s, 0, keepdims=True)
        e = jnp.exp(s - top)
        p = dot(v[j], g[b])
        m.exps[j, b] = e
        m.grad_p[j, b] = p
        m.tops[j, pl.ds(b, 1), :] = top
        m.sums[j, pl.ds(b, 1), :] = jnp.sum(e, 0, keepdims=True)
        m.deltas[j, pl.ds(b, 1), :] = jnp.sum(e * p, 0, keepdims=True)

    def block(dk, dx):
        other = core + dk - 2 * core * dk
        return other * 4 + lax.rem(x + dx, 4)

    def key(dz):
        return lax.rem(z + dz, 4)

    def tiles(count, unroll, which):
        def step(n, carry):
            dk, dx, dz = which(n)
            tile(block(dk, dx), key(dz))
            return carry

        lax.fori_loop(0, count, step, 0, unroll=unroll)

    project(z)
    g_on[1].wait_recv()
    g_on[3].wait_recv()
    far_x = core * 4 + lax.rem(x + 2, 4)
    at.g_first[2].wait_recv()
    q_first[2].wait_recv()
    tiles(2, 2, lambda n: (n, 0, 0))
    for t in range(3):
        for n in range(3):
            piece = jnp.concatenate([m.w[9 * t + 3 * h + n] for h in range(3)], 0)
            m.w_t[t, pl.ds(384 * n, 384), :] = piece.T
    n_on = relay_ring(links, sibling, n_first, m.norm, 0, z, 128, at.zs, False)
    q_on = relay_ring(links, sibling, q_first, q, core * 4, x, 192, at.xs, True)
    g_on[0].wait_recv()
    g_on[2].wait_recv()
    g_last = links.copy(g.at[far_x], g.at[far_x], sibling)
    project(key(1))
    project(key(3))
    tiles(4, 4, lambda n: (n // 2, 0, 1 + 2 * lax.rem(n, 2)))
    q_on[1].wait_recv()
    q_on[3].wait_recv()

    def beside(n):
        dz = n // 4
        return lax.rem(n // 2, 2), 1 + 2 * lax.rem(n, 2), dz + dz // 2

    tiles(12, 4, beside)
    q_on[0].wait_recv()
    q_on[2].wait_recv()
    q_last = links.copy(q.at[far_x], q.at[far_x], sibling)
    n_on[0].wait_recv()
    n_on[1].wait_recv()
    project(key(2))

    def beyond(n):
        dx = n // 2
        return lax.rem(n, 2), dx + dx // 2, 2

    tiles(6, 3, beyond)
    tiles(4, 4, lambda n: (0, 2, n))
    q_last.wait_recv()
    g_last.wait_recv()
    tiles(4, 4, lambda n: (1, 2, n))

    tops = [m.tops[j] for j in range(4)]
    top = functools.reduce(jnp.maximum, tops)
    shift = [jnp.exp(t - top) for t in tops]
    m.stats[0] = top
    m.stats[1] = sum(m.sums[j] * shift[j] for j in range(4))
    m.stats[2] = sum(m.deltas[j] * shift[j] for j in range(4))
    peers = at.xs + at.cross + [sibling]
    shared = [links.copy(m.stats, m.all_stats.at[n], to) for n, to in enumerate(peers)]
    for copy in shared:
        copy.wait_recv()
    parts = [m.stats] + [m.all_stats.at[n] for n in range(7)]
    top = functools.reduce(jnp.maximum, [p[0] for p in parts])
    total = sum(p[1] * jnp.exp(p[0] - top) for p in parts)
    m.delta[...] = sum(p[2] * jnp.exp(p[0] - top) for p in parts) / total
    for j in range(4):
        m.weights[j] = jnp.exp(m.tops[j] - top) / total

    def rows_of(j):
        return pl.ds(pl.multiple_of(256 * j, 256), 256)

    def weigh(b, j):
        prob = m.exps[j, b] * m.weights[j, pl.ds(b, 1), :]
        m.prob[b, rows_of(j), :] = prob.astype(BF16)
        m.grad_s[b, rows_of(j), :] = (prob * (m.grad_p[j, b] - m.delta[pl.ds(b, 1), :])).astype(BF16)

    def key_grad(j):
        for_k = sum(dot_t(m.grad_s[b, rows_of(j), :], q[b]) for b in range(8)) * scale
        for_v = sum(dot_t(m.prob[b, rows_of(j), :], g[b]) for b in range(8))
        return dot_t(w_qkv[:, 384:768], for_k.astype(BF16)) + dot_t(w_qkv[:, 768:], for_v.astype(BF16))

    halves = [pl.ds(0, 192), pl.ds(192, 192)]
    rings = ((at.zs[0], at.zs[2]), (at.xs[0], at.xs[2]))
    by_way, back = {}, []

    def send_far(kind, value):
        m.far[kind] = value.astype(BF16)
        for i in range(2):
            by_way[kind, i] = links.copy(m.far.at[kind, halves[i]], m.via.at[kind, i], rings[kind][i])

    def send_half(kind, i, half, value):
        m.send[kind, i, halves[half]] = value.astype(BF16)
        src, dst = m.send.at[kind, i, halves[half]], m.came.at[kind, i, halves[half]]
        back.append(links.copy(src, dst, rings[kind][i]))

    def send_near(kind, i, value):
        m.nearest[kind, i] = value
        send_half(kind, i, 1 - i, value[192 * (1 - i) : 192 * (2 - i)])

    def send_added(kind):
        for i in range(2):
            by_way[kind, i].wait_recv()
            send_half(kind, i, i, m.nearest[kind, i, halves[i], :] + m.via[kind, i].astype(F32))

    def weigh_all(dk):
        def step(n, carry):
            weigh(block(dk, lax.rem(n, 4)), key(n // 4))
            return carry

        lax.fori_loop(0, 16, step, 0, unroll=4)

    def query_grads(dk, put):
        def step(dx, carry):
            put(dx, dot(k_t[...], m.grad_s[block(dk, dx)]) * scale)
            return carry

        lax.fori_loop(0, 4, step, 0)

    def for_sibling(dx, value):
        m.sib_out[dx] = value.astype(BF16)

    def for_own(dx, value):
        m.own_q[dx] = value

    weigh_all(1)
    query_grads(1, for_sibling)
    sib = links.copy(m.sib_out, m.sib_in, sibling)
    weigh_all(0)
    send_far(0, key_grad(key(2)))
    query_grads(0, for_own)
    sib.wait_recv()

    def query_grad(dx):
        return m.own_q[dx] + m.sib_in[dx].astype(F32)

    send_far(1, query_grad(2))
    send_near(1, 0, query_grad(1))
    send_near(1, 1, query_grad(3))

    def near_keys(i, carry):
        m.nearest[0, i] = key_grad(key(1 + 2 * i))
        return carry

    lax.fori_loop(0, 2, near_keys, 0)
    for i in range(2):
        send_half(0, i, 1 - i, m.nearest[0, i, halves[1 - i], :])
    send_added(0)
    send_added(1)
    m.own_sum[0] = key_grad(z)
    m.own_sum[1] = query_grad(0)
    for copy in back:
        copy.wait_recv()
    by_key, by_query = [
        m.own_sum[n] + m.came[n, 0].astype(F32) + m.came[n, 1].astype(F32) for n in range(2)
    ]
    back_normed = dot(w_qkv[:, :384], by_query.astype(BF16)) + by_key
    scaled = back_normed.astype(BF16).astype(F32) * gain
    centre = m.full[...].astype(F32)
    inner = jnp.mean(centre * scaled, 0, keepdims=True)
    out = m.cot_full[...].astype(F32) + inv * scaled - centre * (inv * inv * inv * inner)
    for b in range(CH):
        for h in range(2):
            m.grad[b, h] = out[96 * b : 96 * b + 96, 128 * h : 128 * h + 128].astype(BF16)
    row_low, row_high = near_rows(at.row)
    for b in range(CH):
        to = at.sources[b]
        links.copy(m.grad.at[b], m.own.at[at.frame], to, own=same(to, at.me), recv=OWN + at.frame)
    for b in range(CH):
        links.copy(m.grad.at[b, 1], m.prev_g.at[at.frame], (row_high, b), recv=PREV + at.frame)
        links.copy(m.grad.at[b, 0], m.next_g.at[at.frame], (row_low, b), recv=NEXT + at.frame)


def tail(links, at, m):
    r, c, x, y_hi, z = at.r, at.c, at.x, at.y_hi, at.z
    xs, zs, across, chs = at.xs, at.zs, at.across, at.chs
    own, act, w_t, every, inv_in, gain_rows = m.own, m.act, m.w_t, m.every, m.inv_in, m.gain_rows
    rows, lines, weight, part, all_part, inner, all_inner = m.rows, m.lines, m.weight, m.part, m.all_part, m.inner, m.all_inner
    mark, flat, out = m.mark, m.flat, m.out
    ring_x = (x, [lax.rem(x + d, 4) for d in range(1, 4)], xs)
    ring_z = (z, [lax.rem(z + d, 4) for d in range(1, 4)], zs)
    ring_y = (y_hi, [1 - y_hi], [across])
    stripes = []
    for n, (base, size, rings) in enumerate(
        (
            (0, 2048, (ring_y, ring_x, ring_z)),
            (2048, 3072, (ring_x, ring_z, ring_y)),
            (5120, 3072, (ring_z, ring_y, ring_x)),
        )
    ):
        steps, at_row = [], base
        for p, (place_on, places, peers) in enumerate(rings):
            size //= len(peers) + 1
            start = at_row
            at_row = at_row + place_on * size
            came, total = getattr(m, "came_%d_%d" % (n, p)), getattr(m, "total_%d_%d" % (n, p))
            steps.append((start, size, places, peers, at_row, came, total))
        stripes.append(steps)

    def rows_at(start, size):
        return pl.ds(pl.multiple_of(start, 16), size)

    def give(steps, p):
        start, size, places, peers, _, came, _ = steps[p]
        sent = []
        for d, peer in enumerate(peers):
            if p == 0:
                src = weight.at[rows_at(start + places[d] * size, size)]
            else:
                src = steps[p - 1][6].at[rows_at(places[d] * size, size)]
            sent.append(links.copy(src, came.at[d], peer))
        return sent

    def take(steps, p, sent):
        start, size, _, peers, mine, came, total = steps[p]
        for copy in sent:
            copy.wait_recv()
        if p == 0:
            value = weight[rows_at(mine, size), :].astype(F32)
        else:
            value = steps[p - 1][6][rows_at(mine - start, size), :].astype(F32)
        for d in range(len(peers)):
            value += came[d].astype(F32)
        total[...] = value.astype(BF16)

    def prepare(f, h):
        y = rows[f, h].astype(F32)
        m.moved[f, :, pl.ds(128 * h, 128)] = jnp.concatenate([move(y, -1), y, move(y, 1)], 0).astype(BF16)

    for f in range(4):
        links.arrive(own.at[f], OWN + f)
    for f in range(4):
        for h in range(2):
            rows[f, h + 1] = own[f, h]
            prepare(f, h + 1)
    for f in range(4):
        links.arrive(m.prev_g.at[f], PREV + f)
        links.arrive(m.next_g.at[f], NEXT + f)
    for f in range(4):
        rows[f, 0] = jnp.where(r == 0, 0.0, m.prev_g[f].astype(F32)).astype(BF16)
        rows[f, 3] = jnp.where(r == ROWS - 1, 0.0, m.next_g[f].astype(F32)).astype(BF16)
        prepare(f, 0)
        prepare(f, 3)
    first = []
    for t in range(3):
        for h in range(3):
            acc = jnp.zeros((288, 384), F32)
            for f in range(4):
                source = f + t - 2
                if source < 0:
                    continue
                acc += dot_t(m.moved[f, :, pl.ds(128 * (2 - h), 256)], act[:, pl.ds(256 * source, 256)])
            for lane in range(3):
                line = (3 * (3 * t + h) + lane) * 288
                weight[pl.ds(line, 288), :] = acc[:, 128 * lane : 128 * lane + 128].astype(BF16)
        if t == 2:
            weight[pl.ds(27 * 288, 416), :] = jnp.zeros((416, 128), BF16)
        first.append(give(stripes[t], 0))
    for f in range(4):
        for h in range(3):
            for k in range(2):
                lines[f, pl.ds(96 * h, 96), pl.ds(128 * k, 128)] = rows[f, 2 - h + k]
    gain = gain_columns(gain_rows, 0)
    for f in range(4):
        acc = jnp.zeros((1152, 256), F32)
        for t in range(3):
            source = f + 2 - t
            if source > 3:
                continue
            acc += dot(w_t[t], lines[source])
        for h in range(2):
            y = acc[:, 128 * h : 128 * h + 128]
            total = move(y[:384], -1) + y[384:768] + move(y[768:], 1)
            v = jnp.concatenate([every[b, f, h] for b in range(CH)], 0).astype(F32)
            before = v * inv_in[2 * f + h : 2 * f + h + 1, :] * gain
            sig = sigmoid(before)
            slope = sig * (1.0 + before * (1.0 - sig))
            inner[2 * f + h : 2 * f + h + 1, :] = jnp.sum(v * slope * gain * total, 0, keepdims=True)
            for b in range(CH):
                part[b, f, h] = total[96 * b : 96 * b + 96].astype(BF16)
    second, third, parts = [], [], []
    parts.append(links.copy(part.at[at.sibling[1]], all_part.at[0], at.sibling))
    joined = links.copy(part.at[(1 - at.y_lo) * 2 + 1 - at.core], m.assist, at.sibling)
    for d in range(3):
        parts.append(links.copy(inner, all_inner.at[d], chs[d]))
    for n, steps in enumerate(stripes):
        take(steps, 0, first[n])
        second.append(give(steps, 1))
    joined.wait_recv()
    for f in range(4):
        both = part[at.c_near, f].astype(F32) + m.assist[f].astype(F32)
        m.near_part[f] = both.astype(BF16)
    parts.append(links.copy(m.near_part, all_part.at[1], at.near))
    for n, steps in enumerate(stripes):
        take(steps, 1, second[n])
        third.append(give(steps, 2))
    spread, kept = [], []
    for n, steps in enumerate(stripes):
        take(steps, 2, third[n])
        _, size, _, peers, mine, _, total = steps[2]
        m.spread[rows_at(mine, size), :] = total[...]
        spread.append([links.copy(total, m.spread.at[rows_at(mine, size)], peer) for peer in peers])
    for p in (1, 0):
        for n, steps in enumerate(stripes):
            for copy in spread[n]:
                copy.wait_recv()
            _, size, _, peers, mine, _, _ = steps[p]
            src = dst = m.spread.at[rows_at(mine, size)]
            if p == 0:
                dst = flat.at[rows_at(mine, size)]
                kept.append(pltpu.make_async_copy(src, dst, mark.at[n]))
                kept[n].start()
            spread[n] = [links.copy(src, dst, peer) for peer in peers]
    for copy in parts:
        copy.wait_recv()
    mean = (inner[...] + all_inner[0] + all_inner[1] + all_inner[2]) / 384.0
    gain = jnp.broadcast_to(gain_rows[c, 0:1, :], (128, 128)).T[:96]
    for f in range(4):
        for h in range(2):
            v = every[c, f, h].astype(F32)
            inv = inv_in[2 * f + h : 2 * f + h + 1, :]
            total = part[c, f, h].astype(F32)
            for d in range(2):
                total += all_part[d, f, h].astype(F32)
            before = v * inv * gain
            sig = sigmoid(before)
            scaled = total * (sig * (1.0 + before * (1.0 - sig))) * gain
            cube = inv * inv * inv * mean[2 * f + h : 2 * f + h + 1, :]
            out[f, h] = (own[f, h].astype(F32) + inv * scaled - v * cube).astype(BF16)
    for copy in kept:
        copy.wait()
    for copy in spread[0] + spread[1] + spread[2]:
        copy.wait_recv()


def whole(links, m):
    at = Place()
    front(links, at, m)
    attention(links, at, m)
    tail(links, at, m)
    links.finish()


def widen_kernel(scale, flat, grad, out, grad_out, near, wide, through, into, back):
    come = [
        pltpu.make_async_copy(flat.at[pl.ds(864 * k, 864)], near.at[k], into.at[k]) for k in range(9)
    ]
    go = [
        pltpu.make_async_copy(wide.at[k], out.at[pl.ds(288 * k, 288)], back.at[k]) for k in range(9)
    ]
    enter = pltpu.make_async_copy(grad, through, into.at[9])
    leave = pltpu.make_async_copy(through, grad_out, back.at[9])
    for copy in come:
        copy.start()
    enter.start()
    for k in range(9):
        if k == 4:
            enter.wait()
            leave.start()
        come[k].wait()
        for lane in range(3):
            piece = near[k, pl.ds(288 * lane, 288), :].astype(F32) * scale
            wide[k, :, pl.ds(128 * lane, 128)] = piece
        go[k].start()
    for copy in go:
        copy.wait()
    leave.wait()


def on_device(features, gain_in, w_conv, gain_attn, w_qkv, w_out, cotangent):
    near, far = pltpu.VMEM, pl.ANY
    held = {
        "feat": (features, far),
        "cot": (cotangent, far),
        "w_far": (w_conv, far),
        "gain_in": (gain_in.reshape(1, 96), near),
        "gain_attn": (gain_attn.reshape(1, 96), near),
        "w_qkv_far": (w_qkv, far),
        "w_out_far": (w_out, far),
    }
    made = {"out": ((4, 2, 96, 128), BF16, near), "flat": ((8192, 128), BF16, far)}
    b16 = {
        "every": (4, 4, 2, 96, 128),
        "w": (27, 96, 384),
        "w_qkv": (384, 1152),
        "w_out": (384, 384),
        "act": (384, 1024),
        "edge_out": (2, 4, 96, 128),
        "edge_in": (2, 4, 96, 128),
        "moved": (4, 288, 512),
        "res": (4, 2, 96, 128),
        "cot_frame": (4, 2, 96, 128),
        "res_frame": (4, 2, 96, 128),
        "full": (384, 256),
        "cot_full": (384, 256),
        "norm": (4, 256, 384),
        "q": (8, 384, 256),
        "g": (8, 384, 256),
        "k": (4, 256, 384),
        "v": (4, 256, 384),
        "k_t": (384, 1024),
        "prob": (8, 1024, 256),
        "grad_s": (8, 1024, 256),
        "far": (2, 384, 256),
        "via": (2, 2, 192, 256),
        "send": (2, 2, 384, 256),
        "came": (2, 2, 384, 256),
        "sib_out": (4, 384, 256),
        "sib_in": (4, 384, 256),
        "grad": (4, 2, 96, 128),
        "own": (4, 2, 96, 128),
        "prev_g": (4, 96, 128),
        "next_g": (4, 96, 128),
        "w_t": (3, 1152, 288),
        "rows": (4, 4, 96, 128),
        "lines": (4, 288, 256),
        "weight": (8192, 128),
        "spread": (8192, 128),
        "part": (4, 4, 2, 96, 128),
        "all_part": (2, 4, 2, 96, 128),
        "assist": (4, 2, 96, 128),
        "near_part": (4, 2, 96, 128),
    }
    for n, (size, counts) in enumerate(((2048, (2, 4, 4)), (3072, (4, 4, 2)), (3072, (4, 2, 4)))):
        for p, count in enumerate(counts):
            size //= count
            b16["came_%d_%d" % (n, p)] = (count - 1, size, 128)
            b16["total_%d_%d" % (n, p)] = (size, 128)
    f32 = {
        "inv_in": (8, 128),
        "conv_own": (4, 2, 96, 128),
        "gain_rows": (4, 8, 128),
        "exps": (4, 8, 256, 256),
        "grad_p": (4, 8, 256, 256),
        "tops": (4, 8, 256),
        "sums": (4, 8, 256),
        "deltas": (4, 8, 256),
        "stats": (3, 8, 256),
        "all_stats": (7, 3, 8, 256),
        "weights": (4, 8, 256),
        "delta": (8, 256),
        "nearest": (2, 2, 384, 256),
        "own_sum": (2, 384, 256),
        "own_q": (4, 384, 256),
        "inner": (8, 128),
        "all_inner": (3, 8, 128),
    }
    scratch = {n: pltpu.VMEM(s, BF16) for n, s in b16.items()}
    scratch |= {n: pltpu.VMEM(s, F32) for n, s in f32.items()}
    scratch["mark"] = pltpu.SemaphoreType.DMA((4,))
    out, flat = fused(0, whole, held, made, scratch, (SENDS, NEXT + 4))
    cell_scale = 1.0 / math.sqrt(32768)
    grad_weights, out = pl.pallas_call(
        functools.partial(widen_kernel, cell_scale),
        out_shape=[jax.ShapeDtypeStruct((2592, 384), F32), jax.ShapeDtypeStruct(out.shape, BF16)],
        in_specs=[pl.BlockSpec(memory_space=pl.ANY)] * 2,
        out_specs=[pl.BlockSpec(memory_space=pl.ANY)] * 2,
        scratch_shapes=[
            pltpu.VMEM((9, 864, 128), BF16),
            pltpu.VMEM((9, 288, 384), F32),
            pltpu.VMEM((4, 2, 96, 128), BF16),
            pltpu.SemaphoreType.DMA((10,)),
            pltpu.SemaphoreType.DMA((10,)),
        ],
        compiler_params=pltpu.CompilerParams(vmem_limit_bytes=VMEM_BYTES),
        name="widen",
    )(flat, out)
    return out, grad_weights.reshape(27, 96, 384)


def solution(mesh):
    return jax.shard_map(
        on_device,
        mesh=mesh,
        in_specs=(
            P(None, "row", "ch", None),
            P("ch"),
            P(None, "ch", None),
            P("ch"),
            P(),
            P(),
            P(None, "row", "ch", None),
        ),
        out_specs=(P(None, "row", "ch", None), P(None, "ch", None)),
        check_vma=False,
    )
```

```python
import functools
import math
import types

import jax
import jax.numpy as jnp
from jax import lax
from jax.experimental import pallas as pl
from jax.experimental.pallas import tpu as pltpu
from jax.sharding import PartitionSpec as P

EPSILON = 1e-06
MESH = pl.DeviceIdType.MESH
F32 = jnp.float32
BF16 = jnp.bfloat16
ROWS = 32
SENDS = 128
COT, RES, OWN, PREV, NEXT = range(SENDS, SENDS + 20, 4)
CH = 4
VMEM_BYTES = 60 * 1024 * 1024


def coords():
    return lax.axis_index("row"), lax.axis_index("ch")


def place(r, c):
    return lax.rem(r, 4), lax.rem(r // 4, 2), r // 8, c // 2, lax.rem(c, 2)


def device(x, y_hi, z, y_lo, core):
    return z * 8 + y_hi * 4 + x, y_lo * 2 + core


def owner(f, row):
    x, y_hi, z, _, _ = place(row, 0)
    return device(x, f // 2, z, f % 2, y_hi)


class Links:
    def __init__(self, send, recv):
        self.send, self.recv, self.sent, self.at = send, recv, [], 0

    def greet(self, peers, count):
        barrier = pltpu.get_barrier_semaphore()
        for peer in peers:
            pl.semaphore_signal(barrier, inc=1, device_id=peer, device_id_type=MESH)
        pl.semaphore_wait(barrier, count)

    def copy(self, src, dst, to, own=None, recv=None):
        k = self.at
        self.at += 1
        mark = self.recv.at[k if recv is None else recv]
        far = pltpu.make_async_remote_copy(
            src_ref=src,
            dst_ref=dst,
            send_sem=self.send.at[k],
            recv_sem=mark,
            device_id=to,
            device_id_type=MESH,
        )
        if own is None:
            far.start()
        else:
            pl.when(jnp.logical_not(own))(far.start)
            pl.when(own)(pltpu.make_async_copy(src, dst, mark).start)
        self.sent.append((far, own))
        return far

    def arrive(self, dst, k):
        pltpu.make_async_copy(dst, dst, self.recv.at[k]).wait()

    def finish(self):
        for far, own in self.sent:
            if own is None:
                far.wait_send()
            else:
                pl.when(jnp.logical_not(own))(far.wait_send)


def fused(cid, body, held, made, scratch, count):
    names = [*held, *made, *scratch]

    def kernel(*refs):
        body(Links(*refs[-2:]), types.SimpleNamespace(**dict(zip(names, refs))))

    return pl.pallas_call(
        kernel,
        out_shape=[jax.ShapeDtypeStruct(s, t) for s, t, _ in made.values()],
        in_specs=[pl.BlockSpec(memory_space=m) for _, m in held.values()],
        out_specs=[pl.BlockSpec(memory_space=m) for _, _, m in made.values()],
        scratch_shapes=[*scratch.values()] + [pltpu.SemaphoreType.DMA((n,)) for n in count],
        compiler_params=pltpu.CompilerParams(
            collective_id=cid, has_side_effects=True, vmem_limit_bytes=VMEM_BYTES
        ),
        name="fused_%d" % cid,
    )(*[array for array, _ in held.values()])


def dot(a, b):
    return lax.dot_general(a, b, (((1,), (0,)), ((), ())), preferred_element_type=F32)


def dot_t(a, b):
    return lax.dot_general(a, b, (((1,), (1,)), ((), ())), preferred_element_type=F32)


def move(block, by):
    lanes = block.shape[1]
    at = lax.broadcasted_iota(jnp.int32, block.shape, 1)
    if by > 0:
        return jnp.where(at == 0, 0.0, pltpu.roll(block, 1, axis=1))
    return jnp.where(at == lanes - 1, 0.0, pltpu.roll(block, lanes - 1, axis=1))


def ch_peers(r, c):
    return [(r, lax.rem(c + d, CH)) for d in range(1, CH)]


def near_rows(r):
    return lax.rem(r + ROWS - 1, ROWS), lax.rem(r + 1, ROWS)


def same(a, b):
    return jnp.logical_and(a[0] == b[0], a[1] == b[1])


def greet_frames(me, sources, targets):
    barrier = pltpu.get_barrier_semaphore()
    for peer in sources:
        def tell(peer=peer):
            pl.semaphore_signal(barrier, inc=1, device_id=peer, device_id_type=MESH)

        pl.when(jnp.logical_not(same(peer, me)))(tell)
    _, y_hi, _, _, core = place(*me)
    pl.semaphore_wait(barrier, len(targets) - 2 + 2 * (core - y_hi) * (core - y_hi))


def sigmoid(v):
    return 1.0 / (1.0 + jnp.exp(-v))


def gain_columns(rows, which):
    blocks = [jnp.broadcast_to(rows[b, which : which + 1, :], (128, 128)).T[:96] for b in range(CH)]
    return jnp.concatenate(blocks, 0)


class Place:
    def __init__(self):
        r, c = self.r, self.c = self.me = coords()
        x, y_hi, z, y_lo, core = self.x, self.y_hi, self.z, self.y_lo, self.core = place(r, c)
        self.slot = core * 4 + x
        self.frame = y_hi * 2 + y_lo
        self.low, self.high = near_rows(r)
        self.c_near = (1 - y_lo) * 2 + core
        self.sibling = (r, y_lo * 2 + 1 - core)
        self.near = (r, self.c_near)
        self.chs = ch_peers(r, c)
        self.xs = [device(lax.rem(x + d, 4), y_hi, z, y_lo, core) for d in range(1, 4)]
        self.cross = [device(lax.rem(x + d, 4), y_hi, z, y_lo, 1 - core) for d in range(1, 4)]
        self.zs = [device(x, y_hi, lax.rem(z + d, 4), y_lo, core) for d in range(1, 4)]
        self.across = device(x, 1 - y_hi, z, y_lo, core)
        self.targets = [owner(f, r) for f in range(4)]
        self.row = z * 8 + core * 4 + x
        self.sources = [(self.row, b) for b in range(CH)]

    def greet(self):
        at = self
        alike = at.chs + at.xs + at.cross + at.zs + [at.across, (at.low, at.c), (at.high, at.c)]
        there = [(i, b) for i in near_rows(at.row) for b in range(CH)]
        whose = [owner(f, i) for i in (at.low, at.high) for f in range(4)]
        greet_frames(at.me, at.targets + at.sources + whose + alike, at.targets + at.sources + there + alike)


def front(links, at, m):
    r, c, near, sibling = at.r, at.c, at.near, at.sibling
    every, act = m.every, m.act
    here = pltpu.make_async_copy(m.feat, every.at[c], m.mark.at[0])
    here.start()
    weights = pltpu.make_async_copy(m.w_far, m.w, m.mark.at[1])
    weights.start()
    projections = [
        pltpu.make_async_copy(m.w_out_far, m.w_out, m.mark.at[2]),
        pltpu.make_async_copy(m.w_qkv_far, m.w_qkv, m.mark.at[3]),
    ]
    for copy in projections:
        copy.start()
    m.gain_rows[c] = jnp.zeros((8, 128), F32)
    pad = jnp.zeros((1, 32), F32)
    m.gain_rows[c, 0:1, :] = jnp.concatenate([m.gain_in[...].astype(F32), pad], 1)
    m.gain_rows[c, 1:2, :] = jnp.concatenate([m.gain_attn[...].astype(F32), pad], 1)
    at.greet()
    pairs = [pl.ds(2 * p, 2) for p in range(2)]
    gains = [links.copy(m.gain_rows.at[c], m.gain_rows.at[c], to) for to in at.chs]
    to_near = [links.copy(m.feat.at[two], every.at[c, two], near) for two in pairs]
    to_sib = links.copy(m.feat, every.at[c], sibling)
    for copy in gains:
        copy.wait_recv()
    gain = gain_columns(m.gain_rows, 0)
    passed = []
    for p, two in enumerate(pairs):
        to_near[p].wait_recv()
        part = every.at[at.c_near, two]
        passed.append(links.copy(part, part, sibling))
    for f in range(4):
        own = same(at.targets[f], at.me)
        links.copy(m.cot.at[f], m.cot_frame.at[c], at.targets[f], own=own, recv=COT + c)

    def activate(n):
        v = jnp.concatenate([every[b, n // 2, lax.rem(n, 2)] for b in range(CH)], 0).astype(F32)
        inv = lax.rsqrt(jnp.mean(v * v, 0, keepdims=True) + EPSILON)
        before = v * inv * gain
        m.inv_in[pl.ds(n, 1), :] = inv
        act[:, pl.ds(pl.multiple_of(128 * n, 128), 128)] = (before * sigmoid(before)).astype(BF16)

    here.wait()
    to_sib.wait_recv()
    weights.wait()
    edges = []
    for p, two in enumerate(pairs):
        passed[p].wait_recv()

        def step(n, carry, p=p):
            activate(4 * p + n)
            return carry

        lax.fori_loop(0, 4, step, 0, unroll=2)
        for f in (2 * p, 2 * p + 1):
            by_tap = []
            for h in range(3):
                acc = jnp.zeros((288, 256), F32)
                for t in range(3):
                    source = f + t - 2
                    if source >= 0:
                        taps = m.w[pl.ds(9 * t + 3 * h, 3)].reshape(288, 384)
                        acc += dot(taps, act[:, pl.ds(256 * source, 256)])
                by_tap.append((acc[:, :128], acc[:, 128:]))
            lines = (
                by_tap[2][0],
                by_tap[2][1] + by_tap[1][0],
                by_tap[1][1] + by_tap[0][0],
                by_tap[0][1],
            )
            lines = [move(y[:96], 1) + y[96:192] + move(y[192:], -1) for y in lines]
            m.edge_out[0, f] = lines[0].astype(BF16)
            m.edge_out[1, f] = lines[3].astype(BF16)
            m.conv_own[f, 0] = lines[1]
            m.conv_own[f, 1] = lines[2]
        edges.append(links.copy(m.edge_out.at[0, two], m.edge_in.at[0, two], (at.low, c)))
        edges.append(links.copy(m.edge_out.at[1, two], m.edge_in.at[1, two], (at.high, c)))
    for b in range(CH):
        links.arrive(m.cot_frame.at[b], COT + b)
    for b in range(CH):
        for h in range(2):
            m.cot_full[pl.ds(96 * b, 96), pl.ds(128 * h, 128)] = m.cot_frame[b, h]
    for copy in projections:
        copy.wait()
    m.g[at.slot] = dot(m.w_out[...], m.cot_full[...]).astype(BF16)
    at.g_first = [links.copy(m.g.at[at.slot], m.g.at[at.slot], to) for to in (at.xs[0], at.xs[2], sibling)]
    for p in range(2):
        edges[2 * p].wait_recv()
        edges[2 * p + 1].wait_recv()
        for f in (2 * p, 2 * p + 1):
            before = jnp.where(r == 0, 0.0, m.edge_in[1, f].astype(F32))
            after = jnp.where(r == ROWS - 1, 0.0, m.edge_in[0, f].astype(F32))
            m.res[f, 0] = (every[c, f, 0].astype(F32) + (m.conv_own[f, 0] + before)).astype(BF16)
            m.res[f, 1] = (every[c, f, 1].astype(F32) + (m.conv_own[f, 1] + after)).astype(BF16)
            own = same(at.targets[f], at.me)
            links.copy(m.res.at[f], m.res_frame.at[c], at.targets[f], own=own, recv=RES + c)


def attention(links, at, m):
    scale = 1.0 / math.sqrt(384)
    x, z, core, slot, sibling = at.x, at.z, at.core, at.slot, at.sibling
    q, g, k, v, k_t = m.q, m.g, m.k, m.v, m.k_t
    w_qkv = m.w_qkv

    def relay_ring(first, ref, base, i, rows, peers, forward):
        on = []
        for side in range(2):
            first[side].wait_recv()
            came = base + lax.rem(i + 3 - 2 * side, 4)
            part = ref.at[came, pl.ds(rows * side, rows)]
            on.append(links.copy(part, part, peers[2 * side]))
            if forward:
                on.append(links.copy(ref.at[came], ref.at[came], sibling))
        return on

    g_on = relay_ring(at.g_first, g, core * 4, x, 192, at.xs, True)
    gain = gain_columns(m.gain_rows, 1)
    gain = jnp.concatenate([gain, gain], 1)
    for b in range(CH):
        links.arrive(m.res_frame.at[b], RES + b)
    for b in range(CH):
        for h in range(2):
            m.full[pl.ds(96 * b, 96), pl.ds(128 * h, 128)] = m.res_frame[b, h]
    centre = m.full[...].astype(F32)
    inv = lax.rsqrt(jnp.mean(centre * centre, 0, keepdims=True) + EPSILON)
    m.norm[z] = (centre * inv * gain).astype(BF16).astype(F32).T.astype(BF16)
    n_first = [links.copy(m.norm.at[z], m.norm.at[z], to) for to in (at.zs[0], at.zs[2])]
    q[slot] = dot(m.norm[z], w_qkv[:, :384]).T.astype(BF16)
    q_first = [links.copy(q.at[slot], q.at[slot], to) for to in (at.xs[0], at.xs[2], sibling)]

    def project(j):
        k[j] = dot(m.norm[j], w_qkv[:, 384:768]).astype(BF16)
        v[j] = dot(m.norm[j], w_qkv[:, 768:]).astype(BF16)
        k_t[:, pl.ds(pl.multiple_of(256 * j, 256), 256)] = k[j].T

    def tile(b, j):
        s = dot(k[j], q[b]) * scale
        top = jnp.max(s, 0, keepdims=True)
        e = jnp.exp(s - top)
        p = dot(v[j], g[b])
        m.exps[j, b] = e
        m.grad_p[j, b] = p
        m.tops[j, pl.ds(b, 1), :] = top
        m.sums[j, pl.ds(b, 1), :] = jnp.sum(e, 0, keepdims=True)
        m.deltas[j, pl.ds(b, 1), :] = jnp.sum(e * p, 0, keepdims=True)

    def block(dk, dx):
        other = core + dk - 2 * core * dk
        return other * 4 + lax.rem(x + dx, 4)

    def key(dz):
        return lax.rem(z + dz, 4)

    def tiles(count, unroll, which):
        def step(n, carry):
            dk, dx, dz = which(n)
            tile(block(dk, dx), key(dz))
            return carry

        lax.fori_loop(0, count, step, 0, unroll=unroll)

    project(z)
    g_on[1].wait_recv()
    g_on[3].wait_recv()
    far_x = core * 4 + lax.rem(x + 2, 4)
    at.g_first[2].wait_recv()
    q_first[2].wait_recv()
    tiles(2, 2, lambda n: (n, 0, 0))
    for t in range(3):
        for n in range(3):
            piece = jnp.concatenate([m.w[9 * t + 3 * h + n] for h in range(3)], 0)
            m.w_t[t, pl.ds(384 * n, 384), :] = piece.T
    n_on = relay_ring(n_first, m.norm, 0, z, 128, at.zs, False)
    q_on = relay_ring(q_first, q, core * 4, x, 192, at.xs, True)
    g_on[0].wait_recv()
    g_on[2].wait_recv()
    g_last = links.copy(g.at[far_x], g.at[far_x], sibling)
    project(key(1))
    project(key(3))
    tiles(4, 4, lambda n: (n // 2, 0, 1 + 2 * lax.rem(n, 2)))
    q_on[1].wait_recv()
    q_on[3].wait_recv()

    def beside(n):
        dz = n // 4
        return lax.rem(n // 2, 2), 1 + 2 * lax.rem(n, 2), dz + dz // 2

    tiles(12, 4, beside)
    q_on[0].wait_recv()
    q_on[2].wait_recv()
    q_last = links.copy(q.at[far_x], q.at[far_x], sibling)
    n_on[0].wait_recv()
    n_on[1].wait_recv()
    project(key(2))

    def beyond(n):
        dx = n // 2
        return lax.rem(n, 2), dx + dx // 2, 2

    tiles(6, 3, beyond)
    tiles(4, 4, lambda n: (0, 2, n))
    q_last.wait_recv()
    g_last.wait_recv()
    tiles(4, 4, lambda n: (1, 2, n))

    tops = [m.tops[j] for j in range(4)]
    top = functools.reduce(jnp.maximum, tops)
    shift = [jnp.exp(t - top) for t in tops]
    m.stats[0] = top
    m.stats[1] = sum(m.sums[j] * shift[j] for j in range(4))
    m.stats[2] = sum(m.deltas[j] * shift[j] for j in range(4))
    peers = at.xs + at.cross + [sibling]
    shared = [links.copy(m.stats, m.all_stats.at[n], to) for n, to in enumerate(peers)]
    for copy in shared:
        copy.wait_recv()
    parts = [m.stats] + [m.all_stats.at[n] for n in range(7)]
    top = functools.reduce(jnp.maximum, [p[0] for p in parts])
    total = sum(p[1] * jnp.exp(p[0] - top) for p in parts)
    m.delta[...] = sum(p[2] * jnp.exp(p[0] - top) for p in parts) / total
    for j in range(4):
        m.weights[j] = jnp.exp(m.tops[j] - top) / total

    def rows_of(j):
        return pl.ds(pl.multiple_of(256 * j, 256), 256)

    def weigh(b, j):
        prob = m.exps[j, b] * m.weights[j, pl.ds(b, 1), :]
        m.prob[b, rows_of(j), :] = prob.astype(BF16)
        m.grad_s[b, rows_of(j), :] = (prob * (m.grad_p[j, b] - m.delta[pl.ds(b, 1), :])).astype(BF16)

    def key_grad(j):
        for_k = sum(dot_t(m.grad_s[b, rows_of(j), :], q[b]) for b in range(8)) * scale
        for_v = sum(dot_t(m.prob[b, rows_of(j), :], g[b]) for b in range(8))
        return dot_t(w_qkv[:, 384:768], for_k.astype(BF16)) + dot_t(w_qkv[:, 768:], for_v.astype(BF16))

    halves = [pl.ds(0, 192), pl.ds(192, 192)]
    rings = ((at.zs[0], at.zs[2]), (at.xs[0], at.xs[2]))
    by_way, back = {}, []

    def send_far(kind, value):
        m.far[kind] = value.astype(BF16)
        for i in range(2):
            by_way[kind, i] = links.copy(m.far.at[kind, halves[i]], m.via.at[kind, i], rings[kind][i])

    def send_half(kind, i, half, value):
        m.send[kind, i, halves[half]] = value.astype(BF16)
        src, dst = m.send.at[kind, i, halves[half]], m.came.at[kind, i, halves[half]]
        back.append(links.copy(src, dst, rings[kind][i]))

    def send_near(kind, i, value):
        m.nearest[kind, i] = value
        send_half(kind, i, 1 - i, value[192 * (1 - i) : 192 * (2 - i)])

    def send_added(kind):
        for i in range(2):
            by_way[kind, i].wait_recv()
            send_half(kind, i, i, m.nearest[kind, i, halves[i], :] + m.via[kind, i].astype(F32))

    def weigh_all(dk):
        def step(n, carry):
            weigh(block(dk, lax.rem(n, 4)), key(n // 4))
            return carry

        lax.fori_loop(0, 16, step, 0, unroll=4)

    def query_grads(dk, put):
        def step(dx, carry):
            put(dx, dot(k_t[...], m.grad_s[block(dk, dx)]) * scale)
            return carry

        lax.fori_loop(0, 4, step, 0)

    def for_sibling(dx, value):
        m.sib_out[dx] = value.astype(BF16)

    def for_own(dx, value):
        m.own_q[dx] = value

    weigh_all(1)
    query_grads(1, for_sibling)
    sib = links.copy(m.sib_out, m.sib_in, sibling)
    weigh_all(0)
    send_far(0, key_grad(key(2)))
    query_grads(0, for_own)
    sib.wait_recv()

    def query_grad(dx):
        return m.own_q[dx] + m.sib_in[dx].astype(F32)

    send_far(1, query_grad(2))
    send_near(1, 0, query_grad(1))
    send_near(1, 1, query_grad(3))

    def near_keys(i, carry):
        m.nearest[0, i] = key_grad(key(1 + 2 * i))
        return carry

    lax.fori_loop(0, 2, near_keys, 0)
    for i in range(2):
        send_half(0, i, 1 - i, m.nearest[0, i, halves[1 - i], :])
    send_added(0)
    send_added(1)
    m.own_sum[0] = key_grad(z)
    m.own_sum[1] = query_grad(0)
    for copy in back:
        copy.wait_recv()
    by_key, by_query = [
        m.own_sum[n] + m.came[n, 0].astype(F32) + m.came[n, 1].astype(F32) for n in range(2)
    ]
    back_normed = dot(w_qkv[:, :384], by_query.astype(BF16)) + by_key
    scaled = back_normed.astype(BF16).astype(F32) * gain
    centre = m.full[...].astype(F32)
    inner = jnp.mean(centre * scaled, 0, keepdims=True)
    out = m.cot_full[...].astype(F32) + inv * scaled - centre * (inv * inv * inv * inner)
    for b in range(CH):
        for h in range(2):
            m.grad[b, h] = out[96 * b : 96 * b + 96, 128 * h : 128 * h + 128].astype(BF16)
    row_low, row_high = near_rows(at.row)
    for b in range(CH):
        to = at.sources[b]
        links.copy(m.grad.at[b], m.own.at[at.frame], to, own=same(to, at.me), recv=OWN + at.frame)
    for b in range(CH):
        links.copy(m.grad.at[b, 1], m.prev_g.at[at.frame], (row_high, b), recv=PREV + at.frame)
        links.copy(m.grad.at[b, 0], m.next_g.at[at.frame], (row_low, b), recv=NEXT + at.frame)


def tail(links, at, m):
    r, c, x, y_hi, z = at.r, at.c, at.x, at.y_hi, at.z
    xs, zs, across, chs = at.xs, at.zs, at.across, at.chs
    own, act, w_t, every, inv_in, gain_rows = m.own, m.act, m.w_t, m.every, m.inv_in, m.gain_rows
    rows, lines, weight, part, all_part, inner, all_inner = m.rows, m.lines, m.weight, m.part, m.all_part, m.inner, m.all_inner
    mark, flat, out = m.mark, m.flat, m.out
    ring_x = (x, [lax.rem(x + d, 4) for d in range(1, 4)], xs)
    ring_z = (z, [lax.rem(z + d, 4) for d in range(1, 4)], zs)
    ring_y = (y_hi, [1 - y_hi], [across])
    stripes = []
    for n, (base, size, rings) in enumerate(
        (
            (0, 2048, (ring_y, ring_x, ring_z)),
            (2048, 3072, (ring_x, ring_z, ring_y)),
            (5120, 3072, (ring_z, ring_y, ring_x)),
        )
    ):
        steps, at_row = [], base
        for p, (place_on, places, peers) in enumerate(rings):
            size //= len(peers) + 1
            start = at_row
            at_row = at_row + place_on * size
            came, total = getattr(m, "came_%d_%d" % (n, p)), getattr(m, "total_%d_%d" % (n, p))
            steps.append((start, size, places, peers, at_row, came, total))
        stripes.append(steps)

    def rows_at(start, size):
        return pl.ds(pl.multiple_of(start, 16), size)

    def give(steps, p):
        start, size, places, peers, _, came, _ = steps[p]
        sent = []
        for d, peer in enumerate(peers):
            if p == 0:
                src = weight.at[rows_at(start + places[d] * size, size)]
            else:
                src = steps[p - 1][6].at[rows_at(places[d] * size, size)]
            sent.append(links.copy(src, came.at[d], peer))
        return sent

    def take(steps, p, sent):
        start, size, _, peers, mine, came, total = steps[p]
        for copy in sent:
            copy.wait_recv()
        if p == 0:
            value = weight[rows_at(mine, size), :].astype(F32)
        else:
            value = steps[p - 1][6][rows_at(mine - start, size), :].astype(F32)
        for d in range(len(peers)):
            value += came[d].astype(F32)
        total[...] = value.astype(BF16)

    def prepare(f, h):
        y = rows[f, h].astype(F32)
        m.moved[f, :, pl.ds(128 * h, 128)] = jnp.concatenate([move(y, -1), y, move(y, 1)], 0).astype(BF16)

    for f in range(4):
        links.arrive(own.at[f], OWN + f)
    for f in range(4):
        for h in range(2):
            rows[f, h + 1] = own[f, h]
            prepare(f, h + 1)
    for f in range(4):
        links.arrive(m.prev_g.at[f], PREV + f)
        links.arrive(m.next_g.at[f], NEXT + f)
    for f in range(4):
        rows[f, 0] = jnp.where(r == 0, 0.0, m.prev_g[f].astype(F32)).astype(BF16)
        rows[f, 3] = jnp.where(r == ROWS - 1, 0.0, m.next_g[f].astype(F32)).astype(BF16)
        prepare(f, 0)
        prepare(f, 3)
    first = []
    for t in range(3):
        for h in range(3):
            acc = jnp.zeros((288, 384), F32)
            for f in range(4):
                source = f + t - 2
                if source < 0:
                    continue
                acc += dot_t(m.moved[f, :, pl.ds(128 * (2 - h), 256)], act[:, pl.ds(256 * source, 256)])
            for lane in range(3):
                line = (3 * (3 * t + h) + lane) * 288
                weight[pl.ds(line, 288), :] = acc[:, 128 * lane : 128 * lane + 128].astype(BF16)
        if t == 2:
            weight[pl.ds(27 * 288, 416), :] = jnp.zeros((416, 128), BF16)
        first.append(give(stripes[t], 0))
    for f in range(4):
        for h in range(3):
            for k in range(2):
                lines[f, pl.ds(96 * h, 96), pl.ds(128 * k, 128)] = rows[f, 2 - h + k]
    gain = gain_columns(gain_rows, 0)
    for f in range(4):
        acc = jnp.zeros((1152, 256), F32)
        for t in range(3):
            source = f + 2 - t
            if source > 3:
                continue
            acc += dot(w_t[t], lines[source])
        for h in range(2):
            y = acc[:, 128 * h : 128 * h + 128]
            total = move(y[:384], -1) + y[384:768] + move(y[768:], 1)
            v = jnp.concatenate([every[b, f, h] for b in range(CH)], 0).astype(F32)
            before = v * inv_in[2 * f + h : 2 * f + h + 1, :] * gain
            sig = sigmoid(before)
            slope = sig * (1.0 + before * (1.0 - sig))
            inner[2 * f + h : 2 * f + h + 1, :] = jnp.sum(v * slope * gain * total, 0, keepdims=True)
            for b in range(CH):
                part[b, f, h] = total[96 * b : 96 * b + 96].astype(BF16)
    second, third, parts = [], [], []
    parts.append(links.copy(part.at[at.sibling[1]], all_part.at[0], at.sibling))
    joined = links.copy(part.at[(1 - at.y_lo) * 2 + 1 - at.core], m.assist, at.sibling)
    for d in range(3):
        parts.append(links.copy(inner, all_inner.at[d], chs[d]))
    for n, steps in enumerate(stripes):
        take(steps, 0, first[n])
        second.append(give(steps, 1))
    for n, steps in enumerate(stripes):
        take(steps, 1, second[n])
        third.append(give(steps, 2))
    joined.wait_recv()
    for f in range(4):
        both = part[at.c_near, f].astype(F32) + m.assist[f].astype(F32)
        m.near_part[f] = both.astype(BF16)
    parts.append(links.copy(m.near_part, all_part.at[1], at.near))
    spread, kept = [], []
    for n, steps in enumerate(stripes):
        take(steps, 2, third[n])
        _, size, _, peers, mine, _, total = steps[2]
        m.spread[rows_at(mine, size), :] = total[...]
        spread.append([links.copy(total, m.spread.at[rows_at(mine, size)], peer) for peer in peers])
    for p in (1, 0):
        for n, steps in enumerate(stripes):
            for copy in spread[n]:
                copy.wait_recv()
            _, size, _, peers, mine, _, _ = steps[p]
            src = dst = m.spread.at[rows_at(mine, size)]
            if p == 0:
                dst = flat.at[rows_at(mine, size)]
                kept.append(pltpu.make_async_copy(src, dst, mark.at[n]))
                kept[n].start()
            spread[n] = [links.copy(src, dst, peer) for peer in peers]
    for copy in parts:
        copy.wait_recv()
    mean = (inner[...] + all_inner[0] + all_inner[1] + all_inner[2]) / 384.0
    gain = jnp.broadcast_to(gain_rows[c, 0:1, :], (128, 128)).T[:96]
    for f in range(4):
        for h in range(2):
            v = every[c, f, h].astype(F32)
            inv = inv_in[2 * f + h : 2 * f + h + 1, :]
            total = part[c, f, h].astype(F32)
            for d in range(2):
                total += all_part[d, f, h].astype(F32)
            before = v * inv * gain
            sig = sigmoid(before)
            scaled = total * (sig * (1.0 + before * (1.0 - sig))) * gain
            cube = inv * inv * inv * mean[2 * f + h : 2 * f + h + 1, :]
            out[f, h] = (own[f, h].astype(F32) + inv * scaled - v * cube).astype(BF16)
    for copy in kept:
        copy.wait()
    for copy in spread[0] + spread[1] + spread[2]:
        copy.wait_recv()


def whole(links, m):
    at = Place()
    front(links, at, m)
    attention(links, at, m)
    tail(links, at, m)
    links.finish()


def widen_kernel(scale, flat, grad, out, grad_out, near, wide, through, into, back):
    come = [
        pltpu.make_async_copy(flat.at[pl.ds(864 * k, 864)], near.at[k], into.at[k]) for k in range(9)
    ]
    go = [
        pltpu.make_async_copy(wide.at[k], out.at[pl.ds(288 * k, 288)], back.at[k]) for k in range(9)
    ]
    enter = pltpu.make_async_copy(grad, through, into.at[9])
    leave = pltpu.make_async_copy(through, grad_out, back.at[9])
    for copy in come:
        copy.start()
    enter.start()
    for k in range(9):
        if k == 4:
            enter.wait()
            leave.start()
        come[k].wait()
        for lane in range(3):
            piece = near[k, pl.ds(288 * lane, 288), :].astype(F32) * scale
            wide[k, :, pl.ds(128 * lane, 128)] = piece
        go[k].start()
    for copy in go:
        copy.wait()
    leave.wait()


def on_device(features, gain_in, w_conv, gain_attn, w_qkv, w_out, cotangent):
    near, far = pltpu.VMEM, pl.ANY
    held = {
        "feat": (features, far),
        "cot": (cotangent, far),
        "w_far": (w_conv, far),
        "gain_in": (gain_in.reshape(1, 96), near),
        "gain_attn": (gain_attn.reshape(1, 96), near),
        "w_qkv_far": (w_qkv, far),
        "w_out_far": (w_out, far),
    }
    made = {"out": ((4, 2, 96, 128), BF16, near), "flat": ((8192, 128), BF16, far)}
    b16 = {
        "every": (4, 4, 2, 96, 128),
        "w": (27, 96, 384),
        "w_qkv": (384, 1152),
        "w_out": (384, 384),
        "act": (384, 1024),
        "edge_out": (2, 4, 96, 128),
        "edge_in": (2, 4, 96, 128),
        "moved": (4, 288, 512),
        "res": (4, 2, 96, 128),
        "cot_frame": (4, 2, 96, 128),
        "res_frame": (4, 2, 96, 128),
        "full": (384, 256),
        "cot_full": (384, 256),
        "norm": (4, 256, 384),
        "q": (8, 384, 256),
        "g": (8, 384, 256),
        "k": (4, 256, 384),
        "v": (4, 256, 384),
        "k_t": (384, 1024),
        "prob": (8, 1024, 256),
        "grad_s": (8, 1024, 256),
        "far": (2, 384, 256),
        "via": (2, 2, 192, 256),
        "send": (2, 2, 384, 256),
        "came": (2, 2, 384, 256),
        "sib_out": (4, 384, 256),
        "sib_in": (4, 384, 256),
        "grad": (4, 2, 96, 128),
        "own": (4, 2, 96, 128),
        "prev_g": (4, 96, 128),
        "next_g": (4, 96, 128),
        "w_t": (3, 1152, 288),
        "rows": (4, 4, 96, 128),
        "lines": (4, 288, 256),
        "weight": (8192, 128),
        "spread": (8192, 128),
        "part": (4, 4, 2, 96, 128),
        "all_part": (2, 4, 2, 96, 128),
        "assist": (4, 2, 96, 128),
        "near_part": (4, 2, 96, 128),
    }
    for n, (size, counts) in enumerate(((2048, (2, 4, 4)), (3072, (4, 4, 2)), (3072, (4, 2, 4)))):
        for p, count in enumerate(counts):
            size //= count
            b16["came_%d_%d" % (n, p)] = (count - 1, size, 128)
            b16["total_%d_%d" % (n, p)] = (size, 128)
    f32 = {
        "inv_in": (8, 128),
        "conv_own": (4, 2, 96, 128),
        "gain_rows": (4, 8, 128),
        "exps": (4, 8, 256, 256),
        "grad_p": (4, 8, 256, 256),
        "tops": (4, 8, 256),
        "sums": (4, 8, 256),
        "deltas": (4, 8, 256),
        "stats": (3, 8, 256),
        "all_stats": (7, 3, 8, 256),
        "weights": (4, 8, 256),
        "delta": (8, 256),
        "nearest": (2, 2, 384, 256),
        "own_sum": (2, 384, 256),
        "own_q": (4, 384, 256),
        "inner": (8, 128),
        "all_inner": (3, 8, 128),
    }
    scratch = {n: pltpu.VMEM(s, BF16) for n, s in b16.items()}
    scratch |= {n: pltpu.VMEM(s, F32) for n, s in f32.items()}
    scratch["mark"] = pltpu.SemaphoreType.DMA((4,))
    out, flat = fused(0, whole, held, made, scratch, (SENDS, NEXT + 4))
    cell_scale = 1.0 / math.sqrt(32768)
    grad_weights, out = pl.pallas_call(
        functools.partial(widen_kernel, cell_scale),
        out_shape=[jax.ShapeDtypeStruct((2592, 384), F32), jax.ShapeDtypeStruct(out.shape, BF16)],
        in_specs=[pl.BlockSpec(memory_space=pl.ANY)] * 2,
        out_specs=[pl.BlockSpec(memory_space=pl.ANY)] * 2,
        scratch_shapes=[
            pltpu.VMEM((9, 864, 128), BF16),
            pltpu.VMEM((9, 288, 384), F32),
            pltpu.VMEM((4, 2, 96, 128), BF16),
            pltpu.SemaphoreType.DMA((10,)),
            pltpu.SemaphoreType.DMA((10,)),
        ],
        compiler_params=pltpu.CompilerParams(vmem_limit_bytes=VMEM_BYTES),
        name="widen",
    )(flat, out)
    return out, grad_weights.reshape(27, 96, 384)


def solution(mesh):
    return jax.shard_map(
        on_device,
        mesh=mesh,
        in_specs=(
            P(None, "row", "ch", None),
            P("ch"),
            P(None, "ch", None),
            P("ch"),
            P(),
            P(),
            P(None, "row", "ch", None),
        ),
        out_specs=(P(None, "row", "ch", None), P(None, "ch", None)),
        check_vma=False,
    )
```
